32 devices in a mesh: ctx: 16 (over z, y, core), tp: 2 (over x).
Axes of the slice: x: 2, y: 2, z: 4, core: 2. Of those that a mesh axis runs over, the one named last changes fastest.
Arguments:
- query_heads: bfloat16 [2048, 8192], P('ctx', 'tp'), may hold values from -32 to 32
- key_heads: bfloat16 [2048, 8192], P('ctx', 'tp'), may hold values from -6 to 6
- value_heads: bfloat16 [2048, 8192], P('ctx', 'tp'), may hold values from -6 to 6
- hyena_query: bfloat16 [2048, 8192], P('ctx', 'tp'), may hold values from -6 to 6
- hyena_key: bfloat16 [2048, 8192], P('ctx', 'tp'), may hold values from -6 to 6
- hyena_value: bfloat16 [2048, 8192], P('ctx', 'tp'), may hold values from -6 to 6
- short_filter: float32 [3, 7, 8192], P(None, None, 'tp'), may hold values from -2 to 2
- long_filter: float32 [2048, 512], P('ctx', 'tp'), may hold values from -0.125 to 0.125
- output_grad: bfloat16 [2048, 8192], P('ctx', 'tp'), may hold values from -70 to 70
Outputs:
- attention: bfloat16 [2048, 8192], P('ctx', 'tp')
- query_grad: bfloat16 [2048, 8192], P('ctx', 'tp')
- key_grad: bfloat16 [2048, 8192], P('ctx', 'tp')
- value_grad: bfloat16 [2048, 8192], P('ctx', 'tp')
- filter_grad: float32 [2048, 512], P('ctx', 'tp')
The draws below stay inside these ranges and needn't reach their ends.
All inputs are finite; a program needn't handle non-finite values.
Results may differ from the reference program's by a relative error of at most 0.0049.
Values may be sent and summed in bfloat16 or wider, within the bound.
No kernel may reach another device: no remote copies, remote signals or barrier semaphores. Data moves between devices by JAX's collectives and lax.ppermute only.
A program may use at most 128 MiB of HBM per device.

```python
import math
import jax
import jax.numpy as jnp
from jax import lax

HEADS = 64
HEAD_DIM = 128
GROUPS = 512
TOK_DEV = 128
SHORT = 7
D = 8192
SEQ = 2048


def draw_pair(key):
    key_query, key_key = jax.random.split(jax.random.fold_in(key, 17), 2)
    queries = jnp.clip(jax.random.normal(key_query, (SEQ, D), jnp.float32), -6.0, 6.0)
    keys = jnp.clip(jax.random.normal(key_key, (SEQ, D), jnp.float32), -6.0, 6.0)
    return (queries, keys)


def draw_query_heads(key, part):
    return draw_pair(key)[0].astype(jnp.bfloat16)


def draw_key_heads(key, part):
    return draw_pair(key)[1].astype(jnp.bfloat16)


def draw_output_grad(key, part):
    key_noise, key_scale = jax.random.split(jax.random.fold_in(key, 29), 2)
    column = jnp.arange(D).astype(jnp.float32) / D
    jitter = jax.random.uniform(key_scale, (D,), jnp.float32)
    spread = jnp.exp(math.log(10.0) * (0.5 * column + 0.5 * jitter))
    noise = jnp.clip(jax.random.normal(key_noise, (SEQ, D), jnp.float32), -4.0, 4.0)
    values = noise * spread[None, :]
    return values.astype(jnp.bfloat16)


def block_scale(stream_key, dims, shards, smallest, top_value):
    def one(axis_at, blocks):
        heights = jax.random.uniform(jax.random.fold_in(jax.random.fold_in(stream_key, 6), axis_at), (blocks,), jnp.float32, smallest / len(shards), top_value / len(shards))
        return jnp.repeat(jnp.exp(heights), dims[axis_at] // blocks).reshape((-1,) + (1,) * (len(dims) - axis_at - 1))

    level = one(*shards[0])
    for cut in shards[1:]:
        level = level * one(*cut)
    return level


def gaussian(own_key, extent, scale, reach, pieces=(), kind=jnp.bfloat16):
    values = jax.random.normal(own_key, extent, jnp.float32) * scale
    if len(pieces) > 0:
        values = block_scale(own_key, extent, pieces, -0.22, 0.18) * values
    return jnp.clip(values, min=-reach, max=reach).astype(kind)


def setup_inputs(seed: int = 0) -> dict:
    arg_keys = jax.random.split(jax.random.key(seed), 10)
    query_heads = draw_query_heads(jax.random.fold_in(arg_keys[9], 71), 0)
    key_heads = draw_key_heads(jax.random.fold_in(arg_keys[9], 71), 0)
    value_heads = gaussian(arg_keys[2], (SEQ, D), 1.0, 6.0, ((0, 16), (1, 2)))
    hyena_query = gaussian(arg_keys[3], (SEQ, D), 1.0, 6.0, ((0, 16), (1, 2)))
    hyena_key = gaussian(arg_keys[4], (SEQ, D), 1.0, 6.0, ((0, 16), (1, 2)))
    hyena_value = gaussian(arg_keys[5], (SEQ, D), 1.0, 6.0, ((0, 16), (1, 2)))
    short_filter = gaussian(arg_keys[6], (3, SHORT, D), SHORT ** -0.5, 2.0, ((2, 2),), jnp.float32)
    long_filter = gaussian(arg_keys[7], (SEQ, GROUPS), SEQ ** -0.5, 0.125, ((0, 16), (1, 2)), jnp.float32)
    output_grad = draw_output_grad(jax.random.fold_in(arg_keys[9], 71), 0)
    return {"query_heads": query_heads, "key_heads": key_heads, "value_heads": value_heads, "hyena_query": hyena_query, "hyena_key": hyena_key, "hyena_value": hyena_value, "short_filter": short_filter, "long_filter": long_filter, "output_grad": output_grad}


def attend_blocks(query_heads, key_heads, value_heads):
    blocks = SEQ // TOK_DEV
    queries = query_heads.astype(jnp.float32).reshape(SEQ, HEADS, HEAD_DIM)
    padding = jnp.zeros((TOK_DEV, HEADS, HEAD_DIM), jnp.float32)
    keys_padded = jnp.concatenate([padding, key_heads.astype(jnp.float32).reshape(SEQ, HEADS, HEAD_DIM)], 0)
    values_padded = jnp.concatenate([padding, value_heads.astype(jnp.float32).reshape(SEQ, HEADS, HEAD_DIM)], 0)

    def single(block):
        start = (block * TOK_DEV).astype(jnp.int32)
        query_rows = lax.dynamic_slice_in_dim(queries, start, TOK_DEV, 0)
        key_rows = lax.dynamic_slice_in_dim(keys_padded, start, 2 * TOK_DEV, 0)
        value_rows = lax.dynamic_slice_in_dim(values_padded, start, 2 * TOK_DEV, 0)
        scores = jnp.einsum('qhd,khd->hqk', query_rows, key_rows) * (1.0 / math.sqrt(HEAD_DIM))
        query_pos = start + jnp.arange(TOK_DEV, dtype=jnp.int32)[:, None]
        key_pos = start - TOK_DEV + jnp.arange(2 * TOK_DEV, dtype=jnp.int32)[None, :]
        allowed = (key_pos <= query_pos) & (key_pos >= 0)
        masked = jnp.where(allowed[None], scores, -jnp.inf)
        largest = lax.optimization_barrier(jnp.max(masked, axis=2, keepdims=True))
        raised = jnp.exp(masked - largest)
        weights = (raised / lax.optimization_barrier(jnp.sum(raised, axis=2, keepdims=True))).astype(jnp.bfloat16)
        mixed = jnp.einsum('hqk,khd->qhd', weights.astype(jnp.float32), value_rows)
        return mixed.astype(jnp.bfloat16)
    result = lax.map(single, jnp.arange(blocks, dtype=jnp.int32))
    return result.reshape(SEQ, HEADS * HEAD_DIM)

def causal_short(signal, filter_taps):
    padded = jnp.concatenate([jnp.zeros((SHORT - 1, D), jnp.float32), signal], 0)
    total = jnp.zeros((SEQ, D), jnp.float32)
    for offset in range(SHORT):
        total = total + filter_taps[offset] * padded[SHORT - 1 - offset:SHORT - 1 - offset + SEQ]
    return total

def anti_short(signal, filter_taps):
    padded = jnp.concatenate([signal, jnp.zeros((SHORT - 1, D), jnp.float32)], 0)
    total = jnp.zeros((SEQ, D), jnp.float32)
    for offset in range(SHORT):
        total = total + filter_taps[offset] * padded[offset:offset + SEQ]
    return total

def long_products(mixed, filter_taps, delta):
    group = math.gcd(D, 512)
    count = D // group
    stacked = jnp.stack([mixed, filter_taps, delta]).reshape(3, SEQ, count, group).transpose(2, 0, 1, 3)

    def one_group(signals):
        spectra = jnp.fft.rfft(signals, n=2 * SEQ, axis=1)
        mixed_spec, filter_spec, delta_spec = (spectra[0], spectra[1], spectra[2])
        conv = jnp.fft.irfft(filter_spec * mixed_spec, n=2 * SEQ, axis=0)[:SEQ]
        grad_mixed = jnp.fft.irfft(jnp.conj(filter_spec) * delta_spec, n=2 * SEQ, axis=0)[:SEQ]
        raw_grad = jnp.fft.irfft(jnp.conj(mixed_spec) * delta_spec, n=2 * SEQ, axis=0)[:SEQ]
        return jnp.stack([conv, grad_mixed, raw_grad]).astype(jnp.float32)
    result = lax.map(one_group, stacked)
    result = result.transpose(1, 2, 0, 3).reshape(3, SEQ, D)
    return (result[0], result[1], result[2])

def reference(query_heads, key_heads, value_heads, hyena_query, hyena_key, hyena_value, short_filter, long_filter, output_grad):
    attention = attend_blocks(query_heads, key_heads, value_heads)
    short_q = causal_short(hyena_query.astype(jnp.float32), short_filter[0])
    short_k = causal_short(hyena_key.astype(jnp.float32), short_filter[1])
    short_v = causal_short(hyena_value.astype(jnp.float32), short_filter[2])
    mixed = short_k * short_v
    upstream = output_grad.astype(jnp.float32)
    grad_conv = upstream * short_q
    channel_filter = jnp.repeat(long_filter, D // GROUPS, axis=1)
    conv, grad_mixed, channel_grad = long_products(mixed, channel_filter, grad_conv)
    raw_grad = lax.optimization_barrier(jnp.sum(channel_grad.reshape(SEQ, GROUPS, D // GROUPS), axis=2))
    grad_short_q = upstream * conv
    grad_short_k = grad_mixed * short_v
    grad_short_v = grad_mixed * short_k
    query_grad = anti_short(grad_short_q, short_filter[0]).astype(jnp.bfloat16)
    key_grad = anti_short(grad_short_k, short_filter[1]).astype(jnp.bfloat16)
    value_grad = anti_short(grad_short_v, short_filter[2]).astype(jnp.bfloat16)
    grad_norm = jnp.sqrt(jnp.sum(raw_grad * raw_grad))
    factor = jnp.minimum(1.0, math.sqrt(SEQ * GROUPS) / grad_norm)
    filter_grad = raw_grad * factor
    return (attention, query_grad, key_grad, value_grad, filter_grad)
```

```python
import functools
import math

import jax
import jax.numpy as jnp
from jax import lax
from jax.experimental import pallas as pl
from jax.experimental.pallas import tpu as pltpu
from jax.sharding import PartitionSpec as P

HEAD_DIM = 128
LANES = 128
EDGE = 8
F32 = jnp.float32
BF16 = jnp.bfloat16
VMEM_BYTES = 40 * 1024 * 1024


def params():
    return pltpu.CompilerParams(vmem_limit_bytes=VMEM_BYTES)


def shifted(block, axis, distance):
    devices = range(lax.axis_size(axis))
    route = [(i - distance, i) for i in devices if i - distance in devices]
    return lax.ppermute(block, axis, route)


def round_up(value, step):
    return -(-value // step) * step


def attend_kernel(place_ref, q_ref, k_ref, v_ref, kp_ref, vp_ref, out_ref):
    rows = q_ref.shape[0]
    row = lax.broadcasted_iota(jnp.int32, (rows, rows), 0)
    col = lax.broadcasted_iota(jnp.int32, (rows, rows), 1)
    own_ok = col <= row
    prev_ok = jnp.broadcast_to(place_ref[0], (rows, rows)) > 0
    contract = (((1,), (1,)), ((), ()))
    for head in range(q_ref.shape[1] // HEAD_DIM):
        at = slice(head * HEAD_DIM, (head + 1) * HEAD_DIM)
        scale = 1.0 / math.sqrt(HEAD_DIM)
        query = q_ref[:, at]
        own = lax.dot_general(query, k_ref[:, at], contract, preferred_element_type=F32) * scale
        prev = lax.dot_general(query, kp_ref[:, at], contract, preferred_element_type=F32) * scale
        own = jnp.where(own_ok, own, -jnp.inf)
        prev = jnp.where(prev_ok, prev, -jnp.inf)
        largest = jnp.max(jnp.maximum(own, prev), axis=1, keepdims=True)
        own = jnp.exp(own - largest)
        prev = jnp.exp(prev - largest)
        total = jnp.sum(own + prev, axis=1, keepdims=True)
        inverse = 1.0 / total
        own = (own * inverse).astype(BF16)
        prev = (prev * inverse).astype(BF16)
        mixed = jnp.dot(own, v_ref[:, at], preferred_element_type=F32) + jnp.dot(
            prev, vp_ref[:, at], preferred_element_type=F32
        )
        out_ref[:, at] = mixed.astype(BF16)


def attend(query, key, value, key_prev, value_prev, position):
    rows, channels = query.shape
    tile = min(512, channels)
    block = pl.BlockSpec((rows, tile), lambda i: (0, i))
    heads = channels // HEAD_DIM
    return pl.pallas_call(
        attend_kernel,
        grid=(channels // tile,),
        in_specs=[pl.BlockSpec(memory_space=pltpu.SMEM)] + [block] * 5,
        out_specs=block,
        out_shape=jax.ShapeDtypeStruct((rows, channels), BF16),
        compiler_params=params(),
        cost_estimate=pl.CostEstimate(
            flops=8 * heads * rows * rows * HEAD_DIM,
            bytes_accessed=12 * rows * channels,
            transcendentals=2 * heads * rows * rows,
        ),
        name="attend",
    )(position.astype(jnp.int32).reshape(1), query, key, value, key_prev, value_prev)


def taps_causal(ext_ref, before, signal, filter_taps):
    rows = signal.shape[0]
    ext_ref[0:EDGE, :] = before
    ext_ref[EDGE : EDGE + rows, :] = signal
    total = filter_taps[0:1] * signal
    for s in range(1, filter_taps.shape[0]):
        total = total + filter_taps[s : s + 1] * ext_ref[EDGE - s : EDGE - s + rows, :]
    return total


def before_kernel(
    cpd, gpd, q_ref, k_ref, v_ref, og_ref, tail_ref, taps_ref, long_ref, send_ref, sk_ref, sv_ref,
    long_rows, ext_q, ext_k, ext_v,
):
    step = pl.program_id(0)
    groups = long_ref.shape[1]
    per_tile, _, rows = send_ref.shape

    @pl.when(step == 0)
    def _():
        long_rows[...] = jnp.zeros_like(long_rows)
        long_rows[0:groups, :] = long_ref[...].T

    for j in range(q_ref.shape[1] // LANES):
        at = slice(j * LANES, (j + 1) * LANES)
        tail = tail_ref[:, at].astype(F32)
        short_q = taps_causal(ext_q.at[j], tail[0:EDGE], q_ref[:, at].astype(F32), taps_ref[0, :, at])
        short_k = taps_causal(
            ext_k.at[j], tail[EDGE : 2 * EDGE], k_ref[:, at].astype(F32), taps_ref[1, :, at]
        )
        short_v = taps_causal(
            ext_v.at[j], tail[2 * EDGE : 3 * EDGE], v_ref[:, at].astype(F32), taps_ref[2, :, at]
        )
        sk_ref[:, at] = short_k
        sv_ref[:, at] = short_v
        mixed = (short_k * short_v).T.astype(BF16)
        delta = (og_ref[:, at].astype(F32) * short_q).T.astype(BF16)
        width = min(cpd, LANES)
        for piece in range(LANES // width):
            channel = j * LANES + piece * width
            dest, low = channel // cpd, channel % cpd
            rows_at = slice(piece * width, (piece + 1) * width)
            send_ref[dest, low : low + width, :] = mixed[rows_at]
            send_ref[dest, cpd + low : cpd + low + width, :] = delta[rows_at]
    filter_rows = send_ref.shape[1] - 2 * cpd
    for dest in range(per_tile):
        first = (step * per_tile + dest) * gpd
        send_ref[dest, 2 * cpd :, :] = long_rows[pl.ds(first, filter_rows), :].astype(BF16)


def before_exchange(query, key, value, out_grad, tail, taps, long_filter, n):
    rows, channels = query.shape
    groups = long_filter.shape[1]
    cpd, gpd = channels // n, groups // n
    tile = min(channels, max(512, cpd))
    per_tile = tile // cpd
    filter_rows = round_up(gpd, 16)
    send_rows = 2 * cpd + filter_rows
    block = pl.BlockSpec((rows, tile), lambda i: (0, i))
    ext = pltpu.VMEM((tile // LANES, rows + EDGE, LANES), F32)
    return pl.pallas_call(
        functools.partial(before_kernel, cpd, gpd),
        grid=(channels // tile,),
        in_specs=[block] * 4
        + [
            pl.BlockSpec((3 * EDGE, tile), lambda i: (0, i)),
            pl.BlockSpec((3, taps.shape[1], tile), lambda i: (0, 0, i)),
            pl.BlockSpec((rows, groups), lambda i: (0, 0)),
        ],
        out_specs=[pl.BlockSpec((per_tile, send_rows, rows), lambda i: (i, 0, 0)), block, block],
        out_shape=[
            jax.ShapeDtypeStruct((n, send_rows, rows), BF16),
            jax.ShapeDtypeStruct((rows, channels), F32),
            jax.ShapeDtypeStruct((rows, channels), F32),
        ],
        scratch_shapes=[pltpu.VMEM((round_up(groups, 8) + filter_rows, rows), F32), ext, ext, ext],
        compiler_params=params(),
        cost_estimate=pl.CostEstimate(
            flops=50 * rows * channels, bytes_accessed=20 * rows * channels, transcendentals=0
        ),
        name="before_exchange",
    )(query, key, value, out_grad, tail, taps, long_filter)


def long_kernel(cpd, gpd, in_ref, out_ref, taps, wide, gram, raw):
    n, send_rows, rows = in_ref.shape
    gw = cpd // gpd
    span = n * rows
    filter_rows = send_rows - 2 * cpd
    for a in range(n):
        taps[:, a * rows : (a + 1) * rows] = in_ref[a, 2 * cpd :, :].astype(F32)
    if gpd < filter_rows:
        raw[...] = jnp.zeros_like(raw)
    row8 = lax.broadcasted_iota(jnp.int32, (8, span), 0)
    row_tile = lax.broadcasted_iota(jnp.int32, (8, rows), 0)
    lane_tile = lax.broadcasted_iota(jnp.int32, (8, rows), 1)
    no_rows = jnp.zeros((gw, rows), BF16)

    def keep_upper(block, first):
        head = jnp.where(lane_tile >= row_tile + first, block[:, :rows], 0.0)
        return jnp.concatenate([head, block[:, rows:]], 1)

    def one_group(g, slot):
        base = jnp.broadcast_to(taps[pl.ds(g, 1), :], (8, span))
        for bit in (1, 2, 4):
            base = jnp.where((row8 & bit) != 0, pltpu.roll(base, bit, 1), base)
        for m in range(0, rows // 8, 2):
            low = base if m == 0 else pltpu.roll(base, 8 * m, 1)
            high = pltpu.roll(base, 8 * m + 8, 1)
            pair = jnp.concatenate([keep_upper(low, 8 * m), keep_upper(high, 8 * m + 8)], 0)
            wide[slot, 8 * m : 8 * m + 16, :] = pair.astype(BF16)
        first = pl.multiple_of(g * gw, gw)
        x = in_ref[:, pl.ds(first, gw), :].reshape(n * gw, rows)
        second = pl.multiple_of(cpd + g * gw, gw)
        d = in_ref[:, pl.ds(second, gw), :].reshape(n * gw, rows)
        x_turned = x.astype(F32).T.astype(BF16)
        conv = None
        back = None
        for k in range(0, n, 2):
            count = (n - k) * gw
            at = slice(k * rows, (k + 2) * rows)
            ahead = jnp.concatenate([no_rows, x[: count - gw]], 0)
            stacked = jnp.concatenate(
                [
                    wide[slot, :, k * rows : (k + 1) * rows],
                    wide[slot, :, (k + 1) * rows : (k + 2) * rows],
                ],
                0,
            )
            part = jnp.dot(
                jnp.concatenate([x[:count], ahead], 1), stacked, preferred_element_type=F32
            )
            conv = part if k == 0 else jnp.concatenate([conv[: k * gw], conv[k * gw :] + part], 0)
            later = jnp.concatenate([d[(k + 1) * gw :], no_rows], 0)
            pairs = jnp.concatenate([d[k * gw :], later], 1)
            part = lax.dot_general(
                pairs, wide[slot, :, at], (((1,), (1,)), ((), ())), preferred_element_type=F32
            )
            back = part if k == 0 else jnp.concatenate([back[:count] + part, back[count:]], 0)
            if k > 0:
                pairs = jnp.concatenate([pairs, jnp.zeros((k * gw, 2 * rows), BF16)], 0)
            gram[slot, :, at] = jnp.dot(x_turned, pairs, preferred_element_type=F32)
        out_ref[:, pl.ds(first, gw), :] = conv.astype(BF16).reshape(n, gw, rows)
        out_ref[:, pl.ds(second, gw), :] = back.astype(BF16).reshape(n, gw, rows)
        total = keep_upper(gram[slot, 0:8, :], 0)
        for m in range(1, rows // 8):
            block = keep_upper(gram[slot, 8 * m : 8 * m + 8, :], 8 * m)
            total = total + pltpu.roll(block, span - 8 * m, 1)
        for bit in (1, 2, 4):
            total = jnp.where((row8 & bit) != 0, pltpu.roll(total, span - bit, 1), total)
        line = jnp.sum(total, axis=0, keepdims=True)
        raw[pl.ds(g, 1), :] = line
        return line * line

    def body(i, squares):
        squares = squares + one_group(2 * i, 0)
        return squares + one_group(2 * i + 1, 1)

    squares = lax.fori_loop(0, gpd // 2, body, jnp.zeros((1, span), F32))
    total = jnp.sum(squares, axis=1, keepdims=True)
    upper = total.astype(BF16).astype(F32)
    lower = total - upper
    for a in range(n):
        out_ref[a, 2 * cpd : 2 * cpd + filter_rows, :] = raw[:, a * rows : (a + 1) * rows].astype(BF16)
    halo_at = 2 * cpd + filter_rows
    row = lax.broadcasted_iota(jnp.int32, (2 * EDGE, 2 * rows), 0)
    lane = lax.broadcasted_iota(jnp.int32, (2 * EDGE, 2 * rows), 1)
    wanted = jnp.where(row < EDGE, row, rows - EDGE + row)
    pick = jnp.where(lane == wanted, 1.0, 0.0).astype(BF16)
    row_out = lax.broadcasted_iota(jnp.int32, (2 * EDGE, rows), 0)
    for a in range(n):
        if a + 1 < n:
            results = jnp.concatenate([out_ref[a + 1, 0:cpd, :], out_ref[a + 1, cpd : 2 * cpd, :]], 1)
            halo = lax.dot_general(
                pick, results, (((1,), (1,)), ((), ())), preferred_element_type=F32
            )
            if cpd < LANES:
                halo = jnp.concatenate([halo, jnp.zeros((2 * EDGE, LANES - cpd), F32)], 1)
        else:
            halo = jnp.zeros((2 * EDGE, max(cpd, LANES)), F32)
        for j in range(halo.shape[1] // LANES):
            tile = halo[:, j * LANES : (j + 1) * LANES]
            tile = jnp.where(row_out == EDGE - 2, upper, jnp.where(row_out == EDGE - 1, lower, tile))
            at = halo_at + 2 * EDGE * j
            out_ref[a, at : at + 2 * EDGE, :] = tile.astype(BF16)


def long_products(received, cpd, gpd):
    n, send_rows, rows = received.shape
    filter_rows = send_rows - 2 * cpd
    out_rows = send_rows + 2 * EDGE * max(1, cpd // LANES)
    span = n * rows
    return pl.pallas_call(
        functools.partial(long_kernel, cpd, gpd),
        in_specs=[pl.BlockSpec(memory_space=pltpu.VMEM)],
        out_specs=pl.BlockSpec(memory_space=pltpu.VMEM),
        out_shape=jax.ShapeDtypeStruct((n, out_rows, rows), BF16),
        scratch_shapes=[
            pltpu.VMEM((filter_rows, span), F32),
            pltpu.VMEM((2, rows, span), BF16),
            pltpu.VMEM((2, rows, span), F32),
            pltpu.VMEM((filter_rows, span), F32),
        ],
        compiler_params=params(),
        cost_estimate=pl.CostEstimate(
            flops=6 * cpd * span * span, bytes_accessed=4 * n * out_rows * rows, transcendentals=0
        ),
        name="long_products",
    )(received)


def taps_anti(ext_ref, signal, after, filter_taps):
    rows = signal.shape[0]
    ext_ref[0:rows, :] = signal
    ext_ref[rows : rows + EDGE, :] = after
    total = filter_taps[0:1] * signal
    for s in range(1, filter_taps.shape[0]):
        total = total + filter_taps[s : s + 1] * ext_ref[s : s + rows, :]
    return total


def short_edge(before, signal, filter_taps):
    both = jnp.concatenate([before, signal], 0)
    total = filter_taps[0:1] * signal
    for s in range(1, filter_taps.shape[0]):
        total = total + filter_taps[s : s + 1] * both[EDGE - s : 2 * EDGE - s]
    return total


def after_kernel(
    cpd, gpd, in_ref, og_ref, sk_ref, sv_ref, k_end, v_end, next_ref, taps_ref,
    dq_ref, dk_ref, dv_ref, raw_ref, raw_rows, ext_q, ext_k, ext_v,
):
    step = pl.program_id(0)
    per_tile, in_rows, rows = in_ref.shape
    groups = raw_ref.shape[1]
    halo_rows = 2 * EDGE * max(1, cpd // LANES)
    halo_at = in_rows - halo_rows
    end_rows = k_end.shape[0]
    for j in range(og_ref.shape[1] // LANES):
        at = slice(j * LANES, (j + 1) * LANES)
        if cpd >= LANES:
            dest, low = j * LANES // cpd, j * LANES % cpd
            conv = in_ref[dest, low : low + LANES, :]
            back = in_ref[dest, cpd + low : cpd + low + LANES, :]
            edge = halo_at + 2 * EDGE * (low // LANES)
            halo = in_ref[dest, edge : edge + 2 * EDGE, :].astype(F32)
        else:
            dests = range(j * LANES // cpd, (j + 1) * LANES // cpd)
            conv = jnp.concatenate([in_ref[d, 0:cpd, :] for d in dests], 0)
            back = jnp.concatenate([in_ref[d, cpd : 2 * cpd, :] for d in dests], 0)
            halo = jnp.concatenate(
                [in_ref[d, halo_at:, :].astype(F32)[:, :cpd] for d in dests], 1
            )
        conv = conv.astype(F32).T
        back = back.astype(F32).T
        following = next_ref[:, at].astype(F32)
        taps_k = taps_ref[1, :, at]
        taps_v = taps_ref[2, :, at]
        next_k = short_edge(
            k_end[:, at].astype(F32)[end_rows - EDGE :], following[EDGE : 2 * EDGE], taps_k
        )
        next_v = short_edge(
            v_end[:, at].astype(F32)[end_rows - EDGE :], following[2 * EDGE : 3 * EDGE], taps_v
        )
        grad_q = og_ref[:, at].astype(F32) * conv
        dq_ref[:, at] = taps_anti(
            ext_q.at[j], grad_q, following[0:EDGE] * halo[0:EDGE], taps_ref[0, :, at]
        ).astype(BF16)
        dk_ref[:, at] = taps_anti(
            ext_k.at[j], back * sv_ref[:, at], halo[EDGE:] * next_v, taps_k
        ).astype(BF16)
        dv_ref[:, at] = taps_anti(
            ext_v.at[j], back * sk_ref[:, at], halo[EDGE:] * next_k, taps_v
        ).astype(BF16)
    for dest in range(per_tile):
        lines = in_ref[dest, 2 * cpd : halo_at, :].astype(F32)
        raw_rows[pl.ds((step * per_tile + dest) * gpd, gpd), :] = lines[:gpd]

    @pl.when(step == pl.num_programs(0) - 1)
    def _():
        raw_ref[...] = raw_rows[...].T


def after_exchange(returned, out_grad, short_k, short_v, key, value, following, taps, groups):
    n, in_rows, rows = returned.shape
    channels = out_grad.shape[1]
    cpd, gpd = channels // n, groups // n
    tile = min(channels, max(512, cpd))
    per_tile = tile // cpd
    block = pl.BlockSpec((rows, tile), lambda i: (0, i))
    end = pl.BlockSpec((16, tile), lambda i: (rows // 16 - 1, i))
    ext = pltpu.VMEM((tile // LANES, rows + EDGE, LANES), F32)
    grad = jax.ShapeDtypeStruct((rows, channels), BF16)
    return pl.pallas_call(
        functools.partial(after_kernel, cpd, gpd),
        grid=(channels // tile,),
        in_specs=[
            pl.BlockSpec((per_tile, in_rows, rows), lambda i: (i, 0, 0)),
            block,
            block,
            block,
            end,
            end,
            pl.BlockSpec((3 * EDGE, tile), lambda i: (0, i)),
            pl.BlockSpec((3, taps.shape[1], tile), lambda i: (0, 0, i)),
        ],
        out_specs=[block, block, block, pl.BlockSpec((rows, groups), lambda i: (0, 0))],
        out_shape=[grad, grad, grad, jax.ShapeDtypeStruct((rows, groups), F32)],
        scratch_shapes=[pltpu.VMEM((groups, rows), F32), ext, ext, ext],
        compiler_params=params(),
        cost_estimate=pl.CostEstimate(
            flops=60 * rows * channels, bytes_accessed=22 * rows * channels, transcendentals=0
        ),
        name="after_exchange",
    )(returned, out_grad, short_k, short_v, key, value, following, taps)


def on_device(
    query_heads,
    key_heads,
    value_heads,
    hyena_query,
    hyena_key,
    hyena_value,
    short_filter,
    long_filter,
    output_grad,
):
    rows, channels = query_heads.shape
    groups = long_filter.shape[1]
    n = lax.axis_size("ctx")
    tp = lax.axis_size("tp")
    cpd, gpd = channels // n, groups // n
    position = lax.axis_index("ctx")
    tail = shifted(
        jnp.concatenate([a[rows - EDGE :] for a in (hyena_query, hyena_key, hyena_value)], 0), "ctx", 1
    )
    key_prev = shifted(key_heads, "ctx", 1)
    value_prev = shifted(value_heads, "ctx", 1)
    following = shifted(
        jnp.concatenate([a[:EDGE] for a in (output_grad, hyena_key, hyena_value)], 0), "ctx", -1
    )
    send, short_k, short_v = before_exchange(
        hyena_query, hyena_key, hyena_value, output_grad, tail, short_filter, long_filter, n
    )
    received = lax.all_to_all(send, "ctx", split_axis=0, concat_axis=0, tiled=True)
    attention = attend(query_heads, key_heads, value_heads, key_prev, value_prev, position)
    results = long_products(received, cpd, gpd)
    returned = lax.all_to_all(results, "ctx", split_axis=0, concat_axis=0, tiled=True)
    norm_at = returned.shape[1] - 2 * EDGE * max(1, cpd // LANES) + EDGE - 2
    own_squares = jnp.sum(returned[:, norm_at : norm_at + 2, 0].astype(F32)).reshape(1, 1)
    squares = own_squares
    for distance in range(1, tp):
        route = [(i, (i + distance) % tp) for i in range(tp)]
        squares = squares + lax.ppermute(own_squares, "tp", route)
    query_grad, key_grad, value_grad, raw_grad = after_exchange(
        returned, output_grad, short_k, short_v, hyena_key, hyena_value, following, short_filter, groups
    )
    bound = math.sqrt(rows * n * groups * tp)
    factor = jnp.minimum(1.0, bound / jnp.sqrt(squares))
    return (attention, query_grad, key_grad, value_grad, raw_grad * factor)


def solution(mesh):
    whole = P("ctx", "tp")
    in_specs = (whole,) * 6 + (P(None, None, "tp"), whole, whole)
    return jax.shard_map(
        on_device, mesh=mesh, in_specs=in_specs, out_specs=(whole,) * 5, check_vma=False
    )
```

```python
import functools
import math

import jax
import jax.numpy as jnp
from jax import lax
from jax.experimental import pallas as pl
from jax.experimental.pallas import tpu as pltpu
from jax.sharding import PartitionSpec as P

HEAD_DIM = 128
LANES = 128
EDGE = 8
F32 = jnp.float32
BF16 = jnp.bfloat16
VMEM_BYTES = 60 * 1024 * 1024


def params():
    return pltpu.CompilerParams(vmem_limit_bytes=VMEM_BYTES)


def shifted(block, axis, distance):
    devices = range(lax.axis_size(axis))
    route = [(i - distance, i) for i in devices if i - distance in devices]
    return lax.ppermute(block, axis, route)


def round_up(value, step):
    return -(-value // step) * step


def attend_kernel(place_ref, q_ref, k_ref, v_ref, kp_ref, vp_ref, out_ref):
    rows = q_ref.shape[0]
    row = lax.broadcasted_iota(jnp.int32, (rows, rows), 0)
    col = lax.broadcasted_iota(jnp.int32, (rows, rows), 1)
    own_ok = col <= row
    prev_ok = jnp.broadcast_to(place_ref[0], (rows, rows)) > 0
    contract = (((1,), (1,)), ((), ()))
    for head in range(q_ref.shape[1] // HEAD_DIM):
        at = slice(head * HEAD_DIM, (head + 1) * HEAD_DIM)
        scale = 1.0 / math.sqrt(HEAD_DIM)
        query = q_ref[:, at]
        own = lax.dot_general(query, k_ref[:, at], contract, preferred_element_type=F32) * scale
        prev = lax.dot_general(query, kp_ref[:, at], contract, preferred_element_type=F32) * scale
        own = jnp.where(own_ok, own, -jnp.inf)
        prev = jnp.where(prev_ok, prev, -jnp.inf)
        largest = jnp.max(jnp.maximum(own, prev), axis=1, keepdims=True)
        own = jnp.exp(own - largest)
        prev = jnp.exp(prev - largest)
        total = jnp.sum(own + prev, axis=1, keepdims=True)
        inverse = 1.0 / total
        own = (own * inverse).astype(BF16)
        prev = (prev * inverse).astype(BF16)
        mixed = jnp.dot(own, v_ref[:, at], preferred_element_type=F32) + jnp.dot(
            prev, vp_ref[:, at], preferred_element_type=F32
        )
        out_ref[:, at] = mixed.astype(BF16)


def attend(query, key, value, key_prev, value_prev, position):
    rows, channels = query.shape
    tile = min(512, channels)
    block = pl.BlockSpec((rows, tile), lambda i: (0, i))
    heads = channels // HEAD_DIM
    return pl.pallas_call(
        attend_kernel,
        grid=(channels // tile,),
        in_specs=[pl.BlockSpec(memory_space=pltpu.SMEM)] + [block] * 5,
        out_specs=block,
        out_shape=jax.ShapeDtypeStruct((rows, channels), BF16),
        compiler_params=params(),
        cost_estimate=pl.CostEstimate(
            flops=8 * heads * rows * rows * HEAD_DIM,
            bytes_accessed=12 * rows * channels,
            transcendentals=2 * heads * rows * rows,
        ),
        name="attend",
    )(position.astype(jnp.int32).reshape(1), query, key, value, key_prev, value_prev)


def taps_causal(ext_ref, before, signal, filter_taps):
    rows = signal.shape[0]
    ext_ref[0:EDGE, :] = before
    ext_ref[EDGE : EDGE + rows, :] = signal
    total = filter_taps[0:1] * signal
    for s in range(1, filter_taps.shape[0]):
        total = total + filter_taps[s : s + 1] * ext_ref[EDGE - s : EDGE - s + rows, :]
    return total


def before_kernel(
    cpd, gpd, q_ref, k_ref, v_ref, og_ref, tail_ref, taps_ref, long_ref, send_ref, sk_ref, sv_ref,
    long_rows, ext_q, ext_k, ext_v,
):
    step = pl.program_id(0)
    groups = long_ref.shape[1]
    per_tile, _, rows = send_ref.shape

    @pl.when(step == 0)
    def _():
        long_rows[...] = jnp.zeros_like(long_rows)
        long_rows[0:groups, :] = long_ref[...].T

    for j in range(q_ref.shape[1] // LANES):
        at = slice(j * LANES, (j + 1) * LANES)
        tail = tail_ref[:, at].astype(F32)
        short_q = taps_causal(ext_q.at[j], tail[0:EDGE], q_ref[:, at].astype(F32), taps_ref[0, :, at])
        short_k = taps_causal(
            ext_k.at[j], tail[EDGE : 2 * EDGE], k_ref[:, at].astype(F32), taps_ref[1, :, at]
        )
        short_v = taps_causal(
            ext_v.at[j], tail[2 * EDGE : 3 * EDGE], v_ref[:, at].astype(F32), taps_ref[2, :, at]
        )
        sk_ref[:, at] = short_k
        sv_ref[:, at] = short_v
        mixed = (short_k * short_v).T.astype(BF16)
        delta = (og_ref[:, at].astype(F32) * short_q).T.astype(BF16)
        width = min(cpd, LANES)
        for piece in range(LANES // width):
            channel = j * LANES + piece * width
            dest, low = channel // cpd, channel % cpd
            rows_at = slice(piece * width, (piece + 1) * width)
            send_ref[dest, low : low + width, :] = mixed[rows_at]
            send_ref[dest, cpd + low : cpd + low + width, :] = delta[rows_at]
    filter_rows = send_ref.shape[1] - 2 * cpd
    for dest in range(per_tile):
        first = (step * per_tile + dest) * gpd
        send_ref[dest, 2 * cpd :, :] = long_rows[pl.ds(first, filter_rows), :].astype(BF16)


def before_exchange(query, key, value, out_grad, tail, taps, long_filter, n, chunk, chunks):
    rows = query.shape[0]
    channels = query.shape[1] // chunks
    groups = long_filter.shape[1] // chunks
    cpd, gpd = channels // n, groups // n
    tile = min(channels, max(512, cpd))
    per_tile = tile // cpd
    filter_rows = round_up(gpd, 16)
    send_rows = 2 * cpd + filter_rows
    first = chunk * channels // tile
    block = pl.BlockSpec((rows, tile), lambda i: (0, first + i))
    own = pl.BlockSpec((rows, tile), lambda i: (0, i))
    ext = pltpu.VMEM((tile // LANES, rows + EDGE, LANES), F32)
    return pl.pallas_call(
        functools.partial(before_kernel, cpd, gpd),
        grid=(channels // tile,),
        in_specs=[block] * 4
        + [
            pl.BlockSpec((3 * EDGE, tile), lambda i: (0, first + i)),
            pl.BlockSpec((3, taps.shape[1], tile), lambda i: (0, 0, first + i)),
            pl.BlockSpec((rows, groups), lambda i: (0, chunk)),
        ],
        out_specs=[pl.BlockSpec((per_tile, send_rows, rows), lambda i: (i, 0, 0)), own, own],
        out_shape=[
            jax.ShapeDtypeStruct((n, send_rows, rows), BF16),
            jax.ShapeDtypeStruct((rows, channels), F32),
            jax.ShapeDtypeStruct((rows, channels), F32),
        ],
        scratch_shapes=[pltpu.VMEM((round_up(groups, 8) + filter_rows, rows), F32), ext, ext, ext],
        compiler_params=params(),
        cost_estimate=pl.CostEstimate(
            flops=50 * rows * channels, bytes_accessed=20 * rows * channels, transcendentals=0
        ),
        name="before_exchange",
    )(query, key, value, out_grad, tail, taps, long_filter)


def long_kernel(cpd, gpd, in_ref, out_ref, taps, wide, gram, raw):
    n, send_rows, rows = in_ref.shape
    gw = cpd // gpd
    span = n * rows
    filter_rows = send_rows - 2 * cpd
    for a in range(n):
        taps[:, a * rows : (a + 1) * rows] = in_ref[a, 2 * cpd :, :].astype(F32)
    if gpd < filter_rows:
        raw[...] = jnp.zeros_like(raw)
    row8 = lax.broadcasted_iota(jnp.int32, (8, span), 0)
    row_tile = lax.broadcasted_iota(jnp.int32, (8, rows), 0)
    lane_tile = lax.broadcasted_iota(jnp.int32, (8, rows), 1)
    no_rows = jnp.zeros((gw, rows), BF16)

    def keep_upper(block, first):
        head = jnp.where(lane_tile >= row_tile + first, block[:, :rows], 0.0)
        return jnp.concatenate([head, block[:, rows:]], 1)

    def one_group(g, slot):
        base = jnp.broadcast_to(taps[pl.ds(g, 1), :], (8, span))
        for bit in (1, 2, 4):
            base = jnp.where((row8 & bit) != 0, pltpu.roll(base, bit, 1), base)
        for m in range(0, rows // 8, 2):
            low = base if m == 0 else pltpu.roll(base, 8 * m, 1)
            high = pltpu.roll(base, 8 * m + 8, 1)
            pair = jnp.concatenate([keep_upper(low, 8 * m), keep_upper(high, 8 * m + 8)], 0)
            wide[slot, 8 * m : 8 * m + 16, :] = pair.astype(BF16)
        first = pl.multiple_of(g * gw, gw)
        x = in_ref[:, pl.ds(first, gw), :].reshape(n * gw, rows)
        second = pl.multiple_of(cpd + g * gw, gw)
        d = in_ref[:, pl.ds(second, gw), :].reshape(n * gw, rows)
        x_turned = x.astype(F32).T.astype(BF16)
        conv = None
        back = None
        for k in range(0, n, 2):
            count = (n - k) * gw
            at = slice(k * rows, (k + 2) * rows)
            ahead = jnp.concatenate([no_rows, x[: count - gw]], 0)
            stacked = jnp.concatenate(
                [
                    wide[slot, :, k * rows : (k + 1) * rows],
                    wide[slot, :, (k + 1) * rows : (k + 2) * rows],
                ],
                0,
            )
            part = jnp.dot(
                jnp.concatenate([x[:count], ahead], 1), stacked, preferred_element_type=F32
            )
            conv = part if k == 0 else jnp.concatenate([conv[: k * gw], conv[k * gw :] + part], 0)
            later = jnp.concatenate([d[(k + 1) * gw :], no_rows], 0)
            pairs = jnp.concatenate([d[k * gw :], later], 1)
            part = lax.dot_general(
                pairs, wide[slot, :, at], (((1,), (1,)), ((), ())), preferred_element_type=F32
            )
            back = part if k == 0 else jnp.concatenate([back[:count] + part, back[count:]], 0)
            if k > 0:
                pairs = jnp.concatenate([pairs, jnp.zeros((k * gw, 2 * rows), BF16)], 0)
            gram[slot, :, at] = jnp.dot(x_turned, pairs, preferred_element_type=F32)
        out_ref[:, pl.ds(first, gw), :] = conv.astype(BF16).reshape(n, gw, rows)
        out_ref[:, pl.ds(second, gw), :] = back.astype(BF16).reshape(n, gw, rows)
        total = keep_upper(gram[slot, 0:8, :], 0)
        for m in range(1, rows // 8):
            block = keep_upper(gram[slot, 8 * m : 8 * m + 8, :], 8 * m)
            total = total + pltpu.roll(block, span - 8 * m, 1)
        for bit in (1, 2, 4):
            total = jnp.where((row8 & bit) != 0, pltpu.roll(total, span - bit, 1), total)
        line = jnp.sum(total, axis=0, keepdims=True)
        raw[pl.ds(g, 1), :] = line
        return line * line

    def body(i, squares):
        squares = squares + one_group(2 * i, 0)
        return squares + one_group(2 * i + 1, 1)

    squares = lax.fori_loop(0, gpd // 2, body, jnp.zeros((1, span), F32))
    total = jnp.sum(squares, axis=1, keepdims=True)
    upper = total.astype(BF16).astype(F32)
    lower = total - upper
    for a in range(n):
        out_ref[a, 2 * cpd : 2 * cpd + filter_rows, :] = raw[:, a * rows : (a + 1) * rows].astype(BF16)
    halo_at = 2 * cpd + filter_rows
    row = lax.broadcasted_iota(jnp.int32, (2 * EDGE, 2 * rows), 0)
    lane = lax.broadcasted_iota(jnp.int32, (2 * EDGE, 2 * rows), 1)
    wanted = jnp.where(row < EDGE, row, rows - EDGE + row)
    pick = jnp.where(lane == wanted, 1.0, 0.0).astype(BF16)
    row_out = lax.broadcasted_iota(jnp.int32, (2 * EDGE, rows), 0)
    for a in range(n):
        if a + 1 < n:
            results = jnp.concatenate([out_ref[a + 1, 0:cpd, :], out_ref[a + 1, cpd : 2 * cpd, :]], 1)
            halo = lax.dot_general(
                pick, results, (((1,), (1,)), ((), ())), preferred_element_type=F32
            )
            if cpd < LANES:
                halo = jnp.concatenate([halo, jnp.zeros((2 * EDGE, LANES - cpd), F32)], 1)
        else:
            halo = jnp.zeros((2 * EDGE, max(cpd, LANES)), F32)
        for j in range(halo.shape[1] // LANES):
            tile = halo[:, j * LANES : (j + 1) * LANES]
            tile = jnp.where(row_out == EDGE - 2, upper, jnp.where(row_out == EDGE - 1, lower, tile))
            at = halo_at + 2 * EDGE * j
            out_ref[a, at : at + 2 * EDGE, :] = tile.astype(BF16)


def long_products(received, cpd, gpd):
    n, send_rows, rows = received.shape
    filter_rows = send_rows - 2 * cpd
    out_rows = send_rows + 2 * EDGE * max(1, cpd // LANES)
    span = n * rows
    return pl.pallas_call(
        functools.partial(long_kernel, cpd, gpd),
        in_specs=[pl.BlockSpec(memory_space=pltpu.VMEM)],
        out_specs=pl.BlockSpec(memory_space=pltpu.VMEM),
        out_shape=jax.ShapeDtypeStruct((n, out_rows, rows), BF16),
        scratch_shapes=[
            pltpu.VMEM((filter_rows, span), F32),
            pltpu.VMEM((2, rows, span), BF16),
            pltpu.VMEM((2, rows, span), F32),
            pltpu.VMEM((filter_rows, span), F32),
        ],
        compiler_params=params(),
        cost_estimate=pl.CostEstimate(
            flops=6 * cpd * span * span, bytes_accessed=4 * n * out_rows * rows, transcendentals=0
        ),
        name="long_products",
    )(received)


def taps_anti(ext_ref, signal, after, filter_taps):
    rows = signal.shape[0]
    ext_ref[0:rows, :] = signal
    ext_ref[rows : rows + EDGE, :] = after
    total = filter_taps[0:1] * signal
    for s in range(1, filter_taps.shape[0]):
        total = total + filter_taps[s : s + 1] * ext_ref[s : s + rows, :]
    return total


def short_edge(before, signal, filter_taps):
    both = jnp.concatenate([before, signal], 0)
    total = filter_taps[0:1] * signal
    for s in range(1, filter_taps.shape[0]):
        total = total + filter_taps[s : s + 1] * both[EDGE - s : 2 * EDGE - s]
    return total


def after_kernel(
    cpd, gpd, in_ref, og_ref, sk_ref, sv_ref, k_end, v_end, next_ref, taps_ref,
    *refs,
):
    dq_ref, dk_ref, dv_ref, raw_ref, raw_rows, ext_q, ext_k, ext_v = refs[-8:]
    step = pl.program_id(0)
    per_tile, in_rows, rows = in_ref.shape
    groups = raw_ref.shape[1]
    halo_rows = 2 * EDGE * max(1, cpd // LANES)
    halo_at = in_rows - halo_rows
    end_rows = k_end.shape[0]
    for j in range(og_ref.shape[1] // LANES):
        at = slice(j * LANES, (j + 1) * LANES)
        if cpd >= LANES:
            dest, low = j * LANES // cpd, j * LANES % cpd
            conv = in_ref[dest, low : low + LANES, :]
            back = in_ref[dest, cpd + low : cpd + low + LANES, :]
            edge = halo_at + 2 * EDGE * (low // LANES)
            halo = in_ref[dest, edge : edge + 2 * EDGE, :].astype(F32)
        else:
            dests = range(j * LANES // cpd, (j + 1) * LANES // cpd)
            conv = jnp.concatenate([in_ref[d, 0:cpd, :] for d in dests], 0)
            back = jnp.concatenate([in_ref[d, cpd : 2 * cpd, :] for d in dests], 0)
            halo = jnp.concatenate(
                [in_ref[d, halo_at:, :].astype(F32)[:, :cpd] for d in dests], 1
            )
        conv = conv.astype(F32).T
        back = back.astype(F32).T
        following = next_ref[:, at].astype(F32)
        taps_k = taps_ref[1, :, at]
        taps_v = taps_ref[2, :, at]
        next_k = short_edge(
            k_end[:, at].astype(F32)[end_rows - EDGE :], following[EDGE : 2 * EDGE], taps_k
        )
        next_v = short_edge(
            v_end[:, at].astype(F32)[end_rows - EDGE :], following[2 * EDGE : 3 * EDGE], taps_v
        )
        grad_q = og_ref[:, at].astype(F32) * conv
        dq_ref[:, at] = taps_anti(
            ext_q.at[j], grad_q, following[0:EDGE] * halo[0:EDGE], taps_ref[0, :, at]
        ).astype(BF16)
        dk_ref[:, at] = taps_anti(
            ext_k.at[j], back * sv_ref[:, at], halo[EDGE:] * next_v, taps_k
        ).astype(BF16)
        dv_ref[:, at] = taps_anti(
            ext_v.at[j], back * sk_ref[:, at], halo[EDGE:] * next_k, taps_v
        ).astype(BF16)
    for dest in range(per_tile):
        lines = in_ref[dest, 2 * cpd : halo_at, :].astype(F32)
        raw_rows[pl.ds((step * per_tile + dest) * gpd, gpd), :] = lines[:gpd]

    @pl.when(step == pl.num_programs(0) - 1)
    def _():
        raw_ref[...] = raw_rows[...].T


def after_exchange(
    returned, out_grad, short_k, short_v, key, value, following, taps, groups, chunk, chunks, grads
):
    n, in_rows, rows = returned.shape
    channels = out_grad.shape[1] // chunks
    groups = groups // chunks
    cpd, gpd = channels // n, groups // n
    tile = min(channels, max(512, cpd))
    per_tile = tile // cpd
    first = chunk * channels // tile
    block = pl.BlockSpec((rows, tile), lambda i: (0, first + i))
    own = pl.BlockSpec((rows, tile), lambda i: (0, i))
    end = pl.BlockSpec((16, tile), lambda i: (rows // 16 - 1, first + i))
    ext = pltpu.VMEM((tile // LANES, rows + EDGE, LANES), F32)
    grad = jax.ShapeDtypeStruct(out_grad.shape, BF16)
    return pl.pallas_call(
        functools.partial(after_kernel, cpd, gpd),
        grid=(channels // tile,),
        in_specs=[
            pl.BlockSpec((per_tile, in_rows, rows), lambda i: (i, 0, 0)),
            block,
            own,
            own,
            end,
            end,
            pl.BlockSpec((3 * EDGE, tile), lambda i: (0, first + i)),
            pl.BlockSpec((3, taps.shape[1], tile), lambda i: (0, 0, first + i)),
        ]
        + [pl.BlockSpec(memory_space=pl.ANY)] * len(grads),
        input_output_aliases={8 + i: i for i in range(len(grads))},
        out_specs=[block, block, block, pl.BlockSpec((rows, groups), lambda i: (0, 0))],
        out_shape=[grad, grad, grad, jax.ShapeDtypeStruct((rows, groups), F32)],
        scratch_shapes=[pltpu.VMEM((groups, rows), F32), ext, ext, ext],
        compiler_params=params(),
        cost_estimate=pl.CostEstimate(
            flops=60 * rows * channels, bytes_accessed=22 * rows * channels, transcendentals=0
        ),
        name="after_exchange",
    )(returned, out_grad, short_k, short_v, key, value, following, taps, *grads)


def on_device(
    query_heads,
    key_heads,
    value_heads,
    hyena_query,
    hyena_key,
    hyena_value,
    short_filter,
    long_filter,
    output_grad,
):
    rows, channels = query_heads.shape
    groups = long_filter.shape[1]
    n = lax.axis_size("ctx")
    tp = lax.axis_size("tp")
    cpd, gpd = channels // n, groups // n
    position = lax.axis_index("ctx")
    tail = shifted(
        jnp.concatenate([a[rows - EDGE :] for a in (hyena_query, hyena_key, hyena_value)], 0), "ctx", 1
    )
    key_prev = shifted(key_heads, "ctx", 1)
    value_prev = shifted(value_heads, "ctx", 1)
    following = shifted(
        jnp.concatenate([a[:EDGE] for a in (output_grad, hyena_key, hyena_value)], 0), "ctx", -1
    )
    chunks = 2 if gpd % 4 == 0 else 1
    cpd, gpd = cpd // chunks, gpd // chunks
    received = []
    shorts = []
    for chunk in range(chunks):
        send, short_k, short_v = before_exchange(
            hyena_query, hyena_key, hyena_value, output_grad, tail, short_filter, long_filter, n, chunk, chunks
        )
        shorts.append((short_k, short_v))
        received.append(lax.all_to_all(send, "ctx", split_axis=0, concat_axis=0, tiled=True))
    attention = attend(query_heads, key_heads, value_heads, key_prev, value_prev, position)
    received[0], attention = lax.optimization_barrier((received[0], attention))
    returned = []
    for chunk in range(chunks):
        results = long_products(received[chunk], cpd, gpd)
        returned.append(lax.all_to_all(results, "ctx", split_axis=0, concat_axis=0, tiled=True))
    norm_at = returned[0].shape[1] - 2 * EDGE * max(1, cpd // LANES) + EDGE - 2
    own_squares = sum(jnp.sum(r[:, norm_at : norm_at + 2, 0].astype(F32)) for r in returned).reshape(1, 1)
    squares = own_squares
    for distance in range(1, tp):
        route = [(i, (i + distance) % tp) for i in range(tp)]
        squares = squares + lax.ppermute(own_squares, "tp", route)
    grads = ()
    raws = []
    for chunk in range(chunks):
        *grads, raw = after_exchange(
            returned[chunk], output_grad, *shorts[chunk], hyena_key, hyena_value, following, short_filter,
            groups, chunk, chunks, grads,
        )
        raws.append(raw)
    bound = math.sqrt(rows * n * groups * tp)
    factor = jnp.minimum(1.0, bound / jnp.sqrt(squares))
    raw_grad = raws[0] if chunks == 1 else jnp.concatenate(raws, 1)
    return (attention, *grads, raw_grad * factor)


def solution(mesh):
    whole = P("ctx", "tp")
    in_specs = (whole,) * 6 + (P(None, None, "tp"), whole, whole)
    return jax.shard_map(
        on_device, mesh=mesh, in_specs=in_specs, out_specs=(whole,) * 5, check_vma=False
    )
```

```python
import functools
import math

import jax
import jax.numpy as jnp
from jax import lax
from jax.experimental import pallas as pl
from jax.experimental.pallas import tpu as pltpu
from jax.sharding import PartitionSpec as P

HEAD_DIM = 128
LANES = 128
EDGE = 8
F32 = jnp.float32
BF16 = jnp.bfloat16
VMEM_BYTES = 60 * 1024 * 1024


def params():
    return pltpu.CompilerParams(vmem_limit_bytes=VMEM_BYTES)


def shifted(block, axis, distance):
    devices = range(lax.axis_size(axis))
    route = [(i - distance, i) for i in devices if i - distance in devices]
    return lax.ppermute(block, axis, route)


def round_up(value, step):
    return -(-value // step) * step


def attend_kernel(place_ref, q_ref, k_ref, v_ref, kp_ref, vp_ref, out_ref):
    rows = q_ref.shape[0]
    row = lax.broadcasted_iota(jnp.int32, (rows, rows), 0)
    col = lax.broadcasted_iota(jnp.int32, (rows, rows), 1)
    own_ok = col <= row
    prev_ok = jnp.broadcast_to(place_ref[0], (rows, rows)) > 0
    contract = (((1,), (1,)), ((), ()))
    for head in range(q_ref.shape[1] // HEAD_DIM):
        at = slice(head * HEAD_DIM, (head + 1) * HEAD_DIM)
        scale = 1.0 / math.sqrt(HEAD_DIM)
        query = q_ref[:, at]
        own = lax.dot_general(query, k_ref[:, at], contract, preferred_element_type=F32) * scale
        prev = lax.dot_general(query, kp_ref[:, at], contract, preferred_element_type=F32) * scale
        own = jnp.where(own_ok, own, -jnp.inf)
        prev = jnp.where(prev_ok, prev, -jnp.inf)
        largest = jnp.max(jnp.maximum(own, prev), axis=1, keepdims=True)
        own = jnp.exp(own - largest)
        prev = jnp.exp(prev - largest)
        total = jnp.sum(own + prev, axis=1, keepdims=True)
        inverse = 1.0 / total
        own = (own * inverse).astype(BF16)
        prev = (prev * inverse).astype(BF16)
        mixed = jnp.dot(own, v_ref[:, at], preferred_element_type=F32) + jnp.dot(
            prev, vp_ref[:, at], preferred_element_type=F32
        )
        out_ref[:, at] = mixed.astype(BF16)


def attend(query, key, value, key_prev, value_prev, position):
    rows, channels = query.shape
    tile = min(512, channels)
    block = pl.BlockSpec((rows, tile), lambda i: (0, i))
    heads = channels // HEAD_DIM
    return pl.pallas_call(
        attend_kernel,
        grid=(channels // tile,),
        in_specs=[pl.BlockSpec(memory_space=pltpu.SMEM)] + [block] * 5,
        out_specs=block,
        out_shape=jax.ShapeDtypeStruct((rows, channels), BF16),
        compiler_params=params(),
        cost_estimate=pl.CostEstimate(
            flops=8 * heads * rows * rows * HEAD_DIM,
            bytes_accessed=12 * rows * channels,
            transcendentals=2 * heads * rows * rows,
        ),
        name="attend",
    )(position.astype(jnp.int32).reshape(1), query, key, value, key_prev, value_prev)


def taps_causal(ext_ref, before, signal, filter_taps):
    rows = signal.shape[0]
    ext_ref[0:EDGE, :] = before
    ext_ref[EDGE : EDGE + rows, :] = signal
    total = filter_taps[0:1] * signal
    for s in range(1, filter_taps.shape[0]):
        total = total + filter_taps[s : s + 1] * ext_ref[EDGE - s : EDGE - s + rows, :]
    return total


def before_kernel(
    cpd, gpd, q_ref, k_ref, v_ref, og_ref, tail_ref, taps_ref, long_ref, send_ref, sk_ref, sv_ref,
    long_rows, ext_q, ext_k, ext_v,
):
    step = pl.program_id(0)
    groups = long_ref.shape[1]
    per_tile, _, rows = send_ref.shape

    @pl.when(step == 0)
    def _():
        long_rows[...] = jnp.zeros_like(long_rows)
        long_rows[0:groups, :] = long_ref[...].T

    for j in range(q_ref.shape[1] // LANES):
        at = slice(j * LANES, (j + 1) * LANES)
        tail = tail_ref[:, at].astype(F32)
        short_q = taps_causal(ext_q.at[j], tail[0:EDGE], q_ref[:, at].astype(F32), taps_ref[0, :, at])
        short_k = taps_causal(
            ext_k.at[j], tail[EDGE : 2 * EDGE], k_ref[:, at].astype(F32), taps_ref[1, :, at]
        )
        short_v = taps_causal(
            ext_v.at[j], tail[2 * EDGE : 3 * EDGE], v_ref[:, at].astype(F32), taps_ref[2, :, at]
        )
        sk_ref[:, at] = short_k
        sv_ref[:, at] = short_v
        mixed = (short_k * short_v).T.astype(BF16)
        delta = (og_ref[:, at].astype(F32) * short_q).T.astype(BF16)
        width = min(cpd, LANES)
        for piece in range(LANES // width):
            channel = j * LANES + piece * width
            dest, low = channel // cpd, channel % cpd
            rows_at = slice(piece * width, (piece + 1) * width)
            send_ref[dest, low : low + width, :] = mixed[rows_at]
            send_ref[dest, cpd + low : cpd + low + width, :] = delta[rows_at]
    filter_rows = send_ref.shape[1] - 2 * cpd
    for dest in range(per_tile):
        first = (step * per_tile + dest) * gpd
        send_ref[dest, 2 * cpd :, :] = long_rows[pl.ds(first, filter_rows), :].astype(BF16)


def before_exchange(query, key, value, out_grad, tail, taps, long_filter, n, chunk, chunks):
    rows = query.shape[0]
    channels = query.shape[1] // chunks
    groups = long_filter.shape[1] // chunks
    cpd, gpd = channels // n, groups // n
    tile = min(channels, max(512, cpd))
    per_tile = tile // cpd
    filter_rows = round_up(gpd, 16)
    send_rows = 2 * cpd + filter_rows
    first = chunk * channels // tile
    block = pl.BlockSpec((rows, tile), lambda i: (0, first + i))
    own = pl.BlockSpec((rows, tile), lambda i: (0, i))
    ext = pltpu.VMEM((tile // LANES, rows + EDGE, LANES), F32)
    return pl.pallas_call(
        functools.partial(before_kernel, cpd, gpd),
        grid=(channels // tile,),
        in_specs=[block] * 4
        + [
            pl.BlockSpec((3 * EDGE, tile), lambda i: (0, first + i)),
            pl.BlockSpec((3, taps.shape[1], tile), lambda i: (0, 0, first + i)),
            pl.BlockSpec((rows, groups), lambda i: (0, chunk)),
        ],
        out_specs=[pl.BlockSpec((per_tile, send_rows, rows), lambda i: (i, 0, 0)), own, own],
        out_shape=[
            jax.ShapeDtypeStruct((n, send_rows, rows), BF16),
            jax.ShapeDtypeStruct((rows, channels), F32),
            jax.ShapeDtypeStruct((rows, channels), F32),
        ],
        scratch_shapes=[pltpu.VMEM((round_up(groups, 8) + filter_rows, rows), F32), ext, ext, ext],
        compiler_params=params(),
        cost_estimate=pl.CostEstimate(
            flops=50 * rows * channels, bytes_accessed=20 * rows * channels, transcendentals=0
        ),
        name="before_exchange",
    )(query, key, value, out_grad, tail, taps, long_filter)


def long_kernel(cpd, gpd, in_ref, out_ref, taps, wide, gram, raw):
    n, send_rows, rows = in_ref.shape
    gw = cpd // gpd
    span = n * rows
    filter_rows = send_rows - 2 * cpd
    for a in range(n):
        taps[:, a * rows : (a + 1) * rows] = in_ref[a, 2 * cpd :, :].astype(F32)
    if gpd < filter_rows:
        raw[...] = jnp.zeros_like(raw)
    row8 = lax.broadcasted_iota(jnp.int32, (8, span), 0)
    row_tile = lax.broadcasted_iota(jnp.int32, (8, rows), 0)
    lane_tile = lax.broadcasted_iota(jnp.int32, (8, rows), 1)
    no_rows = jnp.zeros((gw, rows), BF16)

    def keep_upper(block, first):
        head = jnp.where(lane_tile >= row_tile + first, block[:, :rows], 0.0)
        return jnp.concatenate([head, block[:, rows:]], 1)

    def one_group(g, slot):
        base = jnp.broadcast_to(taps[pl.ds(g, 1), :], (8, span))
        for bit in (1, 2, 4):
            base = jnp.where((row8 & bit) != 0, pltpu.roll(base, bit, 1), base)
        for m in range(0, rows // 8, 2):
            low = base if m == 0 else pltpu.roll(base, 8 * m, 1)
            high = pltpu.roll(base, 8 * m + 8, 1)
            pair = jnp.concatenate([keep_upper(low, 8 * m), keep_upper(high, 8 * m + 8)], 0)
            wide[slot, 8 * m : 8 * m + 16, :] = pair.astype(BF16)
        first = pl.multiple_of(g * gw, gw)
        x = in_ref[:, pl.ds(first, gw), :].reshape(n * gw, rows)
        second = pl.multiple_of(cpd + g * gw, gw)
        d = in_ref[:, pl.ds(second, gw), :].reshape(n * gw, rows)
        x_turned = x.astype(F32).T.astype(BF16)
        conv = None
        back = None
        for k in range(0, n, 2):
            count = (n - k) * gw
            at = slice(k * rows, (k + 2) * rows)
            ahead = jnp.concatenate([no_rows, x[: count - gw]], 0)
            stacked = jnp.concatenate(
                [
                    wide[slot, :, k * rows : (k + 1) * rows],
                    wide[slot, :, (k + 1) * rows : (k + 2) * rows],
                ],
                0,
            )
            part = jnp.dot(
                jnp.concatenate([x[:count], ahead], 1), stacked, preferred_element_type=F32
            )
            conv = part if k == 0 else jnp.concatenate([conv[: k * gw], conv[k * gw :] + part], 0)
            later = jnp.concatenate([d[(k + 1) * gw :], no_rows], 0)
            pairs = jnp.concatenate([d[k * gw :], later], 1)
            part = lax.dot_general(
                pairs, wide[slot, :, at], (((1,), (1,)), ((), ())), preferred_element_type=F32
            )
            back = part if k == 0 else jnp.concatenate([back[:count] + part, back[count:]], 0)
            if k > 0:
                pairs = jnp.concatenate([pairs, jnp.zeros((k * gw, 2 * rows), BF16)], 0)
            gram[slot, :, at] = jnp.dot(x_turned, pairs, preferred_element_type=F32)
        out_ref[:, pl.ds(first, gw), :] = conv.astype(BF16).reshape(n, gw, rows)
        out_ref[:, pl.ds(second, gw), :] = back.astype(BF16).reshape(n, gw, rows)
        total = keep_upper(gram[slot, 0:8, :], 0)
        for m in range(1, rows // 8):
            block = keep_upper(gram[slot, 8 * m : 8 * m + 8, :], 8 * m)
            total = total + pltpu.roll(block, span - 8 * m, 1)
        for bit in (1, 2, 4):
            total = jnp.where((row8 & bit) != 0, pltpu.roll(total, span - bit, 1), total)
        line = jnp.sum(total, axis=0, keepdims=True)
        raw[pl.ds(g, 1), :] = line
        return line * line

    def body(i, squares):
        squares = squares + one_group(2 * i, 0)
        return squares + one_group(2 * i + 1, 1)

    squares = lax.fori_loop(0, gpd // 2, body, jnp.zeros((1, span), F32))
    total = jnp.sum(squares, axis=1, keepdims=True)
    upper = total.astype(BF16).astype(F32)
    lower = total - upper
    for a in range(n):
        out_ref[a, 2 * cpd : 2 * cpd + filter_rows, :] = raw[:, a * rows : (a + 1) * rows].astype(BF16)
    halo_at = 2 * cpd + filter_rows
    row = lax.broadcasted_iota(jnp.int32, (2 * EDGE, 2 * rows), 0)
    lane = lax.broadcasted_iota(jnp.int32, (2 * EDGE, 2 * rows), 1)
    wanted = jnp.where(row < EDGE, row, rows - EDGE + row)
    pick = jnp.where(lane == wanted, 1.0, 0.0).astype(BF16)
    row_out = lax.broadcasted_iota(jnp.int32, (2 * EDGE, rows), 0)
    for a in range(n):
        if a + 1 < n:
            results = jnp.concatenate([out_ref[a + 1, 0:cpd, :], out_ref[a + 1, cpd : 2 * cpd, :]], 1)
            halo = lax.dot_general(
                pick, results, (((1,), (1,)), ((), ())), preferred_element_type=F32
            )
            if cpd < LANES:
                halo = jnp.concatenate([halo, jnp.zeros((2 * EDGE, LANES - cpd), F32)], 1)
        else:
            halo = jnp.zeros((2 * EDGE, max(cpd, LANES)), F32)
        for j in range(halo.shape[1] // LANES):
            tile = halo[:, j * LANES : (j + 1) * LANES]
            tile = jnp.where(row_out == EDGE - 2, upper, jnp.where(row_out == EDGE - 1, lower, tile))
            at = halo_at + 2 * EDGE * j
            out_ref[a, at : at + 2 * EDGE, :] = tile.astype(BF16)


def long_products(received, cpd, gpd):
    n, send_rows, rows = received.shape
    filter_rows = send_rows - 2 * cpd
    out_rows = send_rows + 2 * EDGE * max(1, cpd // LANES)
    span = n * rows
    return pl.pallas_call(
        functools.partial(long_kernel, cpd, gpd),
        in_specs=[pl.BlockSpec(memory_space=pltpu.VMEM)],
        out_specs=pl.BlockSpec(memory_space=pltpu.VMEM),
        out_shape=jax.ShapeDtypeStruct((n, out_rows, rows), BF16),
        scratch_shapes=[
            pltpu.VMEM((filter_rows, span), F32),
            pltpu.VMEM((2, rows, span), BF16),
            pltpu.VMEM((2, rows, span), F32),
            pltpu.VMEM((filter_rows, span), F32),
        ],
        compiler_params=params(),
        cost_estimate=pl.CostEstimate(
            flops=6 * cpd * span * span, bytes_accessed=4 * n * out_rows * rows, transcendentals=0
        ),
        name="long_products",
    )(received)


def taps_anti(ext_ref, signal, after, filter_taps):
    rows = signal.shape[0]
    ext_ref[0:rows, :] = signal
    ext_ref[rows : rows + EDGE, :] = after
    total = filter_taps[0:1] * signal
    for s in range(1, filter_taps.shape[0]):
        total = total + filter_taps[s : s + 1] * ext_ref[s : s + rows, :]
    return total


def short_edge(before, signal, filter_taps):
    both = jnp.concatenate([before, signal], 0)
    total = filter_taps[0:1] * signal
    for s in range(1, filter_taps.shape[0]):
        total = total + filter_taps[s : s + 1] * both[EDGE - s : 2 * EDGE - s]
    return total


def after_kernel(
    cpd, gpd, in_ref, og_ref, sk_ref, sv_ref, k_end, v_end, next_ref, taps_ref,
    *refs,
):
    dq_ref, dk_ref, dv_ref, raw_ref, raw_rows, ext_q, ext_k, ext_v = refs[-8:]
    step = pl.program_id(0)
    per_tile, in_rows, rows = in_ref.shape
    groups = raw_ref.shape[1]
    halo_rows = 2 * EDGE * max(1, cpd // LANES)
    halo_at = in_rows - halo_rows
    end_rows = k_end.shape[0]
    for j in range(og_ref.shape[1] // LANES):
        at = slice(j * LANES, (j + 1) * LANES)
        if cpd >= LANES:
            dest, low = j * LANES // cpd, j * LANES % cpd
            conv = in_ref[dest, low : low + LANES, :]
            back = in_ref[dest, cpd + low : cpd + low + LANES, :]
            edge = halo_at + 2 * EDGE * (low // LANES)
            halo = in_ref[dest, edge : edge + 2 * EDGE, :].astype(F32)
        else:
            dests = range(j * LANES // cpd, (j + 1) * LANES // cpd)
            conv = jnp.concatenate([in_ref[d, 0:cpd, :] for d in dests], 0)
            back = jnp.concatenate([in_ref[d, cpd : 2 * cpd, :] for d in dests], 0)
            halo = jnp.concatenate(
                [in_ref[d, halo_at:, :].astype(F32)[:, :cpd] for d in dests], 1
            )
        conv = conv.astype(F32).T
        back = back.astype(F32).T
        following = next_ref[:, at].astype(F32)
        taps_k = taps_ref[1, :, at]
        taps_v = taps_ref[2, :, at]
        next_k = short_edge(
            k_end[:, at].astype(F32)[end_rows - EDGE :], following[EDGE : 2 * EDGE], taps_k
        )
        next_v = short_edge(
            v_end[:, at].astype(F32)[end_rows - EDGE :], following[2 * EDGE : 3 * EDGE], taps_v
        )
        grad_q = og_ref[:, at].astype(F32) * conv
        dq_ref[:, at] = taps_anti(
            ext_q.at[j], grad_q, following[0:EDGE] * halo[0:EDGE], taps_ref[0, :, at]
        ).astype(BF16)
        dk_ref[:, at] = taps_anti(
            ext_k.at[j], back * sv_ref[:, at], halo[EDGE:] * next_v, taps_k
        ).astype(BF16)
        dv_ref[:, at] = taps_anti(
            ext_v.at[j], back * sk_ref[:, at], halo[EDGE:] * next_k, taps_v
        ).astype(BF16)
    for dest in range(per_tile):
        lines = in_ref[dest, 2 * cpd : halo_at, :].astype(F32)
        raw_rows[pl.ds((step * per_tile + dest) * gpd, gpd), :] = lines[:gpd]

    @pl.when(step == pl.num_programs(0) - 1)
    def _():
        raw_ref[...] = raw_rows[...].T


def after_exchange(
    returned, out_grad, short_k, short_v, key, value, following, taps, groups, chunk, chunks, grads
):
    n, in_rows, rows = returned.shape
    channels = out_grad.shape[1] // chunks
    groups = groups // chunks
    cpd, gpd = channels // n, groups // n
    tile = min(channels, max(512, cpd))
    per_tile = tile // cpd
    first = chunk * channels // tile
    block = pl.BlockSpec((rows, tile), lambda i: (0, first + i))
    own = pl.BlockSpec((rows, tile), lambda i: (0, i))
    end = pl.BlockSpec((16, tile), lambda i: (rows // 16 - 1, first + i))
    ext = pltpu.VMEM((tile // LANES, rows + EDGE, LANES), F32)
    grad = jax.ShapeDtypeStruct(out_grad.shape, BF16)
    return pl.pallas_call(
        functools.partial(after_kernel, cpd, gpd),
        grid=(channels // tile,),
        in_specs=[
            pl.BlockSpec((per_tile, in_rows, rows), lambda i: (i, 0, 0)),
            block,
            own,
            own,
            end,
            end,
            pl.BlockSpec((3 * EDGE, tile), lambda i: (0, first + i)),
            pl.BlockSpec((3, taps.shape[1], tile), lambda i: (0, 0, first + i)),
        ]
        + [pl.BlockSpec(memory_space=pl.ANY)] * len(grads),
        input_output_aliases={8 + i: i for i in range(len(grads))},
        out_specs=[block, block, block, pl.BlockSpec((rows, groups), lambda i: (0, 0))],
        out_shape=[grad, grad, grad, jax.ShapeDtypeStruct((rows, groups), F32)],
        scratch_shapes=[pltpu.VMEM((groups, rows), F32), ext, ext, ext],
        compiler_params=params(),
        cost_estimate=pl.CostEstimate(
            flops=60 * rows * channels, bytes_accessed=22 * rows * channels, transcendentals=0
        ),
        name="after_exchange",
    )(returned, out_grad, short_k, short_v, key, value, following, taps, *grads)


def on_device(
    query_heads,
    key_heads,
    value_heads,
    hyena_query,
    hyena_key,
    hyena_value,
    short_filter,
    long_filter,
    output_grad,
):
    rows, channels = query_heads.shape
    groups = long_filter.shape[1]
    n = lax.axis_size("ctx")
    tp = lax.axis_size("tp")
    cpd, gpd = channels // n, groups // n
    position = lax.axis_index("ctx")
    tail = shifted(
        jnp.concatenate([a[rows - EDGE :] for a in (hyena_query, hyena_key, hyena_value)], 0), "ctx", 1
    )
    key_prev = shifted(key_heads, "ctx", 1)
    value_prev = shifted(value_heads, "ctx", 1)
    following = shifted(
        jnp.concatenate([a[:EDGE] for a in (output_grad, hyena_key, hyena_value)], 0), "ctx", -1
    )
    chunks = 2 if gpd % 4 == 0 else 1
    cpd, gpd = cpd // chunks, gpd // chunks
    received = []
    shorts = []
    for chunk in range(chunks):
        send, short_k, short_v = before_exchange(
            hyena_query, hyena_key, hyena_value, output_grad, tail, short_filter, long_filter, n, chunk, chunks
        )
        if chunk + 1 < chunks:
            send, tail = lax.optimization_barrier((send, tail))
        shorts.append((short_k, short_v))
        received.append(lax.all_to_all(send, "ctx", split_axis=0, concat_axis=0, tiled=True))
    attention = attend(query_heads, key_heads, value_heads, key_prev, value_prev, position)
    received[0], attention = lax.optimization_barrier((received[0], attention))
    returned = []
    for chunk in range(chunks):
        results = long_products(received[chunk], cpd, gpd)
        if chunk + 1 < chunks:
            results, received[chunk + 1] = lax.optimization_barrier((results, received[chunk + 1]))
        returned.append(lax.all_to_all(results, "ctx", split_axis=0, concat_axis=0, tiled=True))
    norm_at = returned[0].shape[1] - 2 * EDGE * max(1, cpd // LANES) + EDGE - 2
    own_squares = sum(jnp.sum(r[:, norm_at : norm_at + 2, 0].astype(F32)) for r in returned).reshape(1, 1)
    squares = own_squares
    for distance in range(1, tp):
        route = [(i, (i + distance) % tp) for i in range(tp)]
        squares = squares + lax.ppermute(own_squares, "tp", route)
    grads = ()
    raws = []
    for chunk in range(chunks):
        *grads, raw = after_exchange(
            returned[chunk], output_grad, *shorts[chunk], hyena_key, hyena_value, following, short_filter,
            groups, chunk, chunks, grads,
        )
        raws.append(raw)
    bound = math.sqrt(rows * n * groups * tp)
    factor = jnp.minimum(1.0, bound / jnp.sqrt(squares))
    raw_grad = raws[0] if chunks == 1 else jnp.concatenate(raws, 1)
    return (attention, *grads, raw_grad * factor)


def solution(mesh):
    whole = P("ctx", "tp")
    in_specs = (whole,) * 6 + (P(None, None, "tp"), whole, whole)
    return jax.shard_map(
        on_device, mesh=mesh, in_specs=in_specs, out_specs=(whole,) * 5, check_vma=False
    )
```

```python
import functools
import math

import jax
import jax.numpy as jnp
from jax import lax
from jax.experimental import pallas as pl
from jax.experimental.pallas import tpu as pltpu
from jax.sharding import PartitionSpec as P

HEAD_DIM = 128
LANES = 128
EDGE = 8
F32 = jnp.float32
BF16 = jnp.bfloat16
VMEM_BYTES = 60 * 1024 * 1024


def params():
    return pltpu.CompilerParams(vmem_limit_bytes=VMEM_BYTES)


def shifted(block, axis, distance):
    devices = range(lax.axis_size(axis))
    route = [(i - distance, i) for i in devices if i - distance in devices]
    return lax.ppermute(block, axis, route)


def round_up(value, step):
    return -(-value // step) * step


def attend_kernel(place_ref, q_ref, k_ref, v_ref, kp_ref, vp_ref, out_ref):
    rows = q_ref.shape[0]
    row = lax.broadcasted_iota(jnp.int32, (rows, rows), 0)
    col = lax.broadcasted_iota(jnp.int32, (rows, rows), 1)
    own_ok = col <= row
    prev_ok = jnp.broadcast_to(place_ref[0], (rows, rows)) > 0
    contract = (((1,), (1,)), ((), ()))
    for head in range(q_ref.shape[1] // HEAD_DIM):
        at = slice(head * HEAD_DIM, (head + 1) * HEAD_DIM)
        scale = 1.0 / math.sqrt(HEAD_DIM)
        query = q_ref[:, at]
        own = lax.dot_general(query, k_ref[:, at], contract, preferred_element_type=F32) * scale
        prev = lax.dot_general(query, kp_ref[:, at], contract, preferred_element_type=F32) * scale
        own = jnp.where(own_ok, own, -jnp.inf)
        prev = jnp.where(prev_ok, prev, -jnp.inf)
        largest = jnp.max(jnp.maximum(own, prev), axis=1, keepdims=True)
        own = jnp.exp(own - largest)
        prev = jnp.exp(prev - largest)
        total = jnp.sum(own + prev, axis=1, keepdims=True)
        inverse = 1.0 / total
        own = (own * inverse).astype(BF16)
        prev = (prev * inverse).astype(BF16)
        mixed = jnp.dot(own, v_ref[:, at], preferred_element_type=F32) + jnp.dot(
            prev, vp_ref[:, at], preferred_element_type=F32
        )
        out_ref[:, at] = mixed.astype(BF16)


def attend(query, key, value, key_prev, value_prev, position):
    rows, channels = query.shape
    tile = min(512, channels)
    block = pl.BlockSpec((rows, tile), lambda i: (0, i))
    heads = channels // HEAD_DIM
    return pl.pallas_call(
        attend_kernel,
        grid=(channels // tile,),
        in_specs=[pl.BlockSpec(memory_space=pltpu.SMEM)] + [block] * 5,
        out_specs=block,
        out_shape=jax.ShapeDtypeStruct((rows, channels), BF16),
        compiler_params=params(),
        cost_estimate=pl.CostEstimate(
            flops=8 * heads * rows * rows * HEAD_DIM,
            bytes_accessed=12 * rows * channels,
            transcendentals=2 * heads * rows * rows,
        ),
        name="attend",
    )(position.astype(jnp.int32).reshape(1), query, key, value, key_prev, value_prev)


def taps_causal(ext_ref, before, signal, filter_taps):
    rows = signal.shape[0]
    ext_ref[0:EDGE, :] = before
    ext_ref[EDGE : EDGE + rows, :] = signal
    total = filter_taps[0:1] * signal
    for s in range(1, filter_taps.shape[0]):
        total = total + filter_taps[s : s + 1] * ext_ref[EDGE - s : EDGE - s + rows, :]
    return total


def before_kernel(
    cpd, gpd, q_ref, k_ref, v_ref, og_ref, tail_ref, taps_ref, long_ref, send_ref, sk_ref, sv_ref,
    long_rows, ext_q, ext_k, ext_v,
):
    step = pl.program_id(0)
    groups = long_ref.shape[1]
    per_tile, _, rows = send_ref.shape

    @pl.when(step == 0)
    def _():
        long_rows[...] = jnp.zeros_like(long_rows)
        long_rows[0:groups, :] = long_ref[...].T

    for j in range(q_ref.shape[1] // LANES):
        at = slice(j * LANES, (j + 1) * LANES)
        tail = tail_ref[:, at].astype(F32)
        short_q = taps_causal(ext_q.at[j], tail[0:EDGE], q_ref[:, at].astype(F32), taps_ref[0, :, at])
        short_k = taps_causal(
            ext_k.at[j], tail[EDGE : 2 * EDGE], k_ref[:, at].astype(F32), taps_ref[1, :, at]
        )
        short_v = taps_causal(
            ext_v.at[j], tail[2 * EDGE : 3 * EDGE], v_ref[:, at].astype(F32), taps_ref[2, :, at]
        )
        sk_ref[:, at] = short_k
        sv_ref[:, at] = short_v
        mixed = (short_k * short_v).T.astype(BF16)
        delta = (og_ref[:, at].astype(F32) * short_q).T.astype(BF16)
        width = min(cpd, LANES)
        for piece in range(LANES // width):
            channel = j * LANES + piece * width
            dest, low = channel // cpd, channel % cpd
            rows_at = slice(piece * width, (piece + 1) * width)
            send_ref[dest, low : low + width, :] = mixed[rows_at]
            send_ref[dest, cpd + low : cpd + low + width, :] = delta[rows_at]
    filter_rows = send_ref.shape[1] - 2 * cpd
    for dest in range(per_tile):
        first = (step * per_tile + dest) * gpd
        send_ref[dest, 2 * cpd :, :] = long_rows[pl.ds(first, filter_rows), :].astype(BF16)


def before_exchange(query, key, value, out_grad, tail, taps, long_filter, n, chunks):
    rows, channels = query.shape
    groups = long_filter.shape[1]
    cpd, gpd = channels // (n * chunks), groups // (n * chunks)
    tile = min(channels // chunks, max(512, cpd))
    per_tile = tile // cpd
    filter_rows = round_up(gpd, 16)
    send_rows = 2 * cpd + filter_rows
    steps = n // per_tile
    block = pl.BlockSpec((rows, tile), lambda i: (0, i))
    ext = pltpu.VMEM((tile // LANES, rows + EDGE, LANES), F32)
    return pl.pallas_call(
        functools.partial(before_kernel, cpd, gpd),
        grid=(channels // tile,),
        in_specs=[block] * 4
        + [
            pl.BlockSpec((3 * EDGE, tile), lambda i: (0, i)),
            pl.BlockSpec((3, taps.shape[1], tile), lambda i: (0, 0, i)),
            pl.BlockSpec((rows, groups), lambda i: (0, 0)),
        ],
        out_specs=[
            pl.BlockSpec((per_tile, send_rows, rows), lambda i: (i % steps, i // steps, 0)),
            block,
            block,
        ],
        out_shape=[
            jax.ShapeDtypeStruct((n, chunks * send_rows, rows), BF16),
            jax.ShapeDtypeStruct((rows, channels), F32),
            jax.ShapeDtypeStruct((rows, channels), F32),
        ],
        scratch_shapes=[pltpu.VMEM((round_up(groups, 8) + filter_rows, rows), F32), ext, ext, ext],
        compiler_params=params(),
        cost_estimate=pl.CostEstimate(
            flops=50 * rows * channels, bytes_accessed=20 * rows * channels, transcendentals=0
        ),
        name="before_exchange",
    )(query, key, value, out_grad, tail, taps, long_filter)


def long_kernel(cpd, gpd, in_ref, out_ref, taps, wide, gram, raw):
    n, send_rows, rows = in_ref.shape
    gw = cpd // gpd
    span = n * rows
    filter_rows = send_rows - 2 * cpd
    for a in range(n):
        taps[:, a * rows : (a + 1) * rows] = in_ref[a, 2 * cpd :, :].astype(F32)
    if gpd < filter_rows:
        raw[...] = jnp.zeros_like(raw)
    row8 = lax.broadcasted_iota(jnp.int32, (8, span), 0)
    row_tile = lax.broadcasted_iota(jnp.int32, (8, rows), 0)
    lane_tile = lax.broadcasted_iota(jnp.int32, (8, rows), 1)
    no_rows = jnp.zeros((gw, rows), BF16)

    def keep_upper(block, first):
        head = jnp.where(lane_tile >= row_tile + first, block[:, :rows], 0.0)
        return jnp.concatenate([head, block[:, rows:]], 1)

    def one_group(g, slot):
        base = jnp.broadcast_to(taps[pl.ds(g, 1), :], (8, span))
        for bit in (1, 2, 4):
            base = jnp.where((row8 & bit) != 0, pltpu.roll(base, bit, 1), base)
        for m in range(0, rows // 8, 2):
            low = base if m == 0 else pltpu.roll(base, 8 * m, 1)
            high = pltpu.roll(base, 8 * m + 8, 1)
            pair = jnp.concatenate([keep_upper(low, 8 * m), keep_upper(high, 8 * m + 8)], 0)
            wide[slot, 8 * m : 8 * m + 16, :] = pair.astype(BF16)
        first = pl.multiple_of(g * gw, gw)
        x = in_ref[:, pl.ds(first, gw), :].reshape(n * gw, rows)
        second = pl.multiple_of(cpd + g * gw, gw)
        d = in_ref[:, pl.ds(second, gw), :].reshape(n * gw, rows)
        x_turned = x.astype(F32).T.astype(BF16)
        conv = None
        back = None
        for k in range(0, n, 2):
            count = (n - k) * gw
            at = slice(k * rows, (k + 2) * rows)
            ahead = jnp.concatenate([no_rows, x[: count - gw]], 0)
            stacked = jnp.concatenate(
                [
                    wide[slot, :, k * rows : (k + 1) * rows],
                    wide[slot, :, (k + 1) * rows : (k + 2) * rows],
                ],
                0,
            )
            part = jnp.dot(
                jnp.concatenate([x[:count], ahead], 1), stacked, preferred_element_type=F32
            )
            conv = part if k == 0 else jnp.concatenate([conv[: k * gw], conv[k * gw :] + part], 0)
            later = jnp.concatenate([d[(k + 1) * gw :], no_rows], 0)
            pairs = jnp.concatenate([d[k * gw :], later], 1)
            part = lax.dot_general(
                pairs, wide[slot, :, at], (((1,), (1,)), ((), ())), preferred_element_type=F32
            )
            back = part if k == 0 else jnp.concatenate([back[:count] + part, back[count:]], 0)
            if k > 0:
                pairs = jnp.concatenate([pairs, jnp.zeros((k * gw, 2 * rows), BF16)], 0)
            gram[slot, :, at] = jnp.dot(x_turned, pairs, preferred_element_type=F32)
        out_ref[:, pl.ds(first, gw), :] = conv.astype(BF16).reshape(n, gw, rows)
        out_ref[:, pl.ds(second, gw), :] = back.astype(BF16).reshape(n, gw, rows)
        total = keep_upper(gram[slot, 0:8, :], 0)
        for m in range(1, rows // 8):
            block = keep_upper(gram[slot, 8 * m : 8 * m + 8, :], 8 * m)
            total = total + pltpu.roll(block, span - 8 * m, 1)
        for bit in (1, 2, 4):
            total = jnp.where((row8 & bit) != 0, pltpu.roll(total, span - bit, 1), total)
        line = jnp.sum(total, axis=0, keepdims=True)
        raw[pl.ds(g, 1), :] = line
        return line * line

    def body(i, squares):
        squares = squares + one_group(2 * i, 0)
        return squares + one_group(2 * i + 1, 1)

    squares = lax.fori_loop(0, gpd // 2, body, jnp.zeros((1, span), F32))
    total = jnp.sum(squares, axis=1, keepdims=True)
    upper = total.astype(BF16).astype(F32)
    lower = total - upper
    for a in range(n):
        out_ref[a, 2 * cpd : 2 * cpd + filter_rows, :] = raw[:, a * rows : (a + 1) * rows].astype(BF16)
    halo_at = 2 * cpd + filter_rows
    row = lax.broadcasted_iota(jnp.int32, (2 * EDGE, 2 * rows), 0)
    lane = lax.broadcasted_iota(jnp.int32, (2 * EDGE, 2 * rows), 1)
    wanted = jnp.where(row < EDGE, row, rows - EDGE + row)
    pick = jnp.where(lane == wanted, 1.0, 0.0).astype(BF16)
    row_out = lax.broadcasted_iota(jnp.int32, (2 * EDGE, rows), 0)
    for a in range(n):
        if a + 1 < n:
            results = jnp.concatenate([out_ref[a + 1, 0:cpd, :], out_ref[a + 1, cpd : 2 * cpd, :]], 1)
            halo = lax.dot_general(
                pick, results, (((1,), (1,)), ((), ())), preferred_element_type=F32
            )
            if cpd < LANES:
                halo = jnp.concatenate([halo, jnp.zeros((2 * EDGE, LANES - cpd), F32)], 1)
        else:
            halo = jnp.zeros((2 * EDGE, max(cpd, LANES)), F32)
        for j in range(halo.shape[1] // LANES):
            tile = halo[:, j * LANES : (j + 1) * LANES]
            tile = jnp.where(row_out == EDGE - 2, upper, jnp.where(row_out == EDGE - 1, lower, tile))
            at = halo_at + 2 * EDGE * j
            out_ref[a, at : at + 2 * EDGE, :] = tile.astype(BF16)


def long_products(received, cpd, gpd, chunk, chunks):
    n, send_rows, rows = received.shape
    send_rows = send_rows // chunks
    filter_rows = send_rows - 2 * cpd
    out_rows = send_rows + 2 * EDGE * max(1, cpd // LANES)
    span = n * rows
    return pl.pallas_call(
        functools.partial(long_kernel, cpd, gpd),
        grid=(1,),
        in_specs=[pl.BlockSpec((n, send_rows, rows), lambda i: (0, chunk, 0))],
        out_specs=pl.BlockSpec((n, out_rows, rows), lambda i: (0, 0, 0)),
        out_shape=jax.ShapeDtypeStruct((n, out_rows, rows), BF16),
        scratch_shapes=[
            pltpu.VMEM((filter_rows, span), F32),
            pltpu.VMEM((2, rows, span), BF16),
            pltpu.VMEM((2, rows, span), F32),
            pltpu.VMEM((filter_rows, span), F32),
        ],
        compiler_params=params(),
        cost_estimate=pl.CostEstimate(
            flops=6 * cpd * span * span, bytes_accessed=4 * n * out_rows * rows, transcendentals=0
        ),
        name="long_products",
    )(received)


def taps_anti(ext_ref, signal, after, filter_taps):
    rows = signal.shape[0]
    ext_ref[0:rows, :] = signal
    ext_ref[rows : rows + EDGE, :] = after
    total = filter_taps[0:1] * signal
    for s in range(1, filter_taps.shape[0]):
        total = total + filter_taps[s : s + 1] * ext_ref[s : s + rows, :]
    return total


def short_edge(before, signal, filter_taps):
    both = jnp.concatenate([before, signal], 0)
    total = filter_taps[0:1] * signal
    for s in range(1, filter_taps.shape[0]):
        total = total + filter_taps[s : s + 1] * both[EDGE - s : 2 * EDGE - s]
    return total


def after_kernel(
    cpd, gpd, in_ref, og_ref, sk_ref, sv_ref, k_end, v_end, next_ref, taps_ref,
    *refs,
):
    dq_ref, dk_ref, dv_ref, raw_ref, raw_rows, ext_q, ext_k, ext_v = refs[-8:]
    step = pl.program_id(0)
    per_tile, in_rows, rows = in_ref.shape
    groups = raw_ref.shape[1]
    halo_rows = 2 * EDGE * max(1, cpd // LANES)
    halo_at = in_rows - halo_rows
    end_rows = k_end.shape[0]
    for j in range(og_ref.shape[1] // LANES):
        at = slice(j * LANES, (j + 1) * LANES)
        if cpd >= LANES:
            dest, low = j * LANES // cpd, j * LANES % cpd
            conv = in_ref[dest, low : low + LANES, :]
            back = in_ref[dest, cpd + low : cpd + low + LANES, :]
            edge = halo_at + 2 * EDGE * (low // LANES)
            halo = in_ref[dest, edge : edge + 2 * EDGE, :].astype(F32)
        else:
            dests = range(j * LANES // cpd, (j + 1) * LANES // cpd)
            conv = jnp.concatenate([in_ref[d, 0:cpd, :] for d in dests], 0)
            back = jnp.concatenate([in_ref[d, cpd : 2 * cpd, :] for d in dests], 0)
            halo = jnp.concatenate(
                [in_ref[d, halo_at:, :].astype(F32)[:, :cpd] for d in dests], 1
            )
        conv = conv.astype(F32).T
        back = back.astype(F32).T
        following = next_ref[:, at].astype(F32)
        taps_k = taps_ref[1, :, at]
        taps_v = taps_ref[2, :, at]
        next_k = short_edge(
            k_end[:, at].astype(F32)[end_rows - EDGE :], following[EDGE : 2 * EDGE], taps_k
        )
        next_v = short_edge(
            v_end[:, at].astype(F32)[end_rows - EDGE :], following[2 * EDGE : 3 * EDGE], taps_v
        )
        grad_q = og_ref[:, at].astype(F32) * conv
        dq_ref[:, at] = taps_anti(
            ext_q.at[j], grad_q, following[0:EDGE] * halo[0:EDGE], taps_ref[0, :, at]
        ).astype(BF16)
        dk_ref[:, at] = taps_anti(
            ext_k.at[j], back * sv_ref[:, at], halo[EDGE:] * next_v, taps_k
        ).astype(BF16)
        dv_ref[:, at] = taps_anti(
            ext_v.at[j], back * sk_ref[:, at], halo[EDGE:] * next_k, taps_v
        ).astype(BF16)
    for dest in range(per_tile):
        lines = in_ref[dest, 2 * cpd : halo_at, :].astype(F32)
        raw_rows[pl.ds((step * per_tile + dest) * gpd, gpd), :] = lines[:gpd]

    @pl.when(step == pl.num_programs(0) - 1)
    def _():
        raw_ref[...] = raw_rows[...].T


def after_exchange(
    returned, out_grad, short_k, short_v, key, value, following, taps, groups, chunk, chunks, grads
):
    n, in_rows, rows = returned.shape
    channels = out_grad.shape[1] // chunks
    groups = groups // chunks
    cpd, gpd = channels // n, groups // n
    tile = min(channels, max(512, cpd))
    per_tile = tile // cpd
    first = chunk * channels // tile
    block = pl.BlockSpec((rows, tile), lambda i: (0, first + i))
    end = pl.BlockSpec((16, tile), lambda i: (rows // 16 - 1, first + i))
    ext = pltpu.VMEM((tile // LANES, rows + EDGE, LANES), F32)
    grad = jax.ShapeDtypeStruct(out_grad.shape, BF16)
    return pl.pallas_call(
        functools.partial(after_kernel, cpd, gpd),
        grid=(channels // tile,),
        in_specs=[
            pl.BlockSpec((per_tile, in_rows, rows), lambda i: (i, 0, 0)),
            block,
            block,
            block,
            end,
            end,
            pl.BlockSpec((3 * EDGE, tile), lambda i: (0, first + i)),
            pl.BlockSpec((3, taps.shape[1], tile), lambda i: (0, 0, first + i)),
        ]
        + [pl.BlockSpec(memory_space=pl.ANY)] * len(grads),
        input_output_aliases={8 + i: i for i in range(len(grads))},
        out_specs=[block, block, block, pl.BlockSpec((rows, groups), lambda i: (0, 0))],
        out_shape=[grad, grad, grad, jax.ShapeDtypeStruct((rows, groups), F32)],
        scratch_shapes=[pltpu.VMEM((groups, rows), F32), ext, ext, ext],
        compiler_params=params(),
        cost_estimate=pl.CostEstimate(
            flops=60 * rows * channels, bytes_accessed=22 * rows * channels, transcendentals=0
        ),
        name="after_exchange",
    )(returned, out_grad, short_k, short_v, key, value, following, taps, *grads)


def on_device(
    query_heads,
    key_heads,
    value_heads,
    hyena_query,
    hyena_key,
    hyena_value,
    short_filter,
    long_filter,
    output_grad,
):
    rows, channels = query_heads.shape
    groups = long_filter.shape[1]
    n = lax.axis_size("ctx")
    tp = lax.axis_size("tp")
    cpd, gpd = channels // n, groups // n
    position = lax.axis_index("ctx")
    tail = shifted(
        jnp.concatenate([a[rows - EDGE :] for a in (hyena_query, hyena_key, hyena_value)], 0), "ctx", 1
    )
    key_prev = shifted(key_heads, "ctx", 1)
    value_prev = shifted(value_heads, "ctx", 1)
    following = shifted(
        jnp.concatenate([a[:EDGE] for a in (output_grad, hyena_key, hyena_value)], 0), "ctx", -1
    )
    chunks = 2 if gpd % 4 == 0 else 1
    cpd, gpd = cpd // chunks, gpd // chunks
    send, short_k, short_v = before_exchange(
        hyena_query, hyena_key, hyena_value, output_grad, tail, short_filter, long_filter, n, chunks
    )
    received = lax.all_to_all(send, "ctx", split_axis=0, concat_axis=0, tiled=True)
    returned = []
    for chunk in range(chunks):
        results = long_products(received, cpd, gpd, chunk, chunks)
        if chunk == 0:
            results, received, key_prev, value_prev = lax.optimization_barrier(
                (results, received, key_prev, value_prev)
            )
        returned.append(lax.all_to_all(results, "ctx", split_axis=0, concat_axis=0, tiled=True))
    attention = attend(query_heads, key_heads, value_heads, key_prev, value_prev, position)
    norm_at = returned[0].shape[1] - 2 * EDGE * max(1, cpd // LANES) + EDGE - 2
    own_squares = sum(jnp.sum(r[:, norm_at : norm_at + 2, 0].astype(F32)) for r in returned).reshape(1, 1)
    squares = own_squares
    for distance in range(1, tp):
        route = [(i, (i + distance) % tp) for i in range(tp)]
        squares = squares + lax.ppermute(own_squares, "tp", route)
    grads = ()
    raws = []
    for chunk in range(chunks):
        *grads, raw = after_exchange(
            returned[chunk], output_grad, short_k, short_v, hyena_key, hyena_value, following, short_filter,
            groups, chunk, chunks, grads,
        )
        raws.append(raw)
    bound = math.sqrt(rows * n * groups * tp)
    factor = jnp.minimum(1.0, bound / jnp.sqrt(squares))
    raw_grad = raws[0] if chunks == 1 else jnp.concatenate(raws, 1)
    return (attention, *grads, raw_grad * factor)


def solution(mesh):
    whole = P("ctx", "tp")
    in_specs = (whole,) * 6 + (P(None, None, "tp"), whole, whole)
    return jax.shard_map(
        on_device, mesh=mesh, in_specs=in_specs, out_specs=(whole,) * 5, check_vma=False
    )
```

```python
import functools
import math

import jax
import jax.numpy as jnp
from jax import lax
from jax.experimental import pallas as pl
from jax.experimental.pallas import tpu as pltpu
from jax.sharding import PartitionSpec as P

HEAD_DIM = 128
LANES = 128
EDGE = 8
F32 = jnp.float32
BF16 = jnp.bfloat16
VMEM_BYTES = 60 * 1024 * 1024


def params():
    return pltpu.CompilerParams(vmem_limit_bytes=VMEM_BYTES)


def shifted(block, axis, distance):
    devices = range(lax.axis_size(axis))
    route = [(i - distance, i) for i in devices if i - distance in devices]
    return lax.ppermute(block, axis, route)


def round_up(value, step):
    return -(-value // step) * step


def reversal(size):
    row = lax.broadcasted_iota(jnp.int32, (size, size), 0)
    col = lax.broadcasted_iota(jnp.int32, (size, size), 1)
    return jnp.where(row + col == size - 1, 1.0, 0.0).astype(BF16)


def attend_kernel(place_ref, q_ref, k_ref, v_ref, kp_ref, vp_ref, out_ref):
    rows = q_ref.shape[0]
    row = lax.broadcasted_iota(jnp.int32, (rows, rows), 0)
    col = lax.broadcasted_iota(jnp.int32, (rows, rows), 1)
    own_ok = col <= row
    prev_ok = jnp.broadcast_to(place_ref[0], (rows, rows)) > 0
    contract = (((1,), (1,)), ((), ()))
    for head in range(q_ref.shape[1] // HEAD_DIM):
        at = slice(head * HEAD_DIM, (head + 1) * HEAD_DIM)
        scale = 1.0 / math.sqrt(HEAD_DIM)
        query = q_ref[:, at]
        own = lax.dot_general(query, k_ref[:, at], contract, preferred_element_type=F32) * scale
        prev = lax.dot_general(query, kp_ref[:, at], contract, preferred_element_type=F32) * scale
        own = jnp.where(own_ok, own, -jnp.inf)
        prev = jnp.where(prev_ok, prev, -jnp.inf)
        largest = jnp.max(jnp.maximum(own, prev), axis=1, keepdims=True)
        own = jnp.exp(own - largest)
        prev = jnp.exp(prev - largest)
        total = jnp.sum(own + prev, axis=1, keepdims=True)
        inverse = 1.0 / total
        own = (own * inverse).astype(BF16)
        prev = (prev * inverse).astype(BF16)
        mixed = jnp.dot(own, v_ref[:, at], preferred_element_type=F32) + jnp.dot(
            prev, vp_ref[:, at], preferred_element_type=F32
        )
        out_ref[:, at] = mixed.astype(BF16)


def attend(query, key, value, key_prev, value_prev, position):
    rows, channels = query.shape
    tile = min(512, channels)
    block = pl.BlockSpec((rows, tile), lambda i: (0, i))
    heads = channels // HEAD_DIM
    return pl.pallas_call(
        attend_kernel,
        grid=(channels // tile,),
        in_specs=[pl.BlockSpec(memory_space=pltpu.SMEM)] + [block] * 5,
        out_specs=block,
        out_shape=jax.ShapeDtypeStruct((rows, channels), BF16),
        compiler_params=params(),
        cost_estimate=pl.CostEstimate(
            flops=8 * heads * rows * rows * HEAD_DIM,
            bytes_accessed=12 * rows * channels,
            transcendentals=2 * heads * rows * rows,
        ),
        name="attend",
    )(position.astype(jnp.int32).reshape(1), query, key, value, key_prev, value_prev)


def taps_causal(ext_ref, before, signal, filter_taps):
    rows = signal.shape[0]
    ext_ref[0:EDGE, :] = before
    ext_ref[EDGE : EDGE + rows, :] = signal
    total = filter_taps[0:1] * signal
    for s in range(1, filter_taps.shape[0]):
        total = total + filter_taps[s : s + 1] * ext_ref[EDGE - s : EDGE - s + rows, :]
    return total


def before_kernel(
    cpd, gpd, q_ref, k_ref, v_ref, og_ref, tail_ref, taps_ref, long_ref, send_ref, sk_ref, sv_ref,
    long_rows, ext_q, ext_k, ext_v,
):
    step = pl.program_id(0)
    groups = long_ref.shape[1]
    per_tile, _, rows = send_ref.shape

    @pl.when(step == 0)
    def _():
        long_rows[...] = jnp.zeros_like(long_rows)
        long_rows[0:groups, :] = long_ref[...].T

    turn = reversal(rows)
    for j in range(q_ref.shape[1] // LANES):
        at = slice(j * LANES, (j + 1) * LANES)
        tail = tail_ref[:, at].astype(F32)
        short_q = taps_causal(ext_q.at[j], tail[0:EDGE], q_ref[:, at].astype(F32), taps_ref[0, :, at])
        short_k = taps_causal(
            ext_k.at[j], tail[EDGE : 2 * EDGE], k_ref[:, at].astype(F32), taps_ref[1, :, at]
        )
        short_v = taps_causal(
            ext_v.at[j], tail[2 * EDGE : 3 * EDGE], v_ref[:, at].astype(F32), taps_ref[2, :, at]
        )
        sk_ref[:, at] = short_k
        sv_ref[:, at] = short_v
        mixed = (short_k * short_v).T.astype(BF16)
        delta = (og_ref[:, at].astype(F32) * short_q).T.astype(BF16)
        delta = jnp.dot(delta, turn, preferred_element_type=F32).astype(BF16)
        width = min(cpd, LANES)
        for piece in range(LANES // width):
            channel = j * LANES + piece * width
            dest, low = channel // cpd, channel % cpd
            rows_at = slice(piece * width, (piece + 1) * width)
            send_ref[dest, low : low + width, :] = mixed[rows_at]
            send_ref[dest, cpd + low : cpd + low + width, :] = delta[rows_at]
    filter_rows = send_ref.shape[1] - 2 * cpd
    for dest in range(per_tile):
        first = (step * per_tile + dest) * gpd
        send_ref[dest, 2 * cpd :, :] = long_rows[pl.ds(first, filter_rows), :].astype(BF16)


def before_exchange(query, key, value, out_grad, tail, taps, long_filter, n, chunks):
    rows, channels = query.shape
    groups = long_filter.shape[1]
    cpd, gpd = channels // (n * chunks), groups // (n * chunks)
    tile = min(channels // chunks, max(512, cpd))
    per_tile = tile // cpd
    filter_rows = round_up(gpd, 16)
    send_rows = 2 * cpd + filter_rows
    steps = n // per_tile
    block = pl.BlockSpec((rows, tile), lambda i: (0, i))
    ext = pltpu.VMEM((tile // LANES, rows + EDGE, LANES), F32)
    return pl.pallas_call(
        functools.partial(before_kernel, cpd, gpd),
        grid=(channels // tile,),
        in_specs=[block] * 4
        + [
            pl.BlockSpec((3 * EDGE, tile), lambda i: (0, i)),
            pl.BlockSpec((3, taps.shape[1], tile), lambda i: (0, 0, i)),
            pl.BlockSpec((rows, groups), lambda i: (0, 0)),
        ],
        out_specs=[
            pl.BlockSpec((per_tile, send_rows, rows), lambda i: (i % steps, i // steps, 0)),
            block,
            block,
        ],
        out_shape=[
            jax.ShapeDtypeStruct((n, chunks * send_rows, rows), BF16),
            jax.ShapeDtypeStruct((rows, channels), F32),
            jax.ShapeDtypeStruct((rows, channels), F32),
        ],
        scratch_shapes=[pltpu.VMEM((round_up(groups, 8) + filter_rows, rows), F32), ext, ext, ext],
        compiler_params=params(),
        cost_estimate=pl.CostEstimate(
            flops=50 * rows * channels, bytes_accessed=20 * rows * channels, transcendentals=0
        ),
        name="before_exchange",
    )(query, key, value, out_grad, tail, taps, long_filter)


def long_kernel(cpd, gpd, in_ref, out_ref, taps, wide, gram, raw):
    n, send_rows, rows = in_ref.shape
    gw = cpd // gpd
    span = n * rows
    filter_rows = send_rows - 2 * cpd
    taps[:, 0:rows] = jnp.zeros((filter_rows, rows), F32)
    for a in range(n):
        taps[:, (a + 1) * rows : (a + 2) * rows] = in_ref[a, 2 * cpd :, :].astype(F32)
    for slot in range(2):
        wide[slot, :, 0:rows] = jnp.zeros((rows, rows), BF16)
        gram[slot, :, span:] = jnp.zeros((rows, rows), F32)
    if gpd < filter_rows:
        raw[...] = jnp.zeros_like(raw)
    turn = reversal(rows)

    def one_group(g, slot):
        line = jnp.broadcast_to(taps[pl.ds(g, 1), :], (16, span + rows))
        base = pltpu.roll(line, 0, 1, stride=1, stride_axis=0).astype(BF16)
        for m in range(rows // 16):
            moved = base if m == 0 else pltpu.roll(base, 16 * m, 1)
            wide[slot, 16 * m : 16 * m + 16, rows:] = moved[:, rows:]
        first = pl.multiple_of(g * gw, gw)
        x = in_ref[:, pl.ds(first, gw), :]
        second = pl.multiple_of(cpd + g * gw, gw)
        d = in_ref[:, pl.ds(second, gw), :]
        both = [jnp.concatenate([x[a], d[n - 1 - a]], 0) for a in range(n)]
        lhs = jnp.concatenate(
            [jnp.concatenate([both[a], both[a + 1]], 1) for a in range(0, n, 2)], 0
        )
        total = None
        for k in range(n // 2):
            skip = 2 * gw * k
            low = 2 * rows * k
            tile = jnp.concatenate(
                [wide[slot, :, low + rows : low + 3 * rows], wide[slot, :, low : low + 2 * rows]], 0
            )
            part = jnp.dot(lhs[: n * gw - skip], tile, preferred_element_type=F32)
            total = part if k == 0 else jnp.concatenate([total[:skip], total[skip:] + part], 0)
        for a in range(n):
            at = slice(a % 2 * rows, (a % 2 + 1) * rows)
            top = a // 2 * 2 * gw
            out_ref[a, pl.ds(first, gw), :] = total[top : top + gw, at].astype(BF16)
            out_ref[n - 1 - a, pl.ds(second, gw), :] = total[top + gw : top + 2 * gw, at].astype(BF16)
        x_turned = x.reshape(n * gw, rows).astype(F32).T.astype(BF16)
        d = d.reshape(n * gw, rows)
        no_rows = jnp.zeros((n * gw, rows), BF16)

        def offset(k):
            held = (k + 1) * gw
            if held == n * gw:
                return d
            return jnp.concatenate([d[n * gw - held :], no_rows[held:]], 0)

        for k in range(0, n, 2):
            pairs = jnp.concatenate([offset(k), offset(k + 1)], 1)
            gram[slot, :, k * rows : (k + 2) * rows] = jnp.dot(
                x_turned, pairs, preferred_element_type=F32
            )
        sums = gram[slot, 0:8, :]
        for m in range(1, rows // 8):
            sums = sums + pltpu.roll(gram[slot, 8 * m : 8 * m + 8, :], 8 * m, 1)
        sums = pltpu.roll(sums, 0, 1, stride=1, stride_axis=0)
        line = jnp.sum(sums, axis=0, keepdims=True)[:, :span]
        raw[pl.ds(g, 1), :] = line
        return line * line

    def body(i, squares):
        squares = squares + one_group(2 * i, 0)
        return squares + one_group(2 * i + 1, 1)

    squares = lax.fori_loop(0, gpd // 2, body, jnp.zeros((1, span), F32))
    total = jnp.sum(squares, axis=1, keepdims=True)
    upper = total.astype(BF16).astype(F32)
    lower = total - upper
    for a in range(n):
        tile = raw[:, (n - 1 - a) * rows : (n - a) * rows].astype(BF16)
        out_ref[a, 2 * cpd : 2 * cpd + filter_rows, :] = jnp.dot(
            tile, turn, preferred_element_type=F32
        ).astype(BF16)
    halo_at = 2 * cpd + filter_rows
    row = lax.broadcasted_iota(jnp.int32, (2 * EDGE, 2 * rows), 0)
    lane = lax.broadcasted_iota(jnp.int32, (2 * EDGE, 2 * rows), 1)
    wanted = jnp.where(row < EDGE, row, 2 * rows - 1 + EDGE - row)
    pick = jnp.where(lane == wanted, 1.0, 0.0).astype(BF16)
    row_out = lax.broadcasted_iota(jnp.int32, (2 * EDGE, rows), 0)
    for a in range(n):
        if a + 1 < n:
            results = jnp.concatenate([out_ref[a + 1, 0:cpd, :], out_ref[a + 1, cpd : 2 * cpd, :]], 1)
            halo = lax.dot_general(
                pick, results, (((1,), (1,)), ((), ())), preferred_element_type=F32
            )
            if cpd < LANES:
                halo = jnp.concatenate([halo, jnp.zeros((2 * EDGE, LANES - cpd), F32)], 1)
        else:
            halo = jnp.zeros((2 * EDGE, max(cpd, LANES)), F32)
        for j in range(halo.shape[1] // LANES):
            tile = halo[:, j * LANES : (j + 1) * LANES]
            tile = jnp.where(row_out == EDGE - 2, upper, jnp.where(row_out == EDGE - 1, lower, tile))
            at = halo_at + 2 * EDGE * j
            out_ref[a, at : at + 2 * EDGE, :] = tile.astype(BF16)


def long_products(received, cpd, gpd, chunk, chunks):
    n, send_rows, rows = received.shape
    send_rows = send_rows // chunks
    filter_rows = send_rows - 2 * cpd
    out_rows = send_rows + 2 * EDGE * max(1, cpd // LANES)
    span = n * rows
    return pl.pallas_call(
        functools.partial(long_kernel, cpd, gpd),
        grid=(1,),
        in_specs=[pl.BlockSpec((n, send_rows, rows), lambda i: (0, chunk, 0))],
        out_specs=pl.BlockSpec((n, out_rows, rows), lambda i: (0, 0, 0)),
        out_shape=jax.ShapeDtypeStruct((n, out_rows, rows), BF16),
        scratch_shapes=[
            pltpu.VMEM((filter_rows, span + rows), F32),
            pltpu.VMEM((2, rows, span + rows), BF16),
            pltpu.VMEM((2, rows, span + rows), F32),
            pltpu.VMEM((filter_rows, span), F32),
        ],
        compiler_params=params(),
        cost_estimate=pl.CostEstimate(
            flops=6 * cpd * span * span, bytes_accessed=4 * n * out_rows * rows, transcendentals=0
        ),
        name="long_products",
    )(received)


def taps_anti(ext_ref, signal, after, filter_taps):
    rows = signal.shape[0]
    ext_ref[0:rows, :] = signal
    ext_ref[rows : rows + EDGE, :] = after
    total = filter_taps[0:1] * signal
    for s in range(1, filter_taps.shape[0]):
        total = total + filter_taps[s : s + 1] * ext_ref[s : s + rows, :]
    return total


def short_edge(before, signal, filter_taps):
    both = jnp.concatenate([before, signal], 0)
    total = filter_taps[0:1] * signal
    for s in range(1, filter_taps.shape[0]):
        total = total + filter_taps[s : s + 1] * both[EDGE - s : 2 * EDGE - s]
    return total


def after_kernel(
    cpd, gpd, in_ref, og_ref, sk_ref, sv_ref, k_end, v_end, next_ref, taps_ref,
    *refs,
):
    dq_ref, dk_ref, dv_ref, raw_ref, raw_rows, ext_q, ext_k, ext_v = refs[-8:]
    step = pl.program_id(0)
    per_tile, in_rows, rows = in_ref.shape
    groups = raw_ref.shape[1]
    halo_rows = 2 * EDGE * max(1, cpd // LANES)
    halo_at = in_rows - halo_rows
    end_rows = k_end.shape[0]
    turn = reversal(rows)
    for j in range(og_ref.shape[1] // LANES):
        at = slice(j * LANES, (j + 1) * LANES)
        if cpd >= LANES:
            dest, low = j * LANES // cpd, j * LANES % cpd
            conv = in_ref[dest, low : low + LANES, :]
            back = in_ref[dest, cpd + low : cpd + low + LANES, :]
            edge = halo_at + 2 * EDGE * (low // LANES)
            halo = in_ref[dest, edge : edge + 2 * EDGE, :].astype(F32)
        else:
            dests = range(j * LANES // cpd, (j + 1) * LANES // cpd)
            conv = jnp.concatenate([in_ref[d, 0:cpd, :] for d in dests], 0)
            back = jnp.concatenate([in_ref[d, cpd : 2 * cpd, :] for d in dests], 0)
            halo = jnp.concatenate(
                [in_ref[d, halo_at:, :].astype(F32)[:, :cpd] for d in dests], 1
            )
        conv = conv.astype(F32).T
        back = jnp.dot(back, turn, preferred_element_type=F32).T
        following = next_ref[:, at].astype(F32)
        taps_k = taps_ref[1, :, at]
        taps_v = taps_ref[2, :, at]
        next_k = short_edge(
            k_end[:, at].astype(F32)[end_rows - EDGE :], following[EDGE : 2 * EDGE], taps_k
        )
        next_v = short_edge(
            v_end[:, at].astype(F32)[end_rows - EDGE :], following[2 * EDGE : 3 * EDGE], taps_v
        )
        grad_q = og_ref[:, at].astype(F32) * conv
        dq_ref[:, at] = taps_anti(
            ext_q.at[j], grad_q, following[0:EDGE] * halo[0:EDGE], taps_ref[0, :, at]
        ).astype(BF16)
        dk_ref[:, at] = taps_anti(
            ext_k.at[j], back * sv_ref[:, at], halo[EDGE:] * next_v, taps_k
        ).astype(BF16)
        dv_ref[:, at] = taps_anti(
            ext_v.at[j], back * sk_ref[:, at], halo[EDGE:] * next_k, taps_v
        ).astype(BF16)
    for dest in range(per_tile):
        lines = in_ref[dest, 2 * cpd : halo_at, :].astype(F32)
        raw_rows[pl.ds((step * per_tile + dest) * gpd, gpd), :] = lines[:gpd]

    @pl.when(step == pl.num_programs(0) - 1)
    def _():
        raw_ref[...] = raw_rows[...].T


def after_exchange(
    returned, out_grad, short_k, short_v, key, value, following, taps, groups, chunk, chunks, grads
):
    n, in_rows, rows = returned.shape
    channels = out_grad.shape[1] // chunks
    groups = groups // chunks
    cpd, gpd = channels // n, groups // n
    tile = min(channels, max(512, cpd))
    per_tile = tile // cpd
    first = chunk * channels // tile
    block = pl.BlockSpec((rows, tile), lambda i: (0, first + i))
    end = pl.BlockSpec((16, tile), lambda i: (rows // 16 - 1, first + i))
    ext = pltpu.VMEM((tile // LANES, rows + EDGE, LANES), F32)
    grad = jax.ShapeDtypeStruct(out_grad.shape, BF16)
    return pl.pallas_call(
        functools.partial(after_kernel, cpd, gpd),
        grid=(channels // tile,),
        in_specs=[
            pl.BlockSpec((per_tile, in_rows, rows), lambda i: (i, 0, 0)),
            block,
            block,
            block,
            end,
            end,
            pl.BlockSpec((3 * EDGE, tile), lambda i: (0, first + i)),
            pl.BlockSpec((3, taps.shape[1], tile), lambda i: (0, 0, first + i)),
        ]
        + [pl.BlockSpec(memory_space=pl.ANY)] * len(grads),
        input_output_aliases={8 + i: i for i in range(len(grads))},
        out_specs=[block, block, block, pl.BlockSpec((rows, groups), lambda i: (0, 0))],
        out_shape=[grad, grad, grad, jax.ShapeDtypeStruct((rows, groups), F32)],
        scratch_shapes=[pltpu.VMEM((groups, rows), F32), ext, ext, ext],
        compiler_params=params(),
        cost_estimate=pl.CostEstimate(
            flops=60 * rows * channels, bytes_accessed=22 * rows * channels, transcendentals=0
        ),
        name="after_exchange",
    )(returned, out_grad, short_k, short_v, key, value, following, taps, *grads)


def on_device(
    query_heads,
    key_heads,
    value_heads,
    hyena_query,
    hyena_key,
    hyena_value,
    short_filter,
    long_filter,
    output_grad,
):
    rows, channels = query_heads.shape
    groups = long_filter.shape[1]
    n = lax.axis_size("ctx")
    tp = lax.axis_size("tp")
    cpd, gpd = channels // n, groups // n
    position = lax.axis_index("ctx")
    tail = shifted(
        jnp.concatenate([a[rows - EDGE :] for a in (hyena_query, hyena_key, hyena_value)], 0), "ctx", 1
    )
    key_prev = shifted(key_heads, "ctx", 1)
    value_prev = shifted(value_heads, "ctx", 1)
    chunks = 2 if gpd % 4 == 0 else 1
    cpd, gpd = cpd // chunks, gpd // chunks
    send, short_k, short_v = before_exchange(
        hyena_query, hyena_key, hyena_value, output_grad, tail, short_filter, long_filter, n, chunks
    )
    send, *sources = lax.optimization_barrier((send, output_grad, hyena_key, hyena_value))
    following = shifted(jnp.concatenate([a[:EDGE] for a in sources], 0), "ctx", -1)
    received = lax.all_to_all(send, "ctx", split_axis=0, concat_axis=0, tiled=True)
    returned = []
    for chunk in range(chunks):
        results = long_products(received, cpd, gpd, chunk, chunks)
        if chunk == 0:
            results, received, key_prev, value_prev = lax.optimization_barrier(
                (results, received, key_prev, value_prev)
            )
        returned.append(lax.all_to_all(results, "ctx", split_axis=0, concat_axis=0, tiled=True))
    attention = attend(query_heads, key_heads, value_heads, key_prev, value_prev, position)
    grads = ()
    raws = []
    norm_at = returned[0].shape[1] - 2 * EDGE * max(1, cpd // LANES) + EDGE - 2
    own_squares = jnp.zeros((1, 1), F32)
    squares = own_squares
    for chunk in range(chunks):
        if chunk > 0:
            returned[chunk], *grads = lax.optimization_barrier((returned[chunk], *grads))
        own_squares = own_squares + jnp.sum(returned[chunk][:, norm_at : norm_at + 2, 0].astype(F32))
        if chunk + 1 == chunks:
            squares = own_squares
            for distance in range(1, tp):
                route = [(i, (i + distance) % tp) for i in range(tp)]
                squares = squares + lax.ppermute(own_squares, "tp", route)
        *grads, raw = after_exchange(
            returned[chunk], output_grad, short_k, short_v, hyena_key, hyena_value, following, short_filter,
            groups, chunk, chunks, grads,
        )
        raws.append(raw)
    bound = math.sqrt(rows * n * groups * tp)
    factor = jnp.minimum(1.0, bound / jnp.sqrt(squares))
    raw_grad = raws[0] if chunks == 1 else jnp.concatenate(raws, 1)
    return (attention, *grads, raw_grad * factor)


def solution(mesh):
    whole = P("ctx", "tp")
    in_specs = (whole,) * 6 + (P(None, None, "tp"), whole, whole)
    return jax.shard_map(
        on_device, mesh=mesh, in_specs=in_specs, out_specs=(whole,) * 5, check_vma=False
    )
```

```python
import functools
import math

import jax
import jax.numpy as jnp
from jax import lax
from jax.experimental import pallas as pl
from jax.experimental.pallas import tpu as pltpu
from jax.sharding import PartitionSpec as P

HEAD_DIM = 128
LANES = 128
EDGE = 8
F32 = jnp.float32
BF16 = jnp.bfloat16
VMEM_BYTES = 60 * 1024 * 1024
LONG_VMEM = 20 * 1024 * 1024


def params(size=VMEM_BYTES):
    return pltpu.CompilerParams(vmem_limit_bytes=size)


def shifted(block, axis, distance):
    devices = range(lax.axis_size(axis))
    route = [(i - distance, i) for i in devices if i - distance in devices]
    return lax.ppermute(block, axis, route)


def total_over(value, axis):
    size = lax.axis_size(axis)
    distance = 1
    while distance < size:
        value = value + lax.ppermute(value, axis, [(i, i ^ distance) for i in range(size)])
        distance *= 2
    return value


def round_up(value, step):
    return -(-value // step) * step


def reversal(size):
    row = lax.broadcasted_iota(jnp.int32, (size, size), 0)
    col = lax.broadcasted_iota(jnp.int32, (size, size), 1)
    return jnp.where(row + col == size - 1, 1.0, 0.0).astype(BF16)


def attend_kernel(place_ref, q_ref, k_ref, v_ref, kp_ref, vp_ref, out_ref):
    rows = q_ref.shape[0]
    row = lax.broadcasted_iota(jnp.int32, (rows, rows), 0)
    col = lax.broadcasted_iota(jnp.int32, (rows, rows), 1)
    own_ok = col <= row
    prev_ok = jnp.broadcast_to(place_ref[0], (rows, rows)) > 0
    contract = (((1,), (1,)), ((), ()))
    for head in range(q_ref.shape[1] // HEAD_DIM):
        at = slice(head * HEAD_DIM, (head + 1) * HEAD_DIM)
        scale = 1.0 / math.sqrt(HEAD_DIM)
        query = q_ref[:, at]
        own = lax.dot_general(query, k_ref[:, at], contract, preferred_element_type=F32) * scale
        prev = lax.dot_general(query, kp_ref[:, at], contract, preferred_element_type=F32) * scale
        own = jnp.where(own_ok, own, -jnp.inf)
        prev = jnp.where(prev_ok, prev, -jnp.inf)
        largest = jnp.max(jnp.maximum(own, prev), axis=1, keepdims=True)
        own = jnp.exp(own - largest)
        prev = jnp.exp(prev - largest)
        total = jnp.sum(own + prev, axis=1, keepdims=True)
        inverse = 1.0 / total
        own = (own * inverse).astype(BF16)
        prev = (prev * inverse).astype(BF16)
        mixed = jnp.dot(own, v_ref[:, at], preferred_element_type=F32) + jnp.dot(
            prev, vp_ref[:, at], preferred_element_type=F32
        )
        out_ref[:, at] = mixed.astype(BF16)


def attend(query, key, value, key_prev, value_prev, position):
    rows, channels = query.shape
    tile = min(512, channels)
    block = pl.BlockSpec((rows, tile), lambda i: (0, i))
    heads = channels // HEAD_DIM
    return pl.pallas_call(
        attend_kernel,
        grid=(channels // tile,),
        in_specs=[pl.BlockSpec(memory_space=pltpu.SMEM)] + [block] * 5,
        out_specs=block,
        out_shape=jax.ShapeDtypeStruct((rows, channels), BF16),
        compiler_params=params(),
        cost_estimate=pl.CostEstimate(
            flops=8 * heads * rows * rows * HEAD_DIM,
            bytes_accessed=12 * rows * channels,
            transcendentals=2 * heads * rows * rows,
        ),
        name="attend",
    )(position.astype(jnp.int32).reshape(1), query, key, value, key_prev, value_prev)


def edge_kernel(first, *refs):
    *sources, out_ref = refs
    parts = [r[...].astype(F32) for r in sources]
    parts = [p[:EDGE] if first else p[p.shape[0] - EDGE :] for p in parts]
    out_ref[...] = jnp.concatenate(parts, 0).astype(BF16)


def edge_rows(arrays, first):
    rows, channels = arrays[0].shape
    block = pl.BlockSpec((16, channels), lambda i: (0 if first else rows // 16 - 1, 0))
    return pl.pallas_call(
        functools.partial(edge_kernel, first),
        grid=(1,),
        in_specs=[block] * len(arrays),
        out_specs=pl.BlockSpec((len(arrays) * EDGE, channels), lambda i: (0, 0)),
        out_shape=jax.ShapeDtypeStruct((len(arrays) * EDGE, channels), BF16),
        compiler_params=params(),
        name="edge_rows",
    )(*arrays)


def taps_causal(ext_ref, before, signal, filter_taps):
    rows = signal.shape[0]
    ext_ref[0:EDGE, :] = before
    ext_ref[EDGE : EDGE + rows, :] = signal
    total = filter_taps[0:1] * signal
    for s in range(1, filter_taps.shape[0]):
        total = total + filter_taps[s : s + 1] * ext_ref[EDGE - s : EDGE - s + rows, :]
    return total


def before_kernel(
    cpd, gpd, q_ref, k_ref, v_ref, og_ref, tail_ref, taps_ref, long_ref, send_ref, sk_ref, sv_ref,
    long_rows, ext_q, ext_k, ext_v,
):
    step = pl.program_id(0)
    groups = long_ref.shape[1]
    per_tile, _, rows = send_ref.shape

    @pl.when(step == 0)
    def _():
        long_rows[...] = jnp.zeros_like(long_rows)
        long_rows[0:groups, :] = long_ref[...].T

    turn = reversal(rows)
    for j in range(q_ref.shape[1] // LANES):
        at = slice(j * LANES, (j + 1) * LANES)
        tail = tail_ref[:, at].astype(F32)
        short_q = taps_causal(ext_q.at[j], tail[0:EDGE], q_ref[:, at].astype(F32), taps_ref[0, :, at])
        short_k = taps_causal(
            ext_k.at[j], tail[EDGE : 2 * EDGE], k_ref[:, at].astype(F32), taps_ref[1, :, at]
        )
        short_v = taps_causal(
            ext_v.at[j], tail[2 * EDGE : 3 * EDGE], v_ref[:, at].astype(F32), taps_ref[2, :, at]
        )
        sk_ref[:, at] = short_k
        sv_ref[:, at] = short_v
        mixed = (short_k * short_v).T.astype(BF16)
        delta = (og_ref[:, at].astype(F32) * short_q).T.astype(BF16)
        delta = jnp.dot(delta, turn, preferred_element_type=F32).astype(BF16)
        width = min(cpd, LANES)
        for piece in range(LANES // width):
            channel = j * LANES + piece * width
            dest, low = channel // cpd, channel % cpd
            rows_at = slice(piece * width, (piece + 1) * width)
            send_ref[dest, low : low + width, :] = mixed[rows_at]
            send_ref[dest, cpd + low : cpd + low + width, :] = delta[rows_at]
    filter_rows = send_ref.shape[1] - 2 * cpd
    for dest in range(per_tile):
        first = (step * per_tile + dest) * gpd
        send_ref[dest, 2 * cpd :, :] = long_rows[pl.ds(first, filter_rows), :].astype(BF16)


def before_exchange(query, key, value, out_grad, tail, taps, long_filter, n, chunks):
    rows, channels = query.shape
    groups = long_filter.shape[1]
    cpd, gpd = channels // (n * chunks), groups // (n * chunks)
    tile = min(channels // chunks, max(512, cpd))
    per_tile = tile // cpd
    filter_rows = round_up(gpd, 16)
    send_rows = 2 * cpd + filter_rows
    steps = n // per_tile
    block = pl.BlockSpec((rows, tile), lambda i: (0, i))
    ext = pltpu.VMEM((tile // LANES, rows + EDGE, LANES), F32)
    return pl.pallas_call(
        functools.partial(before_kernel, cpd, gpd),
        grid=(channels // tile,),
        in_specs=[block] * 4
        + [
            pl.BlockSpec((3 * EDGE, tile), lambda i: (0, i)),
            pl.BlockSpec((3, taps.shape[1], tile), lambda i: (0, 0, i)),
            pl.BlockSpec((rows, groups), lambda i: (0, 0)),
        ],
        out_specs=[
            pl.BlockSpec((per_tile, send_rows, rows), lambda i: (i % steps, i // steps, 0)),
            block,
            block,
        ],
        out_shape=[
            jax.ShapeDtypeStruct((n, chunks * send_rows, rows), BF16),
            jax.ShapeDtypeStruct((rows, channels), F32),
            jax.ShapeDtypeStruct((rows, channels), F32),
        ],
        scratch_shapes=[pltpu.VMEM((round_up(groups, 8) + filter_rows, rows), F32), ext, ext, ext],
        compiler_params=params(),
        cost_estimate=pl.CostEstimate(
            flops=50 * rows * channels, bytes_accessed=20 * rows * channels, transcendentals=0
        ),
        name="before_exchange",
    )(query, key, value, out_grad, tail, taps, long_filter)


def conv_kernel(cpd, gpd, in_ref, *refs):
    *raw_ref, out_ref, taps, wide = refs
    n, send_rows, rows = in_ref.shape
    gw = cpd // gpd
    span = n * rows
    filter_rows = send_rows - 2 * cpd
    taps[:, 0:rows] = jnp.zeros((filter_rows, rows), F32)
    for a in range(n):
        taps[:, (a + 1) * rows : (a + 2) * rows] = in_ref[a, 2 * cpd :, :].astype(F32)
    for slot in range(2):
        wide[slot, :, 0:rows] = jnp.zeros((rows, rows), BF16)

    def one_group(g, slot):
        line = jnp.broadcast_to(taps[pl.ds(g, 1), :], (16, span + rows))
        base = pltpu.roll(line, 0, 1, stride=1, stride_axis=0).astype(BF16)
        for m in range(rows // 16):
            moved = base if m == 0 else pltpu.roll(base, 16 * m, 1)
            wide[slot, 16 * m : 16 * m + 16, rows:] = moved[:, rows:]
        first = pl.multiple_of(g * gw, gw)
        x = in_ref[:, pl.ds(first, gw), :]
        second = pl.multiple_of(cpd + g * gw, gw)
        d = in_ref[:, pl.ds(second, gw), :]
        both = [jnp.concatenate([x[a], d[n - 1 - a]], 0) for a in range(n)]
        lhs = jnp.concatenate(
            [jnp.concatenate([both[a], both[a + 1]], 1) for a in range(0, n, 2)], 0
        )
        total = None
        for k in range(n // 2):
            skip = 2 * gw * k
            low = 2 * rows * k
            tile = jnp.concatenate(
                [wide[slot, :, low + rows : low + 3 * rows], wide[slot, :, low : low + 2 * rows]], 0
            )
            part = jnp.dot(lhs[: n * gw - skip], tile, preferred_element_type=F32)
            total = part if k == 0 else jnp.concatenate([total[:skip], total[skip:] + part], 0)
        for a in range(n):
            at = slice(a % 2 * rows, (a % 2 + 1) * rows)
            top = a // 2 * 2 * gw
            out_ref[a, pl.ds(first, gw), :] = total[top : top + gw, at].astype(BF16)
            out_ref[n - 1 - a, pl.ds(second, gw), :] = total[top + gw : top + 2 * gw, at].astype(BF16)

    def body(i, carry):
        one_group(2 * i, 0)
        one_group(2 * i + 1, 1)
        return carry

    lax.fori_loop(0, gpd // 2, body, 0)
    halo_at = 2 * cpd
    row = lax.broadcasted_iota(jnp.int32, (2 * EDGE, 2 * rows), 0)
    lane = lax.broadcasted_iota(jnp.int32, (2 * EDGE, 2 * rows), 1)
    wanted = jnp.where(row < EDGE, row, 2 * rows - 1 + EDGE - row)
    pick = jnp.where(lane == wanted, 1.0, 0.0).astype(BF16)
    for a in range(n):
        if a + 1 < n:
            results = jnp.concatenate([out_ref[a + 1, 0:cpd, :], out_ref[a + 1, cpd : 2 * cpd, :]], 1)
            halo = lax.dot_general(
                pick, results, (((1,), (1,)), ((), ())), preferred_element_type=F32
            )
            if cpd < LANES:
                halo = jnp.concatenate([halo, jnp.zeros((2 * EDGE, LANES - cpd), F32)], 1)
        else:
            halo = jnp.zeros((2 * EDGE, max(cpd, LANES)), F32)
        for j in range(halo.shape[1] // LANES):
            at = halo_at + 2 * EDGE * j
            out_ref[a, at : at + 2 * EDGE, :] = halo[:, j * LANES : (j + 1) * LANES].astype(BF16)
    for ref in raw_ref:
        out_ref[:, out_ref.shape[1] - ref.shape[1] :, :] = ref[...]


def long_convs(received, raw, cpd, gpd, chunk, chunks):
    n, send_rows, rows = received.shape
    send_rows = send_rows // chunks
    filter_rows = send_rows - 2 * cpd
    out_rows = 2 * cpd + 2 * EDGE * max(1, cpd // LANES) + sum(r.shape[1] for r in raw)
    span = n * rows
    return pl.pallas_call(
        functools.partial(conv_kernel, cpd, gpd),
        grid=(1,),
        in_specs=[pl.BlockSpec((n, send_rows, rows), lambda i: (0, chunk, 0))]
        + [pl.BlockSpec(r.shape, lambda i: (0, 0, 0)) for r in raw],
        out_specs=pl.BlockSpec((n, out_rows, rows), lambda i: (0, 0, 0)),
        out_shape=jax.ShapeDtypeStruct((n, out_rows, rows), BF16),
        scratch_shapes=[
            pltpu.VMEM((filter_rows, span + rows), F32),
            pltpu.VMEM((2, rows, span + rows), BF16),
        ],
        compiler_params=params(LONG_VMEM),
        cost_estimate=pl.CostEstimate(
            flops=4 * cpd * span * span, bytes_accessed=4 * n * out_rows * rows, transcendentals=0
        ),
        name="long_convs",
    )(received, *raw)


def gram_kernel(cpd, gpd, chunks, in_ref, out_ref, squares_ref, gram, raw):
    n, send_rows, rows = in_ref.shape
    send_rows = send_rows // chunks
    gw = cpd // gpd
    span = n * rows
    for slot in range(2):
        gram[slot, :, span:] = jnp.zeros((rows, rows), F32)
    if gpd * chunks < raw.shape[0]:
        raw[...] = jnp.zeros_like(raw)
    no_rows = jnp.zeros((n * gw, rows), BF16)

    def one_group(base, line_at, g, slot):
        first = pl.multiple_of(base + g * gw, gw)
        second = pl.multiple_of(base + cpd + g * gw, gw)
        x = in_ref[:, pl.ds(first, gw), :].reshape(n * gw, rows)
        d = in_ref[:, pl.ds(second, gw), :].reshape(n * gw, rows)
        x_turned = x.astype(F32).T.astype(BF16)

        def offset(k):
            held = (k + 1) * gw
            if held == n * gw:
                return d
            return jnp.concatenate([d[n * gw - held :], no_rows[held:]], 0)

        for k in range(0, n, 2):
            pairs = jnp.concatenate([offset(k), offset(k + 1)], 1)
            gram[slot, :, k * rows : (k + 2) * rows] = jnp.dot(
                x_turned, pairs, preferred_element_type=F32
            )
        sums = gram[slot, 0:8, :]
        for m in range(1, rows // 8):
            sums = sums + pltpu.roll(gram[slot, 8 * m : 8 * m + 8, :], 8 * m, 1)
        sums = pltpu.roll(sums, 0, 1, stride=1, stride_axis=0)
        line = jnp.sum(sums, axis=0, keepdims=True)[:, :span]
        raw[pl.ds(line_at + g, 1), :] = line
        return line * line

    squares = jnp.zeros((1, span), F32)
    for chunk in range(chunks):

        def body(i, total, chunk=chunk):
            total = total + one_group(chunk * send_rows, chunk * gpd, 2 * i, 0)
            return total + one_group(chunk * send_rows, chunk * gpd, 2 * i + 1, 1)

        squares = lax.fori_loop(0, gpd // 2, body, squares)
    squares_ref[...] = jnp.sum(squares, axis=1, keepdims=True)
    turn = reversal(rows)
    for a in range(n):
        tile = raw[:, (n - 1 - a) * rows : (n - a) * rows].astype(BF16)
        out_ref[a] = jnp.dot(tile, turn, preferred_element_type=F32).astype(BF16)


def filter_products(received, cpd, gpd, chunks):
    n, _, rows = received.shape
    span = n * rows
    raw_rows = round_up(gpd * chunks, 16)
    return pl.pallas_call(
        functools.partial(gram_kernel, cpd, gpd, chunks),
        in_specs=[pl.BlockSpec(memory_space=pltpu.VMEM)],
        out_specs=[pl.BlockSpec(memory_space=pltpu.VMEM)] * 2,
        out_shape=[
            jax.ShapeDtypeStruct((n, raw_rows, rows), BF16),
            jax.ShapeDtypeStruct((1, 1), F32),
        ],
        scratch_shapes=[
            pltpu.VMEM((2, rows, span + rows), F32),
            pltpu.VMEM((raw_rows, span), F32),
        ],
        compiler_params=params(LONG_VMEM),
        cost_estimate=pl.CostEstimate(
            flops=2 * cpd * chunks * span * span,
            bytes_accessed=2 * received.size,
            transcendentals=0,
        ),
        name="filter_products",
    )(received)


def taps_anti(ext_ref, signal, after, filter_taps):
    rows = signal.shape[0]
    ext_ref[0:rows, :] = signal
    ext_ref[rows : rows + EDGE, :] = after
    total = filter_taps[0:1] * signal
    for s in range(1, filter_taps.shape[0]):
        total = total + filter_taps[s : s + 1] * ext_ref[s : s + rows, :]
    return total


def short_edge(before, signal, filter_taps):
    both = jnp.concatenate([before, signal], 0)
    total = filter_taps[0:1] * signal
    for s in range(1, filter_taps.shape[0]):
        total = total + filter_taps[s : s + 1] * both[EDGE - s : 2 * EDGE - s]
    return total


def after_kernel(
    cpd, gpd, chunks, last, in_ref, og_ref, sk_ref, sv_ref, k_end, v_end, next_ref, taps_ref, *refs
):
    *refs, ext_q, ext_k, ext_v = refs
    if last:
        *refs, raw_ref, raw_rows = refs
    dq_ref, dk_ref, dv_ref = refs[-3:]
    step = pl.program_id(0)
    per_tile, in_rows, rows = in_ref.shape
    halo_rows = 2 * EDGE * max(1, cpd // LANES)
    halo_at = 2 * cpd
    end_rows = k_end.shape[0]
    turn = reversal(rows)
    for j in range(og_ref.shape[1] // LANES):
        at = slice(j * LANES, (j + 1) * LANES)
        if cpd >= LANES:
            dest, low = j * LANES // cpd, j * LANES % cpd
            conv = in_ref[dest, low : low + LANES, :]
            back = in_ref[dest, cpd + low : cpd + low + LANES, :]
            edge = halo_at + 2 * EDGE * (low // LANES)
            halo = in_ref[dest, edge : edge + 2 * EDGE, :].astype(F32)
        else:
            dests = range(j * LANES // cpd, (j + 1) * LANES // cpd)
            conv = jnp.concatenate([in_ref[d, 0:cpd, :] for d in dests], 0)
            back = jnp.concatenate([in_ref[d, cpd : 2 * cpd, :] for d in dests], 0)
            halo = jnp.concatenate(
                [in_ref[d, halo_at : halo_at + halo_rows, :].astype(F32)[:, :cpd] for d in dests], 1
            )
        conv = conv.astype(F32).T
        back = jnp.dot(back, turn, preferred_element_type=F32).T
        following = next_ref[:, at].astype(F32)
        taps_k = taps_ref[1, :, at]
        taps_v = taps_ref[2, :, at]
        next_k = short_edge(
            k_end[:, at].astype(F32)[end_rows - EDGE :], following[EDGE : 2 * EDGE], taps_k
        )
        next_v = short_edge(
            v_end[:, at].astype(F32)[end_rows - EDGE :], following[2 * EDGE : 3 * EDGE], taps_v
        )
        grad_q = og_ref[:, at].astype(F32) * conv
        dq_ref[:, at] = taps_anti(
            ext_q.at[j], grad_q, following[0:EDGE] * halo[0:EDGE], taps_ref[0, :, at]
        ).astype(BF16)
        dk_ref[:, at] = taps_anti(
            ext_k.at[j], back * sv_ref[:, at], halo[EDGE:] * next_v, taps_k
        ).astype(BF16)
        dv_ref[:, at] = taps_anti(
            ext_v.at[j], back * sk_ref[:, at], halo[EDGE:] * next_k, taps_v
        ).astype(BF16)
    if not last:
        return
    scale = refs[0][0, 0]
    half = raw_rows.shape[0] // chunks
    for dest in range(per_tile):
        lines = in_ref[dest, halo_at + halo_rows :, :].astype(F32)
        for chunk in range(chunks):
            at = chunk * half + (step * per_tile + dest) * gpd
            raw_rows[pl.ds(at, gpd), :] = lines[chunk * gpd : (chunk + 1) * gpd]

    @pl.when(step == pl.num_programs(0) - 1)
    def _():
        raw_ref[...] = raw_rows[...].T * scale


def after_exchange(
    returned, out_grad, short_k, short_v, key, value, following, taps, groups, chunk, chunks, grads, scale
):
    n, in_rows, rows = returned.shape
    channels = out_grad.shape[1] // chunks
    cpd, gpd = channels // n, groups // (n * chunks)
    last = chunk + 1 == chunks
    tile = min(channels, max(512, cpd))
    per_tile = tile // cpd
    first = chunk * channels // tile
    block = pl.BlockSpec((rows, tile), lambda i: (0, first + i))
    end = pl.BlockSpec((16, tile), lambda i: (rows // 16 - 1, first + i))
    ext = pltpu.VMEM((tile // LANES, rows + EDGE, LANES), F32)
    grad = jax.ShapeDtypeStruct(out_grad.shape, BF16)
    return pl.pallas_call(
        functools.partial(after_kernel, cpd, gpd, chunks, last),
        grid=(channels // tile,),
        in_specs=[
            pl.BlockSpec((per_tile, in_rows, rows), lambda i: (i, 0, 0)),
            block,
            block,
            block,
            end,
            end,
            pl.BlockSpec((3 * EDGE, tile), lambda i: (0, first + i)),
            pl.BlockSpec((3, taps.shape[1], tile), lambda i: (0, 0, first + i)),
        ]
        + [pl.BlockSpec(memory_space=pltpu.SMEM)] * len(scale)
        + [pl.BlockSpec(memory_space=pl.ANY)] * len(grads),
        input_output_aliases={8 + len(scale) + i: i for i in range(len(grads))},
        out_specs=[block] * 3 + [pl.BlockSpec((rows, groups), lambda i: (0, 0))] * len(scale),
        out_shape=[grad] * 3 + [jax.ShapeDtypeStruct((rows, groups), F32)] * len(scale),
        scratch_shapes=[pltpu.VMEM((groups, rows), F32)] * len(scale) + [ext, ext, ext],
        compiler_params=params(),
        cost_estimate=pl.CostEstimate(
            flops=60 * rows * channels, bytes_accessed=22 * rows * channels, transcendentals=0
        ),
        name="after_exchange",
    )(returned, out_grad, short_k, short_v, key, value, following, taps, *scale, *grads)


def on_device(
    query_heads,
    key_heads,
    value_heads,
    hyena_query,
    hyena_key,
    hyena_value,
    short_filter,
    long_filter,
    output_grad,
):
    rows, channels = query_heads.shape
    groups = long_filter.shape[1]
    n = lax.axis_size("ctx")
    tp = lax.axis_size("tp")
    cpd, gpd = channels // n, groups // n
    position = lax.axis_index("ctx")
    tail = shifted(edge_rows((hyena_query, hyena_key, hyena_value), False), "ctx", 1)
    key_prev = shifted(key_heads, "ctx", 1)
    value_prev = shifted(value_heads, "ctx", 1)
    chunks = 2 if gpd % 4 == 0 else 1
    cpd, gpd = cpd // chunks, gpd // chunks
    send, short_k, short_v = before_exchange(
        hyena_query, hyena_key, hyena_value, output_grad, tail, short_filter, long_filter, n, chunks
    )
    send, key_prev, *sources = lax.optimization_barrier(
        (send, key_prev, output_grad, hyena_key, hyena_value)
    )
    received = lax.all_to_all(send, "ctx", split_axis=0, concat_axis=0, tiled=True)
    following = shifted(edge_rows(sources, True), "ctx", -1)
    returned = []
    for chunk in range(chunks):
        raw = ()
        if chunk + 1 == chunks:
            *raw, squares = filter_products(received, cpd, gpd, chunks)
            squares = total_over(squares, "tp")
            squares = total_over(squares, "ctx")
        results = long_convs(received, raw, cpd, gpd, chunk, chunks)
        if chunk == 0:
            results, received, value_prev, following = lax.optimization_barrier(
                (results, received, value_prev, following)
            )
        returned.append(lax.all_to_all(results, "ctx", split_axis=0, concat_axis=0, tiled=True))
    attention = attend(query_heads, key_heads, value_heads, key_prev, value_prev, position)
    bound = math.sqrt(rows * n * groups * tp)
    factor = jnp.minimum(1.0, bound / jnp.sqrt(squares))
    grads = ()
    for chunk in range(chunks):
        if chunk > 0:
            returned[chunk], *grads = lax.optimization_barrier((returned[chunk], *grads))
        scale = (factor,) if chunk + 1 == chunks else ()
        grads = after_exchange(
            returned[chunk], output_grad, short_k, short_v, hyena_key, hyena_value, following, short_filter,
            groups, chunk, chunks, grads, scale,
        )
    return (attention, *grads)


def solution(mesh):
    whole = P("ctx", "tp")
    in_specs = (whole,) * 6 + (P(None, None, "tp"), whole, whole)
    return jax.shard_map(
        on_device, mesh=mesh, in_specs=in_specs, out_specs=(whole,) * 5, check_vma=False
    )
```

```python
import functools
import math

import jax
import jax.numpy as jnp
from jax import lax
from jax.experimental import pallas as pl
from jax.experimental.pallas import tpu as pltpu
from jax.sharding import PartitionSpec as P

HEAD_DIM = 128
LANES = 128
EDGE = 8
F32 = jnp.float32
BF16 = jnp.bfloat16
VMEM_BYTES = 60 * 1024 * 1024
LONG_VMEM = 20 * 1024 * 1024


def params(size=VMEM_BYTES):
    return pltpu.CompilerParams(vmem_limit_bytes=size)


def shifted(block, axis, distance):
    devices = range(lax.axis_size(axis))
    route = [(i - distance, i) for i in devices if i - distance in devices]
    return lax.ppermute(block, axis, route)


def total_over(value, axis):
    size = lax.axis_size(axis)
    distance = 1
    while distance < size:
        value = value + lax.ppermute(value, axis, [(i, i ^ distance) for i in range(size)])
        distance *= 2
    return value


def round_up(value, step):
    return -(-value // step) * step


def reversal(size):
    row = lax.broadcasted_iota(jnp.int32, (size, size), 0)
    col = lax.broadcasted_iota(jnp.int32, (size, size), 1)
    return jnp.where(row + col == size - 1, 1.0, 0.0).astype(BF16)


SCALE = 1.0 / math.sqrt(HEAD_DIM)
NT = (((1,), (1,)), ((), ()))


def attend_next_kernel(q_ref, k_ref, v_ref, out_ref, log_ref):
    rows = q_ref.shape[0]
    heads = q_ref.shape[1] // HEAD_DIM
    step = pl.program_id(0)
    lane = lax.broadcasted_iota(jnp.int32, (rows, log_ref.shape[1]), 1)

    @pl.when(step == 0)
    def _():
        log_ref[...] = jnp.zeros_like(log_ref)

    logs = log_ref[...]
    for head in range(heads):
        at = slice(head * HEAD_DIM, (head + 1) * HEAD_DIM)
        score = lax.dot_general(q_ref[:, at], k_ref[:, at], NT, preferred_element_type=F32) * SCALE
        largest = jnp.max(score, axis=1, keepdims=True)
        raised = jnp.exp(score - largest)
        total = jnp.sum(raised, axis=1, keepdims=True)
        weight = (raised * (1.0 / total)).astype(BF16)
        mixed = jnp.dot(weight, v_ref[:, at], preferred_element_type=F32)
        out_ref[:, at] = mixed.astype(BF16)
        logs = jnp.where(lane == step * heads + head, largest + jnp.log(total), logs)
    log_ref[...] = logs


def attend_own_kernel(place_ref, q_ref, k_ref, v_ref, prev_ref, log_ref, out_ref):
    rows = q_ref.shape[0]
    heads = q_ref.shape[1] // HEAD_DIM
    step = pl.program_id(0)
    row = lax.broadcasted_iota(jnp.int32, (rows, rows), 0)
    col = lax.broadcasted_iota(jnp.int32, (rows, rows), 1)
    own_ok = col <= row
    lane = lax.broadcasted_iota(jnp.int32, (rows, log_ref.shape[1]), 1)
    has_prev = jnp.broadcast_to(place_ref[0], (rows, 1)) > 0
    for head in range(heads):
        at = slice(head * HEAD_DIM, (head + 1) * HEAD_DIM)
        log = jnp.sum(
            jnp.where(lane == step * heads + head, log_ref[...], 0.0), axis=1, keepdims=True
        )
        log = jnp.where(has_prev, log, -jnp.inf)
        own = lax.dot_general(q_ref[:, at], k_ref[:, at], NT, preferred_element_type=F32) * SCALE
        own = jnp.where(own_ok, own, -jnp.inf)
        largest = jnp.maximum(jnp.max(own, axis=1, keepdims=True), log)
        own = jnp.exp(own - largest)
        prev = jnp.exp(log - largest)
        inverse = 1.0 / (jnp.sum(own, axis=1, keepdims=True) + prev)
        weight = (own * inverse).astype(BF16)
        mixed = jnp.dot(weight, v_ref[:, at], preferred_element_type=F32)
        mixed = mixed + (prev * inverse) * prev_ref[:, at].astype(F32)
        out_ref[:, at] = mixed.astype(BF16)


def attend_cost(rows, channels):
    heads = channels // HEAD_DIM
    return pl.CostEstimate(
        flops=4 * heads * rows * rows * HEAD_DIM,
        bytes_accessed=10 * rows * channels,
        transcendentals=heads * rows * rows,
    )


def attend_next(query, key, value):
    rows, channels = query.shape
    tile = min(512, channels)
    block = pl.BlockSpec((rows, tile), lambda i: (0, i))
    lanes = round_up(channels // HEAD_DIM, LANES)
    return pl.pallas_call(
        attend_next_kernel,
        grid=(channels // tile,),
        in_specs=[block] * 3,
        out_specs=[block, pl.BlockSpec((rows, lanes), lambda i: (0, 0))],
        out_shape=[
            jax.ShapeDtypeStruct((rows, channels), BF16),
            jax.ShapeDtypeStruct((rows, lanes), F32),
        ],
        compiler_params=params(),
        cost_estimate=attend_cost(rows, channels),
        name="attend_next",
    )(query, key, value)


def attend_own(query, key, value, prev, log, position):
    rows, channels = query.shape
    tile = min(512, channels)
    block = pl.BlockSpec((rows, tile), lambda i: (0, i))
    return pl.pallas_call(
        attend_own_kernel,
        grid=(channels // tile,),
        in_specs=[pl.BlockSpec(memory_space=pltpu.SMEM)]
        + [block] * 4
        + [pl.BlockSpec(log.shape, lambda i: (0, 0))],
        out_specs=block,
        out_shape=jax.ShapeDtypeStruct((rows, channels), BF16),
        compiler_params=params(),
        cost_estimate=attend_cost(rows, channels),
        name="attend_own",
    )(position.astype(jnp.int32).reshape(1), query, key, value, prev, log)


def edge_kernel(first, *refs):
    *sources, out_ref = refs
    parts = [r[...].astype(F32) for r in sources]
    parts = [p[:EDGE] if first else p[p.shape[0] - EDGE :] for p in parts]
    out_ref[...] = jnp.concatenate(parts, 0).astype(BF16)


def edge_rows(arrays, first):
    rows, channels = arrays[0].shape
    block = pl.BlockSpec((16, channels), lambda i: (0 if first else rows // 16 - 1, 0))
    return pl.pallas_call(
        functools.partial(edge_kernel, first),
        grid=(1,),
        in_specs=[block] * len(arrays),
        out_specs=pl.BlockSpec((len(arrays) * EDGE, channels), lambda i: (0, 0)),
        out_shape=jax.ShapeDtypeStruct((len(arrays) * EDGE, channels), BF16),
        compiler_params=params(),
        name="edge_rows",
    )(*arrays)


def taps_causal(ext_ref, before, signal, filter_taps):
    rows = signal.shape[0]
    ext_ref[0:EDGE, :] = before
    ext_ref[EDGE : EDGE + rows, :] = signal
    total = filter_taps[0:1] * signal
    for s in range(1, filter_taps.shape[0]):
        total = total + filter_taps[s : s + 1] * ext_ref[EDGE - s : EDGE - s + rows, :]
    return total


def before_kernel(
    cpd, gpd, q_ref, k_ref, v_ref, og_ref, tail_ref, taps_ref, long_ref, send_ref,
    long_rows, ext_q, ext_k, ext_v,
):
    step = pl.program_id(0)
    groups = long_ref.shape[1]
    per_tile, _, rows = send_ref.shape

    @pl.when(step == 0)
    def _():
        long_rows[...] = jnp.zeros_like(long_rows)
        long_rows[0:groups, :] = long_ref[...].T

    turn = reversal(rows)
    for j in range(q_ref.shape[1] // LANES):
        at = slice(j * LANES, (j + 1) * LANES)
        tail = tail_ref[:, at].astype(F32)
        short_q = taps_causal(ext_q.at[j], tail[0:EDGE], q_ref[:, at].astype(F32), taps_ref[0, :, at])
        short_k = taps_causal(
            ext_k.at[j], tail[EDGE : 2 * EDGE], k_ref[:, at].astype(F32), taps_ref[1, :, at]
        )
        short_v = taps_causal(
            ext_v.at[j], tail[2 * EDGE : 3 * EDGE], v_ref[:, at].astype(F32), taps_ref[2, :, at]
        )
        mixed = (short_k * short_v).T.astype(BF16)
        delta = (og_ref[:, at].astype(F32) * short_q).T.astype(BF16)
        delta = jnp.dot(delta, turn, preferred_element_type=F32).astype(BF16)
        width = min(cpd, LANES)
        for piece in range(LANES // width):
            channel = j * LANES + piece * width
            dest, low = channel // cpd, channel % cpd
            rows_at = slice(piece * width, (piece + 1) * width)
            send_ref[dest, low : low + width, :] = mixed[rows_at]
            send_ref[dest, cpd + low : cpd + low + width, :] = delta[rows_at]
    filter_rows = send_ref.shape[1] - 2 * cpd
    for dest in range(per_tile):
        first = (step * per_tile + dest) * gpd
        send_ref[dest, 2 * cpd :, :] = long_rows[pl.ds(first, filter_rows), :].astype(BF16)


def before_exchange(query, key, value, out_grad, tail, taps, long_filter, n, chunks):
    rows, channels = query.shape
    groups = long_filter.shape[1]
    cpd, gpd = channels // (n * chunks), groups // (n * chunks)
    tile = min(channels // chunks, max(512, cpd))
    per_tile = tile // cpd
    filter_rows = round_up(gpd, 16)
    send_rows = 2 * cpd + filter_rows
    steps = n // per_tile
    block = pl.BlockSpec((rows, tile), lambda i: (0, i))
    ext = pltpu.VMEM((tile // LANES, rows + EDGE, LANES), F32)
    return pl.pallas_call(
        functools.partial(before_kernel, cpd, gpd),
        grid=(channels // tile,),
        in_specs=[block] * 4
        + [
            pl.BlockSpec((3 * EDGE, tile), lambda i: (0, i)),
            pl.BlockSpec((3, taps.shape[1], tile), lambda i: (0, 0, i)),
            pl.BlockSpec((rows, groups), lambda i: (0, 0)),
        ],
        out_specs=pl.BlockSpec((per_tile, send_rows, rows), lambda i: (i % steps, i // steps, 0)),
        out_shape=jax.ShapeDtypeStruct((n, chunks * send_rows, rows), BF16),
        scratch_shapes=[pltpu.VMEM((round_up(groups, 8) + filter_rows, rows), F32), ext, ext, ext],
        compiler_params=params(),
        cost_estimate=pl.CostEstimate(
            flops=50 * rows * channels, bytes_accessed=12 * rows * channels, transcendentals=0
        ),
        name="before_exchange",
    )(query, key, value, out_grad, tail, taps, long_filter)


def conv_kernel(cpd, gpd, in_ref, *refs):
    *raw_ref, out_ref, taps, wide = refs
    n, send_rows, rows = in_ref.shape
    gw = cpd // gpd
    span = n * rows
    filter_rows = send_rows - 2 * cpd
    taps[:, 0:rows] = jnp.zeros((filter_rows, rows), F32)
    for a in range(n):
        taps[:, (a + 1) * rows : (a + 2) * rows] = in_ref[a, 2 * cpd :, :].astype(F32)
    for slot in range(2):
        wide[slot, :, 0:rows] = jnp.zeros((rows, rows), BF16)

    def one_group(g, slot):
        line = jnp.broadcast_to(taps[pl.ds(g, 1), :], (16, span + rows))
        base = pltpu.roll(line, 0, 1, stride=1, stride_axis=0).astype(BF16)
        for m in range(rows // 16):
            moved = base if m == 0 else pltpu.roll(base, 16 * m, 1)
            wide[slot, 16 * m : 16 * m + 16, rows:] = moved[:, rows:]
        first = pl.multiple_of(g * gw, gw)
        x = in_ref[:, pl.ds(first, gw), :]
        second = pl.multiple_of(cpd + g * gw, gw)
        d = in_ref[:, pl.ds(second, gw), :]
        both = [jnp.concatenate([x[a], d[n - 1 - a]], 0) for a in range(n)]
        lhs = jnp.concatenate(
            [jnp.concatenate([both[a], both[a + 1]], 1) for a in range(0, n, 2)], 0
        )
        total = None
        for k in range(n // 2):
            skip = 2 * gw * k
            low = 2 * rows * k
            tile = jnp.concatenate(
                [wide[slot, :, low + rows : low + 3 * rows], wide[slot, :, low : low + 2 * rows]], 0
            )
            part = jnp.dot(lhs[: n * gw - skip], tile, preferred_element_type=F32)
            total = part if k == 0 else jnp.concatenate([total[:skip], total[skip:] + part], 0)
        for a in range(n):
            at = slice(a % 2 * rows, (a % 2 + 1) * rows)
            top = a // 2 * 2 * gw
            out_ref[a, pl.ds(first, gw), :] = total[top : top + gw, at].astype(BF16)
            out_ref[n - 1 - a, pl.ds(second, gw), :] = total[top + gw : top + 2 * gw, at].astype(BF16)

    def body(i, carry):
        one_group(2 * i, 0)
        one_group(2 * i + 1, 1)
        return carry

    lax.fori_loop(0, gpd // 2, body, 0)
    halo_at = 2 * cpd
    row = lax.broadcasted_iota(jnp.int32, (2 * EDGE, 2 * rows), 0)
    lane = lax.broadcasted_iota(jnp.int32, (2 * EDGE, 2 * rows), 1)
    wanted = jnp.where(row < EDGE, row, 2 * rows - 1 + EDGE - row)
    pick = jnp.where(lane == wanted, 1.0, 0.0).astype(BF16)
    for a in range(n):
        if a + 1 < n:
            results = jnp.concatenate([out_ref[a + 1, 0:cpd, :], out_ref[a + 1, cpd : 2 * cpd, :]], 1)
            halo = lax.dot_general(
                pick, results, (((1,), (1,)), ((), ())), preferred_element_type=F32
            )
            if cpd < LANES:
                halo = jnp.concatenate([halo, jnp.zeros((2 * EDGE, LANES - cpd), F32)], 1)
        else:
            halo = jnp.zeros((2 * EDGE, max(cpd, LANES)), F32)
        for j in range(halo.shape[1] // LANES):
            at = halo_at + 2 * EDGE * j
            out_ref[a, at : at + 2 * EDGE, :] = halo[:, j * LANES : (j + 1) * LANES].astype(BF16)
    for ref in raw_ref:
        out_ref[:, out_ref.shape[1] - ref.shape[1] :, :] = ref[...]


def long_convs(received, raw, cpd, gpd, chunk, chunks):
    n, send_rows, rows = received.shape
    send_rows = send_rows // chunks
    filter_rows = send_rows - 2 * cpd
    out_rows = 2 * cpd + 2 * EDGE * max(1, cpd // LANES) + sum(r.shape[1] for r in raw)
    span = n * rows
    return pl.pallas_call(
        functools.partial(conv_kernel, cpd, gpd),
        grid=(1,),
        in_specs=[pl.BlockSpec((n, send_rows, rows), lambda i: (0, chunk, 0))]
        + [pl.BlockSpec(r.shape, lambda i: (0, 0, 0)) for r in raw],
        out_specs=pl.BlockSpec((n, out_rows, rows), lambda i: (0, 0, 0)),
        out_shape=jax.ShapeDtypeStruct((n, out_rows, rows), BF16),
        scratch_shapes=[
            pltpu.VMEM((filter_rows, span + rows), F32),
            pltpu.VMEM((2, rows, span + rows), BF16),
        ],
        compiler_params=params(LONG_VMEM),
        cost_estimate=pl.CostEstimate(
            flops=4 * cpd * span * span, bytes_accessed=4 * n * out_rows * rows, transcendentals=0
        ),
        name="long_convs",
    )(received, *raw)


def gram_kernel(cpd, gpd, chunks, in_ref, out_ref, squares_ref, gram, raw):
    n, send_rows, rows = in_ref.shape
    send_rows = send_rows // chunks
    gw = cpd // gpd
    span = n * rows
    for slot in range(2):
        gram[slot, :, span:] = jnp.zeros((rows, rows), F32)
    if gpd * chunks < raw.shape[0]:
        raw[...] = jnp.zeros_like(raw)
    no_rows = jnp.zeros((n * gw, rows), BF16)

    def one_group(base, line_at, g, slot):
        first = pl.multiple_of(base + g * gw, gw)
        second = pl.multiple_of(base + cpd + g * gw, gw)
        x = in_ref[:, pl.ds(first, gw), :].reshape(n * gw, rows)
        d = in_ref[:, pl.ds(second, gw), :].reshape(n * gw, rows)
        x_turned = x.astype(F32).T.astype(BF16)

        def offset(k):
            held = (k + 1) * gw
            if held == n * gw:
                return d
            return jnp.concatenate([d[n * gw - held :], no_rows[held:]], 0)

        for k in range(0, n, 2):
            pairs = jnp.concatenate([offset(k), offset(k + 1)], 1)
            gram[slot, :, k * rows : (k + 2) * rows] = jnp.dot(
                x_turned, pairs, preferred_element_type=F32
            )
        sums = gram[slot, 0:8, :]
        for m in range(1, rows // 8):
            sums = sums + pltpu.roll(gram[slot, 8 * m : 8 * m + 8, :], 8 * m, 1)
        sums = pltpu.roll(sums, 0, 1, stride=1, stride_axis=0)
        line = jnp.sum(sums, axis=0, keepdims=True)[:, :span]
        raw[pl.ds(line_at + g, 1), :] = line
        return line * line

    squares = jnp.zeros((1, span), F32)
    for chunk in range(chunks):

        def body(i, total, chunk=chunk):
            total = total + one_group(chunk * send_rows, chunk * gpd, 2 * i, 0)
            return total + one_group(chunk * send_rows, chunk * gpd, 2 * i + 1, 1)

        squares = lax.fori_loop(0, gpd // 2, body, squares)
    squares_ref[...] = jnp.sum(squares, axis=1, keepdims=True)
    turn = reversal(rows)
    for a in range(n):
        tile = raw[:, (n - 1 - a) * rows : (n - a) * rows].astype(BF16)
        out_ref[a] = jnp.dot(tile, turn, preferred_element_type=F32).astype(BF16)


def filter_products(received, cpd, gpd, chunks):
    n, _, rows = received.shape
    span = n * rows
    raw_rows = round_up(gpd * chunks, 16)
    return pl.pallas_call(
        functools.partial(gram_kernel, cpd, gpd, chunks),
        in_specs=[pl.BlockSpec(memory_space=pltpu.VMEM)],
        out_specs=[pl.BlockSpec(memory_space=pltpu.VMEM)] * 2,
        out_shape=[
            jax.ShapeDtypeStruct((n, raw_rows, rows), BF16),
            jax.ShapeDtypeStruct((1, 1), F32),
        ],
        scratch_shapes=[
            pltpu.VMEM((2, rows, span + rows), F32),
            pltpu.VMEM((raw_rows, span), F32),
        ],
        compiler_params=params(LONG_VMEM),
        cost_estimate=pl.CostEstimate(
            flops=2 * cpd * chunks * span * span,
            bytes_accessed=2 * received.size,
            transcendentals=0,
        ),
        name="filter_products",
    )(received)


def taps_anti(ext_ref, signal, after, filter_taps):
    rows = signal.shape[0]
    ext_ref[0:rows, :] = signal
    ext_ref[rows : rows + EDGE, :] = after
    total = filter_taps[0:1] * signal
    for s in range(1, filter_taps.shape[0]):
        total = total + filter_taps[s : s + 1] * ext_ref[s : s + rows, :]
    return total


def short_edge(before, signal, filter_taps):
    both = jnp.concatenate([before, signal], 0)
    total = filter_taps[0:1] * signal
    for s in range(1, filter_taps.shape[0]):
        total = total + filter_taps[s : s + 1] * both[EDGE - s : 2 * EDGE - s]
    return total


def after_kernel(
    cpd, gpd, chunks, last, in_ref, og_ref, k_ref, v_ref, tail_ref, next_ref, taps_ref, *refs
):
    *refs, ext_q, ext_k, ext_v, ext_in_k, ext_in_v = refs
    if last:
        *refs, raw_ref, raw_rows = refs
    dq_ref, dk_ref, dv_ref = refs[-3:]
    step = pl.program_id(0)
    per_tile, in_rows, rows = in_ref.shape
    halo_rows = 2 * EDGE * max(1, cpd // LANES)
    halo_at = 2 * cpd
    turn = reversal(rows)
    for j in range(og_ref.shape[1] // LANES):
        at = slice(j * LANES, (j + 1) * LANES)
        if cpd >= LANES:
            dest, low = j * LANES // cpd, j * LANES % cpd
            conv = in_ref[dest, low : low + LANES, :]
            back = in_ref[dest, cpd + low : cpd + low + LANES, :]
            edge = halo_at + 2 * EDGE * (low // LANES)
            halo = in_ref[dest, edge : edge + 2 * EDGE, :].astype(F32)
        else:
            dests = range(j * LANES // cpd, (j + 1) * LANES // cpd)
            conv = jnp.concatenate([in_ref[d, 0:cpd, :] for d in dests], 0)
            back = jnp.concatenate([in_ref[d, cpd : 2 * cpd, :] for d in dests], 0)
            halo = jnp.concatenate(
                [in_ref[d, halo_at : halo_at + halo_rows, :].astype(F32)[:, :cpd] for d in dests], 1
            )
        conv = conv.astype(F32).T
        back = jnp.dot(back, turn, preferred_element_type=F32).T
        following = next_ref[:, at].astype(F32)
        taps_k = taps_ref[1, :, at]
        taps_v = taps_ref[2, :, at]
        tail = tail_ref[:, at].astype(F32)
        key = k_ref[:, at].astype(F32)
        value = v_ref[:, at].astype(F32)
        short_k = taps_causal(ext_in_k.at[j], tail[EDGE : 2 * EDGE], key, taps_k)
        short_v = taps_causal(ext_in_v.at[j], tail[2 * EDGE : 3 * EDGE], value, taps_v)
        next_k = short_edge(key[rows - EDGE :], following[EDGE : 2 * EDGE], taps_k)
        next_v = short_edge(value[rows - EDGE :], following[2 * EDGE : 3 * EDGE], taps_v)
        grad_q = og_ref[:, at].astype(F32) * conv
        dq_ref[:, at] = taps_anti(
            ext_q.at[j], grad_q, following[0:EDGE] * halo[0:EDGE], taps_ref[0, :, at]
        ).astype(BF16)
        dk_ref[:, at] = taps_anti(
            ext_k.at[j], back * short_v, halo[EDGE:] * next_v, taps_k
        ).astype(BF16)
        dv_ref[:, at] = taps_anti(
            ext_v.at[j], back * short_k, halo[EDGE:] * next_k, taps_v
        ).astype(BF16)
    if not last:
        return
    scale = refs[0][0, 0]
    half = raw_rows.shape[0] // chunks
    for dest in range(per_tile):
        lines = in_ref[dest, halo_at + halo_rows :, :].astype(F32)
        for chunk in range(chunks):
            at = chunk * half + (step * per_tile + dest) * gpd
            raw_rows[pl.ds(at, gpd), :] = lines[chunk * gpd : (chunk + 1) * gpd]

    @pl.when(step == pl.num_programs(0) - 1)
    def _():
        raw_ref[...] = raw_rows[...].T * scale


def after_exchange(
    returned, out_grad, key, value, tail, following, taps, groups, chunk, chunks, grads, scale
):
    n, in_rows, rows = returned.shape
    channels = out_grad.shape[1] // chunks
    cpd, gpd = channels // n, groups // (n * chunks)
    last = chunk + 1 == chunks
    tile = min(channels, max(512, cpd))
    per_tile = tile // cpd
    first = chunk * channels // tile
    block = pl.BlockSpec((rows, tile), lambda i: (0, first + i))
    ext = pltpu.VMEM((tile // LANES, rows + EDGE, LANES), F32)
    grad = jax.ShapeDtypeStruct(out_grad.shape, BF16)
    return pl.pallas_call(
        functools.partial(after_kernel, cpd, gpd, chunks, last),
        grid=(channels // tile,),
        in_specs=[
            pl.BlockSpec((per_tile, in_rows, rows), lambda i: (i, 0, 0)),
            block,
            block,
            block,
            pl.BlockSpec((3 * EDGE, tile), lambda i: (0, first + i)),
            pl.BlockSpec((3 * EDGE, tile), lambda i: (0, first + i)),
            pl.BlockSpec((3, taps.shape[1], tile), lambda i: (0, 0, first + i)),
        ]
        + [pl.BlockSpec(memory_space=pltpu.SMEM)] * len(scale)
        + [pl.BlockSpec(memory_space=pl.ANY)] * len(grads),
        input_output_aliases={7 + len(scale) + i: i for i in range(len(grads))},
        out_specs=[block] * 3 + [pl.BlockSpec((rows, groups), lambda i: (0, 0))] * len(scale),
        out_shape=[grad] * 3 + [jax.ShapeDtypeStruct((rows, groups), F32)] * len(scale),
        scratch_shapes=[pltpu.VMEM((groups, rows), F32)] * len(scale) + [ext] * 5,
        compiler_params=params(),
        cost_estimate=pl.CostEstimate(
            flops=90 * rows * channels, bytes_accessed=18 * rows * channels, transcendentals=0
        ),
        name="after_exchange",
    )(returned, out_grad, key, value, tail, following, taps, *scale, *grads)


def on_device(
    query_heads,
    key_heads,
    value_heads,
    hyena_query,
    hyena_key,
    hyena_value,
    short_filter,
    long_filter,
    output_grad,
):
    rows, channels = query_heads.shape
    groups = long_filter.shape[1]
    n = lax.axis_size("ctx")
    tp = lax.axis_size("tp")
    cpd, gpd = channels // n, groups // n
    position = lax.axis_index("ctx")
    tail = shifted(edge_rows((hyena_query, hyena_key, hyena_value), False), "ctx", 1)
    query_next = shifted(query_heads, "ctx", -1)
    chunks = 2 if gpd % 4 == 0 else 1
    cpd, gpd = cpd // chunks, gpd // chunks
    send = before_exchange(
        hyena_query, hyena_key, hyena_value, output_grad, tail, short_filter, long_filter, n, chunks
    )
    send, query_next, *sources = lax.optimization_barrier(
        (send, query_next, output_grad, hyena_key, hyena_value)
    )
    received = lax.all_to_all(send, "ctx", split_axis=0, concat_axis=0, tiled=True)
    following = shifted(edge_rows(sources, True), "ctx", -1)
    part, log = attend_next(query_next, key_heads, value_heads)
    part = shifted(part, "ctx", 1)
    log = shifted(log, "ctx", 1)
    returned = []
    attention = ()
    for chunk in range(chunks):
        raw = ()
        if chunk + 1 == chunks:
            *raw, squares = filter_products(received, cpd, gpd, chunks)
            squares = total_over(squares, "tp")
            squares = total_over(squares, "ctx")
        results = long_convs(received, raw, cpd, gpd, chunk, chunks)
        if chunk == 0:
            results, received, part, log, following = lax.optimization_barrier(
                (results, received, part, log, following)
            )
            attention = attend_own(query_heads, key_heads, value_heads, part, log, position)
        if chunk > 0:
            results, attention = lax.optimization_barrier((results, attention))
        returned.append(lax.all_to_all(results, "ctx", split_axis=0, concat_axis=0, tiled=True))
    bound = math.sqrt(rows * n * groups * tp)
    factor = jnp.minimum(1.0, bound / jnp.sqrt(squares))
    grads = ()
    for chunk in range(chunks):
        if chunk > 0:
            returned[chunk], *grads = lax.optimization_barrier((returned[chunk], *grads))
        scale = (factor,) if chunk + 1 == chunks else ()
        grads = after_exchange(
            returned[chunk], output_grad, hyena_key, hyena_value, tail, following, short_filter, groups,
            chunk, chunks, grads, scale,
        )
    return (attention, *grads)


def solution(mesh):
    whole = P("ctx", "tp")
    in_specs = (whole,) * 6 + (P(None, None, "tp"), whole, whole)
    return jax.shard_map(
        on_device, mesh=mesh, in_specs=in_specs, out_specs=(whole,) * 5, check_vma=False
    )
```

```python
import functools
import math

import jax
import jax.numpy as jnp
from jax import lax
from jax.experimental import pallas as pl
from jax.experimental.pallas import tpu as pltpu
from jax.sharding import PartitionSpec as P

HEAD_DIM = 128
LANES = 128
EDGE = 8
F32 = jnp.float32
BF16 = jnp.bfloat16
VMEM_BYTES = 60 * 1024 * 1024
LONG_VMEM = 20 * 1024 * 1024


def params(size=VMEM_BYTES):
    return pltpu.CompilerParams(vmem_limit_bytes=size)


def shifted(block, axis, distance):
    devices = range(lax.axis_size(axis))
    route = [(i - distance, i) for i in devices if i - distance in devices]
    return lax.ppermute(block, axis, route)


def total_over(value, axis):
    size = lax.axis_size(axis)
    distance = 1
    while distance < size:
        value = value + lax.ppermute(value, axis, [(i, i ^ distance) for i in range(size)])
        distance *= 2
    return value


def round_up(value, step):
    return -(-value // step) * step


def reversal(size):
    row = lax.broadcasted_iota(jnp.int32, (size, size), 0)
    col = lax.broadcasted_iota(jnp.int32, (size, size), 1)
    return jnp.where(row + col == size - 1, 1.0, 0.0).astype(BF16)


SCALE = 1.0 / math.sqrt(HEAD_DIM)
NT = (((1,), (1,)), ((), ()))


def attend_next_kernel(q_ref, k_ref, v_ref, out_ref, log_ref):
    rows = q_ref.shape[0]
    heads = q_ref.shape[1] // HEAD_DIM
    step = pl.program_id(0)
    lane = lax.broadcasted_iota(jnp.int32, (rows, log_ref.shape[1]), 1)

    @pl.when(step == 0)
    def _():
        log_ref[...] = jnp.zeros_like(log_ref)

    places = [slice(head * HEAD_DIM, (head + 1) * HEAD_DIM) for head in range(heads)]
    scores = [
        lax.dot_general(q_ref[:, at], k_ref[:, at], NT, preferred_element_type=F32) * SCALE
        for at in places
    ]
    largest = [jnp.max(score, axis=1, keepdims=True) for score in scores]
    raised = [jnp.exp(score - top) for score, top in zip(scores, largest)]
    totals = [jnp.sum(r, axis=1, keepdims=True) for r in raised]
    weights = [(r * (1.0 / total)).astype(BF16) for r, total in zip(raised, totals)]
    mixed = [
        jnp.dot(weight, v_ref[:, at], preferred_element_type=F32) for weight, at in zip(weights, places)
    ]
    logs = log_ref[...]
    for head, at in enumerate(places):
        out_ref[:, at] = mixed[head].astype(BF16)
        log = largest[head] + jnp.log(totals[head])
        logs = jnp.where(lane == step * heads + head, log, logs)
    log_ref[...] = logs


def attend_own_kernel(place_ref, q_ref, k_ref, v_ref, prev_ref, log_ref, out_ref):
    rows = q_ref.shape[0]
    heads = q_ref.shape[1] // HEAD_DIM
    step = pl.program_id(0)
    row = lax.broadcasted_iota(jnp.int32, (rows, rows), 0)
    col = lax.broadcasted_iota(jnp.int32, (rows, rows), 1)
    own_ok = col <= row
    lane = lax.broadcasted_iota(jnp.int32, (rows, log_ref.shape[1]), 1)
    has_prev = jnp.broadcast_to(place_ref[0], (rows, 1)) > 0
    places = [slice(head * HEAD_DIM, (head + 1) * HEAD_DIM) for head in range(heads)]
    scores = [
        lax.dot_general(q_ref[:, at], k_ref[:, at], NT, preferred_element_type=F32) * SCALE
        for at in places
    ]
    scores = [jnp.where(own_ok, score, -jnp.inf) for score in scores]
    logs = [
        jnp.sum(jnp.where(lane == step * heads + head, log_ref[...], 0.0), axis=1, keepdims=True)
        for head in range(heads)
    ]
    logs = [jnp.where(has_prev, log, -jnp.inf) for log in logs]
    largest = [
        jnp.maximum(jnp.max(score, axis=1, keepdims=True), log) for score, log in zip(scores, logs)
    ]
    raised = [jnp.exp(score - top) for score, top in zip(scores, largest)]
    prevs = [jnp.exp(log - top) for log, top in zip(logs, largest)]
    inverses = [
        1.0 / (jnp.sum(r, axis=1, keepdims=True) + prev) for r, prev in zip(raised, prevs)
    ]
    weights = [(r * inverse).astype(BF16) for r, inverse in zip(raised, inverses)]
    mixed = [
        jnp.dot(weight, v_ref[:, at], preferred_element_type=F32) for weight, at in zip(weights, places)
    ]
    for head, at in enumerate(places):
        total = mixed[head] + (prevs[head] * inverses[head]) * prev_ref[:, at].astype(F32)
        out_ref[:, at] = total.astype(BF16)


def attend_cost(rows, channels):
    heads = channels // HEAD_DIM
    return pl.CostEstimate(
        flops=4 * heads * rows * rows * HEAD_DIM,
        bytes_accessed=10 * rows * channels,
        transcendentals=heads * rows * rows,
    )


def attend_next(query, key, value):
    rows, channels = query.shape
    tile = min(512, channels)
    block = pl.BlockSpec((rows, tile), lambda i: (0, i))
    lanes = round_up(channels // HEAD_DIM, LANES)
    return pl.pallas_call(
        attend_next_kernel,
        grid=(channels // tile,),
        in_specs=[block] * 3,
        out_specs=[block, pl.BlockSpec((rows, lanes), lambda i: (0, 0))],
        out_shape=[
            jax.ShapeDtypeStruct((rows, channels), BF16),
            jax.ShapeDtypeStruct((rows, lanes), F32),
        ],
        compiler_params=params(),
        cost_estimate=attend_cost(rows, channels),
        name="attend_next",
    )(query, key, value)


def attend_own(query, key, value, prev, log, position):
    rows, channels = query.shape
    tile = min(512, channels)
    block = pl.BlockSpec((rows, tile), lambda i: (0, i))
    return pl.pallas_call(
        attend_own_kernel,
        grid=(channels // tile,),
        in_specs=[pl.BlockSpec(memory_space=pltpu.SMEM)]
        + [block] * 4
        + [pl.BlockSpec(log.shape, lambda i: (0, 0))],
        out_specs=block,
        out_shape=jax.ShapeDtypeStruct((rows, channels), BF16),
        compiler_params=params(),
        cost_estimate=attend_cost(rows, channels),
        name="attend_own",
    )(position.astype(jnp.int32).reshape(1), query, key, value, prev, log)


def edge_kernel(first, *refs):
    *sources, out_ref = refs
    parts = [r[...].astype(F32) for r in sources]
    parts = [p[:EDGE] if first else p[p.shape[0] - EDGE :] for p in parts]
    out_ref[...] = jnp.concatenate(parts, 0).astype(BF16)


def edge_rows(arrays, first):
    rows, channels = arrays[0].shape
    block = pl.BlockSpec((16, channels), lambda i: (0 if first else rows // 16 - 1, 0))
    return pl.pallas_call(
        functools.partial(edge_kernel, first),
        grid=(1,),
        in_specs=[block] * len(arrays),
        out_specs=pl.BlockSpec((len(arrays) * EDGE, channels), lambda i: (0, 0)),
        out_shape=jax.ShapeDtypeStruct((len(arrays) * EDGE, channels), BF16),
        compiler_params=params(),
        name="edge_rows",
    )(*arrays)


def taps_causal(ext_ref, before, signal, filter_taps):
    rows = signal.shape[0]
    ext_ref[0:EDGE, :] = before
    ext_ref[EDGE : EDGE + rows, :] = signal
    total = filter_taps[0:1] * signal
    for s in range(1, filter_taps.shape[0]):
        total = total + filter_taps[s : s + 1] * ext_ref[EDGE - s : EDGE - s + rows, :]
    return total


def before_kernel(
    cpd, gpd, q_ref, k_ref, v_ref, og_ref, tail_ref, taps_ref, long_ref, send_ref,
    long_rows, ext_q, ext_k, ext_v,
):
    step = pl.program_id(0)
    groups = long_ref.shape[1]
    per_tile, _, rows = send_ref.shape

    @pl.when(step == 0)
    def _():
        long_rows[...] = jnp.zeros_like(long_rows)
        long_rows[0:groups, :] = long_ref[...].T

    turn = reversal(rows)
    for j in range(q_ref.shape[1] // LANES):
        at = slice(j * LANES, (j + 1) * LANES)
        tail = tail_ref[:, at].astype(F32)
        short_q = taps_causal(ext_q.at[j], tail[0:EDGE], q_ref[:, at].astype(F32), taps_ref[0, :, at])
        short_k = taps_causal(
            ext_k.at[j], tail[EDGE : 2 * EDGE], k_ref[:, at].astype(F32), taps_ref[1, :, at]
        )
        short_v = taps_causal(
            ext_v.at[j], tail[2 * EDGE : 3 * EDGE], v_ref[:, at].astype(F32), taps_ref[2, :, at]
        )
        mixed = (short_k * short_v).T.astype(BF16)
        delta = (og_ref[:, at].astype(F32) * short_q).T.astype(BF16)
        delta = jnp.dot(delta, turn, preferred_element_type=F32).astype(BF16)
        width = min(cpd, LANES)
        for piece in range(LANES // width):
            channel = j * LANES + piece * width
            dest, low = channel // cpd, channel % cpd
            rows_at = slice(piece * width, (piece + 1) * width)
            send_ref[dest, low : low + width, :] = mixed[rows_at]
            send_ref[dest, cpd + low : cpd + low + width, :] = delta[rows_at]
    filter_rows = send_ref.shape[1] - 2 * cpd
    for dest in range(per_tile):
        first = (step * per_tile + dest) * gpd
        send_ref[dest, 2 * cpd :, :] = long_rows[pl.ds(first, filter_rows), :].astype(BF16)


def before_exchange(query, key, value, out_grad, tail, taps, long_filter, n, chunks):
    rows, channels = query.shape
    groups = long_filter.shape[1]
    cpd, gpd = channels // (n * chunks), groups // (n * chunks)
    tile = min(channels // chunks, max(512, cpd))
    per_tile = tile // cpd
    filter_rows = round_up(gpd, 16)
    send_rows = 2 * cpd + filter_rows
    steps = n // per_tile
    block = pl.BlockSpec((rows, tile), lambda i: (0, i))
    ext = pltpu.VMEM((tile // LANES, rows + EDGE, LANES), F32)
    return pl.pallas_call(
        functools.partial(before_kernel, cpd, gpd),
        grid=(channels // tile,),
        in_specs=[block] * 4
        + [
            pl.BlockSpec((3 * EDGE, tile), lambda i: (0, i)),
            pl.BlockSpec((3, taps.shape[1], tile), lambda i: (0, 0, i)),
            pl.BlockSpec((rows, groups), lambda i: (0, 0)),
        ],
        out_specs=pl.BlockSpec((per_tile, send_rows, rows), lambda i: (i % steps, i // steps, 0)),
        out_shape=jax.ShapeDtypeStruct((n, chunks * send_rows, rows), BF16),
        scratch_shapes=[pltpu.VMEM((round_up(groups, 8) + filter_rows, rows), F32), ext, ext, ext],
        compiler_params=params(),
        cost_estimate=pl.CostEstimate(
            flops=50 * rows * channels, bytes_accessed=12 * rows * channels, transcendentals=0
        ),
        name="before_exchange",
    )(query, key, value, out_grad, tail, taps, long_filter)


def conv_kernel(cpd, gpd, in_ref, *refs):
    *raw_ref, out_ref, taps, wide = refs
    upper = lower = 0.0
    if raw_ref:
        *raw_ref, squares_ref = raw_ref
        upper = squares_ref[...].astype(BF16).astype(F32)
        lower = squares_ref[...] - upper
    n, send_rows, rows = in_ref.shape
    gw = cpd // gpd
    span = n * rows
    filter_rows = send_rows - 2 * cpd
    taps[:, 0:rows] = jnp.zeros((filter_rows, rows), F32)
    for a in range(n):
        taps[:, (a + 1) * rows : (a + 2) * rows] = in_ref[a, 2 * cpd :, :].astype(F32)
    for slot in range(2):
        wide[slot, :, 0:rows] = jnp.zeros((rows, rows), BF16)

    def body(i, carry):
        slots = range(2)
        firsts = [pl.multiple_of((2 * i + slot) * gw, gw) for slot in slots]
        seconds = [pl.multiple_of(cpd + (2 * i + slot) * gw, gw) for slot in slots]
        bases = []
        for slot in slots:
            line = jnp.broadcast_to(taps[pl.ds(2 * i + slot, 1), :], (16, span + rows))
            bases.append(pltpu.roll(line, 0, 1, stride=1, stride_axis=0).astype(BF16))
        for m in range(rows // 16):
            for slot in slots:
                moved = bases[slot] if m == 0 else pltpu.roll(bases[slot], 16 * m, 1)
                wide[slot, 16 * m : 16 * m + 16, rows:] = moved[:, rows:]
        stacks = []
        for slot in slots:
            x = in_ref[:, pl.ds(firsts[slot], gw), :]
            d = in_ref[:, pl.ds(seconds[slot], gw), :]
            both = [jnp.concatenate([x[a], d[n - 1 - a]], 0) for a in range(n)]
            stacks.append(
                jnp.concatenate(
                    [jnp.concatenate([both[a], both[a + 1]], 1) for a in range(0, n, 2)], 0
                )
            )
        totals = [None, None]
        for k in range(n // 2):
            skip = 2 * gw * k
            low = 2 * rows * k
            for slot in slots:
                tile = jnp.concatenate(
                    [wide[slot, :, low + rows : low + 3 * rows], wide[slot, :, low : low + 2 * rows]], 0
                )
                part = jnp.dot(stacks[slot][: n * gw - skip], tile, preferred_element_type=F32)
                total = totals[slot]
                totals[slot] = (
                    part if k == 0 else jnp.concatenate([total[:skip], total[skip:] + part], 0)
                )
        for slot in slots:
            total = totals[slot]
            for a in range(n):
                at = slice(a % 2 * rows, (a % 2 + 1) * rows)
                top = a // 2 * 2 * gw
                out_ref[a, pl.ds(firsts[slot], gw), :] = total[top : top + gw, at].astype(BF16)
                out_ref[n - 1 - a, pl.ds(seconds[slot], gw), :] = total[
                    top + gw : top + 2 * gw, at
                ].astype(BF16)
        return carry

    lax.fori_loop(0, gpd // 2, body, 0)
    halo_at = 2 * cpd
    row = lax.broadcasted_iota(jnp.int32, (2 * EDGE, 2 * rows), 0)
    lane = lax.broadcasted_iota(jnp.int32, (2 * EDGE, 2 * rows), 1)
    wanted = jnp.where(row < EDGE, row, 2 * rows - 1 + EDGE - row)
    pick = jnp.where(lane == wanted, 1.0, 0.0).astype(BF16)
    row_out = lax.broadcasted_iota(jnp.int32, (2 * EDGE, rows), 0)
    for a in range(n):
        if a + 1 < n:
            results = jnp.concatenate([out_ref[a + 1, 0:cpd, :], out_ref[a + 1, cpd : 2 * cpd, :]], 1)
            halo = lax.dot_general(
                pick, results, (((1,), (1,)), ((), ())), preferred_element_type=F32
            )
            if cpd < LANES:
                halo = jnp.concatenate([halo, jnp.zeros((2 * EDGE, LANES - cpd), F32)], 1)
        else:
            halo = jnp.zeros((2 * EDGE, max(cpd, LANES)), F32)
        for j in range(halo.shape[1] // LANES):
            at = halo_at + 2 * EDGE * j
            tile = halo[:, j * LANES : (j + 1) * LANES]
            tile = jnp.where(row_out == EDGE - 2, upper, jnp.where(row_out == EDGE - 1, lower, tile))
            out_ref[a, at : at + 2 * EDGE, :] = tile.astype(BF16)
    for ref in raw_ref:
        out_ref[:, out_ref.shape[1] - ref.shape[1] :, :] = ref[...]


def long_convs(received, raw, cpd, gpd, chunk, chunks):
    n, send_rows, rows = received.shape
    send_rows = send_rows // chunks
    filter_rows = send_rows - 2 * cpd
    out_rows = 2 * cpd + 2 * EDGE * max(1, cpd // LANES) + sum(r.shape[1] for r in raw[:1])
    span = n * rows
    return pl.pallas_call(
        functools.partial(conv_kernel, cpd, gpd),
        grid=(1,),
        in_specs=[pl.BlockSpec((n, send_rows, rows), lambda i: (0, chunk, 0))]
        + [pl.BlockSpec(r.shape, lambda i, r=r: (0,) * r.ndim) for r in raw],
        out_specs=pl.BlockSpec((n, out_rows, rows), lambda i: (0, 0, 0)),
        out_shape=jax.ShapeDtypeStruct((n, out_rows, rows), BF16),
        scratch_shapes=[
            pltpu.VMEM((filter_rows, span + rows), F32),
            pltpu.VMEM((2, rows, span + rows), BF16),
        ],
        compiler_params=params(LONG_VMEM),
        cost_estimate=pl.CostEstimate(
            flops=4 * cpd * span * span, bytes_accessed=4 * n * out_rows * rows, transcendentals=0
        ),
        name="long_convs",
    )(received, *raw)


def gram_kernel(cpd, gpd, chunks, in_ref, out_ref, squares_ref, gram, raw):
    n, send_rows, rows = in_ref.shape
    send_rows = send_rows // chunks
    gw = cpd // gpd
    span = n * rows
    for slot in range(2):
        gram[slot, :, span:] = jnp.zeros((rows, rows), F32)
    if gpd * chunks < raw.shape[0]:
        raw[...] = jnp.zeros_like(raw)
    no_rows = jnp.zeros((n * gw, rows), BF16)

    def offset(d, k):
        held = (k + 1) * gw
        if held == n * gw:
            return d
        return jnp.concatenate([d[n * gw - held :], no_rows[held:]], 0)

    squares = jnp.zeros((1, span), F32)
    for chunk in range(chunks):
        base = chunk * send_rows

        def body(i, squares, chunk=chunk, base=base):
            slots = range(2)
            turned, shifting = [], []
            for slot in slots:
                first = pl.multiple_of(base + (2 * i + slot) * gw, gw)
                second = pl.multiple_of(base + cpd + (2 * i + slot) * gw, gw)
                x = in_ref[:, pl.ds(first, gw), :].reshape(n * gw, rows)
                shifting.append(in_ref[:, pl.ds(second, gw), :].reshape(n * gw, rows))
                turned.append(x.astype(F32).T.astype(BF16))
            for k in range(0, n, 2):
                for slot in slots:
                    d = shifting[slot]
                    pairs = jnp.concatenate([offset(d, k), offset(d, k + 1)], 1)
                    gram[slot, :, k * rows : (k + 2) * rows] = jnp.dot(
                        turned[slot], pairs, preferred_element_type=F32
                    )
            sums = [gram[slot, 0:8, :] for slot in slots]
            for m in range(1, rows // 8):
                for slot in slots:
                    block = gram[slot, 8 * m : 8 * m + 8, :]
                    sums[slot] = sums[slot] + pltpu.roll(block, 8 * m, 1)
            sums = [pltpu.roll(total, 0, 1, stride=1, stride_axis=0) for total in sums]
            for slot in slots:
                line = jnp.sum(sums[slot], axis=0, keepdims=True)[:, :span]
                raw[pl.ds(chunk * gpd + 2 * i + slot, 1), :] = line
                squares = squares + line * line
            return squares

        squares = lax.fori_loop(0, gpd // 2, body, squares)
    squares_ref[...] = jnp.sum(squares, axis=1, keepdims=True)
    turn = reversal(rows)
    for a in range(n):
        tile = raw[:, (n - 1 - a) * rows : (n - a) * rows].astype(BF16)
        out_ref[a] = jnp.dot(tile, turn, preferred_element_type=F32).astype(BF16)


def filter_products(received, cpd, gpd, chunks):
    n, _, rows = received.shape
    span = n * rows
    raw_rows = round_up(gpd * chunks, 16)
    return pl.pallas_call(
        functools.partial(gram_kernel, cpd, gpd, chunks),
        in_specs=[pl.BlockSpec(memory_space=pltpu.VMEM)],
        out_specs=[pl.BlockSpec(memory_space=pltpu.VMEM)] * 2,
        out_shape=[
            jax.ShapeDtypeStruct((n, raw_rows, rows), BF16),
            jax.ShapeDtypeStruct((1, 1), F32),
        ],
        scratch_shapes=[
            pltpu.VMEM((2, rows, span + rows), F32),
            pltpu.VMEM((raw_rows, span), F32),
        ],
        compiler_params=params(LONG_VMEM),
        cost_estimate=pl.CostEstimate(
            flops=2 * cpd * chunks * span * span,
            bytes_accessed=2 * received.size,
            transcendentals=0,
        ),
        name="filter_products",
    )(received)


def taps_anti(ext_ref, signal, after, filter_taps):
    rows = signal.shape[0]
    ext_ref[0:rows, :] = signal
    ext_ref[rows : rows + EDGE, :] = after
    total = filter_taps[0:1] * signal
    for s in range(1, filter_taps.shape[0]):
        total = total + filter_taps[s : s + 1] * ext_ref[s : s + rows, :]
    return total


def short_edge(before, signal, filter_taps):
    both = jnp.concatenate([before, signal], 0)
    total = filter_taps[0:1] * signal
    for s in range(1, filter_taps.shape[0]):
        total = total + filter_taps[s : s + 1] * both[EDGE - s : 2 * EDGE - s]
    return total


def after_kernel(
    cpd, gpd, chunks, last, bound, in_ref, og_ref, k_ref, v_ref, tail_ref, next_ref, taps_ref, *refs
):
    *refs, ext_q, ext_k, ext_v, ext_in_k, ext_in_v = refs
    if last:
        *refs, raw_ref, raw_rows, total_ref = refs
    dq_ref, dk_ref, dv_ref = refs[-3:]
    step = pl.program_id(0)
    per_tile, in_rows, rows = in_ref.shape
    halo_rows = 2 * EDGE * max(1, cpd // LANES)
    halo_at = 2 * cpd
    turn = reversal(rows)
    for j in range(og_ref.shape[1] // LANES):
        at = slice(j * LANES, (j + 1) * LANES)
        if cpd >= LANES:
            dest, low = j * LANES // cpd, j * LANES % cpd
            conv = in_ref[dest, low : low + LANES, :]
            back = in_ref[dest, cpd + low : cpd + low + LANES, :]
            edge = halo_at + 2 * EDGE * (low // LANES)
            halo = in_ref[dest, edge : edge + 2 * EDGE, :].astype(F32)
        else:
            dests = range(j * LANES // cpd, (j + 1) * LANES // cpd)
            conv = jnp.concatenate([in_ref[d, 0:cpd, :] for d in dests], 0)
            back = jnp.concatenate([in_ref[d, cpd : 2 * cpd, :] for d in dests], 0)
            halo = jnp.concatenate(
                [in_ref[d, halo_at : halo_at + halo_rows, :].astype(F32)[:, :cpd] for d in dests], 1
            )
        conv = conv.astype(F32).T
        back = jnp.dot(back, turn, preferred_element_type=F32).T
        following = next_ref[:, at].astype(F32)
        taps_k = taps_ref[1, :, at]
        taps_v = taps_ref[2, :, at]
        tail = tail_ref[:, at].astype(F32)
        key = k_ref[:, at].astype(F32)
        value = v_ref[:, at].astype(F32)
        short_k = taps_causal(ext_in_k.at[j], tail[EDGE : 2 * EDGE], key, taps_k)
        short_v = taps_causal(ext_in_v.at[j], tail[2 * EDGE : 3 * EDGE], value, taps_v)
        next_k = short_edge(key[rows - EDGE :], following[EDGE : 2 * EDGE], taps_k)
        next_v = short_edge(value[rows - EDGE :], following[2 * EDGE : 3 * EDGE], taps_v)
        grad_q = og_ref[:, at].astype(F32) * conv
        dq_ref[:, at] = taps_anti(
            ext_q.at[j], grad_q, following[0:EDGE] * halo[0:EDGE], taps_ref[0, :, at]
        ).astype(BF16)
        dk_ref[:, at] = taps_anti(
            ext_k.at[j], back * short_v, halo[EDGE:] * next_v, taps_k
        ).astype(BF16)
        dv_ref[:, at] = taps_anti(
            ext_v.at[j], back * short_k, halo[EDGE:] * next_k, taps_v
        ).astype(BF16)
    if not last:
        return
    squares = jnp.zeros((1, LANES), F32)
    for dest in range(per_tile):
        parts = in_ref[dest, halo_at : halo_at + 2 * EDGE, :].astype(F32)
        squares = squares + parts[EDGE - 2 : EDGE - 1] + parts[EDGE - 1 : EDGE]

    @pl.when(step == 0)
    def _():
        total_ref[...] = jnp.zeros_like(total_ref)

    total_ref[...] = total_ref[...] + squares
    half = raw_rows.shape[0] // chunks
    for dest in range(per_tile):
        lines = in_ref[dest, halo_at + halo_rows :, :].astype(F32)
        for chunk in range(chunks):
            at = chunk * half + (step * per_tile + dest) * gpd
            raw_rows[pl.ds(at, gpd), :] = lines[chunk * gpd : (chunk + 1) * gpd]

    @pl.when(step == pl.num_programs(0) - 1)
    def _():
        factor = jnp.minimum(1.0, bound / jnp.sqrt(total_ref[...]))[:, 0:1]
        raw_ref[...] = raw_rows[...].T * factor


def after_exchange(
    returned, out_grad, key, value, tail, following, taps, groups, chunk, chunks, grads, bound
):
    n, in_rows, rows = returned.shape
    channels = out_grad.shape[1] // chunks
    cpd, gpd = channels // n, groups // (n * chunks)
    last = chunk + 1 == chunks
    tile = min(channels, max(512, cpd))
    per_tile = tile // cpd
    first = chunk * channels // tile
    block = pl.BlockSpec((rows, tile), lambda i: (0, first + i))
    ext = pltpu.VMEM((tile // LANES, rows + EDGE, LANES), F32)
    grad = jax.ShapeDtypeStruct(out_grad.shape, BF16)
    return pl.pallas_call(
        functools.partial(after_kernel, cpd, gpd, chunks, last, bound),
        grid=(channels // tile,),
        in_specs=[
            pl.BlockSpec((per_tile, in_rows, rows), lambda i: (i, 0, 0)),
            block,
            block,
            block,
            pl.BlockSpec((3 * EDGE, tile), lambda i: (0, first + i)),
            pl.BlockSpec((3 * EDGE, tile), lambda i: (0, first + i)),
            pl.BlockSpec((3, taps.shape[1], tile), lambda i: (0, 0, first + i)),
        ]
        + [pl.BlockSpec(memory_space=pl.ANY)] * len(grads),
        input_output_aliases={7 + i: i for i in range(len(grads))},
        out_specs=[block] * 3 + [pl.BlockSpec((rows, groups), lambda i: (0, 0))] * last,
        out_shape=[grad] * 3 + [jax.ShapeDtypeStruct((rows, groups), F32)] * last,
        scratch_shapes=[pltpu.VMEM((groups, rows), F32), pltpu.VMEM((1, LANES), F32)] * last
        + [ext] * 5,
        compiler_params=params(),
        cost_estimate=pl.CostEstimate(
            flops=90 * rows * channels, bytes_accessed=18 * rows * channels, transcendentals=0
        ),
        name="after_exchange",
    )(returned, out_grad, key, value, tail, following, taps, *grads)


def on_device(
    query_heads,
    key_heads,
    value_heads,
    hyena_query,
    hyena_key,
    hyena_value,
    short_filter,
    long_filter,
    output_grad,
):
    rows, channels = query_heads.shape
    groups = long_filter.shape[1]
    n = lax.axis_size("ctx")
    tp = lax.axis_size("tp")
    cpd, gpd = channels // n, groups // n
    position = lax.axis_index("ctx")
    tail = shifted(edge_rows((hyena_query, hyena_key, hyena_value), False), "ctx", 1)
    queries, tail = lax.optimization_barrier((query_heads, tail))
    query_next = shifted(queries, "ctx", -1)
    chunks = 2 if gpd % 4 == 0 else 1
    cpd, gpd = cpd // chunks, gpd // chunks
    send = before_exchange(
        hyena_query, hyena_key, hyena_value, output_grad, tail, short_filter, long_filter, n, chunks
    )
    send, query_next, *sources = lax.optimization_barrier(
        (send, query_next, output_grad, hyena_key, hyena_value)
    )
    received = lax.all_to_all(send, "ctx", split_axis=0, concat_axis=0, tiled=True)
    following = shifted(edge_rows(sources, True), "ctx", -1)
    part, log = attend_next(query_next, key_heads, value_heads)
    part = shifted(part, "ctx", 1)
    log = shifted(log, "ctx", 1)
    returned = []
    for chunk in range(chunks):
        raw = ()
        if chunk + 1 == chunks:
            raw, squares = filter_products(received, cpd, gpd, chunks)
            raw = (raw, total_over(squares, "tp"))
        results = long_convs(received, raw, cpd, gpd, chunk, chunks)
        if chunk == 0:
            results, received, part, log, following = lax.optimization_barrier(
                (results, received, part, log, following)
            )
        returned.append(lax.all_to_all(results, "ctx", split_axis=0, concat_axis=0, tiled=True))
    attention = attend_own(query_heads, key_heads, value_heads, part, log, position)
    bound = math.sqrt(rows * n * groups * tp)
    grads = ()
    for chunk in range(chunks):
        if chunk > 0:
            returned[chunk], attention, *grads = lax.optimization_barrier(
                (returned[chunk], attention, *grads)
            )
        grads = after_exchange(
            returned[chunk], output_grad, hyena_key, hyena_value, tail, following, short_filter, groups,
            chunk, chunks, grads, bound,
        )
    return (attention, *grads)


def solution(mesh):
    whole = P("ctx", "tp")
    in_specs = (whole,) * 6 + (P(None, None, "tp"), whole, whole)
    return jax.shard_map(
        on_device, mesh=mesh, in_specs=in_specs, out_specs=(whole,) * 5, check_vma=False
    )
```

```python
import functools
import math

import jax
import jax.numpy as jnp
from jax import lax
from jax.experimental import pallas as pl
from jax.experimental.pallas import tpu as pltpu
from jax.sharding import PartitionSpec as P

HEAD_DIM = 128
LANES = 128
EDGE = 8
F32 = jnp.float32
BF16 = jnp.bfloat16
VMEM_BYTES = 60 * 1024 * 1024
LONG_VMEM = 20 * 1024 * 1024


def params(size=VMEM_BYTES):
    return pltpu.CompilerParams(vmem_limit_bytes=size)


def shifted(block, axis, distance):
    devices = range(lax.axis_size(axis))
    route = [(i - distance, i) for i in devices if i - distance in devices]
    return lax.ppermute(block, axis, route)


def total_over(value, axis):
    size = lax.axis_size(axis)
    distance = 1
    while distance < size:
        value = value + lax.ppermute(value, axis, [(i, i ^ distance) for i in range(size)])
        distance *= 2
    return value


def round_up(value, step):
    return -(-value // step) * step


def reversal(size):
    row = lax.broadcasted_iota(jnp.int32, (size, size), 0)
    col = lax.broadcasted_iota(jnp.int32, (size, size), 1)
    return jnp.where(row + col == size - 1, 1.0, 0.0).astype(BF16)


SCALE = 1.0 / math.sqrt(HEAD_DIM)
NT = (((1,), (1,)), ((), ()))


def attend_kernel(place_ref, q_ref, k_ref, v_ref, kp_ref, vp_ref, out_ref):
    rows = q_ref.shape[0]
    heads = q_ref.shape[1] // HEAD_DIM
    row = lax.broadcasted_iota(jnp.int32, (rows, rows), 0)
    col = lax.broadcasted_iota(jnp.int32, (rows, rows), 1)
    own_ok = col <= row
    prev_ok = jnp.broadcast_to(place_ref[0], (rows, rows)) > 0
    places = [slice(head * HEAD_DIM, (head + 1) * HEAD_DIM) for head in range(heads)]

    def scores(ref, allowed):
        products = [
            lax.dot_general(q_ref[:, at], ref[:, at], NT, preferred_element_type=F32) for at in places
        ]
        return [jnp.where(allowed, product * SCALE, -jnp.inf) for product in products]

    own, prev = scores(k_ref, own_ok), scores(kp_ref, prev_ok)
    largest = [jnp.max(jnp.maximum(o, p), axis=1, keepdims=True) for o, p in zip(own, prev)]
    own = [jnp.exp(o - top) for o, top in zip(own, largest)]
    prev = [jnp.exp(p - top) for p, top in zip(prev, largest)]
    totals = [jnp.sum(o + p, axis=1, keepdims=True) for o, p in zip(own, prev)]
    inverses = [1.0 / total for total in totals]
    own = [(o * inverse).astype(BF16) for o, inverse in zip(own, inverses)]
    prev = [(p * inverse).astype(BF16) for p, inverse in zip(prev, inverses)]
    mixed = [
        jnp.dot(o, v_ref[:, at], preferred_element_type=F32)
        + jnp.dot(p, vp_ref[:, at], preferred_element_type=F32)
        for o, p, at in zip(own, prev, places)
    ]
    for head, at in enumerate(places):
        out_ref[:, at] = mixed[head].astype(BF16)


def attend(query, key, value, key_prev, value_prev, position):
    rows, channels = query.shape
    tile = min(512, channels)
    heads = channels // HEAD_DIM
    block = pl.BlockSpec((rows, tile), lambda i: (0, i))
    return pl.pallas_call(
        attend_kernel,
        grid=(channels // tile,),
        in_specs=[pl.BlockSpec(memory_space=pltpu.SMEM)] + [block] * 5,
        out_specs=block,
        out_shape=jax.ShapeDtypeStruct((rows, channels), BF16),
        compiler_params=params(LONG_VMEM),
        cost_estimate=pl.CostEstimate(
            flops=8 * heads * rows * rows * HEAD_DIM,
            bytes_accessed=12 * rows * channels,
            transcendentals=2 * heads * rows * rows,
        ),
        name="attend",
    )(position.astype(jnp.int32).reshape(1), query, key, value, key_prev, value_prev)


def edge_kernel(first, *refs):
    *sources, out_ref = refs
    parts = [r[...].astype(F32) for r in sources]
    parts = [p[:EDGE] if first else p[p.shape[0] - EDGE :] for p in parts]
    out_ref[...] = jnp.concatenate(parts, 0).astype(BF16)


def edge_rows(arrays, first):
    rows, channels = arrays[0].shape
    block = pl.BlockSpec((16, channels), lambda i: (0 if first else rows // 16 - 1, 0))
    return pl.pallas_call(
        functools.partial(edge_kernel, first),
        grid=(1,),
        in_specs=[block] * len(arrays),
        out_specs=pl.BlockSpec((len(arrays) * EDGE, channels), lambda i: (0, 0)),
        out_shape=jax.ShapeDtypeStruct((len(arrays) * EDGE, channels), BF16),
        compiler_params=params(),
        name="edge_rows",
    )(*arrays)


def taps_causal(ext_ref, befores, signals, filters):
    rows = signals[0].shape[0]
    for j, signal in enumerate(signals):
        ext_ref[j, 0:EDGE, :] = befores[j]
        ext_ref[j, EDGE : EDGE + rows, :] = signal
    totals = [taps[0:1] * signal for signal, taps in zip(signals, filters)]
    for s in range(1, filters[0].shape[0]):
        for j, taps in enumerate(filters):
            totals[j] = totals[j] + taps[s : s + 1] * ext_ref[j, EDGE - s : EDGE - s + rows, :]
    return totals


def columns_of(width):
    return [slice(j * LANES, (j + 1) * LANES) for j in range(width // LANES)]


def before_kernel(
    cpd, gpd, q_ref, k_ref, v_ref, og_ref, tail_ref, taps_ref, long_ref, send_ref,
    long_rows, ext_q, ext_k, ext_v,
):
    step = pl.program_id(0)
    groups = long_ref.shape[1]
    per_tile, _, rows = send_ref.shape

    @pl.when(step == 0)
    def _():
        long_rows[...] = jnp.zeros_like(long_rows)
        long_rows[0:groups, :] = long_ref[...].T

    turn = reversal(rows)
    places = columns_of(q_ref.shape[1])
    tails = [tail_ref[:, at].astype(F32) for at in places]

    def short(which, ref, ext):
        return taps_causal(
            ext,
            [tail[which * EDGE : (which + 1) * EDGE] for tail in tails],
            [ref[:, at].astype(F32) for at in places],
            [taps_ref[which, :, at] for at in places],
        )

    short_k, short_v = short(1, k_ref, ext_k), short(2, v_ref, ext_v)
    mixed = [(k * v).T.astype(BF16) for k, v in zip(short_k, short_v)]
    short_q = short(0, q_ref, ext_q)
    delta = [(og_ref[:, at].astype(F32) * q).T.astype(BF16) for q, at in zip(short_q, places)]
    delta = [jnp.dot(d, turn, preferred_element_type=F32).astype(BF16) for d in delta]
    width = min(cpd, LANES)
    for j in range(len(places)):
        for piece in range(LANES // width):
            channel = j * LANES + piece * width
            dest, low = channel // cpd, channel % cpd
            rows_at = slice(piece * width, (piece + 1) * width)
            send_ref[dest, low : low + width, :] = mixed[j][rows_at]
            send_ref[dest, cpd + low : cpd + low + width, :] = delta[j][rows_at]
    filter_rows = send_ref.shape[1] - 2 * cpd
    for dest in range(per_tile):
        first = (step * per_tile + dest) * gpd
        send_ref[dest, 2 * cpd :, :] = long_rows[pl.ds(first, filter_rows), :].astype(BF16)


def before_exchange(query, key, value, out_grad, tail, taps, long_filter, n, chunks):
    rows, channels = query.shape
    groups = long_filter.shape[1]
    cpd, gpd = channels // (n * chunks), groups // (n * chunks)
    tile = min(channels // chunks, max(512, cpd))
    per_tile = tile // cpd
    filter_rows = round_up(gpd, 16)
    send_rows = 2 * cpd + filter_rows
    steps = n // per_tile
    block = pl.BlockSpec((rows, tile), lambda i: (0, i))
    ext = pltpu.VMEM((tile // LANES, rows + EDGE, LANES), F32)
    return pl.pallas_call(
        functools.partial(before_kernel, cpd, gpd),
        grid=(channels // tile,),
        in_specs=[block] * 4
        + [
            pl.BlockSpec((3 * EDGE, tile), lambda i: (0, i)),
            pl.BlockSpec((3, taps.shape[1], tile), lambda i: (0, 0, i)),
            pl.BlockSpec((rows, groups), lambda i: (0, 0)),
        ],
        out_specs=pl.BlockSpec((per_tile, send_rows, rows), lambda i: (i % steps, i // steps, 0)),
        out_shape=jax.ShapeDtypeStruct((n, chunks * send_rows, rows), BF16),
        scratch_shapes=[pltpu.VMEM((round_up(groups, 8) + filter_rows, rows), F32), ext, ext, ext],
        compiler_params=params(),
        cost_estimate=pl.CostEstimate(
            flops=50 * rows * channels, bytes_accessed=12 * rows * channels, transcendentals=0
        ),
        name="before_exchange",
    )(query, key, value, out_grad, tail, taps, long_filter)


def conv_kernel(cpd, gpd, in_ref, *refs):
    *raw_ref, out_ref, taps, wide = refs
    upper = lower = 0.0
    if raw_ref:
        *raw_ref, squares_ref = raw_ref
        upper = squares_ref[...].astype(BF16).astype(F32)
        lower = squares_ref[...] - upper
    n, send_rows, rows = in_ref.shape
    gw = cpd // gpd
    span = n * rows
    filter_rows = send_rows - 2 * cpd
    taps[:, 0:rows] = jnp.zeros((filter_rows, rows), F32)
    for a in range(n):
        taps[:, (a + 1) * rows : (a + 2) * rows] = in_ref[a, 2 * cpd :, :].astype(F32)
    for slot in range(2):
        wide[slot, :, 0:rows] = jnp.zeros((rows, rows), BF16)

    def body(i, carry):
        slots = range(2)
        firsts = [pl.multiple_of((2 * i + slot) * gw, gw) for slot in slots]
        seconds = [pl.multiple_of(cpd + (2 * i + slot) * gw, gw) for slot in slots]
        bases = []
        for slot in slots:
            line = jnp.broadcast_to(taps[pl.ds(2 * i + slot, 1), :], (16, span + rows))
            bases.append(pltpu.roll(line, 0, 1, stride=1, stride_axis=0).astype(BF16))
        for m in range(rows // 16):
            for slot in slots:
                moved = bases[slot] if m == 0 else pltpu.roll(bases[slot], 16 * m, 1)
                wide[slot, 16 * m : 16 * m + 16, rows:] = moved[:, rows:]
        stacks = []
        for slot in slots:
            x = in_ref[:, pl.ds(firsts[slot], gw), :]
            d = in_ref[:, pl.ds(seconds[slot], gw), :]
            both = [jnp.concatenate([x[a], d[n - 1 - a]], 0) for a in range(n)]
            stacks.append(
                jnp.concatenate(
                    [jnp.concatenate([both[a], both[a + 1]], 1) for a in range(0, n, 2)], 0
                )
            )
        totals = [None, None]
        for k in range(n // 2):
            skip = 2 * gw * k
            low = 2 * rows * k
            for slot in slots:
                tile = jnp.concatenate(
                    [wide[slot, :, low + rows : low + 3 * rows], wide[slot, :, low : low + 2 * rows]], 0
                )
                part = jnp.dot(stacks[slot][: n * gw - skip], tile, preferred_element_type=F32)
                total = totals[slot]
                totals[slot] = (
                    part if k == 0 else jnp.concatenate([total[:skip], total[skip:] + part], 0)
                )
        for slot in slots:
            total = totals[slot]
            for a in range(n):
                at = slice(a % 2 * rows, (a % 2 + 1) * rows)
                top = a // 2 * 2 * gw
                out_ref[a, pl.ds(firsts[slot], gw), :] = total[top : top + gw, at].astype(BF16)
                out_ref[n - 1 - a, pl.ds(seconds[slot], gw), :] = total[
                    top + gw : top + 2 * gw, at
                ].astype(BF16)
        return carry

    lax.fori_loop(0, gpd // 2, body, 0)
    halo_at = 2 * cpd
    row = lax.broadcasted_iota(jnp.int32, (2 * EDGE, 2 * rows), 0)
    lane = lax.broadcasted_iota(jnp.int32, (2 * EDGE, 2 * rows), 1)
    wanted = jnp.where(row < EDGE, row, 2 * rows - 1 + EDGE - row)
    pick = jnp.where(lane == wanted, 1.0, 0.0).astype(BF16)
    row_out = lax.broadcasted_iota(jnp.int32, (2 * EDGE, rows), 0)
    for a in range(n):
        if a + 1 < n:
            results = jnp.concatenate([out_ref[a + 1, 0:cpd, :], out_ref[a + 1, cpd : 2 * cpd, :]], 1)
            halo = lax.dot_general(
                pick, results, (((1,), (1,)), ((), ())), preferred_element_type=F32
            )
            if cpd < LANES:
                halo = jnp.concatenate([halo, jnp.zeros((2 * EDGE, LANES - cpd), F32)], 1)
        else:
            halo = jnp.zeros((2 * EDGE, max(cpd, LANES)), F32)
        for j in range(halo.shape[1] // LANES):
            at = halo_at + 2 * EDGE * j
            tile = halo[:, j * LANES : (j + 1) * LANES]
            tile = jnp.where(row_out == EDGE - 2, upper, jnp.where(row_out == EDGE - 1, lower, tile))
            out_ref[a, at : at + 2 * EDGE, :] = tile.astype(BF16)
    for ref in raw_ref:
        out_ref[:, out_ref.shape[1] - ref.shape[1] :, :] = ref[...]


def long_convs(received, raw, cpd, gpd, chunk, chunks):
    n, send_rows, rows = received.shape
    send_rows = send_rows // chunks
    filter_rows = send_rows - 2 * cpd
    out_rows = 2 * cpd + 2 * EDGE * max(1, cpd // LANES) + sum(r.shape[1] for r in raw[:1])
    span = n * rows
    return pl.pallas_call(
        functools.partial(conv_kernel, cpd, gpd),
        grid=(1,),
        in_specs=[pl.BlockSpec((n, send_rows, rows), lambda i: (0, chunk, 0))]
        + [pl.BlockSpec(r.shape, lambda i, r=r: (0,) * r.ndim) for r in raw],
        out_specs=pl.BlockSpec((n, out_rows, rows), lambda i: (0, 0, 0)),
        out_shape=jax.ShapeDtypeStruct((n, out_rows, rows), BF16),
        scratch_shapes=[
            pltpu.VMEM((filter_rows, span + rows), F32),
            pltpu.VMEM((2, rows, span + rows), BF16),
        ],
        compiler_params=params(LONG_VMEM),
        cost_estimate=pl.CostEstimate(
            flops=4 * cpd * span * span, bytes_accessed=4 * n * out_rows * rows, transcendentals=0
        ),
        name="long_convs",
    )(received, *raw)


def gram_kernel(cpd, gpd, chunks, in_ref, out_ref, squares_ref, gram, raw):
    n, send_rows, rows = in_ref.shape
    send_rows = send_rows // chunks
    gw = cpd // gpd
    span = n * rows
    for slot in range(2):
        gram[slot, :, span:] = jnp.zeros((rows, rows), F32)
    if gpd * chunks < raw.shape[0]:
        raw[...] = jnp.zeros_like(raw)
    no_rows = jnp.zeros((n * gw, rows), BF16)

    def offset(d, k):
        held = (k + 1) * gw
        if held == n * gw:
            return d
        return jnp.concatenate([d[n * gw - held :], no_rows[held:]], 0)

    squares = jnp.zeros((1, span), F32)
    for chunk in range(chunks):
        base = chunk * send_rows

        def body(i, squares, chunk=chunk, base=base):
            slots = range(2)
            turned, shifting = [], []
            for slot in slots:
                first = pl.multiple_of(base + (2 * i + slot) * gw, gw)
                second = pl.multiple_of(base + cpd + (2 * i + slot) * gw, gw)
                x = in_ref[:, pl.ds(first, gw), :].reshape(n * gw, rows)
                shifting.append(in_ref[:, pl.ds(second, gw), :].reshape(n * gw, rows))
                turned.append(x.astype(F32).T.astype(BF16))
            for k in range(0, n, 2):
                for slot in slots:
                    d = shifting[slot]
                    pairs = jnp.concatenate([offset(d, k), offset(d, k + 1)], 1)
                    gram[slot, :, k * rows : (k + 2) * rows] = jnp.dot(
                        turned[slot], pairs, preferred_element_type=F32
                    )
            sums = [gram[slot, 0:8, :] for slot in slots]
            for m in range(1, rows // 8):
                for slot in slots:
                    block = gram[slot, 8 * m : 8 * m + 8, :]
                    sums[slot] = sums[slot] + pltpu.roll(block, 8 * m, 1)
            sums = [pltpu.roll(total, 0, 1, stride=1, stride_axis=0) for total in sums]
            for slot in slots:
                line = jnp.sum(sums[slot], axis=0, keepdims=True)[:, :span]
                raw[pl.ds(chunk * gpd + 2 * i + slot, 1), :] = line
                squares = squares + line * line
            return squares

        squares = lax.fori_loop(0, gpd // 2, body, squares)
    squares_ref[...] = jnp.sum(squares, axis=1, keepdims=True)
    turn = reversal(rows)
    for a in range(n):
        tile = raw[:, (n - 1 - a) * rows : (n - a) * rows].astype(BF16)
        out_ref[a] = jnp.dot(tile, turn, preferred_element_type=F32).astype(BF16)


def filter_products(received, cpd, gpd, chunks):
    n, _, rows = received.shape
    span = n * rows
    raw_rows = round_up(gpd * chunks, 16)
    return pl.pallas_call(
        functools.partial(gram_kernel, cpd, gpd, chunks),
        in_specs=[pl.BlockSpec(memory_space=pltpu.VMEM)],
        out_specs=[pl.BlockSpec(memory_space=pltpu.VMEM)] * 2,
        out_shape=[
            jax.ShapeDtypeStruct((n, raw_rows, rows), BF16),
            jax.ShapeDtypeStruct((1, 1), F32),
        ],
        scratch_shapes=[
            pltpu.VMEM((2, rows, span + rows), F32),
            pltpu.VMEM((raw_rows, span), F32),
        ],
        compiler_params=params(LONG_VMEM),
        cost_estimate=pl.CostEstimate(
            flops=2 * cpd * chunks * span * span,
            bytes_accessed=2 * received.size,
            transcendentals=0,
        ),
        name="filter_products",
    )(received)


def taps_anti(ext_ref, signals, afters, filters):
    rows = signals[0].shape[0]
    for j, signal in enumerate(signals):
        ext_ref[j, 0:rows, :] = signal
        ext_ref[j, rows : rows + EDGE, :] = afters[j]
    totals = [taps[0:1] * signal for signal, taps in zip(signals, filters)]
    for s in range(1, filters[0].shape[0]):
        for j, taps in enumerate(filters):
            totals[j] = totals[j] + taps[s : s + 1] * ext_ref[j, s : s + rows, :]
    return totals


def short_edge(before, signal, filter_taps):
    both = jnp.concatenate([before, signal], 0)
    total = filter_taps[0:1] * signal
    for s in range(1, filter_taps.shape[0]):
        total = total + filter_taps[s : s + 1] * both[EDGE - s : 2 * EDGE - s]
    return total


def after_kernel(
    cpd, gpd, chunks, last, bound, in_ref, og_ref, k_ref, v_ref, tail_ref, next_ref, taps_ref, *refs
):
    *refs, ext_q, ext_k, ext_v, ext_in_k, ext_in_v = refs
    if last:
        *refs, raw_ref, raw_rows, total_ref = refs
    dq_ref, dk_ref, dv_ref = refs[-3:]
    step = pl.program_id(0)
    per_tile, in_rows, rows = in_ref.shape
    halo_rows = 2 * EDGE * max(1, cpd // LANES)
    halo_at = 2 * cpd
    turn = reversal(rows)
    places = columns_of(og_ref.shape[1])
    tails = [tail_ref[:, at].astype(F32) for at in places]
    nexts = [next_ref[:, at].astype(F32) for at in places]
    convs, backs, halos = [], [], []
    for j in range(len(places)):
        if cpd >= LANES:
            dest, low = j * LANES // cpd, j * LANES % cpd
            conv = in_ref[dest, low : low + LANES, :]
            back = in_ref[dest, cpd + low : cpd + low + LANES, :]
            edge = halo_at + 2 * EDGE * (low // LANES)
            halo = in_ref[dest, edge : edge + 2 * EDGE, :].astype(F32)
        else:
            dests = range(j * LANES // cpd, (j + 1) * LANES // cpd)
            conv = jnp.concatenate([in_ref[d, 0:cpd, :] for d in dests], 0)
            back = jnp.concatenate([in_ref[d, cpd : 2 * cpd, :] for d in dests], 0)
            halo = jnp.concatenate(
                [in_ref[d, halo_at : halo_at + halo_rows, :].astype(F32)[:, :cpd] for d in dests], 1
            )
        convs.append(conv)
        backs.append(back)
        halos.append(halo)
    convs = [conv.astype(F32).T for conv in convs]
    backs = [jnp.dot(back, turn, preferred_element_type=F32) for back in backs]
    backs = [back.T for back in backs]
    taps = [[taps_ref[which, :, at] for at in places] for which in range(3)]
    keys = [k_ref[:, at].astype(F32) for at in places]
    values = [v_ref[:, at].astype(F32) for at in places]
    short_k = taps_causal(ext_in_k, [tail[EDGE : 2 * EDGE] for tail in tails], keys, taps[1])
    short_v = taps_causal(ext_in_v, [tail[2 * EDGE : 3 * EDGE] for tail in tails], values, taps[2])
    next_k = [
        short_edge(k[rows - EDGE :], f[EDGE : 2 * EDGE], t) for k, f, t in zip(keys, nexts, taps[1])
    ]
    next_v = [
        short_edge(v[rows - EDGE :], f[2 * EDGE : 3 * EDGE], t)
        for v, f, t in zip(values, nexts, taps[2])
    ]

    def store(ref, ext, signals, afters, filters):
        for at, total in zip(places, taps_anti(ext, signals, afters, filters)):
            ref[:, at] = total.astype(BF16)

    store(
        dq_ref,
        ext_q,
        [og_ref[:, at].astype(F32) * conv for at, conv in zip(places, convs)],
        [f[0:EDGE] * halo[0:EDGE] for f, halo in zip(nexts, halos)],
        taps[0],
    )
    store(
        dk_ref,
        ext_k,
        [back * v for back, v in zip(backs, short_v)],
        [halo[EDGE:] * v for halo, v in zip(halos, next_v)],
        taps[1],
    )
    store(
        dv_ref,
        ext_v,
        [back * k for back, k in zip(backs, short_k)],
        [halo[EDGE:] * k for halo, k in zip(halos, next_k)],
        taps[2],
    )
    if not last:
        return
    squares = jnp.zeros((1, LANES), F32)
    for dest in range(per_tile):
        parts = in_ref[dest, halo_at : halo_at + 2 * EDGE, :].astype(F32)
        squares = squares + parts[EDGE - 2 : EDGE - 1] + parts[EDGE - 1 : EDGE]

    @pl.when(step == 0)
    def _():
        total_ref[...] = jnp.zeros_like(total_ref)

    total_ref[...] = total_ref[...] + squares
    half = raw_rows.shape[0] // chunks
    for dest in range(per_tile):
        lines = in_ref[dest, halo_at + halo_rows :, :].astype(F32)
        for chunk in range(chunks):
            at = chunk * half + (step * per_tile + dest) * gpd
            raw_rows[pl.ds(at, gpd), :] = lines[chunk * gpd : (chunk + 1) * gpd]

    @pl.when(step == pl.num_programs(0) - 1)
    def _():
        factor = jnp.minimum(1.0, bound / jnp.sqrt(total_ref[...]))[:, 0:1]
        raw_ref[...] = raw_rows[...].T * factor


def after_exchange(
    returned, out_grad, key, value, tail, following, taps, groups, chunk, chunks, grads, bound
):
    n, in_rows, rows = returned.shape
    channels = out_grad.shape[1] // chunks
    cpd, gpd = channels // n, groups // (n * chunks)
    last = chunk + 1 == chunks
    tile = min(channels, max(512, cpd))
    per_tile = tile // cpd
    first = chunk * channels // tile
    block = pl.BlockSpec((rows, tile), lambda i: (0, first + i))
    ext = pltpu.VMEM((tile // LANES, rows + EDGE, LANES), F32)
    grad = jax.ShapeDtypeStruct(out_grad.shape, BF16)
    return pl.pallas_call(
        functools.partial(after_kernel, cpd, gpd, chunks, last, bound),
        grid=(channels // tile,),
        in_specs=[
            pl.BlockSpec((per_tile, in_rows, rows), lambda i: (i, 0, 0)),
            block,
            block,
            block,
            pl.BlockSpec((3 * EDGE, tile), lambda i: (0, first + i)),
            pl.BlockSpec((3 * EDGE, tile), lambda i: (0, first + i)),
            pl.BlockSpec((3, taps.shape[1], tile), lambda i: (0, 0, first + i)),
        ]
        + [pl.BlockSpec(memory_space=pl.ANY)] * len(grads),
        input_output_aliases={7 + i: i for i in range(len(grads))},
        out_specs=[block] * 3 + [pl.BlockSpec((rows, groups), lambda i: (0, 0))] * last,
        out_shape=[grad] * 3 + [jax.ShapeDtypeStruct((rows, groups), F32)] * last,
        scratch_shapes=[pltpu.VMEM((groups, rows), F32), pltpu.VMEM((1, LANES), F32)] * last
        + [ext] * 5,
        compiler_params=params(LONG_VMEM),
        cost_estimate=pl.CostEstimate(
            flops=90 * rows * channels, bytes_accessed=18 * rows * channels, transcendentals=0
        ),
        name="after_exchange",
    )(returned, out_grad, key, value, tail, following, taps, *grads)


def on_device(
    query_heads,
    key_heads,
    value_heads,
    hyena_query,
    hyena_key,
    hyena_value,
    short_filter,
    long_filter,
    output_grad,
):
    rows, channels = query_heads.shape
    groups = long_filter.shape[1]
    n = lax.axis_size("ctx")
    tp = lax.axis_size("tp")
    cpd, gpd = channels // n, groups // n
    position = lax.axis_index("ctx")
    tail = shifted(edge_rows((hyena_query, hyena_key, hyena_value), False), "ctx", 1)
    key_prev = shifted(key_heads, "ctx", 1)
    value_prev = shifted(value_heads, "ctx", 1)
    chunks = 2 if gpd % 4 == 0 else 1
    cpd, gpd = cpd // chunks, gpd // chunks
    send = before_exchange(
        hyena_query, hyena_key, hyena_value, output_grad, tail, short_filter, long_filter, n, chunks
    )
    send, *sources = lax.optimization_barrier((send, output_grad, hyena_key, hyena_value))
    received = lax.all_to_all(send, "ctx", split_axis=0, concat_axis=0, tiled=True)
    following = shifted(edge_rows(sources, True), "ctx", -1)
    returned = []
    for chunk in range(chunks):
        raw = ()
        if chunk + 1 == chunks:
            raw, squares = filter_products(received, cpd, gpd, chunks)
            raw, key_prev, value_prev = lax.optimization_barrier((raw, key_prev, value_prev))
            raw = (raw, total_over(squares, "tp"))
        results = long_convs(received, raw, cpd, gpd, chunk, chunks)
        if chunk == 0:
            results, received, following = lax.optimization_barrier((results, received, following))
        returned.append(lax.all_to_all(results, "ctx", split_axis=0, concat_axis=0, tiled=True))
    attention = attend(query_heads, key_heads, value_heads, key_prev, value_prev, position)
    bound = math.sqrt(rows * n * groups * tp)
    grads = ()
    for chunk in range(chunks):
        if chunk > 0:
            returned[chunk], attention, *grads = lax.optimization_barrier(
                (returned[chunk], attention, *grads)
            )
        grads = after_exchange(
            returned[chunk], output_grad, hyena_key, hyena_value, tail, following, short_filter, groups,
            chunk, chunks, grads, bound,
        )
    return (attention, *grads)


def solution(mesh):
    whole = P("ctx", "tp")
    in_specs = (whole,) * 6 + (P(None, None, "tp"), whole, whole)
    return jax.shard_map(
        on_device, mesh=mesh, in_specs=in_specs, out_specs=(whole,) * 5, check_vma=False
    )
```

```python
import functools
import math

import jax
import jax.numpy as jnp
from jax import lax
from jax.experimental import pallas as pl
from jax.experimental.pallas import tpu as pltpu
from jax.sharding import PartitionSpec as P

HEAD_DIM = 128
LANES = 128
EDGE = 8
F32 = jnp.float32
BF16 = jnp.bfloat16
VMEM_BYTES = 60 * 1024 * 1024
LONG_VMEM = 20 * 1024 * 1024


def params(size=VMEM_BYTES):
    return pltpu.CompilerParams(vmem_limit_bytes=size)


def shifted(block, axis, distance):
    devices = range(lax.axis_size(axis))
    route = [(i - distance, i) for i in devices if i - distance in devices]
    return lax.ppermute(block, axis, route)


def total_over(value, axis):
    size = lax.axis_size(axis)
    distance = 1
    while distance < size:
        value = value + lax.ppermute(value, axis, [(i, i ^ distance) for i in range(size)])
        distance *= 2
    return value


def round_up(value, step):
    return -(-value // step) * step


def reversal(size):
    row = lax.broadcasted_iota(jnp.int32, (size, size), 0)
    col = lax.broadcasted_iota(jnp.int32, (size, size), 1)
    return jnp.where(row + col == size - 1, 1.0, 0.0).astype(BF16)


SCALE = 1.0 / math.sqrt(HEAD_DIM)
NT = (((1,), (1,)), ((), ()))


LOG_LANES = 32


def places_of(width):
    return [slice(head * HEAD_DIM, (head + 1) * HEAD_DIM) for head in range(width // HEAD_DIM)]


def attend_next_kernel(q_ref, k_ref, v_ref, out_ref, logs_ref):
    rows, width = q_ref.shape
    heads = width // HEAD_DIM
    step = pl.program_id(0)
    lane = lax.broadcasted_iota(jnp.int32, (rows, LANES), 1)

    @pl.when(step == 0)
    def _():
        logs_ref[...] = jnp.zeros_like(logs_ref)

    places = places_of(width)
    scores = [
        lax.dot_general(q_ref[:, at], k_ref[:, at], NT, preferred_element_type=F32) * SCALE
        for at in places
    ]
    largest = [jnp.max(score, axis=1, keepdims=True) for score in scores]
    raised = [jnp.exp(score - top) for score, top in zip(scores, largest)]
    totals = [jnp.sum(r, axis=1, keepdims=True) for r in raised]
    weights = [(r * (1.0 / total)).astype(BF16) for r, total in zip(raised, totals)]
    mixed = [
        jnp.dot(weight, v_ref[:, at], preferred_element_type=F32) for weight, at in zip(weights, places)
    ]
    logs = logs_ref[...]
    for head in range(heads):
        log = largest[head] + jnp.log(totals[head])
        logs = jnp.where(lane == step * heads + head, log, logs)
    logs_ref[...] = logs
    first = pl.multiple_of(step * width, LANES)
    out_ref[:, pl.ds(first, width)] = jnp.concatenate([m.astype(BF16) for m in mixed], 1)

    @pl.when(step == pl.num_programs(0) - 1)
    def _():
        upper = logs.astype(BF16).astype(F32)
        middle = (logs - upper).astype(BF16).astype(F32)
        lower = logs - upper - middle
        terms = upper + pltpu.roll(middle, LOG_LANES, 1) + pltpu.roll(lower, 2 * LOG_LANES, 1)
        out_ref[:, out_ref.shape[1] - LANES :] = terms.astype(BF16)


def attend_own_kernel(
    steps, place_ref, q_ref, k_ref, v_ref, part0_ref, part1_ref, log0_ref, log1_ref, out_ref
):
    rows, width = q_ref.shape
    heads = width // HEAD_DIM
    step = pl.program_id(0)
    row = lax.broadcasted_iota(jnp.int32, (rows, rows), 0)
    col = lax.broadcasted_iota(jnp.int32, (rows, rows), 1)
    own_ok = col <= row
    lane = lax.broadcasted_iota(jnp.int32, (rows, LANES), 1)
    has_prev = jnp.broadcast_to(place_ref[0], (rows, 1)) > 0
    late = step >= steps
    places = places_of(width)
    terms = jnp.where(late, log1_ref[...].astype(F32), log0_ref[...].astype(F32))
    first = jnp.where(late, step - steps, step) * heads
    scores = [
        lax.dot_general(q_ref[:, at], k_ref[:, at], NT, preferred_element_type=F32) * SCALE
        for at in places
    ]
    scores = [jnp.where(own_ok, score, -jnp.inf) for score in scores]
    logs = [
        jnp.sum(
            jnp.where((lane & (LOG_LANES - 1)) == first + head, terms, 0.0), axis=1, keepdims=True
        )
        for head in range(heads)
    ]
    logs = [jnp.where(has_prev, log, -jnp.inf) for log in logs]
    largest = [
        jnp.maximum(jnp.max(score, axis=1, keepdims=True), log) for score, log in zip(scores, logs)
    ]
    raised = [jnp.exp(score - top) for score, top in zip(scores, largest)]
    prevs = [jnp.exp(log - top) for log, top in zip(logs, largest)]
    inverses = [
        1.0 / (jnp.sum(r, axis=1, keepdims=True) + prev) for r, prev in zip(raised, prevs)
    ]
    weights = [(r * inverse).astype(BF16) for r, inverse in zip(raised, inverses)]
    mixed = [
        jnp.dot(weight, v_ref[:, at], preferred_element_type=F32) for weight, at in zip(weights, places)
    ]
    for head, at in enumerate(places):
        part = jnp.where(late, part1_ref[:, at].astype(F32), part0_ref[:, at].astype(F32))
        total = mixed[head] + (prevs[head] * inverses[head]) * part
        out_ref[:, at] = total.astype(BF16)


def attend_cost(rows, channels):
    heads = channels // HEAD_DIM
    return pl.CostEstimate(
        flops=4 * heads * rows * rows * HEAD_DIM,
        bytes_accessed=10 * rows * channels,
        transcendentals=heads * rows * rows,
    )


def attend_next(query, key, value, part):
    rows, channels = query.shape
    tile = min(512, channels)
    steps = channels // tile
    there = pl.BlockSpec((rows, tile), lambda i: (0, part * steps + i))
    return pl.pallas_call(
        attend_next_kernel,
        grid=(steps,),
        in_specs=[pl.BlockSpec((rows, tile), lambda i: (0, i)), there, there],
        out_specs=pl.BlockSpec((rows, channels + LANES), lambda i: (0, 0)),
        out_shape=jax.ShapeDtypeStruct((rows, channels + LANES), BF16),
        scratch_shapes=[pltpu.VMEM((rows, LANES), F32)],
        compiler_params=params(),
        cost_estimate=attend_cost(rows, channels),
        name="attend_next",
    )(query, key, value)


def attend_own(query, key, value, parts, position):
    rows, channels = query.shape
    tile = min(512, channels // 2)
    steps = channels // 2 // tile
    block = pl.BlockSpec((rows, tile), lambda i: (0, i))
    log_at = channels // 2 // LANES
    log = pl.BlockSpec((rows, LANES), lambda i: (0, log_at))
    return pl.pallas_call(
        functools.partial(attend_own_kernel, steps),
        grid=(2 * steps,),
        in_specs=[
            pl.BlockSpec(memory_space=pltpu.SMEM),
            block,
            block,
            block,
            pl.BlockSpec((rows, tile), lambda i: (0, jnp.minimum(i, steps - 1))),
            pl.BlockSpec((rows, tile), lambda i: (0, jnp.maximum(i - steps, 0))),
            log,
            log,
        ],
        out_specs=block,
        out_shape=jax.ShapeDtypeStruct((rows, channels), BF16),
        compiler_params=params(),
        cost_estimate=attend_cost(rows, channels),
        name="attend_own",
    )(position.astype(jnp.int32).reshape(1), query, key, value, *parts, *parts)


def edge_kernel(first, *refs):
    *sources, out_ref = refs
    parts = [r[...].astype(F32) for r in sources]
    parts = [p[:EDGE] if first else p[p.shape[0] - EDGE :] for p in parts]
    out_ref[...] = jnp.concatenate(parts, 0).astype(BF16)


def edge_rows(arrays, first):
    rows, channels = arrays[0].shape
    block = pl.BlockSpec((16, channels), lambda i: (0 if first else rows // 16 - 1, 0))
    return pl.pallas_call(
        functools.partial(edge_kernel, first),
        grid=(1,),
        in_specs=[block] * len(arrays),
        out_specs=pl.BlockSpec((len(arrays) * EDGE, channels), lambda i: (0, 0)),
        out_shape=jax.ShapeDtypeStruct((len(arrays) * EDGE, channels), BF16),
        compiler_params=params(),
        name="edge_rows",
    )(*arrays)


def taps_causal(ext_ref, befores, signals, filters):
    rows = signals[0].shape[0]
    for j, signal in enumerate(signals):
        ext_ref[j, 0:EDGE, :] = befores[j]
        ext_ref[j, EDGE : EDGE + rows, :] = signal
    totals = [taps[0:1] * signal for signal, taps in zip(signals, filters)]
    for s in range(1, filters[0].shape[0]):
        for j, taps in enumerate(filters):
            totals[j] = totals[j] + taps[s : s + 1] * ext_ref[j, EDGE - s : EDGE - s + rows, :]
    return totals


def columns_of(width):
    return [slice(j * LANES, (j + 1) * LANES) for j in range(width // LANES)]


def before_kernel(
    cpd, gpd, q_ref, k_ref, v_ref, og_ref, tail_ref, taps_ref, long_ref, send_ref,
    long_rows, ext_q, ext_k, ext_v,
):
    step = pl.program_id(0)
    groups = long_ref.shape[1]
    per_tile, _, rows = send_ref.shape

    @pl.when(step == 0)
    def _():
        long_rows[...] = jnp.zeros_like(long_rows)
        long_rows[0:groups, :] = long_ref[...].T

    turn = reversal(rows)
    places = columns_of(q_ref.shape[1])
    tails = [tail_ref[:, at].astype(F32) for at in places]

    def short(which, ref, ext):
        return taps_causal(
            ext,
            [tail[which * EDGE : (which + 1) * EDGE] for tail in tails],
            [ref[:, at].astype(F32) for at in places],
            [taps_ref[which, :, at] for at in places],
        )

    short_k, short_v = short(1, k_ref, ext_k), short(2, v_ref, ext_v)
    mixed = [(k * v).T.astype(BF16) for k, v in zip(short_k, short_v)]
    short_q = short(0, q_ref, ext_q)
    delta = [(og_ref[:, at].astype(F32) * q).T.astype(BF16) for q, at in zip(short_q, places)]
    delta = [jnp.dot(d, turn, preferred_element_type=F32).astype(BF16) for d in delta]
    width = min(cpd, LANES)
    for j in range(len(places)):
        for piece in range(LANES // width):
            channel = j * LANES + piece * width
            dest, low = channel // cpd, channel % cpd
            rows_at = slice(piece * width, (piece + 1) * width)
            send_ref[dest, low : low + width, :] = mixed[j][rows_at]
            send_ref[dest, cpd + low : cpd + low + width, :] = delta[j][rows_at]
    filter_rows = send_ref.shape[1] - 2 * cpd
    for dest in range(per_tile):
        first = (step * per_tile + dest) * gpd
        send_ref[dest, 2 * cpd :, :] = long_rows[pl.ds(first, filter_rows), :].astype(BF16)


def before_exchange(query, key, value, out_grad, tail, taps, long_filter, n, chunks):
    rows, channels = query.shape
    groups = long_filter.shape[1]
    cpd, gpd = channels // (n * chunks), groups // (n * chunks)
    tile = min(channels // chunks, max(512, cpd))
    per_tile = tile // cpd
    filter_rows = round_up(gpd, 16)
    send_rows = 2 * cpd + filter_rows
    steps = n // per_tile
    block = pl.BlockSpec((rows, tile), lambda i: (0, i))
    ext = pltpu.VMEM((tile // LANES, rows + EDGE, LANES), F32)
    return pl.pallas_call(
        functools.partial(before_kernel, cpd, gpd),
        grid=(channels // tile,),
        in_specs=[block] * 4
        + [
            pl.BlockSpec((3 * EDGE, tile), lambda i: (0, i)),
            pl.BlockSpec((3, taps.shape[1], tile), lambda i: (0, 0, i)),
            pl.BlockSpec((rows, groups), lambda i: (0, 0)),
        ],
        out_specs=pl.BlockSpec((per_tile, send_rows, rows), lambda i: (i % steps, i // steps, 0)),
        out_shape=jax.ShapeDtypeStruct((n, chunks * send_rows, rows), BF16),
        scratch_shapes=[pltpu.VMEM((round_up(groups, 8) + filter_rows, rows), F32), ext, ext, ext],
        compiler_params=params(),
        cost_estimate=pl.CostEstimate(
            flops=50 * rows * channels, bytes_accessed=12 * rows * channels, transcendentals=0
        ),
        name="before_exchange",
    )(query, key, value, out_grad, tail, taps, long_filter)


def conv_kernel(cpd, gpd, in_ref, *refs):
    *raw_ref, out_ref, taps, wide = refs
    upper = lower = 0.0
    if raw_ref:
        *raw_ref, squares_ref = raw_ref
        upper = squares_ref[...].astype(BF16).astype(F32)
        lower = squares_ref[...] - upper
    n, send_rows, rows = in_ref.shape
    gw = cpd // gpd
    span = n * rows
    filter_rows = send_rows - 2 * cpd
    taps[:, 0:rows] = jnp.zeros((filter_rows, rows), F32)
    for a in range(n):
        taps[:, (a + 1) * rows : (a + 2) * rows] = in_ref[a, 2 * cpd :, :].astype(F32)
    for slot in range(2):
        wide[slot, :, 0:rows] = jnp.zeros((rows, rows), BF16)

    def body(i, carry):
        slots = range(2)
        firsts = [pl.multiple_of((2 * i + slot) * gw, gw) for slot in slots]
        seconds = [pl.multiple_of(cpd + (2 * i + slot) * gw, gw) for slot in slots]
        bases = []
        for slot in slots:
            line = jnp.broadcast_to(taps[pl.ds(2 * i + slot, 1), :], (16, span + rows))
            bases.append(pltpu.roll(line, 0, 1, stride=1, stride_axis=0).astype(BF16))
        for m in range(rows // 16):
            for slot in slots:
                moved = bases[slot] if m == 0 else pltpu.roll(bases[slot], 16 * m, 1)
                wide[slot, 16 * m : 16 * m + 16, rows:] = moved[:, rows:]
        stacks = []
        for slot in slots:
            x = in_ref[:, pl.ds(firsts[slot], gw), :]
            d = in_ref[:, pl.ds(seconds[slot], gw), :]
            both = [jnp.concatenate([x[a], d[n - 1 - a]], 0) for a in range(n)]
            stacks.append(
                jnp.concatenate(
                    [jnp.concatenate([both[a], both[a + 1]], 1) for a in range(0, n, 2)], 0
                )
            )
        totals = [None, None]
        for k in range(n // 2):
            skip = 2 * gw * k
            low = 2 * rows * k
            for slot in slots:
                tile = jnp.concatenate(
                    [wide[slot, :, low + rows : low + 3 * rows], wide[slot, :, low : low + 2 * rows]], 0
                )
                part = jnp.dot(stacks[slot][: n * gw - skip], tile, preferred_element_type=F32)
                total = totals[slot]
                totals[slot] = (
                    part if k == 0 else jnp.concatenate([total[:skip], total[skip:] + part], 0)
                )
        for slot in slots:
            total = totals[slot]
            for a in range(n):
                at = slice(a % 2 * rows, (a % 2 + 1) * rows)
                top = a // 2 * 2 * gw
                out_ref[a, pl.ds(firsts[slot], gw), :] = total[top : top + gw, at].astype(BF16)
                out_ref[n - 1 - a, pl.ds(seconds[slot], gw), :] = total[
                    top + gw : top + 2 * gw, at
                ].astype(BF16)
        return carry

    lax.fori_loop(0, gpd // 2, body, 0)
    halo_at = 2 * cpd
    row = lax.broadcasted_iota(jnp.int32, (2 * EDGE, 2 * rows), 0)
    lane = lax.broadcasted_iota(jnp.int32, (2 * EDGE, 2 * rows), 1)
    wanted = jnp.where(row < EDGE, row, 2 * rows - 1 + EDGE - row)
    pick = jnp.where(lane == wanted, 1.0, 0.0).astype(BF16)
    row_out = lax.broadcasted_iota(jnp.int32, (2 * EDGE, rows), 0)
    for a in range(n):
        if a + 1 < n:
            results = jnp.concatenate([out_ref[a + 1, 0:cpd, :], out_ref[a + 1, cpd : 2 * cpd, :]], 1)
            halo = lax.dot_general(
                pick, results, (((1,), (1,)), ((), ())), preferred_element_type=F32
            )
            if cpd < LANES:
                halo = jnp.concatenate([halo, jnp.zeros((2 * EDGE, LANES - cpd), F32)], 1)
        else:
            halo = jnp.zeros((2 * EDGE, max(cpd, LANES)), F32)
        for j in range(halo.shape[1] // LANES):
            at = halo_at + 2 * EDGE * j
            tile = halo[:, j * LANES : (j + 1) * LANES]
            tile = jnp.where(row_out == EDGE - 2, upper, jnp.where(row_out == EDGE - 1, lower, tile))
            out_ref[a, at : at + 2 * EDGE, :] = tile.astype(BF16)
    for ref in raw_ref:
        out_ref[:, out_ref.shape[1] - ref.shape[1] :, :] = ref[...]


def long_convs(received, raw, cpd, gpd, chunk, chunks):
    n, send_rows, rows = received.shape
    send_rows = send_rows // chunks
    filter_rows = send_rows - 2 * cpd
    out_rows = 2 * cpd + 2 * EDGE * max(1, cpd // LANES) + sum(r.shape[1] for r in raw[:1])
    span = n * rows
    return pl.pallas_call(
        functools.partial(conv_kernel, cpd, gpd),
        grid=(1,),
        in_specs=[pl.BlockSpec((n, send_rows, rows), lambda i: (0, chunk, 0))]
        + [pl.BlockSpec(r.shape, lambda i, r=r: (0,) * r.ndim) for r in raw],
        out_specs=pl.BlockSpec((n, out_rows, rows), lambda i: (0, 0, 0)),
        out_shape=jax.ShapeDtypeStruct((n, out_rows, rows), BF16),
        scratch_shapes=[
            pltpu.VMEM((filter_rows, span + rows), F32),
            pltpu.VMEM((2, rows, span + rows), BF16),
        ],
        compiler_params=params(LONG_VMEM),
        cost_estimate=pl.CostEstimate(
            flops=4 * cpd * span * span, bytes_accessed=4 * n * out_rows * rows, transcendentals=0
        ),
        name="long_convs",
    )(received, *raw)


def gram_kernel(cpd, gpd, chunks, in_ref, out_ref, squares_ref, gram, raw):
    n, send_rows, rows = in_ref.shape
    send_rows = send_rows // chunks
    gw = cpd // gpd
    span = n * rows
    for slot in range(2):
        gram[slot, :, span:] = jnp.zeros((rows, rows), F32)
    if gpd * chunks < raw.shape[0]:
        raw[...] = jnp.zeros_like(raw)
    no_rows = jnp.zeros((n * gw, rows), BF16)

    def offset(d, k):
        held = (k + 1) * gw
        if held == n * gw:
            return d
        return jnp.concatenate([d[n * gw - held :], no_rows[held:]], 0)

    squares = jnp.zeros((1, span), F32)
    for chunk in range(chunks):
        base = chunk * send_rows

        def body(i, squares, chunk=chunk, base=base):
            slots = range(2)
            turned, shifting = [], []
            for slot in slots:
                first = pl.multiple_of(base + (2 * i + slot) * gw, gw)
                second = pl.multiple_of(base + cpd + (2 * i + slot) * gw, gw)
                x = in_ref[:, pl.ds(first, gw), :].reshape(n * gw, rows)
                shifting.append(in_ref[:, pl.ds(second, gw), :].reshape(n * gw, rows))
                turned.append(x.astype(F32).T.astype(BF16))
            for k in range(0, n, 2):
                for slot in slots:
                    d = shifting[slot]
                    pairs = jnp.concatenate([offset(d, k), offset(d, k + 1)], 1)
                    gram[slot, :, k * rows : (k + 2) * rows] = jnp.dot(
                        turned[slot], pairs, preferred_element_type=F32
                    )
            sums = [gram[slot, 0:8, :] for slot in slots]
            for m in range(1, rows // 8):
                for slot in slots:
                    block = gram[slot, 8 * m : 8 * m + 8, :]
                    sums[slot] = sums[slot] + pltpu.roll(block, 8 * m, 1)
            sums = [pltpu.roll(total, 0, 1, stride=1, stride_axis=0) for total in sums]
            for slot in slots:
                line = jnp.sum(sums[slot], axis=0, keepdims=True)[:, :span]
                raw[pl.ds(chunk * gpd + 2 * i + slot, 1), :] = line
                squares = squares + line * line
            return squares

        squares = lax.fori_loop(0, gpd // 2, body, squares)
    squares_ref[...] = jnp.sum(squares, axis=1, keepdims=True)
    turn = reversal(rows)
    for a in range(n):
        tile = raw[:, (n - 1 - a) * rows : (n - a) * rows].astype(BF16)
        out_ref[a] = jnp.dot(tile, turn, preferred_element_type=F32).astype(BF16)


def filter_products(received, cpd, gpd, chunks):
    n, _, rows = received.shape
    span = n * rows
    raw_rows = round_up(gpd * chunks, 16)
    return pl.pallas_call(
        functools.partial(gram_kernel, cpd, gpd, chunks),
        in_specs=[pl.BlockSpec(memory_space=pltpu.VMEM)],
        out_specs=[pl.BlockSpec(memory_space=pltpu.VMEM)] * 2,
        out_shape=[
            jax.ShapeDtypeStruct((n, raw_rows, rows), BF16),
            jax.ShapeDtypeStruct((1, 1), F32),
        ],
        scratch_shapes=[
            pltpu.VMEM((2, rows, span + rows), F32),
            pltpu.VMEM((raw_rows, span), F32),
        ],
        compiler_params=params(LONG_VMEM),
        cost_estimate=pl.CostEstimate(
            flops=2 * cpd * chunks * span * span,
            bytes_accessed=2 * received.size,
            transcendentals=0,
        ),
        name="filter_products",
    )(received)


def taps_anti(ext_ref, signals, afters, filters):
    rows = signals[0].shape[0]
    for j, signal in enumerate(signals):
        ext_ref[j, 0:rows, :] = signal
        ext_ref[j, rows : rows + EDGE, :] = afters[j]
    totals = [taps[0:1] * signal for signal, taps in zip(signals, filters)]
    for s in range(1, filters[0].shape[0]):
        for j, taps in enumerate(filters):
            totals[j] = totals[j] + taps[s : s + 1] * ext_ref[j, s : s + rows, :]
    return totals


def short_edge(before, signal, filter_taps):
    both = jnp.concatenate([before, signal], 0)
    total = filter_taps[0:1] * signal
    for s in range(1, filter_taps.shape[0]):
        total = total + filter_taps[s : s + 1] * both[EDGE - s : 2 * EDGE - s]
    return total


def after_kernel(
    cpd, gpd, chunks, last, bound, in_ref, og_ref, k_ref, v_ref, tail_ref, next_ref, taps_ref, *refs
):
    *refs, ext_q, ext_k, ext_v, ext_in_k, ext_in_v = refs
    if last:
        *refs, raw_ref, raw_rows, total_ref = refs
    dq_ref, dk_ref, dv_ref = refs[-3:]
    step = pl.program_id(0)
    per_tile, in_rows, rows = in_ref.shape
    halo_rows = 2 * EDGE * max(1, cpd // LANES)
    halo_at = 2 * cpd
    turn = reversal(rows)
    places = columns_of(og_ref.shape[1])
    tails = [tail_ref[:, at].astype(F32) for at in places]
    nexts = [next_ref[:, at].astype(F32) for at in places]
    convs, backs, halos = [], [], []
    for j in range(len(places)):
        if cpd >= LANES:
            dest, low = j * LANES // cpd, j * LANES % cpd
            conv = in_ref[dest, low : low + LANES, :]
            back = in_ref[dest, cpd + low : cpd + low + LANES, :]
            edge = halo_at + 2 * EDGE * (low // LANES)
            halo = in_ref[dest, edge : edge + 2 * EDGE, :].astype(F32)
        else:
            dests = range(j * LANES // cpd, (j + 1) * LANES // cpd)
            conv = jnp.concatenate([in_ref[d, 0:cpd, :] for d in dests], 0)
            back = jnp.concatenate([in_ref[d, cpd : 2 * cpd, :] for d in dests], 0)
            halo = jnp.concatenate(
                [in_ref[d, halo_at : halo_at + halo_rows, :].astype(F32)[:, :cpd] for d in dests], 1
            )
        convs.append(conv)
        backs.append(back)
        halos.append(halo)
    convs = [conv.astype(F32).T for conv in convs]
    backs = [jnp.dot(back, turn, preferred_element_type=F32) for back in backs]
    backs = [back.T for back in backs]
    taps = [[taps_ref[which, :, at] for at in places] for which in range(3)]
    keys = [k_ref[:, at].astype(F32) for at in places]
    values = [v_ref[:, at].astype(F32) for at in places]
    short_k = taps_causal(ext_in_k, [tail[EDGE : 2 * EDGE] for tail in tails], keys, taps[1])
    short_v = taps_causal(ext_in_v, [tail[2 * EDGE : 3 * EDGE] for tail in tails], values, taps[2])
    next_k = [
        short_edge(k[rows - EDGE :], f[EDGE : 2 * EDGE], t) for k, f, t in zip(keys, nexts, taps[1])
    ]
    next_v = [
        short_edge(v[rows - EDGE :], f[2 * EDGE : 3 * EDGE], t)
        for v, f, t in zip(values, nexts, taps[2])
    ]

    def store(ref, ext, signals, afters, filters):
        for at, total in zip(places, taps_anti(ext, signals, afters, filters)):
            ref[:, at] = total.astype(BF16)

    store(
        dq_ref,
        ext_q,
        [og_ref[:, at].astype(F32) * conv for at, conv in zip(places, convs)],
        [f[0:EDGE] * halo[0:EDGE] for f, halo in zip(nexts, halos)],
        taps[0],
    )
    store(
        dk_ref,
        ext_k,
        [back * v for back, v in zip(backs, short_v)],
        [halo[EDGE:] * v for halo, v in zip(halos, next_v)],
        taps[1],
    )
    store(
        dv_ref,
        ext_v,
        [back * k for back, k in zip(backs, short_k)],
        [halo[EDGE:] * k for halo, k in zip(halos, next_k)],
        taps[2],
    )
    if not last:
        return
    squares = jnp.zeros((1, LANES), F32)
    for dest in range(per_tile):
        parts = in_ref[dest, halo_at : halo_at + 2 * EDGE, :].astype(F32)
        squares = squares + parts[EDGE - 2 : EDGE - 1] + parts[EDGE - 1 : EDGE]

    @pl.when(step == 0)
    def _():
        total_ref[...] = jnp.zeros_like(total_ref)

    total_ref[...] = total_ref[...] + squares
    half = raw_rows.shape[0] // chunks
    for dest in range(per_tile):
        lines = in_ref[dest, halo_at + halo_rows :, :].astype(F32)
        for chunk in range(chunks):
            at = chunk * half + (step * per_tile + dest) * gpd
            raw_rows[pl.ds(at, gpd), :] = lines[chunk * gpd : (chunk + 1) * gpd]

    @pl.when(step == pl.num_programs(0) - 1)
    def _():
        factor = jnp.minimum(1.0, bound / jnp.sqrt(total_ref[...]))[:, 0:1]
        raw_ref[...] = raw_rows[...].T * factor


def after_exchange(
    returned, out_grad, key, value, tail, following, taps, groups, chunk, chunks, grads, bound
):
    n, in_rows, rows = returned.shape
    channels = out_grad.shape[1] // chunks
    cpd, gpd = channels // n, groups // (n * chunks)
    last = chunk + 1 == chunks
    tile = min(channels, max(512, cpd))
    per_tile = tile // cpd
    first = chunk * channels // tile
    block = pl.BlockSpec((rows, tile), lambda i: (0, first + i))
    ext = pltpu.VMEM((tile // LANES, rows + EDGE, LANES), F32)
    grad = jax.ShapeDtypeStruct(out_grad.shape, BF16)
    return pl.pallas_call(
        functools.partial(after_kernel, cpd, gpd, chunks, last, bound),
        grid=(channels // tile,),
        in_specs=[
            pl.BlockSpec((per_tile, in_rows, rows), lambda i: (i, 0, 0)),
            block,
            block,
            block,
            pl.BlockSpec((3 * EDGE, tile), lambda i: (0, first + i)),
            pl.BlockSpec((3 * EDGE, tile), lambda i: (0, first + i)),
            pl.BlockSpec((3, taps.shape[1], tile), lambda i: (0, 0, first + i)),
        ]
        + [pl.BlockSpec(memory_space=pl.ANY)] * len(grads),
        input_output_aliases={7 + i: i for i in range(len(grads))},
        out_specs=[block] * 3 + [pl.BlockSpec((rows, groups), lambda i: (0, 0))] * last,
        out_shape=[grad] * 3 + [jax.ShapeDtypeStruct((rows, groups), F32)] * last,
        scratch_shapes=[pltpu.VMEM((groups, rows), F32), pltpu.VMEM((1, LANES), F32)] * last
        + [ext] * 5,
        compiler_params=params(),
        cost_estimate=pl.CostEstimate(
            flops=90 * rows * channels, bytes_accessed=18 * rows * channels, transcendentals=0
        ),
        name="after_exchange",
    )(returned, out_grad, key, value, tail, following, taps, *grads)


def on_device(
    query_heads,
    key_heads,
    value_heads,
    hyena_query,
    hyena_key,
    hyena_value,
    short_filter,
    long_filter,
    output_grad,
):
    rows, channels = query_heads.shape
    groups = long_filter.shape[1]
    n = lax.axis_size("ctx")
    tp = lax.axis_size("tp")
    cpd, gpd = channels // n, groups // n
    position = lax.axis_index("ctx")
    tail = shifted(edge_rows((hyena_query, hyena_key, hyena_value), False), "ctx", 1)
    half = channels // 2
    early, tail = lax.optimization_barrier((query_heads[:, :half], tail))
    early = shifted(early, "ctx", -1)
    chunks = 2 if gpd % 4 == 0 else 1
    cpd, gpd = cpd // chunks, gpd // chunks
    send = before_exchange(
        hyena_query, hyena_key, hyena_value, output_grad, tail, short_filter, long_filter, n, chunks
    )
    send, early, late, *sources = lax.optimization_barrier(
        (send, early, query_heads[:, half:], output_grad, hyena_key, hyena_value)
    )
    received = lax.all_to_all(send, "ctx", split_axis=0, concat_axis=0, tiled=True)
    following = shifted(edge_rows(sources, True), "ctx", -1)
    late = shifted(late, "ctx", -1)
    parts = [shifted(attend_next(early, key_heads, value_heads, 0), "ctx", 1)]
    returned = []
    for chunk in range(chunks):
        raw = ()
        if chunk + 1 == chunks:
            raw, squares = filter_products(received, cpd, gpd, chunks)
            raw = (raw, total_over(squares, "tp"))
        results = long_convs(received, raw, cpd, gpd, chunk, chunks)
        if chunk == 0:
            results, received, following, late, parts[0] = lax.optimization_barrier(
                (results, received, following, late, parts[0])
            )
            parts.append(shifted(attend_next(late, key_heads, value_heads, 1), "ctx", 1))
        else:
            results, parts[1] = lax.optimization_barrier((results, parts[1]))
        returned.append(lax.all_to_all(results, "ctx", split_axis=0, concat_axis=0, tiled=True))
    attention = attend_own(query_heads, key_heads, value_heads, parts, position)
    bound = math.sqrt(rows * n * groups * tp)
    grads = ()
    for chunk in range(chunks):
        if chunk > 0:
            returned[chunk], attention, *grads = lax.optimization_barrier(
                (returned[chunk], attention, *grads)
            )
        grads = after_exchange(
            returned[chunk], output_grad, hyena_key, hyena_value, tail, following, short_filter, groups,
            chunk, chunks, grads, bound,
        )
    return (attention, *grads)


def solution(mesh):
    whole = P("ctx", "tp")
    in_specs = (whole,) * 6 + (P(None, None, "tp"), whole, whole)
    return jax.shard_map(
        on_device, mesh=mesh, in_specs=in_specs, out_specs=(whole,) * 5, check_vma=False
    )
```

```python
import functools
import math

import jax
import jax.numpy as jnp
from jax import lax
from jax.experimental import pallas as pl
from jax.experimental.pallas import tpu as pltpu
from jax.sharding import PartitionSpec as P

HEAD_DIM = 128
LANES = 128
EDGE = 8
F32 = jnp.float32
BF16 = jnp.bfloat16
VMEM_BYTES = 60 * 1024 * 1024
LONG_VMEM = 20 * 1024 * 1024


def params(size=VMEM_BYTES):
    return pltpu.CompilerParams(vmem_limit_bytes=size)


def shifted(block, axis, distance):
    devices = range(lax.axis_size(axis))
    route = [(i - distance, i) for i in devices if i - distance in devices]
    return lax.ppermute(block, axis, route)


def total_over(value, axis):
    size = lax.axis_size(axis)
    distance = 1
    while distance < size:
        value = value + lax.ppermute(value, axis, [(i, i ^ distance) for i in range(size)])
        distance *= 2
    return value


def round_up(value, step):
    return -(-value // step) * step


def reversal(size):
    row = lax.broadcasted_iota(jnp.int32, (size, size), 0)
    col = lax.broadcasted_iota(jnp.int32, (size, size), 1)
    return jnp.where(row + col == size - 1, 1.0, 0.0).astype(BF16)


SCALE = 1.0 / math.sqrt(HEAD_DIM)
NT = (((1,), (1,)), ((), ()))


LOG_LANES = 32


def places_of(width):
    return [slice(head * HEAD_DIM, (head + 1) * HEAD_DIM) for head in range(width // HEAD_DIM)]


def attend_next_kernel(q_ref, k_ref, v_ref, out_ref, logs_ref):
    rows, width = q_ref.shape
    heads = width // HEAD_DIM
    step = pl.program_id(0)
    lane = lax.broadcasted_iota(jnp.int32, (rows, LANES), 1)

    @pl.when(step == 0)
    def _():
        logs_ref[...] = jnp.zeros_like(logs_ref)

    places = places_of(width)
    scores = [
        lax.dot_general(q_ref[:, at], k_ref[:, at], NT, preferred_element_type=F32) * SCALE
        for at in places
    ]
    largest = [jnp.max(score, axis=1, keepdims=True) for score in scores]
    raised = [jnp.exp(score - top) for score, top in zip(scores, largest)]
    totals = [jnp.sum(r, axis=1, keepdims=True) for r in raised]
    weights = [(r * (1.0 / total)).astype(BF16) for r, total in zip(raised, totals)]
    mixed = [
        jnp.dot(weight, v_ref[:, at], preferred_element_type=F32) for weight, at in zip(weights, places)
    ]
    logs = logs_ref[...]
    for head in range(heads):
        log = largest[head] + jnp.log(totals[head])
        logs = jnp.where(lane == step * heads + head, log, logs)
    logs_ref[...] = logs
    first = pl.multiple_of(step * width, LANES)
    out_ref[:, pl.ds(first, width)] = jnp.concatenate([m.astype(BF16) for m in mixed], 1)

    @pl.when(step == pl.num_programs(0) - 1)
    def _():
        upper = logs.astype(BF16).astype(F32)
        middle = (logs - upper).astype(BF16).astype(F32)
        lower = logs - upper - middle
        terms = upper + pltpu.roll(middle, LOG_LANES, 1) + pltpu.roll(lower, 2 * LOG_LANES, 1)
        out_ref[:, out_ref.shape[1] - LANES :] = terms.astype(BF16)


def attend_merge_kernel(place_ref, q_ref, k_ref, v_ref, part_ref, log_ref, _, out_ref):
    rows, width = q_ref.shape
    heads = width // HEAD_DIM
    step = pl.program_id(0)
    row = lax.broadcasted_iota(jnp.int32, (rows, rows), 0)
    col = lax.broadcasted_iota(jnp.int32, (rows, rows), 1)
    own_ok = col <= row
    lane = lax.broadcasted_iota(jnp.int32, (rows, LANES), 1) & (LOG_LANES - 1)
    has_prev = jnp.broadcast_to(place_ref[0], (rows, 1)) > 0
    places = places_of(width)
    terms = log_ref[...].astype(F32)
    scores = [
        lax.dot_general(q_ref[:, at], k_ref[:, at], NT, preferred_element_type=F32) * SCALE
        for at in places
    ]
    scores = [jnp.where(own_ok, score, -jnp.inf) for score in scores]
    logs = [
        jnp.sum(jnp.where(lane == step * heads + head, terms, 0.0), axis=1, keepdims=True)
        for head in range(heads)
    ]
    logs = [jnp.where(has_prev, log, -jnp.inf) for log in logs]
    largest = [
        jnp.maximum(jnp.max(score, axis=1, keepdims=True), log) for score, log in zip(scores, logs)
    ]
    raised = [jnp.exp(score - top) for score, top in zip(scores, largest)]
    prevs = [jnp.exp(log - top) for log, top in zip(logs, largest)]
    inverses = [
        1.0 / (jnp.sum(r, axis=1, keepdims=True) + prev) for r, prev in zip(raised, prevs)
    ]
    weights = [(r * inverse).astype(BF16) for r, inverse in zip(raised, inverses)]
    mixed = [
        jnp.dot(weight, v_ref[:, at], preferred_element_type=F32) for weight, at in zip(weights, places)
    ]
    for head, at in enumerate(places):
        total = mixed[head] + (prevs[head] * inverses[head]) * part_ref[:, at].astype(F32)
        out_ref[:, at] = total.astype(BF16)


def attend_whole_kernel(place_ref, q_ref, k_ref, v_ref, kp_ref, vp_ref, out_ref):
    rows, width = q_ref.shape
    row = lax.broadcasted_iota(jnp.int32, (rows, rows), 0)
    col = lax.broadcasted_iota(jnp.int32, (rows, rows), 1)
    own_ok = col <= row
    prev_ok = jnp.broadcast_to(place_ref[0], (rows, rows)) > 0
    places = places_of(width)

    def scores(ref, allowed):
        products = [
            lax.dot_general(q_ref[:, at], ref[:, at], NT, preferred_element_type=F32) for at in places
        ]
        return [jnp.where(allowed, product * SCALE, -jnp.inf) for product in products]

    own, prev = scores(k_ref, own_ok), scores(kp_ref, prev_ok)
    largest = [jnp.max(jnp.maximum(o, p), axis=1, keepdims=True) for o, p in zip(own, prev)]
    own = [jnp.exp(o - top) for o, top in zip(own, largest)]
    prev = [jnp.exp(p - top) for p, top in zip(prev, largest)]
    totals = [jnp.sum(o + p, axis=1, keepdims=True) for o, p in zip(own, prev)]
    inverses = [1.0 / total for total in totals]
    own = [(o * inverse).astype(BF16) for o, inverse in zip(own, inverses)]
    prev = [(p * inverse).astype(BF16) for p, inverse in zip(prev, inverses)]
    mixed = [
        jnp.dot(o, v_ref[:, at], preferred_element_type=F32)
        + jnp.dot(p, vp_ref[:, at], preferred_element_type=F32)
        for o, p, at in zip(own, prev, places)
    ]
    for head, at in enumerate(places):
        out_ref[:, at] = mixed[head].astype(BF16)


def attend_cost(rows, channels):
    heads = channels // HEAD_DIM
    return pl.CostEstimate(
        flops=4 * heads * rows * rows * HEAD_DIM,
        bytes_accessed=10 * rows * channels,
        transcendentals=heads * rows * rows,
    )


def attend_next(query, key, value):
    rows, channels = query.shape
    tile = min(512, channels)
    block = pl.BlockSpec((rows, tile), lambda i: (0, i))
    return pl.pallas_call(
        attend_next_kernel,
        grid=(channels // tile,),
        in_specs=[block] * 3,
        out_specs=pl.BlockSpec((rows, channels + LANES), lambda i: (0, 0)),
        out_shape=jax.ShapeDtypeStruct((rows, channels + LANES), BF16),
        scratch_shapes=[pltpu.VMEM((rows, LANES), F32)],
        compiler_params=params(LONG_VMEM),
        cost_estimate=attend_cost(rows, channels),
        name="attend_next",
    )(query, key, value)


def attend(query, key, value, part, previous, position):
    rows, channels = query.shape
    half = channels // 2
    tile = min(512, half)
    steps = half // tile
    place = position.astype(jnp.int32).reshape(1)
    smem = pl.BlockSpec(memory_space=pltpu.SMEM)
    first = pl.BlockSpec((rows, tile), lambda i: (0, i))
    second = pl.BlockSpec((rows, tile), lambda i: (0, steps + i))
    out = jax.ShapeDtypeStruct((rows, channels), BF16)
    whole = pl.pallas_call(
        attend_whole_kernel,
        grid=(steps,),
        in_specs=[smem, second, second, second, first, pl.BlockSpec((rows, tile), lambda i: (1, i))],
        out_specs=second,
        out_shape=out,
        compiler_params=params(LONG_VMEM),
        cost_estimate=attend_cost(rows, channels),
        name="attend_whole",
    )(place, query, key, value, previous, previous)
    log_at = half // LANES
    return pl.pallas_call(
        attend_merge_kernel,
        grid=(steps,),
        in_specs=[
            smem,
            first,
            first,
            first,
            first,
            pl.BlockSpec((rows, LANES), lambda i: (0, log_at)),
            pl.BlockSpec(memory_space=pl.ANY),
        ],
        out_specs=first,
        out_shape=out,
        input_output_aliases={6: 0},
        compiler_params=params(LONG_VMEM),
        cost_estimate=attend_cost(rows, half),
        name="attend_merge",
    )(place, query, key, value, part, part, whole)


def edge_kernel(first, *refs):
    *sources, out_ref = refs
    parts = [r[...].astype(F32) for r in sources]
    parts = [p[:EDGE] if first else p[p.shape[0] - EDGE :] for p in parts]
    out_ref[...] = jnp.concatenate(parts, 0).astype(BF16)


def edge_rows(arrays, first):
    rows, channels = arrays[0].shape
    block = pl.BlockSpec((16, channels), lambda i: (0 if first else rows // 16 - 1, 0))
    return pl.pallas_call(
        functools.partial(edge_kernel, first),
        grid=(1,),
        in_specs=[block] * len(arrays),
        out_specs=pl.BlockSpec((len(arrays) * EDGE, channels), lambda i: (0, 0)),
        out_shape=jax.ShapeDtypeStruct((len(arrays) * EDGE, channels), BF16),
        compiler_params=params(),
        name="edge_rows",
    )(*arrays)


def taps_causal(ext_ref, befores, signals, filters):
    rows = signals[0].shape[0]
    for j, signal in enumerate(signals):
        ext_ref[j, 0:EDGE, :] = befores[j]
        ext_ref[j, EDGE : EDGE + rows, :] = signal
    totals = [taps[0:1] * signal for signal, taps in zip(signals, filters)]
    for s in range(1, filters[0].shape[0]):
        for j, taps in enumerate(filters):
            totals[j] = totals[j] + taps[s : s + 1] * ext_ref[j, EDGE - s : EDGE - s + rows, :]
    return totals


def columns_of(width):
    return [slice(j * LANES, (j + 1) * LANES) for j in range(width // LANES)]


def before_kernel(
    cpd, gpd, q_ref, k_ref, v_ref, og_ref, tail_ref, taps_ref, long_ref, send_ref,
    long_rows, ext_q, ext_k, ext_v,
):
    step = pl.program_id(0)
    groups = long_ref.shape[1]
    per_tile, _, rows = send_ref.shape

    @pl.when(step == 0)
    def _():
        long_rows[...] = jnp.zeros_like(long_rows)
        long_rows[0:groups, :] = long_ref[...].T

    turn = reversal(rows)
    places = columns_of(q_ref.shape[1])
    tails = [tail_ref[:, at].astype(F32) for at in places]

    def short(which, ref, ext):
        return taps_causal(
            ext,
            [tail[which * EDGE : (which + 1) * EDGE] for tail in tails],
            [ref[:, at].astype(F32) for at in places],
            [taps_ref[which, :, at] for at in places],
        )

    short_k, short_v = short(1, k_ref, ext_k), short(2, v_ref, ext_v)
    mixed = [(k * v).T.astype(BF16) for k, v in zip(short_k, short_v)]
    short_q = short(0, q_ref, ext_q)
    delta = [(og_ref[:, at].astype(F32) * q).T.astype(BF16) for q, at in zip(short_q, places)]
    delta = [jnp.dot(d, turn, preferred_element_type=F32).astype(BF16) for d in delta]
    width = min(cpd, LANES)
    for j in range(len(places)):
        for piece in range(LANES // width):
            channel = j * LANES + piece * width
            dest, low = channel // cpd, channel % cpd
            rows_at = slice(piece * width, (piece + 1) * width)
            send_ref[dest, low : low + width, :] = mixed[j][rows_at]
            send_ref[dest, cpd + low : cpd + low + width, :] = delta[j][rows_at]
    filter_rows = send_ref.shape[1] - 2 * cpd
    for dest in range(per_tile):
        first = (step * per_tile + dest) * gpd
        send_ref[dest, 2 * cpd :, :] = long_rows[pl.ds(first, filter_rows), :].astype(BF16)


def before_exchange(query, key, value, out_grad, tail, taps, long_filter, n, chunks):
    rows, channels = query.shape
    groups = long_filter.shape[1]
    cpd, gpd = channels // (n * chunks), groups // (n * chunks)
    tile = min(channels // chunks, max(512, cpd))
    per_tile = tile // cpd
    filter_rows = round_up(gpd, 16)
    send_rows = 2 * cpd + filter_rows
    steps = n // per_tile
    block = pl.BlockSpec((rows, tile), lambda i: (0, i))
    ext = pltpu.VMEM((tile // LANES, rows + EDGE, LANES), F32)
    return pl.pallas_call(
        functools.partial(before_kernel, cpd, gpd),
        grid=(channels // tile,),
        in_specs=[block] * 4
        + [
            pl.BlockSpec((3 * EDGE, tile), lambda i: (0, i)),
            pl.BlockSpec((3, taps.shape[1], tile), lambda i: (0, 0, i)),
            pl.BlockSpec((rows, groups), lambda i: (0, 0)),
        ],
        out_specs=pl.BlockSpec((per_tile, send_rows, rows), lambda i: (i % steps, i // steps, 0)),
        out_shape=jax.ShapeDtypeStruct((n, chunks * send_rows, rows), BF16),
        scratch_shapes=[pltpu.VMEM((round_up(groups, 8) + filter_rows, rows), F32), ext, ext, ext],
        compiler_params=params(),
        cost_estimate=pl.CostEstimate(
            flops=50 * rows * channels, bytes_accessed=12 * rows * channels, transcendentals=0
        ),
        name="before_exchange",
    )(query, key, value, out_grad, tail, taps, long_filter)


def conv_kernel(cpd, gpd, in_ref, *refs):
    *raw_ref, out_ref, taps, wide = refs
    upper = lower = 0.0
    if raw_ref:
        *raw_ref, squares_ref = raw_ref
        upper = squares_ref[...].astype(BF16).astype(F32)
        lower = squares_ref[...] - upper
    n, send_rows, rows = in_ref.shape
    gw = cpd // gpd
    span = n * rows
    filter_rows = send_rows - 2 * cpd
    taps[:, 0:rows] = jnp.zeros((filter_rows, rows), F32)
    for a in range(n):
        taps[:, (a + 1) * rows : (a + 2) * rows] = in_ref[a, 2 * cpd :, :].astype(F32)
    for slot in range(2):
        wide[slot, :, 0:rows] = jnp.zeros((rows, rows), BF16)

    def body(i, carry):
        slots = range(2)
        firsts = [pl.multiple_of((2 * i + slot) * gw, gw) for slot in slots]
        seconds = [pl.multiple_of(cpd + (2 * i + slot) * gw, gw) for slot in slots]
        bases = []
        for slot in slots:
            line = jnp.broadcast_to(taps[pl.ds(2 * i + slot, 1), :], (16, span + rows))
            bases.append(pltpu.roll(line, 0, 1, stride=1, stride_axis=0).astype(BF16))
        for m in range(rows // 16):
            for slot in slots:
                moved = bases[slot] if m == 0 else pltpu.roll(bases[slot], 16 * m, 1)
                wide[slot, 16 * m : 16 * m + 16, rows:] = moved[:, rows:]
        stacks = []
        for slot in slots:
            x = in_ref[:, pl.ds(firsts[slot], gw), :]
            d = in_ref[:, pl.ds(seconds[slot], gw), :]
            both = [jnp.concatenate([x[a], d[n - 1 - a]], 0) for a in range(n)]
            stacks.append(
                jnp.concatenate(
                    [jnp.concatenate([both[a], both[a + 1]], 1) for a in range(0, n, 2)], 0
                )
            )
        totals = [None, None]
        for k in range(n // 2):
            skip = 2 * gw * k
            low = 2 * rows * k
            for slot in slots:
                tile = jnp.concatenate(
                    [wide[slot, :, low + rows : low + 3 * rows], wide[slot, :, low : low + 2 * rows]], 0
                )
                part = jnp.dot(stacks[slot][: n * gw - skip], tile, preferred_element_type=F32)
                total = totals[slot]
                totals[slot] = (
                    part if k == 0 else jnp.concatenate([total[:skip], total[skip:] + part], 0)
                )
        for slot in slots:
            total = totals[slot]
            for a in range(n):
                at = slice(a % 2 * rows, (a % 2 + 1) * rows)
                top = a // 2 * 2 * gw
                out_ref[a, pl.ds(firsts[slot], gw), :] = total[top : top + gw, at].astype(BF16)
                out_ref[n - 1 - a, pl.ds(seconds[slot], gw), :] = total[
                    top + gw : top + 2 * gw, at
                ].astype(BF16)
        return carry

    lax.fori_loop(0, gpd // 2, body, 0)
    halo_at = 2 * cpd
    row = lax.broadcasted_iota(jnp.int32, (2 * EDGE, 2 * rows), 0)
    lane = lax.broadcasted_iota(jnp.int32, (2 * EDGE, 2 * rows), 1)
    wanted = jnp.where(row < EDGE, row, 2 * rows - 1 + EDGE - row)
    pick = jnp.where(lane == wanted, 1.0, 0.0).astype(BF16)
    row_out = lax.broadcasted_iota(jnp.int32, (2 * EDGE, rows), 0)
    for a in range(n):
        if a + 1 < n:
            results = jnp.concatenate([out_ref[a + 1, 0:cpd, :], out_ref[a + 1, cpd : 2 * cpd, :]], 1)
            halo = lax.dot_general(
                pick, results, (((1,), (1,)), ((), ())), preferred_element_type=F32
            )
            if cpd < LANES:
                halo = jnp.concatenate([halo, jnp.zeros((2 * EDGE, LANES - cpd), F32)], 1)
        else:
            halo = jnp.zeros((2 * EDGE, max(cpd, LANES)), F32)
        for j in range(halo.shape[1] // LANES):
            at = halo_at + 2 * EDGE * j
            tile = halo[:, j * LANES : (j + 1) * LANES]
            tile = jnp.where(row_out == EDGE - 2, upper, jnp.where(row_out == EDGE - 1, lower, tile))
            out_ref[a, at : at + 2 * EDGE, :] = tile.astype(BF16)
    for ref in raw_ref:
        out_ref[:, out_ref.shape[1] - ref.shape[1] :, :] = ref[...]


def long_convs(received, raw, cpd, gpd, chunk, chunks):
    n, send_rows, rows = received.shape
    send_rows = send_rows // chunks
    filter_rows = send_rows - 2 * cpd
    out_rows = 2 * cpd + 2 * EDGE * max(1, cpd // LANES) + sum(r.shape[1] for r in raw[:1])
    span = n * rows
    return pl.pallas_call(
        functools.partial(conv_kernel, cpd, gpd),
        grid=(1,),
        in_specs=[pl.BlockSpec((n, send_rows, rows), lambda i: (0, chunk, 0))]
        + [pl.BlockSpec(r.shape, lambda i, r=r: (0,) * r.ndim) for r in raw],
        out_specs=pl.BlockSpec((n, out_rows, rows), lambda i: (0, 0, 0)),
        out_shape=jax.ShapeDtypeStruct((n, out_rows, rows), BF16),
        scratch_shapes=[
            pltpu.VMEM((filter_rows, span + rows), F32),
            pltpu.VMEM((2, rows, span + rows), BF16),
        ],
        compiler_params=params(LONG_VMEM),
        cost_estimate=pl.CostEstimate(
            flops=4 * cpd * span * span, bytes_accessed=4 * n * out_rows * rows, transcendentals=0
        ),
        name="long_convs",
    )(received, *raw)


def gram_kernel(cpd, gpd, chunks, in_ref, out_ref, squares_ref, gram, raw):
    n, send_rows, rows = in_ref.shape
    send_rows = send_rows // chunks
    gw = cpd // gpd
    span = n * rows
    for slot in range(2):
        gram[slot, :, span:] = jnp.zeros((rows, rows), F32)
    if gpd * chunks < raw.shape[0]:
        raw[...] = jnp.zeros_like(raw)
    no_rows = jnp.zeros((n * gw, rows), BF16)

    def offset(d, k):
        held = (k + 1) * gw
        if held == n * gw:
            return d
        return jnp.concatenate([d[n * gw - held :], no_rows[held:]], 0)

    squares = jnp.zeros((1, span), F32)
    for chunk in range(chunks):
        base = chunk * send_rows

        def body(i, squares, chunk=chunk, base=base):
            slots = range(2)
            turned, shifting = [], []
            for slot in slots:
                first = pl.multiple_of(base + (2 * i + slot) * gw, gw)
                second = pl.multiple_of(base + cpd + (2 * i + slot) * gw, gw)
                x = in_ref[:, pl.ds(first, gw), :].reshape(n * gw, rows)
                shifting.append(in_ref[:, pl.ds(second, gw), :].reshape(n * gw, rows))
                turned.append(x.astype(F32).T.astype(BF16))
            for k in range(0, n, 2):
                for slot in slots:
                    d = shifting[slot]
                    pairs = jnp.concatenate([offset(d, k), offset(d, k + 1)], 1)
                    gram[slot, :, k * rows : (k + 2) * rows] = jnp.dot(
                        turned[slot], pairs, preferred_element_type=F32
                    )
            sums = [gram[slot, 0:8, :] for slot in slots]
            for m in range(1, rows // 8):
                for slot in slots:
                    block = gram[slot, 8 * m : 8 * m + 8, :]
                    sums[slot] = sums[slot] + pltpu.roll(block, 8 * m, 1)
            sums = [pltpu.roll(total, 0, 1, stride=1, stride_axis=0) for total in sums]
            for slot in slots:
                line = jnp.sum(sums[slot], axis=0, keepdims=True)[:, :span]
                raw[pl.ds(chunk * gpd + 2 * i + slot, 1), :] = line
                squares = squares + line * line
            return squares

        squares = lax.fori_loop(0, gpd // 2, body, squares)
    squares_ref[...] = jnp.sum(squares, axis=1, keepdims=True)
    turn = reversal(rows)
    for a in range(n):
        tile = raw[:, (n - 1 - a) * rows : (n - a) * rows].astype(BF16)
        out_ref[a] = jnp.dot(tile, turn, preferred_element_type=F32).astype(BF16)


def filter_products(received, cpd, gpd, chunks):
    n, _, rows = received.shape
    span = n * rows
    raw_rows = round_up(gpd * chunks, 16)
    return pl.pallas_call(
        functools.partial(gram_kernel, cpd, gpd, chunks),
        in_specs=[pl.BlockSpec(memory_space=pltpu.VMEM)],
        out_specs=[pl.BlockSpec(memory_space=pltpu.VMEM)] * 2,
        out_shape=[
            jax.ShapeDtypeStruct((n, raw_rows, rows), BF16),
            jax.ShapeDtypeStruct((1, 1), F32),
        ],
        scratch_shapes=[
            pltpu.VMEM((2, rows, span + rows), F32),
            pltpu.VMEM((raw_rows, span), F32),
        ],
        compiler_params=params(LONG_VMEM),
        cost_estimate=pl.CostEstimate(
            flops=2 * cpd * chunks * span * span,
            bytes_accessed=2 * received.size,
            transcendentals=0,
        ),
        name="filter_products",
    )(received)


def taps_anti(ext_ref, signals, afters, filters):
    rows = signals[0].shape[0]
    for j, signal in enumerate(signals):
        ext_ref[j, 0:rows, :] = signal
        ext_ref[j, rows : rows + EDGE, :] = afters[j]
    totals = [taps[0:1] * signal for signal, taps in zip(signals, filters)]
    for s in range(1, filters[0].shape[0]):
        for j, taps in enumerate(filters):
            totals[j] = totals[j] + taps[s : s + 1] * ext_ref[j, s : s + rows, :]
    return totals


def short_edge(before, signal, filter_taps):
    both = jnp.concatenate([before, signal], 0)
    total = filter_taps[0:1] * signal
    for s in range(1, filter_taps.shape[0]):
        total = total + filter_taps[s : s + 1] * both[EDGE - s : 2 * EDGE - s]
    return total


def after_kernel(
    cpd, gpd, chunks, last, bound, in_ref, og_ref, k_ref, v_ref, tail_ref, next_ref, taps_ref, *refs
):
    *refs, ext_q, ext_k, ext_v, ext_in_k, ext_in_v = refs
    if last:
        *refs, raw_ref, raw_rows, total_ref = refs
    dq_ref, dk_ref, dv_ref = refs[-3:]
    step = pl.program_id(0)
    per_tile, in_rows, rows = in_ref.shape
    halo_rows = 2 * EDGE * max(1, cpd // LANES)
    halo_at = 2 * cpd
    turn = reversal(rows)
    places = columns_of(og_ref.shape[1])
    tails = [tail_ref[:, at].astype(F32) for at in places]
    nexts = [next_ref[:, at].astype(F32) for at in places]
    convs, backs, halos = [], [], []
    for j in range(len(places)):
        if cpd >= LANES:
            dest, low = j * LANES // cpd, j * LANES % cpd
            conv = in_ref[dest, low : low + LANES, :]
            back = in_ref[dest, cpd + low : cpd + low + LANES, :]
            edge = halo_at + 2 * EDGE * (low // LANES)
            halo = in_ref[dest, edge : edge + 2 * EDGE, :].astype(F32)
        else:
            dests = range(j * LANES // cpd, (j + 1) * LANES // cpd)
            conv = jnp.concatenate([in_ref[d, 0:cpd, :] for d in dests], 0)
            back = jnp.concatenate([in_ref[d, cpd : 2 * cpd, :] for d in dests], 0)
            halo = jnp.concatenate(
                [in_ref[d, halo_at : halo_at + halo_rows, :].astype(F32)[:, :cpd] for d in dests], 1
            )
        convs.append(conv)
        backs.append(back)
        halos.append(halo)
    convs = [conv.astype(F32).T for conv in convs]
    backs = [jnp.dot(back, turn, preferred_element_type=F32) for back in backs]
    backs = [back.T for back in backs]
    taps = [[taps_ref[which, :, at] for at in places] for which in range(3)]
    keys = [k_ref[:, at].astype(F32) for at in places]
    values = [v_ref[:, at].astype(F32) for at in places]
    short_k = taps_causal(ext_in_k, [tail[EDGE : 2 * EDGE] for tail in tails], keys, taps[1])
    short_v = taps_causal(ext_in_v, [tail[2 * EDGE : 3 * EDGE] for tail in tails], values, taps[2])
    next_k = [
        short_edge(k[rows - EDGE :], f[EDGE : 2 * EDGE], t) for k, f, t in zip(keys, nexts, taps[1])
    ]
    next_v = [
        short_edge(v[rows - EDGE :], f[2 * EDGE : 3 * EDGE], t)
        for v, f, t in zip(values, nexts, taps[2])
    ]

    def store(ref, ext, signals, afters, filters):
        for at, total in zip(places, taps_anti(ext, signals, afters, filters)):
            ref[:, at] = total.astype(BF16)

    store(
        dq_ref,
        ext_q,
        [og_ref[:, at].astype(F32) * conv for at, conv in zip(places, convs)],
        [f[0:EDGE] * halo[0:EDGE] for f, halo in zip(nexts, halos)],
        taps[0],
    )
    store(
        dk_ref,
        ext_k,
        [back * v for back, v in zip(backs, short_v)],
        [halo[EDGE:] * v for halo, v in zip(halos, next_v)],
        taps[1],
    )
    store(
        dv_ref,
        ext_v,
        [back * k for back, k in zip(backs, short_k)],
        [halo[EDGE:] * k for halo, k in zip(halos, next_k)],
        taps[2],
    )
    if not last:
        return
    squares = jnp.zeros((1, LANES), F32)
    for dest in range(per_tile):
        parts = in_ref[dest, halo_at : halo_at + 2 * EDGE, :].astype(F32)
        squares = squares + parts[EDGE - 2 : EDGE - 1] + parts[EDGE - 1 : EDGE]

    @pl.when(step == 0)
    def _():
        total_ref[...] = jnp.zeros_like(total_ref)

    total_ref[...] = total_ref[...] + squares
    half = raw_rows.shape[0] // chunks
    for dest in range(per_tile):
        lines = in_ref[dest, halo_at + halo_rows :, :].astype(F32)
        for chunk in range(chunks):
            at = chunk * half + (step * per_tile + dest) * gpd
            raw_rows[pl.ds(at, gpd), :] = lines[chunk * gpd : (chunk + 1) * gpd]

    @pl.when(step == pl.num_programs(0) - 1)
    def _():
        factor = jnp.minimum(1.0, bound / jnp.sqrt(total_ref[...]))[:, 0:1]
        raw_ref[...] = raw_rows[...].T * factor


def after_exchange(
    returned, out_grad, key, value, tail, following, taps, groups, chunk, chunks, grads, bound
):
    n, in_rows, rows = returned.shape
    channels = out_grad.shape[1] // chunks
    cpd, gpd = channels // n, groups // (n * chunks)
    last = chunk + 1 == chunks
    tile = min(channels, max(512, cpd))
    per_tile = tile // cpd
    first = chunk * channels // tile
    block = pl.BlockSpec((rows, tile), lambda i: (0, first + i))
    ext = pltpu.VMEM((tile // LANES, rows + EDGE, LANES), F32)
    grad = jax.ShapeDtypeStruct(out_grad.shape, BF16)
    return pl.pallas_call(
        functools.partial(after_kernel, cpd, gpd, chunks, last, bound),
        grid=(channels // tile,),
        in_specs=[
            pl.BlockSpec((per_tile, in_rows, rows), lambda i: (i, 0, 0)),
            block,
            block,
            block,
            pl.BlockSpec((3 * EDGE, tile), lambda i: (0, first + i)),
            pl.BlockSpec((3 * EDGE, tile), lambda i: (0, first + i)),
            pl.BlockSpec((3, taps.shape[1], tile), lambda i: (0, 0, first + i)),
        ]
        + [pl.BlockSpec(memory_space=pl.ANY)] * len(grads),
        input_output_aliases={7 + i: i for i in range(len(grads))},
        out_specs=[block] * 3 + [pl.BlockSpec((rows, groups), lambda i: (0, 0))] * last,
        out_shape=[grad] * 3 + [jax.ShapeDtypeStruct((rows, groups), F32)] * last,
        scratch_shapes=[pltpu.VMEM((groups, rows), F32), pltpu.VMEM((1, LANES), F32)] * last
        + [ext] * 5,
        compiler_params=params(),
        cost_estimate=pl.CostEstimate(
            flops=90 * rows * channels, bytes_accessed=18 * rows * channels, transcendentals=0
        ),
        name="after_exchange",
    )(returned, out_grad, key, value, tail, following, taps, *grads)


def on_device(
    query_heads,
    key_heads,
    value_heads,
    hyena_query,
    hyena_key,
    hyena_value,
    short_filter,
    long_filter,
    output_grad,
):
    rows, channels = query_heads.shape
    groups = long_filter.shape[1]
    n = lax.axis_size("ctx")
    tp = lax.axis_size("tp")
    cpd, gpd = channels // n, groups // n
    position = lax.axis_index("ctx")
    tail = shifted(edge_rows((hyena_query, hyena_key, hyena_value), False), "ctx", 1)
    half = channels // 2
    chunks = 2 if gpd % 4 == 0 else 1
    cpd, gpd = cpd // chunks, gpd // chunks
    send = before_exchange(
        hyena_query, hyena_key, hyena_value, output_grad, tail, short_filter, long_filter, n, chunks
    )
    send, query, key, value, *sources = lax.optimization_barrier(
        (send, query_heads, key_heads, value_heads, output_grad, hyena_key, hyena_value)
    )
    received = lax.all_to_all(send, "ctx", split_axis=0, concat_axis=0, tiled=True)
    query_next = shifted(query[:, :half], "ctx", -1)
    previous = shifted(jnp.concatenate([key[:, half:], value[:, half:]], 0), "ctx", 1)
    returned = []
    for chunk in range(chunks):
        raw = ()
        if chunk + 1 == chunks:
            raw, squares = filter_products(received, cpd, gpd, chunks)
            raw = (raw, total_over(squares, "tp"))
        results = long_convs(received, raw, cpd, gpd, chunk, chunks)
        if chunk == 0:
            results, received, query_next, previous, *sources = lax.optimization_barrier(
                (results, received, query_next, previous, *sources)
            )
            part = shifted(attend_next(query_next, key_heads, value_heads), "ctx", 1)
            following = shifted(edge_rows(sources, True), "ctx", -1)
        else:
            results, part, following = lax.optimization_barrier((results, part, following))
        returned.append(lax.all_to_all(results, "ctx", split_axis=0, concat_axis=0, tiled=True))
    attention = attend(query_heads, key_heads, value_heads, part, previous, position)
    bound = math.sqrt(rows * n * groups * tp)
    grads = ()
    for chunk in range(chunks):
        if chunk > 0:
            returned[chunk], attention, *grads = lax.optimization_barrier(
                (returned[chunk], attention, *grads)
            )
        grads = after_exchange(
            returned[chunk], output_grad, hyena_key, hyena_value, tail, following, short_filter, groups,
            chunk, chunks, grads, bound,
        )
    return (attention, *grads)


def solution(mesh):
    whole = P("ctx", "tp")
    in_specs = (whole,) * 6 + (P(None, None, "tp"), whole, whole)
    return jax.shard_map(
        on_device, mesh=mesh, in_specs=in_specs, out_specs=(whole,) * 5, check_vma=False
    )
```

```python
import functools
import math

import jax
import jax.numpy as jnp
from jax import lax
from jax.experimental import pallas as pl
from jax.experimental.pallas import tpu as pltpu
from jax.sharding import PartitionSpec as P

HEAD_DIM = 128
LANES = 128
EDGE = 8
F32 = jnp.float32
BF16 = jnp.bfloat16
VMEM_BYTES = 60 * 1024 * 1024
LONG_VMEM = 20 * 1024 * 1024


def params(size=VMEM_BYTES):
    return pltpu.CompilerParams(vmem_limit_bytes=size)


def shifted(block, axis, distance):
    devices = range(lax.axis_size(axis))
    route = [(i - distance, i) for i in devices if i - distance in devices]
    return lax.ppermute(block, axis, route)


def total_over(value, axis):
    size = lax.axis_size(axis)
    distance = 1
    while distance < size:
        value = value + lax.ppermute(value, axis, [(i, i ^ distance) for i in range(size)])
        distance *= 2
    return value


def round_up(value, step):
    return -(-value // step) * step


def reversal(size):
    row = lax.broadcasted_iota(jnp.int32, (size, size), 0)
    col = lax.broadcasted_iota(jnp.int32, (size, size), 1)
    return jnp.where(row + col == size - 1, 1.0, 0.0).astype(BF16)


SCALE = 1.0 / math.sqrt(HEAD_DIM)
NT = (((1,), (1,)), ((), ()))


LOG_LANES = 32


def places_of(width):
    return [slice(head * HEAD_DIM, (head + 1) * HEAD_DIM) for head in range(width // HEAD_DIM)]


def attend_next_kernel(q_ref, k_ref, v_ref, out_ref, logs_ref):
    rows, width = q_ref.shape
    heads = width // HEAD_DIM
    step = pl.program_id(0)
    lane = lax.broadcasted_iota(jnp.int32, (rows, LANES), 1)

    @pl.when(step == 0)
    def _():
        logs_ref[...] = jnp.zeros_like(logs_ref)

    places = places_of(width)
    scores = [
        lax.dot_general(q_ref[:, at], k_ref[:, at], NT, preferred_element_type=F32) * SCALE
        for at in places
    ]
    largest = [jnp.max(score, axis=1, keepdims=True) for score in scores]
    raised = [jnp.exp(score - top) for score, top in zip(scores, largest)]
    totals = [jnp.sum(r, axis=1, keepdims=True) for r in raised]
    weights = [(r * (1.0 / total)).astype(BF16) for r, total in zip(raised, totals)]
    mixed = [
        jnp.dot(weight, v_ref[:, at], preferred_element_type=F32) for weight, at in zip(weights, places)
    ]
    logs = logs_ref[...]
    for head in range(heads):
        log = largest[head] + jnp.log(totals[head])
        logs = jnp.where(lane == step * heads + head, log, logs)
    logs_ref[...] = logs
    first = pl.multiple_of(step * width, LANES)
    out_ref[:, pl.ds(first, width)] = jnp.concatenate([m.astype(BF16) for m in mixed], 1)

    @pl.when(step == pl.num_programs(0) - 1)
    def _():
        upper = logs.astype(BF16).astype(F32)
        middle = (logs - upper).astype(BF16).astype(F32)
        lower = logs - upper - middle
        terms = upper + pltpu.roll(middle, LOG_LANES, 1) + pltpu.roll(lower, 2 * LOG_LANES, 1)
        out_ref[:, out_ref.shape[1] - LANES :] = terms.astype(BF16)


def attend_merge_kernel(place_ref, q_ref, k_ref, v_ref, part_ref, log_ref, _, out_ref):
    rows, width = q_ref.shape
    heads = width // HEAD_DIM
    step = pl.program_id(0)
    row = lax.broadcasted_iota(jnp.int32, (rows, rows), 0)
    col = lax.broadcasted_iota(jnp.int32, (rows, rows), 1)
    own_ok = col <= row
    lane = lax.broadcasted_iota(jnp.int32, (rows, LANES), 1) & (LOG_LANES - 1)
    has_prev = jnp.broadcast_to(place_ref[0], (rows, 1)) > 0
    places = places_of(width)
    terms = log_ref[...].astype(F32)
    scores = [
        lax.dot_general(q_ref[:, at], k_ref[:, at], NT, preferred_element_type=F32) * SCALE
        for at in places
    ]
    scores = [jnp.where(own_ok, score, -jnp.inf) for score in scores]
    logs = [
        jnp.sum(jnp.where(lane == step * heads + head, terms, 0.0), axis=1, keepdims=True)
        for head in range(heads)
    ]
    logs = [jnp.where(has_prev, log, -jnp.inf) for log in logs]
    largest = [
        jnp.maximum(jnp.max(score, axis=1, keepdims=True), log) for score, log in zip(scores, logs)
    ]
    raised = [jnp.exp(score - top) for score, top in zip(scores, largest)]
    prevs = [jnp.exp(log - top) for log, top in zip(logs, largest)]
    inverses = [
        1.0 / (jnp.sum(r, axis=1, keepdims=True) + prev) for r, prev in zip(raised, prevs)
    ]
    weights = [(r * inverse).astype(BF16) for r, inverse in zip(raised, inverses)]
    mixed = [
        jnp.dot(weight, v_ref[:, at], preferred_element_type=F32) for weight, at in zip(weights, places)
    ]
    for head, at in enumerate(places):
        total = mixed[head] + (prevs[head] * inverses[head]) * part_ref[:, at].astype(F32)
        out_ref[:, at] = total.astype(BF16)


def attend_whole_kernel(place_ref, q_ref, k_ref, v_ref, kp_ref, vp_ref, out_ref):
    rows, width = q_ref.shape
    row = lax.broadcasted_iota(jnp.int32, (rows, rows), 0)
    col = lax.broadcasted_iota(jnp.int32, (rows, rows), 1)
    own_ok = col <= row
    prev_ok = jnp.broadcast_to(place_ref[0], (rows, rows)) > 0
    places = places_of(width)

    def scores(ref, allowed):
        products = [
            lax.dot_general(q_ref[:, at], ref[:, at], NT, preferred_element_type=F32) for at in places
        ]
        return [jnp.where(allowed, product * SCALE, -jnp.inf) for product in products]

    own, prev = scores(k_ref, own_ok), scores(kp_ref, prev_ok)
    largest = [jnp.max(jnp.maximum(o, p), axis=1, keepdims=True) for o, p in zip(own, prev)]
    own = [jnp.exp(o - top) for o, top in zip(own, largest)]
    prev = [jnp.exp(p - top) for p, top in zip(prev, largest)]
    totals = [jnp.sum(o + p, axis=1, keepdims=True) for o, p in zip(own, prev)]
    inverses = [1.0 / total for total in totals]
    own = [(o * inverse).astype(BF16) for o, inverse in zip(own, inverses)]
    prev = [(p * inverse).astype(BF16) for p, inverse in zip(prev, inverses)]
    mixed = [
        jnp.dot(o, v_ref[:, at], preferred_element_type=F32)
        + jnp.dot(p, vp_ref[:, at], preferred_element_type=F32)
        for o, p, at in zip(own, prev, places)
    ]
    for head, at in enumerate(places):
        out_ref[:, at] = mixed[head].astype(BF16)


def attend_cost(rows, channels):
    heads = channels // HEAD_DIM
    return pl.CostEstimate(
        flops=4 * heads * rows * rows * HEAD_DIM,
        bytes_accessed=10 * rows * channels,
        transcendentals=heads * rows * rows,
    )


def attend_next(query, key, value):
    rows, channels = query.shape
    tile = min(512, channels)
    block = pl.BlockSpec((rows, tile), lambda i: (0, i))
    return pl.pallas_call(
        attend_next_kernel,
        grid=(channels // tile,),
        in_specs=[block] * 3,
        out_specs=pl.BlockSpec((rows, channels + LANES), lambda i: (0, 0)),
        out_shape=jax.ShapeDtypeStruct((rows, channels + LANES), BF16),
        scratch_shapes=[pltpu.VMEM((rows, LANES), F32)],
        compiler_params=params(LONG_VMEM),
        cost_estimate=attend_cost(rows, channels),
        name="attend_next",
    )(query, key, value)


def attend(query, key, value, part, previous, position):
    rows, channels = query.shape
    half = channels // 2
    tile = min(512, half)
    steps = half // tile
    place = position.astype(jnp.int32).reshape(1)
    smem = pl.BlockSpec(memory_space=pltpu.SMEM)
    first = pl.BlockSpec((rows, tile), lambda i: (0, i))
    second = pl.BlockSpec((rows, tile), lambda i: (0, steps + i))
    out = jax.ShapeDtypeStruct((rows, channels), BF16)
    whole = pl.pallas_call(
        attend_whole_kernel,
        grid=(steps,),
        in_specs=[smem, second, second, second, first, pl.BlockSpec((rows, tile), lambda i: (1, i))],
        out_specs=second,
        out_shape=out,
        compiler_params=params(LONG_VMEM),
        cost_estimate=attend_cost(rows, channels),
        name="attend_whole",
    )(place, query, key, value, previous, previous)
    log_at = half // LANES
    return pl.pallas_call(
        attend_merge_kernel,
        grid=(steps,),
        in_specs=[
            smem,
            first,
            first,
            first,
            first,
            pl.BlockSpec((rows, LANES), lambda i: (0, log_at)),
            pl.BlockSpec(memory_space=pl.ANY),
        ],
        out_specs=first,
        out_shape=out,
        input_output_aliases={6: 0},
        compiler_params=params(LONG_VMEM),
        cost_estimate=attend_cost(rows, half),
        name="attend_merge",
    )(place, query, key, value, part, part, whole)


def edge_kernel(first, *refs):
    *sources, out_ref = refs
    parts = [r[...].astype(F32) for r in sources]
    parts = [p[:EDGE] if first else p[p.shape[0] - EDGE :] for p in parts]
    out_ref[...] = jnp.concatenate(parts, 0).astype(BF16)


def edge_rows(arrays, first):
    rows, channels = arrays[0].shape
    block = pl.BlockSpec((16, channels), lambda i: (0 if first else rows // 16 - 1, 0))
    return pl.pallas_call(
        functools.partial(edge_kernel, first),
        grid=(1,),
        in_specs=[block] * len(arrays),
        out_specs=pl.BlockSpec((len(arrays) * EDGE, channels), lambda i: (0, 0)),
        out_shape=jax.ShapeDtypeStruct((len(arrays) * EDGE, channels), BF16),
        compiler_params=params(),
        name="edge_rows",
    )(*arrays)


def taps_causal(ext_ref, befores, signals, filters):
    rows = signals[0].shape[0]
    for j, signal in enumerate(signals):
        ext_ref[j, 0:EDGE, :] = befores[j]
        ext_ref[j, EDGE : EDGE + rows, :] = signal
    totals = [taps[0:1] * signal for signal, taps in zip(signals, filters)]
    for s in range(1, filters[0].shape[0]):
        for j, taps in enumerate(filters):
            totals[j] = totals[j] + taps[s : s + 1] * ext_ref[j, EDGE - s : EDGE - s + rows, :]
    return totals


def columns_of(width):
    return [slice(j * LANES, (j + 1) * LANES) for j in range(width // LANES)]


PAIR = 2


def put_pairs(ref, dest, channel, gw, first, second):
    width = PAIR * gw
    for piece in range(first.shape[0] // width):
        at = slice(piece * width, (piece + 1) * width)
        low = 2 * (channel + piece * width)
        ref[dest, low : low + width, :] = first[at]
        ref[dest, low + width : low + 2 * width, :] = second[at]


def get_pairs(ref, dest, channel, count, gw, which):
    width = PAIR * gw
    lows = [2 * (channel + low) + which * width for low in range(0, count, width)]
    return jnp.concatenate([ref[dest, low : low + width, :] for low in lows], 0)


def before_kernel(cpd, gpd, chunks, *refs):
    *refs, long_ref, send_ref, long_rows, ext_q, ext_k, ext_v = refs
    step = pl.program_id(0)
    groups = long_ref.shape[1]
    per_tile, send_rows, rows = send_ref.shape
    gw = cpd // gpd
    filter_rows = send_rows - 2 * cpd * chunks
    half = groups // chunks

    @pl.when(step == 0)
    def _():
        long_rows[...] = jnp.zeros_like(long_rows)
        long_rows[0:groups, :] = long_ref[...].T

    turn = reversal(rows)
    for chunk in range(chunks):
        q_ref, k_ref, v_ref, og_ref, tail_ref, taps_ref = refs[6 * chunk : 6 * chunk + 6]
        places = columns_of(q_ref.shape[1])
        tails = [tail_ref[:, at].astype(F32) for at in places]

        def short(which, ref, ext, tails=tails, places=places, taps_ref=taps_ref, chunk=chunk):
            return taps_causal(
                ext.at[chunk],
                [tail[which * EDGE : (which + 1) * EDGE] for tail in tails],
                [ref[:, at].astype(F32) for at in places],
                [taps_ref[which, :, at] for at in places],
            )

        short_k, short_v = short(1, k_ref, ext_k), short(2, v_ref, ext_v)
        mixed = [(k * v).T.astype(BF16) for k, v in zip(short_k, short_v)]
        short_q = short(0, q_ref, ext_q)
        delta = [(og_ref[:, at].astype(F32) * q).T.astype(BF16) for q, at in zip(short_q, places)]
        delta = [jnp.dot(d, turn, preferred_element_type=F32).astype(BF16) for d in delta]
        width = min(cpd, LANES)
        for j in range(len(places)):
            for piece in range(LANES // width):
                channel = j * LANES + piece * width
                dest, low = channel // cpd, channel % cpd
                at = slice(piece * width, (piece + 1) * width)
                put_pairs(send_ref, dest, chunk * cpd + low, gw, mixed[j][at], delta[j][at])
    for dest in range(per_tile):
        lines = []
        for chunk in range(chunks):
            first = chunk * half + (step * per_tile + dest) * gpd
            lines.append(long_rows[pl.ds(first, filter_rows if chunks == 1 else gpd), :])
        send_ref[dest, 2 * cpd * chunks :, :] = jnp.concatenate(lines, 0).astype(BF16)


def before_exchange(query, key, value, out_grad, tail, taps, long_filter, n, chunks):
    rows, channels = query.shape
    groups = long_filter.shape[1]
    cpd, gpd = channels // (n * chunks), groups // (n * chunks)
    tile = min(channels // chunks, max(512 // chunks, cpd))
    per_tile = tile // cpd
    filter_rows = round_up(gpd * chunks, 16)
    send_rows = 2 * cpd * chunks + filter_rows
    steps = n // per_tile
    specs = []
    for chunk in range(chunks):
        first = chunk * steps
        specs += [pl.BlockSpec((rows, tile), lambda i, f=first: (0, f + i))] * 4
        specs.append(pl.BlockSpec((3 * EDGE, tile), lambda i, f=first: (0, f + i)))
        specs.append(pl.BlockSpec((3, taps.shape[1], tile), lambda i, f=first: (0, 0, f + i)))
    ext = pltpu.VMEM((chunks, tile // LANES, rows + EDGE, LANES), F32)
    return pl.pallas_call(
        functools.partial(before_kernel, cpd, gpd, chunks),
        grid=(steps,),
        in_specs=specs + [pl.BlockSpec((rows, groups), lambda i: (0, 0))],
        out_specs=pl.BlockSpec((per_tile, send_rows, rows), lambda i: (i, 0, 0)),
        out_shape=jax.ShapeDtypeStruct((n, send_rows, rows), BF16),
        scratch_shapes=[pltpu.VMEM((round_up(groups, 8) + filter_rows, rows), F32), ext, ext, ext],
        compiler_params=params(),
        cost_estimate=pl.CostEstimate(
            flops=50 * rows * channels, bytes_accessed=12 * rows * channels, transcendentals=0
        ),
        name="before_exchange",
    )(*((query, key, value, out_grad, tail, taps) * chunks), long_filter)


def conv_kernel(cpd, gpd, chunk, in_ref, filter_ref, *refs):
    *raw_ref, out_ref, taps, wide = refs
    step = pl.program_id(0)
    n, _, rows = in_ref.shape
    gw = cpd // gpd
    span = n * rows
    slots = range(PAIR)

    @pl.when(step == 0)
    def _():
        taps[:, 0:rows] = jnp.zeros((taps.shape[0], rows), F32)
        for a in range(n):
            taps[:, (a + 1) * rows : (a + 2) * rows] = filter_ref[a].astype(F32)
        for slot in slots:
            wide[slot, :, 0:rows] = jnp.zeros((rows, rows), BF16)

    bases = []
    for slot in slots:
        line = taps[pl.ds(chunk * gpd + PAIR * step + slot, 1), :]
        line = jnp.broadcast_to(line, (16, span + rows))
        bases.append(pltpu.roll(line, 0, 1, stride=1, stride_axis=0).astype(BF16))
    for m in range(rows // 16):
        for slot in slots:
            moved = bases[slot] if m == 0 else pltpu.roll(bases[slot], 16 * m, 1)
            wide[slot, 16 * m : 16 * m + 16, rows:] = moved[:, rows:]
    stacks = []
    for slot in slots:
        x = in_ref[:, slot * gw : (slot + 1) * gw, :]
        d = in_ref[:, (PAIR + slot) * gw : (PAIR + slot + 1) * gw, :]
        both = [jnp.concatenate([x[a], d[n - 1 - a]], 0) for a in range(n)]
        stacks.append(
            jnp.concatenate([jnp.concatenate([both[a], both[a + 1]], 1) for a in range(0, n, 2)], 0)
        )
    totals = [None] * PAIR
    for k in range(n // 2):
        skip = 2 * gw * k
        low = 2 * rows * k
        for slot in slots:
            tile = jnp.concatenate(
                [wide[slot, :, low + rows : low + 3 * rows], wide[slot, :, low : low + 2 * rows]], 0
            )
            part = jnp.dot(stacks[slot][: n * gw - skip], tile, preferred_element_type=F32)
            total = totals[slot]
            totals[slot] = part if k == 0 else jnp.concatenate([total[:skip], total[skip:] + part], 0)
    for slot in slots:
        total = totals[slot]
        first = pl.multiple_of(2 * PAIR * gw * step + slot * gw, gw)
        second = pl.multiple_of(2 * PAIR * gw * step + (PAIR + slot) * gw, gw)
        for a in range(n):
            at = slice(a % 2 * rows, (a % 2 + 1) * rows)
            top = a // 2 * 2 * gw
            out_ref[a, pl.ds(first, gw), :] = total[top : top + gw, at].astype(BF16)
            out_ref[n - 1 - a, pl.ds(second, gw), :] = total[top + gw : top + 2 * gw, at].astype(BF16)

    @pl.when(step == pl.num_programs(0) - 1)
    def _():
        finish_conv(cpd, gw, out_ref, raw_ref)


def finish_conv(cpd, gw, out_ref, raw_ref):
    n, _, rows = out_ref.shape
    upper = lower = 0.0
    if raw_ref:
        *raw_ref, squares_ref = raw_ref
        upper = squares_ref[...].astype(BF16).astype(F32)
        lower = squares_ref[...] - upper
    halo_at = 2 * cpd
    row = lax.broadcasted_iota(jnp.int32, (2 * EDGE, 2 * rows), 0)
    lane = lax.broadcasted_iota(jnp.int32, (2 * EDGE, 2 * rows), 1)
    wanted = jnp.where(row < EDGE, row, 2 * rows - 1 + EDGE - row)
    pick = jnp.where(lane == wanted, 1.0, 0.0).astype(BF16)
    row_out = lax.broadcasted_iota(jnp.int32, (2 * EDGE, rows), 0)
    for a in range(n):
        if a + 1 < n:
            results = [get_pairs(out_ref, a + 1, 0, cpd, gw, which) for which in range(2)]
            results = jnp.concatenate(results, 1)
            halo = lax.dot_general(
                pick, results, (((1,), (1,)), ((), ())), preferred_element_type=F32
            )
            if cpd < LANES:
                halo = jnp.concatenate([halo, jnp.zeros((2 * EDGE, LANES - cpd), F32)], 1)
        else:
            halo = jnp.zeros((2 * EDGE, max(cpd, LANES)), F32)
        for j in range(halo.shape[1] // LANES):
            at = halo_at + 2 * EDGE * j
            tile = halo[:, j * LANES : (j + 1) * LANES]
            tile = jnp.where(row_out == EDGE - 2, upper, jnp.where(row_out == EDGE - 1, lower, tile))
            out_ref[a, at : at + 2 * EDGE, :] = tile.astype(BF16)
    for ref in raw_ref:
        out_ref[:, out_ref.shape[1] - ref.shape[1] :, :] = ref[...]


def long_convs(received, raw, cpd, gpd, chunk, chunks):
    n, send_rows, rows = received.shape
    filter_rows = send_rows - 2 * cpd * chunks
    out_rows = 2 * cpd + 2 * EDGE * max(1, cpd // LANES) + sum(r.shape[1] for r in raw[:1])
    span = n * rows
    pairs = gpd // PAIR
    pair_rows = 2 * cpd // pairs
    filter_at = 2 * cpd * chunks // filter_rows
    return pl.pallas_call(
        functools.partial(conv_kernel, cpd, gpd, chunk),
        grid=(pairs,),
        in_specs=[
            pl.BlockSpec((n, pair_rows, rows), lambda i: (0, chunk * pairs + i, 0)),
            pl.BlockSpec((n, filter_rows, rows), lambda i: (0, filter_at, 0)),
        ]
        + [pl.BlockSpec(r.shape, lambda i, r=r: (0,) * r.ndim) for r in raw],
        out_specs=pl.BlockSpec((n, out_rows, rows), lambda i: (0, 0, 0)),
        out_shape=jax.ShapeDtypeStruct((n, out_rows, rows), BF16),
        scratch_shapes=[
            pltpu.VMEM((filter_rows, span + rows), F32),
            pltpu.VMEM((PAIR, rows, span + rows), BF16),
        ],
        compiler_params=params(),
        cost_estimate=pl.CostEstimate(
            flops=4 * cpd * span * span, bytes_accessed=4 * n * out_rows * rows, transcendentals=0
        ),
        name="long_convs",
    )(received, received, *raw)


def gram_kernel(gw, in_ref, out_ref, squares_ref, gram, raw, total_ref):
    step = pl.program_id(0)
    n, _, rows = in_ref.shape
    span = n * rows
    slots = range(PAIR)

    @pl.when(step == 0)
    def _():
        for slot in slots:
            gram[slot, :, span:] = jnp.zeros((rows, rows), F32)
        raw[...] = jnp.zeros_like(raw)
        total_ref[...] = jnp.zeros_like(total_ref)

    no_rows = jnp.zeros((n * gw, rows), BF16)

    def offset(d, k):
        held = (k + 1) * gw
        if held == n * gw:
            return d
        return jnp.concatenate([d[n * gw - held :], no_rows[held:]], 0)

    turned, shifting = [], []
    for slot in slots:
        x = in_ref[:, slot * gw : (slot + 1) * gw, :].reshape(n * gw, rows)
        d = in_ref[:, (PAIR + slot) * gw : (PAIR + slot + 1) * gw, :]
        shifting.append(d.reshape(n * gw, rows))
        turned.append(x.astype(F32).T.astype(BF16))
    for k in range(0, n, 2):
        for slot in slots:
            d = shifting[slot]
            pairs = jnp.concatenate([offset(d, k), offset(d, k + 1)], 1)
            gram[slot, :, k * rows : (k + 2) * rows] = jnp.dot(
                turned[slot], pairs, preferred_element_type=F32
            )
    sums = [gram[slot, 0:8, :] for slot in slots]
    for m in range(1, rows // 8):
        for slot in slots:
            sums[slot] = sums[slot] + pltpu.roll(gram[slot, 8 * m : 8 * m + 8, :], 8 * m, 1)
    sums = [pltpu.roll(total, 0, 1, stride=1, stride_axis=0) for total in sums]
    for slot in slots:
        line = jnp.sum(sums[slot], axis=0, keepdims=True)[:, :span]
        raw[pl.ds(PAIR * step + slot, 1), :] = line
        total_ref[...] = total_ref[...] + line * line

    @pl.when(step == pl.num_programs(0) - 1)
    def _():
        squares_ref[...] = jnp.sum(total_ref[...], axis=1, keepdims=True)
        turn = reversal(rows)
        for a in range(n):
            tile = raw[:, (n - 1 - a) * rows : (n - a) * rows].astype(BF16)
            out_ref[a] = jnp.dot(tile, turn, preferred_element_type=F32).astype(BF16)


def filter_products(received, cpd, gpd, chunks):
    n, _, rows = received.shape
    span = n * rows
    raw_rows = round_up(gpd * chunks, 16)
    pairs = gpd * chunks // PAIR
    pair_rows = 2 * cpd * chunks // pairs
    return pl.pallas_call(
        functools.partial(gram_kernel, cpd // gpd),
        grid=(pairs,),
        in_specs=[pl.BlockSpec((n, pair_rows, rows), lambda i: (0, i, 0))],
        out_specs=[
            pl.BlockSpec((n, raw_rows, rows), lambda i: (0, 0, 0)),
            pl.BlockSpec((1, 1), lambda i: (0, 0)),
        ],
        out_shape=[
            jax.ShapeDtypeStruct((n, raw_rows, rows), BF16),
            jax.ShapeDtypeStruct((1, 1), F32),
        ],
        scratch_shapes=[
            pltpu.VMEM((PAIR, rows, span + rows), F32),
            pltpu.VMEM((raw_rows, span), F32),
            pltpu.VMEM((1, span), F32),
        ],
        compiler_params=params(),
        cost_estimate=pl.CostEstimate(
            flops=2 * cpd * chunks * span * span,
            bytes_accessed=2 * received.size,
            transcendentals=0,
        ),
        name="filter_products",
    )(received)


def taps_anti(ext_ref, signals, afters, filters):
    rows = signals[0].shape[0]
    for j, signal in enumerate(signals):
        ext_ref[j, 0:rows, :] = signal
        ext_ref[j, rows : rows + EDGE, :] = afters[j]
    totals = [taps[0:1] * signal for signal, taps in zip(signals, filters)]
    for s in range(1, filters[0].shape[0]):
        for j, taps in enumerate(filters):
            totals[j] = totals[j] + taps[s : s + 1] * ext_ref[j, s : s + rows, :]
    return totals


def short_edge(before, signal, filter_taps):
    both = jnp.concatenate([before, signal], 0)
    total = filter_taps[0:1] * signal
    for s in range(1, filter_taps.shape[0]):
        total = total + filter_taps[s : s + 1] * both[EDGE - s : 2 * EDGE - s]
    return total


def after_kernel(
    cpd, gpd, chunks, last, bound, in_ref, og_ref, k_ref, v_ref, tail_ref, next_ref, taps_ref, *refs
):
    *refs, ext_q, ext_k, ext_v, ext_in_k, ext_in_v = refs
    if last:
        *refs, raw_ref, raw_rows, total_ref = refs
    dq_ref, dk_ref, dv_ref = refs[-3:]
    step = pl.program_id(0)
    per_tile, in_rows, rows = in_ref.shape
    halo_rows = 2 * EDGE * max(1, cpd // LANES)
    halo_at = 2 * cpd
    turn = reversal(rows)
    places = columns_of(og_ref.shape[1])
    tails = [tail_ref[:, at].astype(F32) for at in places]
    nexts = [next_ref[:, at].astype(F32) for at in places]
    convs, backs, halos = [], [], []
    for j in range(len(places)):
        if cpd >= LANES:
            dest, low = j * LANES // cpd, j * LANES % cpd
            conv = get_pairs(in_ref, dest, low, LANES, cpd // gpd, 0)
            back = get_pairs(in_ref, dest, low, LANES, cpd // gpd, 1)
            edge = halo_at + 2 * EDGE * (low // LANES)
            halo = in_ref[dest, edge : edge + 2 * EDGE, :].astype(F32)
        else:
            dests = range(j * LANES // cpd, (j + 1) * LANES // cpd)
            conv = jnp.concatenate([get_pairs(in_ref, d, 0, cpd, cpd // gpd, 0) for d in dests], 0)
            back = jnp.concatenate([get_pairs(in_ref, d, 0, cpd, cpd // gpd, 1) for d in dests], 0)
            halo = jnp.concatenate(
                [in_ref[d, halo_at : halo_at + halo_rows, :].astype(F32)[:, :cpd] for d in dests], 1
            )
        convs.append(conv)
        backs.append(back)
        halos.append(halo)
    convs = [conv.astype(F32).T for conv in convs]
    backs = [jnp.dot(back, turn, preferred_element_type=F32) for back in backs]
    backs = [back.T for back in backs]
    taps = [[taps_ref[which, :, at] for at in places] for which in range(3)]
    keys = [k_ref[:, at].astype(F32) for at in places]
    values = [v_ref[:, at].astype(F32) for at in places]
    short_k = taps_causal(ext_in_k, [tail[EDGE : 2 * EDGE] for tail in tails], keys, taps[1])
    short_v = taps_causal(ext_in_v, [tail[2 * EDGE : 3 * EDGE] for tail in tails], values, taps[2])
    next_k = [
        short_edge(k[rows - EDGE :], f[EDGE : 2 * EDGE], t) for k, f, t in zip(keys, nexts, taps[1])
    ]
    next_v = [
        short_edge(v[rows - EDGE :], f[2 * EDGE : 3 * EDGE], t)
        for v, f, t in zip(values, nexts, taps[2])
    ]

    def store(ref, ext, signals, afters, filters):
        for at, total in zip(places, taps_anti(ext, signals, afters, filters)):
            ref[:, at] = total.astype(BF16)

    store(
        dq_ref,
        ext_q,
        [og_ref[:, at].astype(F32) * conv for at, conv in zip(places, convs)],
        [f[0:EDGE] * halo[0:EDGE] for f, halo in zip(nexts, halos)],
        taps[0],
    )
    store(
        dk_ref,
        ext_k,
        [back * v for back, v in zip(backs, short_v)],
        [halo[EDGE:] * v for halo, v in zip(halos, next_v)],
        taps[1],
    )
    store(
        dv_ref,
        ext_v,
        [back * k for back, k in zip(backs, short_k)],
        [halo[EDGE:] * k for halo, k in zip(halos, next_k)],
        taps[2],
    )
    if not last:
        return
    squares = jnp.zeros((1, LANES), F32)
    for dest in range(per_tile):
        parts = in_ref[dest, halo_at : halo_at + 2 * EDGE, :].astype(F32)
        squares = squares + parts[EDGE - 2 : EDGE - 1] + parts[EDGE - 1 : EDGE]

    @pl.when(step == 0)
    def _():
        total_ref[...] = jnp.zeros_like(total_ref)

    total_ref[...] = total_ref[...] + squares
    half = raw_rows.shape[0] // chunks
    for dest in range(per_tile):
        lines = in_ref[dest, halo_at + halo_rows :, :].astype(F32)
        for chunk in range(chunks):
            at = chunk * half + (step * per_tile + dest) * gpd
            raw_rows[pl.ds(at, gpd), :] = lines[chunk * gpd : (chunk + 1) * gpd]

    @pl.when(step == pl.num_programs(0) - 1)
    def _():
        factor = jnp.minimum(1.0, bound / jnp.sqrt(total_ref[...]))[:, 0:1]
        raw_ref[...] = raw_rows[...].T * factor


def after_exchange(
    returned, out_grad, key, value, tail, following, taps, groups, chunk, chunks, grads, bound
):
    n, in_rows, rows = returned.shape
    channels = out_grad.shape[1] // chunks
    cpd, gpd = channels // n, groups // (n * chunks)
    last = chunk + 1 == chunks
    tile = min(channels, max(512, cpd))
    per_tile = tile // cpd
    first = chunk * channels // tile
    block = pl.BlockSpec((rows, tile), lambda i: (0, first + i))
    ext = pltpu.VMEM((tile // LANES, rows + EDGE, LANES), F32)
    grad = jax.ShapeDtypeStruct(out_grad.shape, BF16)
    return pl.pallas_call(
        functools.partial(after_kernel, cpd, gpd, chunks, last, bound),
        grid=(channels // tile,),
        in_specs=[
            pl.BlockSpec((per_tile, in_rows, rows), lambda i: (i, 0, 0)),
            block,
            block,
            block,
            pl.BlockSpec((3 * EDGE, tile), lambda i: (0, first + i)),
            pl.BlockSpec((3 * EDGE, tile), lambda i: (0, first + i)),
            pl.BlockSpec((3, taps.shape[1], tile), lambda i: (0, 0, first + i)),
        ]
        + [pl.BlockSpec(memory_space=pl.ANY)] * len(grads),
        input_output_aliases={7 + i: i for i in range(len(grads))},
        out_specs=[block] * 3 + [pl.BlockSpec((rows, groups), lambda i: (0, 0))] * last,
        out_shape=[grad] * 3 + [jax.ShapeDtypeStruct((rows, groups), F32)] * last,
        scratch_shapes=[pltpu.VMEM((groups, rows), F32), pltpu.VMEM((1, LANES), F32)] * last
        + [ext] * 5,
        compiler_params=params(),
        cost_estimate=pl.CostEstimate(
            flops=90 * rows * channels, bytes_accessed=18 * rows * channels, transcendentals=0
        ),
        name="after_exchange",
    )(returned, out_grad, key, value, tail, following, taps, *grads)


def on_device(
    query_heads,
    key_heads,
    value_heads,
    hyena_query,
    hyena_key,
    hyena_value,
    short_filter,
    long_filter,
    output_grad,
):
    rows, channels = query_heads.shape
    groups = long_filter.shape[1]
    n = lax.axis_size("ctx")
    tp = lax.axis_size("tp")
    cpd, gpd = channels // n, groups // n
    position = lax.axis_index("ctx")
    tail = shifted(edge_rows((hyena_query, hyena_key, hyena_value), False), "ctx", 1)
    half = channels // 2
    chunks = 2 if gpd % 4 == 0 else 1
    cpd, gpd = cpd // chunks, gpd // chunks
    send = before_exchange(
        hyena_query, hyena_key, hyena_value, output_grad, tail, short_filter, long_filter, n, chunks
    )
    send, query, key, value, *sources = lax.optimization_barrier(
        (send, query_heads, key_heads, value_heads, output_grad, hyena_key, hyena_value)
    )
    received = lax.all_to_all(send, "ctx", split_axis=0, concat_axis=0, tiled=True)
    query_next = shifted(query[:, :half], "ctx", -1)
    previous = shifted(jnp.concatenate([key[:, half:], value[:, half:]], 0), "ctx", 1)
    returned = []
    for chunk in range(chunks):
        raw = ()
        if chunk + 1 == chunks:
            raw, squares = filter_products(received, cpd, gpd, chunks)
            raw = (raw, total_over(squares, "tp"))
        results = long_convs(received, raw, cpd, gpd, chunk, chunks)
        if chunk == 0:
            results, received, query_next, previous, *sources = lax.optimization_barrier(
                (results, received, query_next, previous, *sources)
            )
            part = shifted(attend_next(query_next, key_heads, value_heads), "ctx", 1)
            following = shifted(edge_rows(sources, True), "ctx", -1)
        else:
            results, part, following = lax.optimization_barrier((results, part, following))
        returned.append(lax.all_to_all(results, "ctx", split_axis=0, concat_axis=0, tiled=True))
    attention = attend(query_heads, key_heads, value_heads, part, previous, position)
    bound = math.sqrt(rows * n * groups * tp)
    grads = ()
    for chunk in range(chunks):
        if chunk > 0:
            returned[chunk], attention, *grads = lax.optimization_barrier(
                (returned[chunk], attention, *grads)
            )
        grads = after_exchange(
            returned[chunk], output_grad, hyena_key, hyena_value, tail, following, short_filter, groups,
            chunk, chunks, grads, bound,
        )
    return (attention, *grads)


def solution(mesh):
    whole = P("ctx", "tp")
    in_specs = (whole,) * 6 + (P(None, None, "tp"), whole, whole)
    return jax.shard_map(
        on_device, mesh=mesh, in_specs=in_specs, out_specs=(whole,) * 5, check_vma=False
    )
```

```python
import functools
import math

import jax
import jax.numpy as jnp
from jax import lax
from jax.experimental import pallas as pl
from jax.experimental.pallas import tpu as pltpu
from jax.sharding import PartitionSpec as P

HEAD_DIM = 128
LANES = 128
EDGE = 8
F32 = jnp.float32
BF16 = jnp.bfloat16
VMEM_BYTES = 60 * 1024 * 1024
LONG_VMEM = 24 * 1024 * 1024


def params(size=VMEM_BYTES):
    return pltpu.CompilerParams(vmem_limit_bytes=size)


def shifted(block, axis, distance):
    devices = range(lax.axis_size(axis))
    route = [(i - distance, i) for i in devices if i - distance in devices]
    return lax.ppermute(block, axis, route)


def total_over(value, axis):
    size = lax.axis_size(axis)
    distance = 1
    while distance < size:
        value = value + lax.ppermute(value, axis, [(i, i ^ distance) for i in range(size)])
        distance *= 2
    return value


def round_up(value, step):
    return -(-value // step) * step


def reversal(size):
    row = lax.broadcasted_iota(jnp.int32, (size, size), 0)
    col = lax.broadcasted_iota(jnp.int32, (size, size), 1)
    return jnp.where(row + col == size - 1, 1.0, 0.0).astype(BF16)


SCALE = 1.0 / math.sqrt(HEAD_DIM)
NT = (((1,), (1,)), ((), ()))


LOG_LANES = 32


def places_of(width):
    return [slice(head * HEAD_DIM, (head + 1) * HEAD_DIM) for head in range(width // HEAD_DIM)]


def attend_next_kernel(q_ref, k_ref, v_ref, out_ref, logs_ref):
    rows, width = q_ref.shape
    heads = width // HEAD_DIM
    step = pl.program_id(0)
    lane = lax.broadcasted_iota(jnp.int32, (rows, LANES), 1)

    @pl.when(step == 0)
    def _():
        logs_ref[...] = jnp.zeros_like(logs_ref)

    places = places_of(width)
    scores = [
        lax.dot_general(q_ref[:, at], k_ref[:, at], NT, preferred_element_type=F32) * SCALE
        for at in places
    ]
    largest = [jnp.max(score, axis=1, keepdims=True) for score in scores]
    raised = [jnp.exp(score - top) for score, top in zip(scores, largest)]
    totals = [jnp.sum(r, axis=1, keepdims=True) for r in raised]
    weights = [(r * (1.0 / total)).astype(BF16) for r, total in zip(raised, totals)]
    mixed = [
        jnp.dot(weight, v_ref[:, at], preferred_element_type=F32) for weight, at in zip(weights, places)
    ]
    logs = logs_ref[...]
    for head in range(heads):
        log = largest[head] + jnp.log(totals[head])
        logs = jnp.where(lane == step * heads + head, log, logs)
    logs_ref[...] = logs
    first = pl.multiple_of(step * width, LANES)
    out_ref[:, pl.ds(first, width)] = jnp.concatenate([m.astype(BF16) for m in mixed], 1)

    @pl.when(step == pl.num_programs(0) - 1)
    def _():
        upper = logs.astype(BF16).astype(F32)
        middle = (logs - upper).astype(BF16).astype(F32)
        lower = logs - upper - middle
        terms = upper + pltpu.roll(middle, LOG_LANES, 1) + pltpu.roll(lower, 2 * LOG_LANES, 1)
        out_ref[:, out_ref.shape[1] - LANES :] = terms.astype(BF16)


def attend_merge_kernel(place_ref, q_ref, k_ref, v_ref, part_ref, log_ref, _, out_ref):
    rows, width = q_ref.shape
    heads = width // HEAD_DIM
    step = pl.program_id(0)
    row = lax.broadcasted_iota(jnp.int32, (rows, rows), 0)
    col = lax.broadcasted_iota(jnp.int32, (rows, rows), 1)
    own_ok = col <= row
    lane = lax.broadcasted_iota(jnp.int32, (rows, LANES), 1) & (LOG_LANES - 1)
    has_prev = jnp.broadcast_to(place_ref[0], (rows, 1)) > 0
    places = places_of(width)
    terms = log_ref[...].astype(F32)
    scores = [
        lax.dot_general(q_ref[:, at], k_ref[:, at], NT, preferred_element_type=F32) * SCALE
        for at in places
    ]
    scores = [jnp.where(own_ok, score, -jnp.inf) for score in scores]
    logs = [
        jnp.sum(jnp.where(lane == step * heads + head, terms, 0.0), axis=1, keepdims=True)
        for head in range(heads)
    ]
    logs = [jnp.where(has_prev, log, -jnp.inf) for log in logs]
    largest = [
        jnp.maximum(jnp.max(score, axis=1, keepdims=True), log) for score, log in zip(scores, logs)
    ]
    raised = [jnp.exp(score - top) for score, top in zip(scores, largest)]
    prevs = [jnp.exp(log - top) for log, top in zip(logs, largest)]
    inverses = [
        1.0 / (jnp.sum(r, axis=1, keepdims=True) + prev) for r, prev in zip(raised, prevs)
    ]
    weights = [(r * inverse).astype(BF16) for r, inverse in zip(raised, inverses)]
    mixed = [
        jnp.dot(weight, v_ref[:, at], preferred_element_type=F32) for weight, at in zip(weights, places)
    ]
    for head, at in enumerate(places):
        total = mixed[head] + (prevs[head] * inverses[head]) * part_ref[:, at].astype(F32)
        out_ref[:, at] = total.astype(BF16)


def attend_whole_kernel(place_ref, q_ref, k_ref, v_ref, kp_ref, vp_ref, out_ref):
    rows, width = q_ref.shape
    row = lax.broadcasted_iota(jnp.int32, (rows, rows), 0)
    col = lax.broadcasted_iota(jnp.int32, (rows, rows), 1)
    own_ok = col <= row
    prev_ok = jnp.broadcast_to(place_ref[0], (rows, rows)) > 0
    places = places_of(width)

    def scores(ref, allowed):
        products = [
            lax.dot_general(q_ref[:, at], ref[:, at], NT, preferred_element_type=F32) for at in places
        ]
        return [jnp.where(allowed, product * SCALE, -jnp.inf) for product in products]

    own, prev = scores(k_ref, own_ok), scores(kp_ref, prev_ok)
    largest = [jnp.max(jnp.maximum(o, p), axis=1, keepdims=True) for o, p in zip(own, prev)]
    own = [jnp.exp(o - top) for o, top in zip(own, largest)]
    prev = [jnp.exp(p - top) for p, top in zip(prev, largest)]
    totals = [jnp.sum(o + p, axis=1, keepdims=True) for o, p in zip(own, prev)]
    inverses = [1.0 / total for total in totals]
    own = [(o * inverse).astype(BF16) for o, inverse in zip(own, inverses)]
    prev = [(p * inverse).astype(BF16) for p, inverse in zip(prev, inverses)]
    mixed = [
        jnp.dot(o, v_ref[:, at], preferred_element_type=F32)
        + jnp.dot(p, vp_ref[:, at], preferred_element_type=F32)
        for o, p, at in zip(own, prev, places)
    ]
    for head, at in enumerate(places):
        out_ref[:, at] = mixed[head].astype(BF16)


def attend_cost(rows, channels):
    heads = channels // HEAD_DIM
    return pl.CostEstimate(
        flops=4 * heads * rows * rows * HEAD_DIM,
        bytes_accessed=10 * rows * channels,
        transcendentals=heads * rows * rows,
    )


def attend_next(query, key, value):
    rows, channels = query.shape
    tile = min(512, channels)
    block = pl.BlockSpec((rows, tile), lambda i: (0, i))
    return pl.pallas_call(
        attend_next_kernel,
        grid=(channels // tile,),
        in_specs=[block] * 3,
        out_specs=pl.BlockSpec((rows, channels + LANES), lambda i: (0, 0)),
        out_shape=jax.ShapeDtypeStruct((rows, channels + LANES), BF16),
        scratch_shapes=[pltpu.VMEM((rows, LANES), F32)],
        compiler_params=params(LONG_VMEM),
        cost_estimate=attend_cost(rows, channels),
        name="attend_next",
    )(query, key, value)


def attend(query, key, value, part, previous, position):
    rows, channels = query.shape
    half = channels // 2
    tile = min(512, half)
    steps = half // tile
    place = position.astype(jnp.int32).reshape(1)
    smem = pl.BlockSpec(memory_space=pltpu.SMEM)
    first = pl.BlockSpec((rows, tile), lambda i: (0, i))
    second = pl.BlockSpec((rows, tile), lambda i: (0, steps + i))
    out = jax.ShapeDtypeStruct((rows, channels), BF16)
    whole = pl.pallas_call(
        attend_whole_kernel,
        grid=(steps,),
        in_specs=[smem, second, second, second, first, pl.BlockSpec((rows, tile), lambda i: (1, i))],
        out_specs=second,
        out_shape=out,
        compiler_params=params(LONG_VMEM),
        cost_estimate=attend_cost(rows, channels),
        name="attend_whole",
    )(place, query, key, value, previous, previous)
    log_at = half // LANES
    return pl.pallas_call(
        attend_merge_kernel,
        grid=(steps,),
        in_specs=[
            smem,
            first,
            first,
            first,
            first,
            pl.BlockSpec((rows, LANES), lambda i: (0, log_at)),
            pl.BlockSpec(memory_space=pl.ANY),
        ],
        out_specs=first,
        out_shape=out,
        input_output_aliases={6: 0},
        compiler_params=params(LONG_VMEM),
        cost_estimate=attend_cost(rows, half),
        name="attend_merge",
    )(place, query, key, value, part, part, whole)


def edge_kernel(first, *refs):
    *sources, out_ref = refs
    parts = [r[...].astype(F32) for r in sources]
    parts = [p[:EDGE] if first else p[p.shape[0] - EDGE :] for p in parts]
    out_ref[...] = jnp.concatenate(parts, 0).astype(BF16)


def edge_rows(arrays, first):
    rows, channels = arrays[0].shape
    block = pl.BlockSpec((16, channels), lambda i: (0 if first else rows // 16 - 1, 0))
    return pl.pallas_call(
        functools.partial(edge_kernel, first),
        grid=(1,),
        in_specs=[block] * len(arrays),
        out_specs=pl.BlockSpec((len(arrays) * EDGE, channels), lambda i: (0, 0)),
        out_shape=jax.ShapeDtypeStruct((len(arrays) * EDGE, channels), BF16),
        compiler_params=params(LONG_VMEM if first else VMEM_BYTES),
        name="edge_rows",
    )(*arrays)


def taps_causal(ext_ref, befores, signals, filters):
    rows = signals[0].shape[0]
    for j, signal in enumerate(signals):
        ext_ref[j, 0:EDGE, :] = befores[j]
        ext_ref[j, EDGE : EDGE + rows, :] = signal
    totals = [taps[0:1] * signal for signal, taps in zip(signals, filters)]
    for s in range(1, filters[0].shape[0]):
        for j, taps in enumerate(filters):
            totals[j] = totals[j] + taps[s : s + 1] * ext_ref[j, EDGE - s : EDGE - s + rows, :]
    return totals


def columns_of(width):
    return [slice(j * LANES, (j + 1) * LANES) for j in range(width // LANES)]


PAIR = 2


def put_pairs(ref, dest, channel, gw, first, second):
    width = PAIR * gw
    for piece in range(first.shape[0] // width):
        at = slice(piece * width, (piece + 1) * width)
        low = 2 * (channel + piece * width)
        ref[dest, low : low + width, :] = first[at]
        ref[dest, low + width : low + 2 * width, :] = second[at]


def get_pairs(ref, dest, channel, count, gw, which):
    width = PAIR * gw
    lows = [2 * (channel + low) + which * width for low in range(0, count, width)]
    return jnp.concatenate([ref[dest, low : low + width, :] for low in lows], 0)


def before_kernel(cpd, gpd, chunks, *refs):
    *refs, long_ref, send_ref, long_rows, ext_q, ext_k, ext_v = refs
    step = pl.program_id(0)
    groups = long_ref.shape[1]
    per_tile, send_rows, rows = send_ref.shape
    gw = cpd // gpd
    filter_rows = send_rows - 2 * cpd * chunks
    half = groups // chunks

    @pl.when(step == 0)
    def _():
        long_rows[...] = jnp.zeros_like(long_rows)
        long_rows[0:groups, :] = long_ref[...].T

    turn = reversal(rows)
    for chunk in range(chunks):
        q_ref, k_ref, v_ref, og_ref, tail_ref, taps_ref = refs[6 * chunk : 6 * chunk + 6]
        places = columns_of(q_ref.shape[1])
        tails = [tail_ref[:, at].astype(F32) for at in places]

        def short(which, ref, ext, tails=tails, places=places, taps_ref=taps_ref, chunk=chunk):
            return taps_causal(
                ext.at[chunk],
                [tail[which * EDGE : (which + 1) * EDGE] for tail in tails],
                [ref[:, at].astype(F32) for at in places],
                [taps_ref[which, :, at] for at in places],
            )

        short_k, short_v = short(1, k_ref, ext_k), short(2, v_ref, ext_v)
        mixed = [(k * v).T.astype(BF16) for k, v in zip(short_k, short_v)]
        short_q = short(0, q_ref, ext_q)
        delta = [(og_ref[:, at].astype(F32) * q).T.astype(BF16) for q, at in zip(short_q, places)]
        delta = [jnp.dot(d, turn, preferred_element_type=F32).astype(BF16) for d in delta]
        width = min(cpd, LANES)
        for j in range(len(places)):
            for piece in range(LANES // width):
                channel = j * LANES + piece * width
                dest, low = channel // cpd, channel % cpd
                at = slice(piece * width, (piece + 1) * width)
                put_pairs(send_ref, dest, chunk * cpd + low, gw, mixed[j][at], delta[j][at])
    for dest in range(per_tile):
        lines = []
        for chunk in range(chunks):
            first = chunk * half + (step * per_tile + dest) * gpd
            lines.append(long_rows[pl.ds(first, filter_rows if chunks == 1 else gpd), :])
        send_ref[dest, 2 * cpd * chunks :, :] = jnp.concatenate(lines, 0).astype(BF16)


def before_exchange(query, key, value, out_grad, tail, taps, long_filter, n, chunks):
    rows, channels = query.shape
    groups = long_filter.shape[1]
    cpd, gpd = channels // (n * chunks), groups // (n * chunks)
    tile = min(channels // chunks, max(512 // chunks, cpd))
    per_tile = tile // cpd
    filter_rows = round_up(gpd * chunks, 16)
    send_rows = 2 * cpd * chunks + filter_rows
    steps = n // per_tile
    specs = []
    for chunk in range(chunks):
        first = chunk * steps
        specs += [pl.BlockSpec((rows, tile), lambda i, f=first: (0, f + i))] * 4
        specs.append(pl.BlockSpec((3 * EDGE, tile), lambda i, f=first: (0, f + i)))
        specs.append(pl.BlockSpec((3, taps.shape[1], tile), lambda i, f=first: (0, 0, f + i)))
    ext = pltpu.VMEM((chunks, tile // LANES, rows + EDGE, LANES), F32)
    return pl.pallas_call(
        functools.partial(before_kernel, cpd, gpd, chunks),
        grid=(steps,),
        in_specs=specs + [pl.BlockSpec((rows, groups), lambda i: (0, 0))],
        out_specs=pl.BlockSpec((per_tile, send_rows, rows), lambda i: (i, 0, 0)),
        out_shape=jax.ShapeDtypeStruct((n, send_rows, rows), BF16),
        scratch_shapes=[pltpu.VMEM((round_up(groups, 8) + filter_rows, rows), F32), ext, ext, ext],
        compiler_params=params(),
        cost_estimate=pl.CostEstimate(
            flops=50 * rows * channels, bytes_accessed=12 * rows * channels, transcendentals=0
        ),
        name="before_exchange",
    )(*((query, key, value, out_grad, tail, taps) * chunks), long_filter)


def conv_kernel(cpd, gpd, chunk, in_ref, filter_ref, *refs):
    *raw_ref, out_ref, taps, wide = refs
    step = pl.program_id(0)
    n, _, rows = in_ref.shape
    gw = cpd // gpd
    span = n * rows
    slots = range(PAIR)

    @pl.when(step == 0)
    def _():
        taps[:, 0:rows] = jnp.zeros((taps.shape[0], rows), F32)
        for a in range(n):
            taps[:, (a + 1) * rows : (a + 2) * rows] = filter_ref[a].astype(F32)
        for slot in slots:
            wide[slot, :, 0:rows] = jnp.zeros((rows, rows), BF16)

    bases = []
    for slot in slots:
        line = taps[pl.ds(chunk * gpd + PAIR * step + slot, 1), :]
        line = jnp.broadcast_to(line, (16, span + rows))
        bases.append(pltpu.roll(line, 0, 1, stride=1, stride_axis=0).astype(BF16))
    for m in range(rows // 16):
        for slot in slots:
            moved = bases[slot] if m == 0 else pltpu.roll(bases[slot], 16 * m, 1)
            wide[slot, 16 * m : 16 * m + 16, rows:] = moved[:, rows:]
    stacks = []
    for slot in slots:
        x = in_ref[:, slot * gw : (slot + 1) * gw, :]
        d = in_ref[:, (PAIR + slot) * gw : (PAIR + slot + 1) * gw, :]
        both = [jnp.concatenate([x[a], d[n - 1 - a]], 0) for a in range(n)]
        stacks.append(
            jnp.concatenate([jnp.concatenate([both[a], both[a + 1]], 1) for a in range(0, n, 2)], 0)
        )
    totals = [None] * PAIR
    for k in range(n // 2):
        skip = 2 * gw * k
        low = 2 * rows * k
        for slot in slots:
            tile = jnp.concatenate(
                [wide[slot, :, low + rows : low + 3 * rows], wide[slot, :, low : low + 2 * rows]], 0
            )
            part = jnp.dot(stacks[slot][: n * gw - skip], tile, preferred_element_type=F32)
            total = totals[slot]
            totals[slot] = part if k == 0 else jnp.concatenate([total[:skip], total[skip:] + part], 0)
    for slot in slots:
        total = totals[slot]
        first = pl.multiple_of(2 * PAIR * gw * step + slot * gw, gw)
        second = pl.multiple_of(2 * PAIR * gw * step + (PAIR + slot) * gw, gw)
        for a in range(n):
            at = slice(a % 2 * rows, (a % 2 + 1) * rows)
            top = a // 2 * 2 * gw
            out_ref[a, pl.ds(first, gw), :] = total[top : top + gw, at].astype(BF16)
            out_ref[n - 1 - a, pl.ds(second, gw), :] = total[top + gw : top + 2 * gw, at].astype(BF16)

    @pl.when(step == pl.num_programs(0) - 1)
    def _():
        finish_conv(cpd, gw, out_ref, raw_ref)


def finish_conv(cpd, gw, out_ref, raw_ref):
    n, _, rows = out_ref.shape
    upper = lower = 0.0
    if raw_ref:
        *raw_ref, squares_ref = raw_ref
        upper = squares_ref[...].astype(BF16).astype(F32)
        lower = squares_ref[...] - upper
    halo_at = 2 * cpd
    row = lax.broadcasted_iota(jnp.int32, (2 * EDGE, 2 * rows), 0)
    lane = lax.broadcasted_iota(jnp.int32, (2 * EDGE, 2 * rows), 1)
    wanted = jnp.where(row < EDGE, row, 2 * rows - 1 + EDGE - row)
    pick = jnp.where(lane == wanted, 1.0, 0.0).astype(BF16)
    row_out = lax.broadcasted_iota(jnp.int32, (2 * EDGE, rows), 0)
    for a in range(n):
        if a + 1 < n:
            results = [get_pairs(out_ref, a + 1, 0, cpd, gw, which) for which in range(2)]
            results = jnp.concatenate(results, 1)
            halo = lax.dot_general(
                pick, results, (((1,), (1,)), ((), ())), preferred_element_type=F32
            )
            if cpd < LANES:
                halo = jnp.concatenate([halo, jnp.zeros((2 * EDGE, LANES - cpd), F32)], 1)
        else:
            halo = jnp.zeros((2 * EDGE, max(cpd, LANES)), F32)
        for j in range(halo.shape[1] // LANES):
            at = halo_at + 2 * EDGE * j
            tile = halo[:, j * LANES : (j + 1) * LANES]
            tile = jnp.where(row_out == EDGE - 2, upper, jnp.where(row_out == EDGE - 1, lower, tile))
            out_ref[a, at : at + 2 * EDGE, :] = tile.astype(BF16)
    for ref in raw_ref:
        out_ref[:, out_ref.shape[1] - ref.shape[1] :, :] = ref[...]


def long_convs(received, raw, cpd, gpd, chunk, chunks):
    n, send_rows, rows = received.shape
    filter_rows = send_rows - 2 * cpd * chunks
    out_rows = 2 * cpd + 2 * EDGE * max(1, cpd // LANES) + sum(r.shape[1] for r in raw[:1])
    span = n * rows
    pairs = gpd // PAIR
    pair_rows = 2 * cpd // pairs
    filter_at = 2 * cpd * chunks // filter_rows
    return pl.pallas_call(
        functools.partial(conv_kernel, cpd, gpd, chunk),
        grid=(pairs,),
        in_specs=[
            pl.BlockSpec((n, pair_rows, rows), lambda i: (0, chunk * pairs + i, 0)),
            pl.BlockSpec((n, filter_rows, rows), lambda i: (0, filter_at, 0)),
        ]
        + [pl.BlockSpec(r.shape, lambda i, r=r: (0,) * r.ndim) for r in raw],
        out_specs=pl.BlockSpec((n, out_rows, rows), lambda i: (0, 0, 0)),
        out_shape=jax.ShapeDtypeStruct((n, out_rows, rows), BF16),
        scratch_shapes=[
            pltpu.VMEM((filter_rows, span + rows), F32),
            pltpu.VMEM((PAIR, rows, span + rows), BF16),
        ],
        compiler_params=params(LONG_VMEM),
        cost_estimate=pl.CostEstimate(
            flops=4 * cpd * span * span, bytes_accessed=4 * n * out_rows * rows, transcendentals=0
        ),
        name="long_convs",
    )(received, received, *raw)


def gram_kernel(gw, in_ref, out_ref, squares_ref, gram, raw, total_ref):
    step = pl.program_id(0)
    n, _, rows = in_ref.shape
    span = n * rows
    slots = range(PAIR)

    @pl.when(step == 0)
    def _():
        for slot in slots:
            gram[slot, :, span:] = jnp.zeros((rows, rows), F32)
        raw[...] = jnp.zeros_like(raw)
        total_ref[...] = jnp.zeros_like(total_ref)

    no_rows = jnp.zeros((n * gw, rows), BF16)

    def offset(d, k):
        held = (k + 1) * gw
        if held == n * gw:
            return d
        return jnp.concatenate([d[n * gw - held :], no_rows[held:]], 0)

    turned, shifting = [], []
    for slot in slots:
        x = in_ref[:, slot * gw : (slot + 1) * gw, :].reshape(n * gw, rows)
        d = in_ref[:, (PAIR + slot) * gw : (PAIR + slot + 1) * gw, :]
        shifting.append(d.reshape(n * gw, rows))
        turned.append(x.astype(F32).T.astype(BF16))
    for k in range(0, n, 2):
        for slot in slots:
            d = shifting[slot]
            pairs = jnp.concatenate([offset(d, k), offset(d, k + 1)], 1)
            gram[slot, :, k * rows : (k + 2) * rows] = jnp.dot(
                turned[slot], pairs, preferred_element_type=F32
            )
    sums = [gram[slot, 0:8, :] for slot in slots]
    for m in range(1, rows // 8):
        for slot in slots:
            sums[slot] = sums[slot] + pltpu.roll(gram[slot, 8 * m : 8 * m + 8, :], 8 * m, 1)
    sums = [pltpu.roll(total, 0, 1, stride=1, stride_axis=0) for total in sums]
    for slot in slots:
        line = jnp.sum(sums[slot], axis=0, keepdims=True)[:, :span]
        raw[pl.ds(PAIR * step + slot, 1), :] = line
        total_ref[...] = total_ref[...] + line * line

    @pl.when(step == pl.num_programs(0) - 1)
    def _():
        squares_ref[...] = jnp.sum(total_ref[...], axis=1, keepdims=True)
        turn = reversal(rows)
        for a in range(n):
            tile = raw[:, (n - 1 - a) * rows : (n - a) * rows].astype(BF16)
            out_ref[a] = jnp.dot(tile, turn, preferred_element_type=F32).astype(BF16)


def filter_products(received, cpd, gpd, chunks):
    n, _, rows = received.shape
    span = n * rows
    raw_rows = round_up(gpd * chunks, 16)
    pairs = gpd * chunks // PAIR
    pair_rows = 2 * cpd * chunks // pairs
    return pl.pallas_call(
        functools.partial(gram_kernel, cpd // gpd),
        grid=(pairs,),
        in_specs=[pl.BlockSpec((n, pair_rows, rows), lambda i: (0, i, 0))],
        out_specs=[
            pl.BlockSpec((n, raw_rows, rows), lambda i: (0, 0, 0)),
            pl.BlockSpec((1, 1), lambda i: (0, 0)),
        ],
        out_shape=[
            jax.ShapeDtypeStruct((n, raw_rows, rows), BF16),
            jax.ShapeDtypeStruct((1, 1), F32),
        ],
        scratch_shapes=[
            pltpu.VMEM((PAIR, rows, span + rows), F32),
            pltpu.VMEM((raw_rows, span), F32),
            pltpu.VMEM((1, span), F32),
        ],
        compiler_params=params(LONG_VMEM),
        cost_estimate=pl.CostEstimate(
            flops=2 * cpd * chunks * span * span,
            bytes_accessed=2 * received.size,
            transcendentals=0,
        ),
        name="filter_products",
    )(received)


def taps_anti(ext_ref, signals, afters, filters):
    rows = signals[0].shape[0]
    for j, signal in enumerate(signals):
        ext_ref[j, 0:rows, :] = signal
        ext_ref[j, rows : rows + EDGE, :] = afters[j]
    totals = [taps[0:1] * signal for signal, taps in zip(signals, filters)]
    for s in range(1, filters[0].shape[0]):
        for j, taps in enumerate(filters):
            totals[j] = totals[j] + taps[s : s + 1] * ext_ref[j, s : s + rows, :]
    return totals


def short_edge(before, signal, filter_taps):
    both = jnp.concatenate([before, signal], 0)
    total = filter_taps[0:1] * signal
    for s in range(1, filter_taps.shape[0]):
        total = total + filter_taps[s : s + 1] * both[EDGE - s : 2 * EDGE - s]
    return total


def after_kernel(
    cpd, gpd, chunks, last, bound, in_ref, og_ref, k_ref, v_ref, tail_ref, next_ref, taps_ref, *refs
):
    *refs, ext_q, ext_k, ext_v, ext_in_k, ext_in_v = refs
    if last:
        *refs, raw_ref, raw_rows, total_ref = refs
    dq_ref, dk_ref, dv_ref = refs[-3:]
    step = pl.program_id(0)
    per_tile, in_rows, rows = in_ref.shape
    halo_rows = 2 * EDGE * max(1, cpd // LANES)
    halo_at = 2 * cpd
    turn = reversal(rows)
    places = columns_of(og_ref.shape[1])
    tails = [tail_ref[:, at].astype(F32) for at in places]
    nexts = [next_ref[:, at].astype(F32) for at in places]
    convs, backs, halos = [], [], []
    for j in range(len(places)):
        if cpd >= LANES:
            dest, low = j * LANES // cpd, j * LANES % cpd
            conv = get_pairs(in_ref, dest, low, LANES, cpd // gpd, 0)
            back = get_pairs(in_ref, dest, low, LANES, cpd // gpd, 1)
            edge = halo_at + 2 * EDGE * (low // LANES)
            halo = in_ref[dest, edge : edge + 2 * EDGE, :].astype(F32)
        else:
            dests = range(j * LANES // cpd, (j + 1) * LANES // cpd)
            conv = jnp.concatenate([get_pairs(in_ref, d, 0, cpd, cpd // gpd, 0) for d in dests], 0)
            back = jnp.concatenate([get_pairs(in_ref, d, 0, cpd, cpd // gpd, 1) for d in dests], 0)
            halo = jnp.concatenate(
                [in_ref[d, halo_at : halo_at + halo_rows, :].astype(F32)[:, :cpd] for d in dests], 1
            )
        convs.append(conv)
        backs.append(back)
        halos.append(halo)
    convs = [conv.astype(F32).T for conv in convs]
    backs = [jnp.dot(back, turn, preferred_element_type=F32) for back in backs]
    backs = [back.T for back in backs]
    taps = [[taps_ref[which, :, at] for at in places] for which in range(3)]
    keys = [k_ref[:, at].astype(F32) for at in places]
    values = [v_ref[:, at].astype(F32) for at in places]
    short_k = taps_causal(ext_in_k, [tail[EDGE : 2 * EDGE] for tail in tails], keys, taps[1])
    short_v = taps_causal(ext_in_v, [tail[2 * EDGE : 3 * EDGE] for tail in tails], values, taps[2])
    next_k = [
        short_edge(k[rows - EDGE :], f[EDGE : 2 * EDGE], t) for k, f, t in zip(keys, nexts, taps[1])
    ]
    next_v = [
        short_edge(v[rows - EDGE :], f[2 * EDGE : 3 * EDGE], t)
        for v, f, t in zip(values, nexts, taps[2])
    ]

    def store(ref, ext, signals, afters, filters):
        for at, total in zip(places, taps_anti(ext, signals, afters, filters)):
            ref[:, at] = total.astype(BF16)

    store(
        dq_ref,
        ext_q,
        [og_ref[:, at].astype(F32) * conv for at, conv in zip(places, convs)],
        [f[0:EDGE] * halo[0:EDGE] for f, halo in zip(nexts, halos)],
        taps[0],
    )
    store(
        dk_ref,
        ext_k,
        [back * v for back, v in zip(backs, short_v)],
        [halo[EDGE:] * v for halo, v in zip(halos, next_v)],
        taps[1],
    )
    store(
        dv_ref,
        ext_v,
        [back * k for back, k in zip(backs, short_k)],
        [halo[EDGE:] * k for halo, k in zip(halos, next_k)],
        taps[2],
    )
    if not last:
        return
    squares = jnp.zeros((1, LANES), F32)
    for dest in range(per_tile):
        parts = in_ref[dest, halo_at : halo_at + 2 * EDGE, :].astype(F32)
        squares = squares + parts[EDGE - 2 : EDGE - 1] + parts[EDGE - 1 : EDGE]

    @pl.when(step == 0)
    def _():
        total_ref[...] = jnp.zeros_like(total_ref)

    total_ref[...] = total_ref[...] + squares
    half = raw_rows.shape[0] // chunks
    for dest in range(per_tile):
        lines = in_ref[dest, halo_at + halo_rows :, :].astype(F32)
        for chunk in range(chunks):
            at = chunk * half + (step * per_tile + dest) * gpd
            raw_rows[pl.ds(at, gpd), :] = lines[chunk * gpd : (chunk + 1) * gpd]

    @pl.when(step == pl.num_programs(0) - 1)
    def _():
        factor = jnp.minimum(1.0, bound / jnp.sqrt(total_ref[...]))[:, 0:1]
        raw_ref[...] = raw_rows[...].T * factor


def after_exchange(
    returned, out_grad, key, value, tail, following, taps, groups, chunk, chunks, grads, bound
):
    n, in_rows, rows = returned.shape
    channels = out_grad.shape[1] // chunks
    cpd, gpd = channels // n, groups // (n * chunks)
    last = chunk + 1 == chunks
    tile = min(channels, max(512, cpd))
    per_tile = tile // cpd
    first = chunk * channels // tile
    block = pl.BlockSpec((rows, tile), lambda i: (0, first + i))
    ext = pltpu.VMEM((tile // LANES, rows + EDGE, LANES), F32)
    grad = jax.ShapeDtypeStruct(out_grad.shape, BF16)
    return pl.pallas_call(
        functools.partial(after_kernel, cpd, gpd, chunks, last, bound),
        grid=(channels // tile,),
        in_specs=[
            pl.BlockSpec((per_tile, in_rows, rows), lambda i: (i, 0, 0)),
            block,
            block,
            block,
            pl.BlockSpec((3 * EDGE, tile), lambda i: (0, first + i)),
            pl.BlockSpec((3 * EDGE, tile), lambda i: (0, first + i)),
            pl.BlockSpec((3, taps.shape[1], tile), lambda i: (0, 0, first + i)),
        ]
        + [pl.BlockSpec(memory_space=pl.ANY)] * len(grads),
        input_output_aliases={7 + i: i for i in range(len(grads))},
        out_specs=[block] * 3 + [pl.BlockSpec((rows, groups), lambda i: (0, 0))] * last,
        out_shape=[grad] * 3 + [jax.ShapeDtypeStruct((rows, groups), F32)] * last,
        scratch_shapes=[pltpu.VMEM((groups, rows), F32), pltpu.VMEM((1, LANES), F32)] * last
        + [ext] * 5,
        compiler_params=params(LONG_VMEM),
        cost_estimate=pl.CostEstimate(
            flops=90 * rows * channels, bytes_accessed=18 * rows * channels, transcendentals=0
        ),
        name="after_exchange",
    )(returned, out_grad, key, value, tail, following, taps, *grads)


def on_device(
    query_heads,
    key_heads,
    value_heads,
    hyena_query,
    hyena_key,
    hyena_value,
    short_filter,
    long_filter,
    output_grad,
):
    rows, channels = query_heads.shape
    groups = long_filter.shape[1]
    n = lax.axis_size("ctx")
    tp = lax.axis_size("tp")
    cpd, gpd = channels // n, groups // n
    position = lax.axis_index("ctx")
    tail = shifted(edge_rows((hyena_query, hyena_key, hyena_value), False), "ctx", 1)
    half = channels // 2
    chunks = 2 if gpd % 4 == 0 else 1
    cpd, gpd = cpd // chunks, gpd // chunks
    send = before_exchange(
        hyena_query, hyena_key, hyena_value, output_grad, tail, short_filter, long_filter, n, chunks
    )
    send, query, key, value, *sources = lax.optimization_barrier(
        (send, query_heads, key_heads, value_heads, output_grad, hyena_key, hyena_value)
    )
    received = lax.all_to_all(send, "ctx", split_axis=0, concat_axis=0, tiled=True)
    following = shifted(edge_rows(sources, True), "ctx", -1)
    query_next = shifted(query[:, :half], "ctx", -1)
    previous = shifted(jnp.concatenate([key[:, half:], value[:, half:]], 0), "ctx", 1)
    returned = []
    for chunk in range(chunks):
        raw = ()
        if chunk + 1 == chunks:
            raw, squares = filter_products(received, cpd, gpd, chunks)
            query_next, raw, squares = lax.optimization_barrier((query_next, raw, squares))
            raw = (raw, total_over(squares, "tp"))
        results = long_convs(received, raw, cpd, gpd, chunk, chunks)
        if chunk + 1 == chunks:
            part = shifted(attend_next(query_next, key_heads, value_heads), "ctx", 1)
        if chunk == 0:
            results, received, query_next, previous, following = lax.optimization_barrier(
                (results, received, query_next, previous, following)
            )
        else:
            results, part = lax.optimization_barrier((results, part))
        returned.append(lax.all_to_all(results, "ctx", split_axis=0, concat_axis=0, tiled=True))
    attention = attend(query_heads, key_heads, value_heads, part, previous, position)
    bound = math.sqrt(rows * n * groups * tp)
    grads = ()
    for chunk in range(chunks):
        if chunk > 0:
            returned[chunk], attention, *grads = lax.optimization_barrier(
                (returned[chunk], attention, *grads)
            )
        grads = after_exchange(
            returned[chunk], output_grad, hyena_key, hyena_value, tail, following, short_filter, groups,
            chunk, chunks, grads, bound,
        )
    return (attention, *grads)


def solution(mesh):
    whole = P("ctx", "tp")
    in_specs = (whole,) * 6 + (P(None, None, "tp"), whole, whole)
    return jax.shard_map(
        on_device, mesh=mesh, in_specs=in_specs, out_specs=(whole,) * 5, check_vma=False
    )
```

```python
import functools
import math

import jax
import jax.numpy as jnp
from jax import lax
from jax.experimental import pallas as pl
from jax.experimental.pallas import tpu as pltpu
from jax.sharding import PartitionSpec as P

HEAD_DIM = 128
LANES = 128
EDGE = 8
F32 = jnp.float32
BF16 = jnp.bfloat16
VMEM_BYTES = 60 * 1024 * 1024
LONG_VMEM = 24 * 1024 * 1024


def params(size=VMEM_BYTES):
    return pltpu.CompilerParams(vmem_limit_bytes=size)


def shifted(block, axis, distance):
    devices = range(lax.axis_size(axis))
    route = [(i - distance, i) for i in devices if i - distance in devices]
    return lax.ppermute(block, axis, route)


def total_over(value, axis):
    size = lax.axis_size(axis)
    distance = 1
    while distance < size:
        value = value + lax.ppermute(value, axis, [(i, i ^ distance) for i in range(size)])
        distance *= 2
    return value


def round_up(value, step):
    return -(-value // step) * step


def reversal(size):
    row = lax.broadcasted_iota(jnp.int32, (size, size), 0)
    col = lax.broadcasted_iota(jnp.int32, (size, size), 1)
    return jnp.where(row + col == size - 1, 1.0, 0.0).astype(BF16)


SCALE = 1.0 / math.sqrt(HEAD_DIM)
NT = (((1,), (1,)), ((), ()))


LOG_LANES = 32


def places_of(width):
    return [slice(head * HEAD_DIM, (head + 1) * HEAD_DIM) for head in range(width // HEAD_DIM)]


def attend_part_kernel(causal, q_ref, k_ref, v_ref, out_ref, logs_ref):
    rows, width = q_ref.shape
    heads = width // HEAD_DIM
    step = pl.program_id(0)
    row = lax.broadcasted_iota(jnp.int32, (rows, rows), 0)
    col = lax.broadcasted_iota(jnp.int32, (rows, rows), 1)
    lane = lax.broadcasted_iota(jnp.int32, (rows, LANES), 1)

    @pl.when(step == 0)
    def _():
        logs_ref[...] = jnp.zeros_like(logs_ref)

    places = places_of(width)
    scores = [
        lax.dot_general(q_ref[:, at], k_ref[:, at], NT, preferred_element_type=F32) * SCALE
        for at in places
    ]
    if causal:
        scores = [jnp.where(col <= row, score, -jnp.inf) for score in scores]
    largest = [jnp.max(score, axis=1, keepdims=True) for score in scores]
    raised = [jnp.exp(score - top) for score, top in zip(scores, largest)]
    totals = [jnp.sum(r, axis=1, keepdims=True) for r in raised]
    weights = [(r * (1.0 / total)).astype(BF16) for r, total in zip(raised, totals)]
    mixed = [
        jnp.dot(weight, v_ref[:, at], preferred_element_type=F32) for weight, at in zip(weights, places)
    ]
    logs = logs_ref[...]
    for head in range(heads):
        log = largest[head] + jnp.log(totals[head])
        logs = jnp.where(lane == step * heads + head, log, logs)
    logs_ref[...] = logs
    first = pl.multiple_of(step * width, LANES)
    out_ref[:, pl.ds(first, width)] = jnp.concatenate([m.astype(BF16) for m in mixed], 1)

    @pl.when(step == pl.num_programs(0) - 1)
    def _():
        upper = logs.astype(BF16).astype(F32)
        middle = (logs - upper).astype(BF16).astype(F32)
        lower = logs - upper - middle
        terms = upper + pltpu.roll(middle, LOG_LANES, 1) + pltpu.roll(lower, 2 * LOG_LANES, 1)
        out_ref[:, out_ref.shape[1] - LANES :] = terms.astype(BF16)


def combine_kernel(place_ref, own_ref, prev_ref, own_log_ref, prev_log_ref, _, out_ref, own_share, prev_share):
    rows, width = own_ref.shape
    heads = width // HEAD_DIM
    step = pl.program_id(0)
    lane = lax.broadcasted_iota(jnp.int32, (rows, LANES), 1)

    @pl.when(step == 0)
    def _():
        def joined(ref):
            terms = ref[...].astype(F32)
            middle = pltpu.roll(terms, LANES - LOG_LANES, 1)
            return terms + (middle + pltpu.roll(terms, LANES - 2 * LOG_LANES, 1))

        own = joined(own_log_ref)
        has_prev = jnp.broadcast_to(place_ref[0], (rows, LANES)) > 0
        prev = jnp.where(has_prev, joined(prev_log_ref), -jnp.inf)
        largest = jnp.maximum(own, prev)
        own, prev = jnp.exp(own - largest), jnp.exp(prev - largest)
        inverse = 1.0 / (own + prev)
        own_share[...] = own * inverse
        prev_share[...] = prev * inverse

    def column(ref, head):
        return jnp.sum(jnp.where(lane == step * heads + head, ref[...], 0.0), axis=1, keepdims=True)

    owns = [column(own_share, head) for head in range(heads)]
    prevs = [column(prev_share, head) for head in range(heads)]
    for head, at in enumerate(places_of(width)):
        total = owns[head] * own_ref[:, at].astype(F32) + prevs[head] * prev_ref[:, at].astype(F32)
        out_ref[:, at] = total.astype(BF16)


def attend_whole_kernel(place_ref, q_ref, k_ref, v_ref, kp_ref, vp_ref, out_ref):
    rows, width = q_ref.shape
    row = lax.broadcasted_iota(jnp.int32, (rows, rows), 0)
    col = lax.broadcasted_iota(jnp.int32, (rows, rows), 1)
    own_ok = col <= row
    prev_ok = jnp.broadcast_to(place_ref[0], (rows, rows)) > 0
    places = places_of(width)

    def scores(ref, allowed):
        products = [
            lax.dot_general(q_ref[:, at], ref[:, at], NT, preferred_element_type=F32) for at in places
        ]
        return [jnp.where(allowed, product * SCALE, -jnp.inf) for product in products]

    own, prev = scores(k_ref, own_ok), scores(kp_ref, prev_ok)
    largest = [jnp.max(jnp.maximum(o, p), axis=1, keepdims=True) for o, p in zip(own, prev)]
    own = [jnp.exp(o - top) for o, top in zip(own, largest)]
    prev = [jnp.exp(p - top) for p, top in zip(prev, largest)]
    totals = [jnp.sum(o + p, axis=1, keepdims=True) for o, p in zip(own, prev)]
    inverses = [1.0 / total for total in totals]
    own = [(o * inverse).astype(BF16) for o, inverse in zip(own, inverses)]
    prev = [(p * inverse).astype(BF16) for p, inverse in zip(prev, inverses)]
    mixed = [
        jnp.dot(o, v_ref[:, at], preferred_element_type=F32)
        + jnp.dot(p, vp_ref[:, at], preferred_element_type=F32)
        for o, p, at in zip(own, prev, places)
    ]
    for head, at in enumerate(places):
        out_ref[:, at] = mixed[head].astype(BF16)


def attend_cost(rows, channels):
    heads = channels // HEAD_DIM
    return pl.CostEstimate(
        flops=4 * heads * rows * rows * HEAD_DIM,
        bytes_accessed=10 * rows * channels,
        transcendentals=heads * rows * rows,
    )


def attend_part(query, key, value, channels, causal):
    rows = query.shape[0]
    tile = min(512, channels)
    block = pl.BlockSpec((rows, tile), lambda i: (0, i))
    return pl.pallas_call(
        functools.partial(attend_part_kernel, causal),
        grid=(channels // tile,),
        in_specs=[block] * 3,
        out_specs=pl.BlockSpec((rows, channels + LANES), lambda i: (0, 0)),
        out_shape=jax.ShapeDtypeStruct((rows, channels + LANES), BF16),
        scratch_shapes=[pltpu.VMEM((rows, LANES), F32)],
        compiler_params=params(LONG_VMEM),
        cost_estimate=attend_cost(rows, channels),
        name="attend_part",
    )(query, key, value)


def attend_whole(query, key, value, previous, place):
    rows, channels = query.shape
    half = channels // 2
    tile = min(512, half)
    steps = half // tile
    first = pl.BlockSpec((rows, tile), lambda i: (0, i))
    second = pl.BlockSpec((rows, tile), lambda i: (0, steps + i))
    return pl.pallas_call(
        attend_whole_kernel,
        grid=(steps,),
        in_specs=[
            pl.BlockSpec(memory_space=pltpu.SMEM),
            second,
            second,
            second,
            first,
            pl.BlockSpec((rows, tile), lambda i: (1, i)),
        ],
        out_specs=second,
        out_shape=jax.ShapeDtypeStruct((rows, channels), BF16),
        compiler_params=params(LONG_VMEM),
        cost_estimate=attend_cost(rows, channels),
        name="attend_whole",
    )(place, query, key, value, previous, previous)


def combine(own, prev, whole, place):
    rows, channels = whole.shape
    half = channels // 2
    tile = min(512, half)
    block = pl.BlockSpec((rows, tile), lambda i: (0, i))
    log_at = half // LANES
    log = pl.BlockSpec((rows, LANES), lambda i: (0, log_at))
    share = pltpu.VMEM((rows, LANES), F32)
    return pl.pallas_call(
        combine_kernel,
        grid=(half // tile,),
        in_specs=[pl.BlockSpec(memory_space=pltpu.SMEM), block, block, log, log]
        + [pl.BlockSpec(memory_space=pl.ANY)],
        out_specs=block,
        out_shape=jax.ShapeDtypeStruct((rows, channels), BF16),
        input_output_aliases={5: 0},
        scratch_shapes=[share, share],
        compiler_params=params(),
        cost_estimate=attend_cost(rows, half // 4),
        name="combine",
    )(place, own, prev, own, prev, whole)


def edge_kernel(first, *refs):
    *sources, out_ref = refs
    parts = [r[...].astype(F32) for r in sources]
    parts = [p[:EDGE] if first else p[p.shape[0] - EDGE :] for p in parts]
    out_ref[...] = jnp.concatenate(parts, 0).astype(BF16)


def edge_rows(arrays, first):
    rows, channels = arrays[0].shape
    block = pl.BlockSpec((16, channels), lambda i: (0 if first else rows // 16 - 1, 0))
    return pl.pallas_call(
        functools.partial(edge_kernel, first),
        grid=(1,),
        in_specs=[block] * len(arrays),
        out_specs=pl.BlockSpec((len(arrays) * EDGE, channels), lambda i: (0, 0)),
        out_shape=jax.ShapeDtypeStruct((len(arrays) * EDGE, channels), BF16),
        compiler_params=params(LONG_VMEM if first else VMEM_BYTES),
        name="edge_rows",
    )(*arrays)


def taps_causal(ext_ref, befores, signals, filters):
    rows = signals[0].shape[0]
    for j, signal in enumerate(signals):
        ext_ref[j, 0:EDGE, :] = befores[j]
        ext_ref[j, EDGE : EDGE + rows, :] = signal
    totals = [taps[0:1] * signal for signal, taps in zip(signals, filters)]
    for s in range(1, filters[0].shape[0]):
        for j, taps in enumerate(filters):
            totals[j] = totals[j] + taps[s : s + 1] * ext_ref[j, EDGE - s : EDGE - s + rows, :]
    return totals


def columns_of(width):
    return [slice(j * LANES, (j + 1) * LANES) for j in range(width // LANES)]


PAIR = 2


def put_pairs(ref, dest, channel, gw, first, second):
    width = PAIR * gw
    for piece in range(first.shape[0] // width):
        at = slice(piece * width, (piece + 1) * width)
        low = 2 * (channel + piece * width)
        ref[dest, low : low + width, :] = first[at]
        ref[dest, low + width : low + 2 * width, :] = second[at]


def get_pairs(ref, dest, channel, count, gw, which):
    width = PAIR * gw
    lows = [2 * (channel + low) + which * width for low in range(0, count, width)]
    return jnp.concatenate([ref[dest, low : low + width, :] for low in lows], 0)


def before_kernel(cpd, gpd, chunks, *refs):
    *refs, long_ref, send_ref, long_rows, ext_q, ext_k, ext_v = refs
    step = pl.program_id(0)
    groups = long_ref.shape[1]
    per_tile, send_rows, rows = send_ref.shape
    gw = cpd // gpd
    filter_rows = send_rows - 2 * cpd * chunks
    half = groups // chunks

    @pl.when(step == 0)
    def _():
        long_rows[...] = jnp.zeros_like(long_rows)
        long_rows[0:groups, :] = long_ref[...].T

    turn = reversal(rows)
    for chunk in range(chunks):
        q_ref, k_ref, v_ref, og_ref, tail_ref, taps_ref = refs[6 * chunk : 6 * chunk + 6]
        places = columns_of(q_ref.shape[1])
        tails = [tail_ref[:, at].astype(F32) for at in places]

        def short(which, ref, ext, tails=tails, places=places, taps_ref=taps_ref, chunk=chunk):
            return taps_causal(
                ext.at[chunk],
                [tail[which * EDGE : (which + 1) * EDGE] for tail in tails],
                [ref[:, at].astype(F32) for at in places],
                [taps_ref[which, :, at] for at in places],
            )

        short_k, short_v = short(1, k_ref, ext_k), short(2, v_ref, ext_v)
        mixed = [(k * v).T.astype(BF16) for k, v in zip(short_k, short_v)]
        short_q = short(0, q_ref, ext_q)
        delta = [(og_ref[:, at].astype(F32) * q).T.astype(BF16) for q, at in zip(short_q, places)]
        delta = [jnp.dot(d, turn, preferred_element_type=F32).astype(BF16) for d in delta]
        width = min(cpd, LANES)
        for j in range(len(places)):
            for piece in range(LANES // width):
                channel = j * LANES + piece * width
                dest, low = channel // cpd, channel % cpd
                at = slice(piece * width, (piece + 1) * width)
                put_pairs(send_ref, dest, chunk * cpd + low, gw, mixed[j][at], delta[j][at])
    for dest in range(per_tile):
        lines = []
        for chunk in range(chunks):
            first = chunk * half + (step * per_tile + dest) * gpd
            lines.append(long_rows[pl.ds(first, filter_rows if chunks == 1 else gpd), :])
        send_ref[dest, 2 * cpd * chunks :, :] = jnp.concatenate(lines, 0).astype(BF16)


def before_exchange(query, key, value, out_grad, tail, taps, long_filter, n, chunks):
    rows, channels = query.shape
    groups = long_filter.shape[1]
    cpd, gpd = channels // (n * chunks), groups // (n * chunks)
    tile = min(channels // chunks, max(512 // chunks, cpd))
    per_tile = tile // cpd
    filter_rows = round_up(gpd * chunks, 16)
    send_rows = 2 * cpd * chunks + filter_rows
    steps = n // per_tile
    specs = []
    for chunk in range(chunks):
        first = chunk * steps
        specs += [pl.BlockSpec((rows, tile), lambda i, f=first: (0, f + i))] * 4
        specs.append(pl.BlockSpec((3 * EDGE, tile), lambda i, f=first: (0, f + i)))
        specs.append(pl.BlockSpec((3, taps.shape[1], tile), lambda i, f=first: (0, 0, f + i)))
    ext = pltpu.VMEM((chunks, tile // LANES, rows + EDGE, LANES), F32)
    return pl.pallas_call(
        functools.partial(before_kernel, cpd, gpd, chunks),
        grid=(steps,),
        in_specs=specs + [pl.BlockSpec((rows, groups), lambda i: (0, 0))],
        out_specs=pl.BlockSpec((per_tile, send_rows, rows), lambda i: (i, 0, 0)),
        out_shape=jax.ShapeDtypeStruct((n, send_rows, rows), BF16),
        scratch_shapes=[pltpu.VMEM((round_up(groups, 8) + filter_rows, rows), F32), ext, ext, ext],
        compiler_params=params(),
        cost_estimate=pl.CostEstimate(
            flops=50 * rows * channels, bytes_accessed=12 * rows * channels, transcendentals=0
        ),
        name="before_exchange",
    )(*((query, key, value, out_grad, tail, taps) * chunks), long_filter)


def conv_kernel(cpd, gpd, chunk, in_ref, filter_ref, *refs):
    *raw_ref, out_ref, taps, wide = refs
    step = pl.program_id(0)
    n, _, rows = in_ref.shape
    gw = cpd // gpd
    span = n * rows
    slots = range(PAIR)

    @pl.when(step == 0)
    def _():
        taps[:, 0:rows] = jnp.zeros((taps.shape[0], rows), F32)
        for a in range(n):
            taps[:, (a + 1) * rows : (a + 2) * rows] = filter_ref[a].astype(F32)
        for slot in slots:
            wide[slot, :, 0:rows] = jnp.zeros((rows, rows), BF16)

    bases = []
    for slot in slots:
        line = taps[pl.ds(chunk * gpd + PAIR * step + slot, 1), :]
        line = jnp.broadcast_to(line, (16, span + rows))
        bases.append(pltpu.roll(line, 0, 1, stride=1, stride_axis=0).astype(BF16))
    for m in range(rows // 16):
        for slot in slots:
            moved = bases[slot] if m == 0 else pltpu.roll(bases[slot], 16 * m, 1)
            wide[slot, 16 * m : 16 * m + 16, rows:] = moved[:, rows:]
    stacks = []
    for slot in slots:
        x = in_ref[:, slot * gw : (slot + 1) * gw, :]
        d = in_ref[:, (PAIR + slot) * gw : (PAIR + slot + 1) * gw, :]
        both = [jnp.concatenate([x[a], d[n - 1 - a]], 0) for a in range(n)]
        stacks.append(
            jnp.concatenate([jnp.concatenate([both[a], both[a + 1]], 1) for a in range(0, n, 2)], 0)
        )
    totals = [None] * PAIR
    for k in range(n // 2):
        skip = 2 * gw * k
        low = 2 * rows * k
        for slot in slots:
            tile = jnp.concatenate(
                [wide[slot, :, low + rows : low + 3 * rows], wide[slot, :, low : low + 2 * rows]], 0
            )
            part = jnp.dot(stacks[slot][: n * gw - skip], tile, preferred_element_type=F32)
            total = totals[slot]
            totals[slot] = part if k == 0 else jnp.concatenate([total[:skip], total[skip:] + part], 0)
    for slot in slots:
        total = totals[slot]
        first = pl.multiple_of(2 * PAIR * gw * step + slot * gw, gw)
        second = pl.multiple_of(2 * PAIR * gw * step + (PAIR + slot) * gw, gw)
        for a in range(n):
            at = slice(a % 2 * rows, (a % 2 + 1) * rows)
            top = a // 2 * 2 * gw
            out_ref[a, pl.ds(first, gw), :] = total[top : top + gw, at].astype(BF16)
            out_ref[n - 1 - a, pl.ds(second, gw), :] = total[top + gw : top + 2 * gw, at].astype(BF16)

    @pl.when(step == pl.num_programs(0) - 1)
    def _():
        finish_conv(cpd, gw, out_ref, raw_ref)


def finish_conv(cpd, gw, out_ref, raw_ref):
    n, _, rows = out_ref.shape
    upper = lower = 0.0
    if raw_ref:
        *raw_ref, squares_ref = raw_ref
        upper = squares_ref[...].astype(BF16).astype(F32)
        lower = squares_ref[...] - upper
    halo_at = 2 * cpd
    row = lax.broadcasted_iota(jnp.int32, (2 * EDGE, 2 * rows), 0)
    lane = lax.broadcasted_iota(jnp.int32, (2 * EDGE, 2 * rows), 1)
    wanted = jnp.where(row < EDGE, row, 2 * rows - 1 + EDGE - row)
    pick = jnp.where(lane == wanted, 1.0, 0.0).astype(BF16)
    row_out = lax.broadcasted_iota(jnp.int32, (2 * EDGE, rows), 0)
    for a in range(n):
        if a + 1 < n:
            results = [get_pairs(out_ref, a + 1, 0, cpd, gw, which) for which in range(2)]
            results = jnp.concatenate(results, 1)
            halo = lax.dot_general(
                pick, results, (((1,), (1,)), ((), ())), preferred_element_type=F32
            )
            if cpd < LANES:
                halo = jnp.concatenate([halo, jnp.zeros((2 * EDGE, LANES - cpd), F32)], 1)
        else:
            halo = jnp.zeros((2 * EDGE, max(cpd, LANES)), F32)
        for j in range(halo.shape[1] // LANES):
            at = halo_at + 2 * EDGE * j
            tile = halo[:, j * LANES : (j + 1) * LANES]
            tile = jnp.where(row_out == EDGE - 2, upper, jnp.where(row_out == EDGE - 1, lower, tile))
            out_ref[a, at : at + 2 * EDGE, :] = tile.astype(BF16)
    for ref in raw_ref:
        out_ref[:, out_ref.shape[1] - ref.shape[1] :, :] = ref[...]


def long_convs(received, raw, cpd, gpd, chunk, chunks):
    n, send_rows, rows = received.shape
    filter_rows = send_rows - 2 * cpd * chunks
    out_rows = 2 * cpd + 2 * EDGE * max(1, cpd // LANES) + sum(r.shape[1] for r in raw[:1])
    span = n * rows
    pairs = gpd // PAIR
    pair_rows = 2 * cpd // pairs
    filter_at = 2 * cpd * chunks // filter_rows
    return pl.pallas_call(
        functools.partial(conv_kernel, cpd, gpd, chunk),
        grid=(pairs,),
        in_specs=[
            pl.BlockSpec((n, pair_rows, rows), lambda i: (0, chunk * pairs + i, 0)),
            pl.BlockSpec((n, filter_rows, rows), lambda i: (0, filter_at, 0)),
        ]
        + [pl.BlockSpec(r.shape, lambda i, r=r: (0,) * r.ndim) for r in raw],
        out_specs=pl.BlockSpec((n, out_rows, rows), lambda i: (0, 0, 0)),
        out_shape=jax.ShapeDtypeStruct((n, out_rows, rows), BF16),
        scratch_shapes=[
            pltpu.VMEM((filter_rows, span + rows), F32),
            pltpu.VMEM((PAIR, rows, span + rows), BF16),
        ],
        compiler_params=params(LONG_VMEM),
        cost_estimate=pl.CostEstimate(
            flops=4 * cpd * span * span, bytes_accessed=4 * n * out_rows * rows, transcendentals=0
        ),
        name="long_convs",
    )(received, received, *raw)


def gram_kernel(gw, in_ref, out_ref, squares_ref, gram, raw, total_ref):
    step = pl.program_id(0)
    n, _, rows = in_ref.shape
    span = n * rows
    slots = range(PAIR)

    @pl.when(step == 0)
    def _():
        for slot in slots:
            gram[slot, :, span:] = jnp.zeros((rows, rows), F32)
        raw[...] = jnp.zeros_like(raw)
        total_ref[...] = jnp.zeros_like(total_ref)

    no_rows = jnp.zeros((n * gw, rows), BF16)

    def offset(d, k):
        held = (k + 1) * gw
        if held == n * gw:
            return d
        return jnp.concatenate([d[n * gw - held :], no_rows[held:]], 0)

    turned, shifting = [], []
    for slot in slots:
        x = in_ref[:, slot * gw : (slot + 1) * gw, :].reshape(n * gw, rows)
        d = in_ref[:, (PAIR + slot) * gw : (PAIR + slot + 1) * gw, :]
        shifting.append(d.reshape(n * gw, rows))
        turned.append(x.astype(F32).T.astype(BF16))
    for k in range(0, n, 2):
        for slot in slots:
            d = shifting[slot]
            pairs = jnp.concatenate([offset(d, k), offset(d, k + 1)], 1)
            gram[slot, :, k * rows : (k + 2) * rows] = jnp.dot(
                turned[slot], pairs, preferred_element_type=F32
            )
    sums = [gram[slot, 0:8, :] for slot in slots]
    for m in range(1, rows // 8):
        for slot in slots:
            sums[slot] = sums[slot] + pltpu.roll(gram[slot, 8 * m : 8 * m + 8, :], 8 * m, 1)
    sums = [pltpu.roll(total, 0, 1, stride=1, stride_axis=0) for total in sums]
    for slot in slots:
        line = jnp.sum(sums[slot], axis=0, keepdims=True)[:, :span]
        raw[pl.ds(PAIR * step + slot, 1), :] = line
        total_ref[...] = total_ref[...] + line * line

    @pl.when(step == pl.num_programs(0) - 1)
    def _():
        squares_ref[...] = jnp.sum(total_ref[...], axis=1, keepdims=True)
        turn = reversal(rows)
        for a in range(n):
            tile = raw[:, (n - 1 - a) * rows : (n - a) * rows].astype(BF16)
            out_ref[a] = jnp.dot(tile, turn, preferred_element_type=F32).astype(BF16)


def filter_products(received, cpd, gpd, chunks):
    n, _, rows = received.shape
    span = n * rows
    raw_rows = round_up(gpd * chunks, 16)
    pairs = gpd * chunks // PAIR
    pair_rows = 2 * cpd * chunks // pairs
    return pl.pallas_call(
        functools.partial(gram_kernel, cpd // gpd),
        grid=(pairs,),
        in_specs=[pl.BlockSpec((n, pair_rows, rows), lambda i: (0, i, 0))],
        out_specs=[
            pl.BlockSpec((n, raw_rows, rows), lambda i: (0, 0, 0)),
            pl.BlockSpec((1, 1), lambda i: (0, 0)),
        ],
        out_shape=[
            jax.ShapeDtypeStruct((n, raw_rows, rows), BF16),
            jax.ShapeDtypeStruct((1, 1), F32),
        ],
        scratch_shapes=[
            pltpu.VMEM((PAIR, rows, span + rows), F32),
            pltpu.VMEM((raw_rows, span), F32),
            pltpu.VMEM((1, span), F32),
        ],
        compiler_params=params(LONG_VMEM),
        cost_estimate=pl.CostEstimate(
            flops=2 * cpd * chunks * span * span,
            bytes_accessed=2 * received.size,
            transcendentals=0,
        ),
        name="filter_products",
    )(received)


def taps_anti(ext_ref, signals, afters, filters):
    rows = signals[0].shape[0]
    for j, signal in enumerate(signals):
        ext_ref[j, 0:rows, :] = signal
        ext_ref[j, rows : rows + EDGE, :] = afters[j]
    totals = [taps[0:1] * signal for signal, taps in zip(signals, filters)]
    for s in range(1, filters[0].shape[0]):
        for j, taps in enumerate(filters):
            totals[j] = totals[j] + taps[s : s + 1] * ext_ref[j, s : s + rows, :]
    return totals


def short_edge(before, signal, filter_taps):
    both = jnp.concatenate([before, signal], 0)
    total = filter_taps[0:1] * signal
    for s in range(1, filter_taps.shape[0]):
        total = total + filter_taps[s : s + 1] * both[EDGE - s : 2 * EDGE - s]
    return total


def after_kernel(
    cpd, gpd, chunks, last, bound, in_ref, og_ref, k_ref, v_ref, tail_ref, next_ref, taps_ref, *refs
):
    *refs, ext_q, ext_k, ext_v, ext_in_k, ext_in_v = refs
    if last:
        *refs, raw_ref, raw_rows, total_ref = refs
    dq_ref, dk_ref, dv_ref = refs[-3:]
    step = pl.program_id(0)
    per_tile, in_rows, rows = in_ref.shape
    halo_rows = 2 * EDGE * max(1, cpd // LANES)
    halo_at = 2 * cpd
    turn = reversal(rows)
    places = columns_of(og_ref.shape[1])
    tails = [tail_ref[:, at].astype(F32) for at in places]
    nexts = [next_ref[:, at].astype(F32) for at in places]
    convs, backs, halos = [], [], []
    for j in range(len(places)):
        if cpd >= LANES:
            dest, low = j * LANES // cpd, j * LANES % cpd
            conv = get_pairs(in_ref, dest, low, LANES, cpd // gpd, 0)
            back = get_pairs(in_ref, dest, low, LANES, cpd // gpd, 1)
            edge = halo_at + 2 * EDGE * (low // LANES)
            halo = in_ref[dest, edge : edge + 2 * EDGE, :].astype(F32)
        else:
            dests = range(j * LANES // cpd, (j + 1) * LANES // cpd)
            conv = jnp.concatenate([get_pairs(in_ref, d, 0, cpd, cpd // gpd, 0) for d in dests], 0)
            back = jnp.concatenate([get_pairs(in_ref, d, 0, cpd, cpd // gpd, 1) for d in dests], 0)
            halo = jnp.concatenate(
                [in_ref[d, halo_at : halo_at + halo_rows, :].astype(F32)[:, :cpd] for d in dests], 1
            )
        convs.append(conv)
        backs.append(back)
        halos.append(halo)
    convs = [conv.astype(F32).T for conv in convs]
    backs = [jnp.dot(back, turn, preferred_element_type=F32) for back in backs]
    backs = [back.T for back in backs]
    taps = [[taps_ref[which, :, at] for at in places] for which in range(3)]
    keys = [k_ref[:, at].astype(F32) for at in places]
    values = [v_ref[:, at].astype(F32) for at in places]
    short_k = taps_causal(ext_in_k, [tail[EDGE : 2 * EDGE] for tail in tails], keys, taps[1])
    short_v = taps_causal(ext_in_v, [tail[2 * EDGE : 3 * EDGE] for tail in tails], values, taps[2])
    next_k = [
        short_edge(k[rows - EDGE :], f[EDGE : 2 * EDGE], t) for k, f, t in zip(keys, nexts, taps[1])
    ]
    next_v = [
        short_edge(v[rows - EDGE :], f[2 * EDGE : 3 * EDGE], t)
        for v, f, t in zip(values, nexts, taps[2])
    ]

    def store(ref, ext, signals, afters, filters):
        for at, total in zip(places, taps_anti(ext, signals, afters, filters)):
            ref[:, at] = total.astype(BF16)

    store(
        dq_ref,
        ext_q,
        [og_ref[:, at].astype(F32) * conv for at, conv in zip(places, convs)],
        [f[0:EDGE] * halo[0:EDGE] for f, halo in zip(nexts, halos)],
        taps[0],
    )
    store(
        dk_ref,
        ext_k,
        [back * v for back, v in zip(backs, short_v)],
        [halo[EDGE:] * v for halo, v in zip(halos, next_v)],
        taps[1],
    )
    store(
        dv_ref,
        ext_v,
        [back * k for back, k in zip(backs, short_k)],
        [halo[EDGE:] * k for halo, k in zip(halos, next_k)],
        taps[2],
    )
    if not last:
        return
    squares = jnp.zeros((1, LANES), F32)
    for dest in range(per_tile):
        parts = in_ref[dest, halo_at : halo_at + 2 * EDGE, :].astype(F32)
        squares = squares + parts[EDGE - 2 : EDGE - 1] + parts[EDGE - 1 : EDGE]

    @pl.when(step == 0)
    def _():
        total_ref[...] = jnp.zeros_like(total_ref)

    total_ref[...] = total_ref[...] + squares
    half = raw_rows.shape[0] // chunks
    for dest in range(per_tile):
        lines = in_ref[dest, halo_at + halo_rows :, :].astype(F32)
        for chunk in range(chunks):
            at = chunk * half + (step * per_tile + dest) * gpd
            raw_rows[pl.ds(at, gpd), :] = lines[chunk * gpd : (chunk + 1) * gpd]

    @pl.when(step == pl.num_programs(0) - 1)
    def _():
        factor = jnp.minimum(1.0, bound / jnp.sqrt(total_ref[...]))[:, 0:1]
        raw_ref[...] = raw_rows[...].T * factor


def after_exchange(
    returned, out_grad, key, value, tail, following, taps, groups, chunk, chunks, grads, bound
):
    n, in_rows, rows = returned.shape
    channels = out_grad.shape[1] // chunks
    cpd, gpd = channels // n, groups // (n * chunks)
    last = chunk + 1 == chunks
    tile = min(channels, max(512, cpd))
    per_tile = tile // cpd
    first = chunk * channels // tile
    block = pl.BlockSpec((rows, tile), lambda i: (0, first + i))
    ext = pltpu.VMEM((tile // LANES, rows + EDGE, LANES), F32)
    grad = jax.ShapeDtypeStruct(out_grad.shape, BF16)
    return pl.pallas_call(
        functools.partial(after_kernel, cpd, gpd, chunks, last, bound),
        grid=(channels // tile,),
        in_specs=[
            pl.BlockSpec((per_tile, in_rows, rows), lambda i: (i, 0, 0)),
            block,
            block,
            block,
            pl.BlockSpec((3 * EDGE, tile), lambda i: (0, first + i)),
            pl.BlockSpec((3 * EDGE, tile), lambda i: (0, first + i)),
            pl.BlockSpec((3, taps.shape[1], tile), lambda i: (0, 0, first + i)),
        ]
        + [pl.BlockSpec(memory_space=pl.ANY)] * len(grads),
        input_output_aliases={7 + i: i for i in range(len(grads))},
        out_specs=[block] * 3 + [pl.BlockSpec((rows, groups), lambda i: (0, 0))] * last,
        out_shape=[grad] * 3 + [jax.ShapeDtypeStruct((rows, groups), F32)] * last,
        scratch_shapes=[pltpu.VMEM((groups, rows), F32), pltpu.VMEM((1, LANES), F32)] * last
        + [ext] * 5,
        compiler_params=params(),
        cost_estimate=pl.CostEstimate(
            flops=90 * rows * channels, bytes_accessed=18 * rows * channels, transcendentals=0
        ),
        name="after_exchange",
    )(returned, out_grad, key, value, tail, following, taps, *grads)


def on_device(
    query_heads,
    key_heads,
    value_heads,
    hyena_query,
    hyena_key,
    hyena_value,
    short_filter,
    long_filter,
    output_grad,
):
    rows, channels = query_heads.shape
    groups = long_filter.shape[1]
    n = lax.axis_size("ctx")
    tp = lax.axis_size("tp")
    cpd, gpd = channels // n, groups // n
    position = lax.axis_index("ctx")
    tail = shifted(edge_rows((hyena_query, hyena_key, hyena_value), False), "ctx", 1)
    half = channels // 2
    chunks = 2 if gpd % 4 == 0 else 1
    cpd, gpd = cpd // chunks, gpd // chunks
    send = before_exchange(
        hyena_query, hyena_key, hyena_value, output_grad, tail, short_filter, long_filter, n, chunks
    )
    send, query, key, value, *sources = lax.optimization_barrier(
        (send, query_heads, key_heads, value_heads, output_grad, hyena_key, hyena_value)
    )
    received = lax.all_to_all(send, "ctx", split_axis=0, concat_axis=0, tiled=True)
    following = shifted(edge_rows(sources, True), "ctx", -1)
    query_next = shifted(query[:, :half], "ctx", -1)
    previous = shifted(jnp.concatenate([key[:, half:], value[:, half:]], 0), "ctx", 1)
    returned = []
    for chunk in range(chunks):
        raw = ()
        if chunk + 1 == chunks:
            raw, squares = filter_products(received, cpd, gpd, chunks)
            query_next, raw, squares = lax.optimization_barrier((query_next, raw, squares))
            raw = (raw, total_over(squares, "tp"))
        results = long_convs(received, raw, cpd, gpd, chunk, chunks)
        if chunk + 1 == chunks:
            part = attend_part(query_next, key_heads, value_heads, half, False)
            results, part = lax.optimization_barrier((results, part))
        if chunk == 0:
            results, received, query_next, previous, following = lax.optimization_barrier(
                (results, received, query_next, previous, following)
            )
        returned.append(lax.all_to_all(results, "ctx", split_axis=0, concat_axis=0, tiled=True))
    part = shifted(part, "ctx", 1)
    place = position.astype(jnp.int32).reshape(1)
    whole = attend_whole(query_heads, key_heads, value_heads, previous, place)
    own = attend_part(query_heads, key_heads, value_heads, half, True)
    bound = math.sqrt(rows * n * groups * tp)
    grads = ()
    for chunk in range(chunks):
        if chunk > 0:
            returned[chunk], whole, own, *grads = lax.optimization_barrier(
                (returned[chunk], whole, own, *grads)
            )
        grads = after_exchange(
            returned[chunk], output_grad, hyena_key, hyena_value, tail, following, short_filter, groups,
            chunk, chunks, grads, bound,
        )
    part, *grads = lax.optimization_barrier((part, *grads))
    return (combine(own, part, whole, place), *grads)


def solution(mesh):
    whole = P("ctx", "tp")
    in_specs = (whole,) * 6 + (P(None, None, "tp"), whole, whole)
    return jax.shard_map(
        on_device, mesh=mesh, in_specs=in_specs, out_specs=(whole,) * 5, check_vma=False
    )
```

```python
import functools
import math

import jax
import jax.numpy as jnp
from jax import lax
from jax.experimental import pallas as pl
from jax.experimental.pallas import tpu as pltpu
from jax.sharding import PartitionSpec as P

HEAD_DIM = 128
LANES = 128
EDGE = 8
F32 = jnp.float32
BF16 = jnp.bfloat16
VMEM_BYTES = 60 * 1024 * 1024
LONG_VMEM = 24 * 1024 * 1024


def params(size=VMEM_BYTES):
    return pltpu.CompilerParams(vmem_limit_bytes=size)


def shifted(block, axis, distance):
    devices = range(lax.axis_size(axis))
    route = [(i - distance, i) for i in devices if i - distance in devices]
    return lax.ppermute(block, axis, route)


def total_over(value, axis):
    size = lax.axis_size(axis)
    distance = 1
    while distance < size:
        value = value + lax.ppermute(value, axis, [(i, i ^ distance) for i in range(size)])
        distance *= 2
    return value


def round_up(value, step):
    return -(-value // step) * step


def reversal(size):
    row = lax.broadcasted_iota(jnp.int32, (size, size), 0)
    col = lax.broadcasted_iota(jnp.int32, (size, size), 1)
    return jnp.where(row + col == size - 1, 1.0, 0.0).astype(BF16)


SCALE = 1.0 / math.sqrt(HEAD_DIM)
NT = (((1,), (1,)), ((), ()))


LOG_LANES = 32


def places_of(width):
    return [slice(head * HEAD_DIM, (head + 1) * HEAD_DIM) for head in range(width // HEAD_DIM)]


def attend_part_kernel(causal, q_ref, k_ref, v_ref, out_ref, logs_ref):
    rows, width = q_ref.shape
    heads = width // HEAD_DIM
    step = pl.program_id(0)
    row = lax.broadcasted_iota(jnp.int32, (rows, rows), 0)
    col = lax.broadcasted_iota(jnp.int32, (rows, rows), 1)
    lane = lax.broadcasted_iota(jnp.int32, (rows, LANES), 1)

    @pl.when(step == 0)
    def _():
        logs_ref[...] = jnp.zeros_like(logs_ref)

    places = places_of(width)
    scores = [
        lax.dot_general(q_ref[:, at], k_ref[:, at], NT, preferred_element_type=F32) * SCALE
        for at in places
    ]
    if causal:
        scores = [jnp.where(col <= row, score, -jnp.inf) for score in scores]
    largest = [jnp.max(score, axis=1, keepdims=True) for score in scores]
    raised = [jnp.exp(score - top) for score, top in zip(scores, largest)]
    totals = [jnp.sum(r, axis=1, keepdims=True) for r in raised]
    weights = [(r * (1.0 / total)).astype(BF16) for r, total in zip(raised, totals)]
    mixed = [
        jnp.dot(weight, v_ref[:, at], preferred_element_type=F32) for weight, at in zip(weights, places)
    ]
    logs = logs_ref[...]
    for head in range(heads):
        log = largest[head] + jnp.log(totals[head])
        logs = jnp.where(lane == step * heads + head, log, logs)
    logs_ref[...] = logs
    first = pl.multiple_of(step * width, LANES)
    out_ref[:, pl.ds(first, width)] = jnp.concatenate([m.astype(BF16) for m in mixed], 1)

    @pl.when(step == pl.num_programs(0) - 1)
    def _():
        upper = logs.astype(BF16).astype(F32)
        middle = (logs - upper).astype(BF16).astype(F32)
        lower = logs - upper - middle
        terms = upper + pltpu.roll(middle, LOG_LANES, 1) + pltpu.roll(lower, 2 * LOG_LANES, 1)
        out_ref[:, out_ref.shape[1] - LANES :] = terms.astype(BF16)


def combine_kernel(place_ref, own_ref, prev_ref, own_log_ref, prev_log_ref, _, out_ref, own_share, prev_share):
    rows, width = own_ref.shape
    heads = width // HEAD_DIM
    step = pl.program_id(0)
    @pl.when(step == 0)
    def _():
        def joined(ref):
            terms = ref[...].astype(F32)
            middle = pltpu.roll(terms, LANES - LOG_LANES, 1)
            return terms + (middle + pltpu.roll(terms, LANES - 2 * LOG_LANES, 1))

        own = joined(own_log_ref)
        has_prev = jnp.broadcast_to(place_ref[0], (rows, LANES)) > 0
        prev = jnp.where(has_prev, joined(prev_log_ref), -jnp.inf)
        largest = jnp.maximum(own, prev)
        own, prev = jnp.exp(own - largest), jnp.exp(prev - largest)
        inverse = 1.0 / (own + prev)
        own_share[...] = own * inverse
        prev_share[...] = prev * inverse

    row = lax.broadcasted_iota(jnp.int32, (LANES, width), 0)
    col = lax.broadcasted_iota(jnp.int32, (LANES, width), 1)
    spread = jnp.where(row == step * heads + col // HEAD_DIM, 1.0, 0.0).astype(BF16)

    def spread_out(ref):
        upper = ref[...].astype(BF16)
        lower = (ref[...] - upper.astype(F32)).astype(BF16)
        return jnp.dot(upper, spread, preferred_element_type=F32) + jnp.dot(
            lower, spread, preferred_element_type=F32
        )

    total = spread_out(own_share) * own_ref[...].astype(F32)
    total = total + spread_out(prev_share) * prev_ref[...].astype(F32)
    out_ref[...] = total.astype(BF16)


def attend_whole_kernel(place_ref, q_ref, k_ref, v_ref, kp_ref, vp_ref, out_ref):
    rows, width = q_ref.shape
    row = lax.broadcasted_iota(jnp.int32, (rows, rows), 0)
    col = lax.broadcasted_iota(jnp.int32, (rows, rows), 1)
    own_ok = col <= row
    prev_ok = jnp.broadcast_to(place_ref[0], (rows, rows)) > 0
    places = places_of(width)

    def scores(ref, allowed):
        products = [
            lax.dot_general(q_ref[:, at], ref[:, at], NT, preferred_element_type=F32) for at in places
        ]
        return [jnp.where(allowed, product * SCALE, -jnp.inf) for product in products]

    own, prev = scores(k_ref, own_ok), scores(kp_ref, prev_ok)
    largest = [jnp.max(jnp.maximum(o, p), axis=1, keepdims=True) for o, p in zip(own, prev)]
    own = [jnp.exp(o - top) for o, top in zip(own, largest)]
    prev = [jnp.exp(p - top) for p, top in zip(prev, largest)]
    totals = [jnp.sum(o + p, axis=1, keepdims=True) for o, p in zip(own, prev)]
    inverses = [1.0 / total for total in totals]
    own = [(o * inverse).astype(BF16) for o, inverse in zip(own, inverses)]
    prev = [(p * inverse).astype(BF16) for p, inverse in zip(prev, inverses)]
    mixed = [
        jnp.dot(o, v_ref[:, at], preferred_element_type=F32)
        + jnp.dot(p, vp_ref[:, at], preferred_element_type=F32)
        for o, p, at in zip(own, prev, places)
    ]
    for head, at in enumerate(places):
        out_ref[:, at] = mixed[head].astype(BF16)


def attend_cost(rows, channels):
    heads = channels // HEAD_DIM
    return pl.CostEstimate(
        flops=4 * heads * rows * rows * HEAD_DIM,
        bytes_accessed=10 * rows * channels,
        transcendentals=heads * rows * rows,
    )


def attend_part(query, key, value, channels, causal):
    rows = query.shape[0]
    tile = min(512, channels)
    block = pl.BlockSpec((rows, tile), lambda i: (0, i))
    return pl.pallas_call(
        functools.partial(attend_part_kernel, causal),
        grid=(channels // tile,),
        in_specs=[block] * 3,
        out_specs=pl.BlockSpec((rows, channels + LANES), lambda i: (0, 0)),
        out_shape=jax.ShapeDtypeStruct((rows, channels + LANES), BF16),
        scratch_shapes=[pltpu.VMEM((rows, LANES), F32)],
        compiler_params=params(LONG_VMEM),
        cost_estimate=attend_cost(rows, channels),
        name="attend_part",
    )(query, key, value)


def attend_whole(query, key, value, key_prev, value_prev, place):
    rows, channels = query.shape
    half = channels // 2
    tile = min(512, half)
    steps = half // tile
    first = pl.BlockSpec((rows, tile), lambda i: (0, i))
    second = pl.BlockSpec((rows, tile), lambda i: (0, steps + i))
    return pl.pallas_call(
        attend_whole_kernel,
        grid=(steps,),
        in_specs=[
            pl.BlockSpec(memory_space=pltpu.SMEM),
            second,
            second,
            second,
            first,
            first,
        ],
        out_specs=second,
        out_shape=jax.ShapeDtypeStruct((rows, channels), BF16),
        compiler_params=params(LONG_VMEM),
        cost_estimate=attend_cost(rows, channels),
        name="attend_whole",
    )(place, query, key, value, key_prev, value_prev)


def combine(own, prev, whole, place):
    rows, channels = whole.shape
    half = channels // 2
    tile = min(1024, half)
    block = pl.BlockSpec((rows, tile), lambda i: (0, i))
    log_at = half // LANES
    log = pl.BlockSpec((rows, LANES), lambda i: (0, log_at))
    share = pltpu.VMEM((rows, LANES), F32)
    return pl.pallas_call(
        combine_kernel,
        grid=(half // tile,),
        in_specs=[pl.BlockSpec(memory_space=pltpu.SMEM), block, block, log, log]
        + [pl.BlockSpec(memory_space=pl.ANY)],
        out_specs=block,
        out_shape=jax.ShapeDtypeStruct((rows, channels), BF16),
        input_output_aliases={5: 0},
        scratch_shapes=[share, share],
        compiler_params=params(),
        cost_estimate=attend_cost(rows, half // 4),
        name="combine",
    )(place, own, prev, own, prev, whole)


def edge_kernel(first, *refs):
    *sources, out_ref = refs
    parts = [r[...].astype(F32) for r in sources]
    parts = [p[:EDGE] if first else p[p.shape[0] - EDGE :] for p in parts]
    out_ref[...] = jnp.concatenate(parts, 0).astype(BF16)


def edge_rows(arrays, first):
    rows, channels = arrays[0].shape
    block = pl.BlockSpec((16, channels), lambda i: (0 if first else rows // 16 - 1, 0))
    return pl.pallas_call(
        functools.partial(edge_kernel, first),
        grid=(1,),
        in_specs=[block] * len(arrays),
        out_specs=pl.BlockSpec((len(arrays) * EDGE, channels), lambda i: (0, 0)),
        out_shape=jax.ShapeDtypeStruct((len(arrays) * EDGE, channels), BF16),
        compiler_params=params(LONG_VMEM if first else VMEM_BYTES),
        name="edge_rows",
    )(*arrays)


def taps_causal(ext_ref, befores, signals, filters):
    rows = signals[0].shape[0]
    for j, signal in enumerate(signals):
        ext_ref[j, 0:EDGE, :] = befores[j]
        ext_ref[j, EDGE : EDGE + rows, :] = signal
    totals = [taps[0:1] * signal for signal, taps in zip(signals, filters)]
    for s in range(1, filters[0].shape[0]):
        for j, taps in enumerate(filters):
            totals[j] = totals[j] + taps[s : s + 1] * ext_ref[j, EDGE - s : EDGE - s + rows, :]
    return totals


def columns_of(width):
    return [slice(j * LANES, (j + 1) * LANES) for j in range(width // LANES)]


PAIR = 2


def put_pairs(ref, dest, channel, gw, first, second):
    width = PAIR * gw
    for piece in range(first.shape[0] // width):
        at = slice(piece * width, (piece + 1) * width)
        low = 2 * (channel + piece * width)
        ref[dest, low : low + width, :] = first[at]
        ref[dest, low + width : low + 2 * width, :] = second[at]


def get_pairs(ref, dest, channel, count, gw, which):
    width = PAIR * gw
    lows = [2 * (channel + low) + which * width for low in range(0, count, width)]
    return jnp.concatenate([ref[dest, low : low + width, :] for low in lows], 0)


def before_kernel(cpd, gpd, chunks, *refs):
    *refs, long_ref, send_ref, long_rows, ext_q, ext_k, ext_v = refs
    step = pl.program_id(0)
    groups = long_ref.shape[1]
    per_tile, send_rows, rows = send_ref.shape
    gw = cpd // gpd
    filter_rows = send_rows - 2 * cpd * chunks
    half = groups // chunks

    @pl.when(step == 0)
    def _():
        long_rows[...] = jnp.zeros_like(long_rows)
        long_rows[0:groups, :] = long_ref[...].T

    turn = reversal(rows)
    for chunk in range(chunks):
        q_ref, k_ref, v_ref, og_ref, tail_ref, taps_ref = refs[6 * chunk : 6 * chunk + 6]
        places = columns_of(q_ref.shape[1])
        tails = [tail_ref[:, at].astype(F32) for at in places]

        def short(which, ref, ext, tails=tails, places=places, taps_ref=taps_ref, chunk=chunk):
            return taps_causal(
                ext.at[chunk],
                [tail[which * EDGE : (which + 1) * EDGE] for tail in tails],
                [ref[:, at].astype(F32) for at in places],
                [taps_ref[which, :, at] for at in places],
            )

        short_k, short_v = short(1, k_ref, ext_k), short(2, v_ref, ext_v)
        mixed = [(k * v).T.astype(BF16) for k, v in zip(short_k, short_v)]
        short_q = short(0, q_ref, ext_q)
        delta = [(og_ref[:, at].astype(F32) * q).T.astype(BF16) for q, at in zip(short_q, places)]
        delta = [jnp.dot(d, turn, preferred_element_type=F32).astype(BF16) for d in delta]
        width = min(cpd, LANES)
        for j in range(len(places)):
            for piece in range(LANES // width):
                channel = j * LANES + piece * width
                dest, low = channel // cpd, channel % cpd
                at = slice(piece * width, (piece + 1) * width)
                put_pairs(send_ref, dest, chunk * cpd + low, gw, mixed[j][at], delta[j][at])
    for dest in range(per_tile):
        lines = []
        for chunk in range(chunks):
            first = chunk * half + (step * per_tile + dest) * gpd
            lines.append(long_rows[pl.ds(first, filter_rows if chunks == 1 else gpd), :])
        send_ref[dest, 2 * cpd * chunks :, :] = jnp.concatenate(lines, 0).astype(BF16)


def before_exchange(query, key, value, out_grad, tail, taps, long_filter, n, chunks):
    rows, channels = query.shape
    groups = long_filter.shape[1]
    cpd, gpd = channels // (n * chunks), groups // (n * chunks)
    tile = min(channels // chunks, max(512 // chunks, cpd))
    per_tile = tile // cpd
    filter_rows = round_up(gpd * chunks, 16)
    send_rows = 2 * cpd * chunks + filter_rows
    steps = n // per_tile
    specs = []
    for chunk in range(chunks):
        first = chunk * steps
        specs += [pl.BlockSpec((rows, tile), lambda i, f=first: (0, f + i))] * 4
        specs.append(pl.BlockSpec((3 * EDGE, tile), lambda i, f=first: (0, f + i)))
        specs.append(pl.BlockSpec((3, taps.shape[1], tile), lambda i, f=first: (0, 0, f + i)))
    ext = pltpu.VMEM((chunks, tile // LANES, rows + EDGE, LANES), F32)
    return pl.pallas_call(
        functools.partial(before_kernel, cpd, gpd, chunks),
        grid=(steps,),
        in_specs=specs + [pl.BlockSpec((rows, groups), lambda i: (0, 0))],
        out_specs=pl.BlockSpec((per_tile, send_rows, rows), lambda i: (i, 0, 0)),
        out_shape=jax.ShapeDtypeStruct((n, send_rows, rows), BF16),
        scratch_shapes=[pltpu.VMEM((round_up(groups, 8) + filter_rows, rows), F32), ext, ext, ext],
        compiler_params=params(),
        cost_estimate=pl.CostEstimate(
            flops=50 * rows * channels, bytes_accessed=12 * rows * channels, transcendentals=0
        ),
        name="before_exchange",
    )(*((query, key, value, out_grad, tail, taps) * chunks), long_filter)


def conv_kernel(cpd, gpd, chunk, in_ref, filter_ref, *refs):
    *raw_ref, out_ref, taps, wide = refs
    step = pl.program_id(0)
    n, _, rows = in_ref.shape
    gw = cpd // gpd
    span = n * rows
    slots = range(PAIR)

    @pl.when(step == 0)
    def _():
        taps[:, 0:rows] = jnp.zeros((taps.shape[0], rows), F32)
        for a in range(n):
            taps[:, (a + 1) * rows : (a + 2) * rows] = filter_ref[a].astype(F32)
        for slot in slots:
            wide[slot, :, 0:rows] = jnp.zeros((rows, rows), BF16)

    bases = []
    for slot in slots:
        line = taps[pl.ds(chunk * gpd + PAIR * step + slot, 1), :]
        line = jnp.broadcast_to(line, (16, span + rows))
        bases.append(pltpu.roll(line, 0, 1, stride=1, stride_axis=0).astype(BF16))
    for m in range(rows // 16):
        for slot in slots:
            moved = bases[slot] if m == 0 else pltpu.roll(bases[slot], 16 * m, 1)
            wide[slot, 16 * m : 16 * m + 16, rows:] = moved[:, rows:]
    stacks = []
    for slot in slots:
        x = in_ref[:, slot * gw : (slot + 1) * gw, :]
        d = in_ref[:, (PAIR + slot) * gw : (PAIR + slot + 1) * gw, :]
        both = [jnp.concatenate([x[a], d[n - 1 - a]], 0) for a in range(n)]
        stacks.append(
            jnp.concatenate([jnp.concatenate([both[a], both[a + 1]], 1) for a in range(0, n, 2)], 0)
        )
    totals = [None] * PAIR
    for k in range(n // 2):
        skip = 2 * gw * k
        low = 2 * rows * k
        for slot in slots:
            tile = jnp.concatenate(
                [wide[slot, :, low + rows : low + 3 * rows], wide[slot, :, low : low + 2 * rows]], 0
            )
            part = jnp.dot(stacks[slot][: n * gw - skip], tile, preferred_element_type=F32)
            total = totals[slot]
            totals[slot] = part if k == 0 else jnp.concatenate([total[:skip], total[skip:] + part], 0)
    for slot in slots:
        total = totals[slot]
        first = pl.multiple_of(2 * PAIR * gw * step + slot * gw, gw)
        second = pl.multiple_of(2 * PAIR * gw * step + (PAIR + slot) * gw, gw)
        for a in range(n):
            at = slice(a % 2 * rows, (a % 2 + 1) * rows)
            top = a // 2 * 2 * gw
            out_ref[a, pl.ds(first, gw), :] = total[top : top + gw, at].astype(BF16)
            out_ref[n - 1 - a, pl.ds(second, gw), :] = total[top + gw : top + 2 * gw, at].astype(BF16)

    @pl.when(step == pl.num_programs(0) - 1)
    def _():
        finish_conv(cpd, gw, out_ref, raw_ref)


def finish_conv(cpd, gw, out_ref, raw_ref):
    n, _, rows = out_ref.shape
    upper = lower = 0.0
    if raw_ref:
        *raw_ref, squares_ref = raw_ref
        upper = squares_ref[...].astype(BF16).astype(F32)
        lower = squares_ref[...] - upper
    halo_at = 2 * cpd
    row = lax.broadcasted_iota(jnp.int32, (2 * EDGE, 2 * rows), 0)
    lane = lax.broadcasted_iota(jnp.int32, (2 * EDGE, 2 * rows), 1)
    wanted = jnp.where(row < EDGE, row, 2 * rows - 1 + EDGE - row)
    pick = jnp.where(lane == wanted, 1.0, 0.0).astype(BF16)
    row_out = lax.broadcasted_iota(jnp.int32, (2 * EDGE, rows), 0)
    for a in range(n):
        if a + 1 < n:
            results = [get_pairs(out_ref, a + 1, 0, cpd, gw, which) for which in range(2)]
            results = jnp.concatenate(results, 1)
            halo = lax.dot_general(
                pick, results, (((1,), (1,)), ((), ())), preferred_element_type=F32
            )
            if cpd < LANES:
                halo = jnp.concatenate([halo, jnp.zeros((2 * EDGE, LANES - cpd), F32)], 1)
        else:
            halo = jnp.zeros((2 * EDGE, max(cpd, LANES)), F32)
        for j in range(halo.shape[1] // LANES):
            at = halo_at + 2 * EDGE * j
            tile = halo[:, j * LANES : (j + 1) * LANES]
            tile = jnp.where(row_out == EDGE - 2, upper, jnp.where(row_out == EDGE - 1, lower, tile))
            out_ref[a, at : at + 2 * EDGE, :] = tile.astype(BF16)
    for ref in raw_ref:
        out_ref[:, out_ref.shape[1] - ref.shape[1] :, :] = ref[...]


def long_convs(received, raw, cpd, gpd, chunk, chunks):
    n, send_rows, rows = received.shape
    filter_rows = send_rows - 2 * cpd * chunks
    out_rows = 2 * cpd + 2 * EDGE * max(1, cpd // LANES) + sum(r.shape[1] for r in raw[:1])
    span = n * rows
    pairs = gpd // PAIR
    pair_rows = 2 * cpd // pairs
    filter_at = 2 * cpd * chunks // filter_rows
    return pl.pallas_call(
        functools.partial(conv_kernel, cpd, gpd, chunk),
        grid=(pairs,),
        in_specs=[
            pl.BlockSpec((n, pair_rows, rows), lambda i: (0, chunk * pairs + i, 0)),
            pl.BlockSpec((n, filter_rows, rows), lambda i: (0, filter_at, 0)),
        ]
        + [pl.BlockSpec(r.shape, lambda i, r=r: (0,) * r.ndim) for r in raw],
        out_specs=pl.BlockSpec((n, out_rows, rows), lambda i: (0, 0, 0)),
        out_shape=jax.ShapeDtypeStruct((n, out_rows, rows), BF16),
        scratch_shapes=[
            pltpu.VMEM((filter_rows, span + rows), F32),
            pltpu.VMEM((PAIR, rows, span + rows), BF16),
        ],
        compiler_params=params(LONG_VMEM),
        cost_estimate=pl.CostEstimate(
            flops=4 * cpd * span * span, bytes_accessed=4 * n * out_rows * rows, transcendentals=0
        ),
        name="long_convs",
    )(received, received, *raw)


def gram_kernel(gw, in_ref, out_ref, squares_ref, gram, raw, total_ref):
    step = pl.program_id(0)
    n, _, rows = in_ref.shape
    span = n * rows
    slots = range(PAIR)

    @pl.when(step == 0)
    def _():
        for slot in slots:
            gram[slot, :, span:] = jnp.zeros((rows, rows), F32)
        raw[...] = jnp.zeros_like(raw)
        total_ref[...] = jnp.zeros_like(total_ref)

    no_rows = jnp.zeros((n * gw, rows), BF16)

    def offset(d, k):
        held = (k + 1) * gw
        if held == n * gw:
            return d
        return jnp.concatenate([d[n * gw - held :], no_rows[held:]], 0)

    turned, shifting = [], []
    for slot in slots:
        x = in_ref[:, slot * gw : (slot + 1) * gw, :].reshape(n * gw, rows)
        d = in_ref[:, (PAIR + slot) * gw : (PAIR + slot + 1) * gw, :]
        shifting.append(d.reshape(n * gw, rows))
        turned.append(x.astype(F32).T.astype(BF16))
    for k in range(0, n, 2):
        for slot in slots:
            d = shifting[slot]
            pairs = jnp.concatenate([offset(d, k), offset(d, k + 1)], 1)
            gram[slot, :, k * rows : (k + 2) * rows] = jnp.dot(
                turned[slot], pairs, preferred_element_type=F32
            )
    sums = [gram[slot, 0:8, :] for slot in slots]
    for m in range(1, rows // 8):
        for slot in slots:
            sums[slot] = sums[slot] + pltpu.roll(gram[slot, 8 * m : 8 * m + 8, :], 8 * m, 1)
    sums = [pltpu.roll(total, 0, 1, stride=1, stride_axis=0) for total in sums]
    for slot in slots:
        line = jnp.sum(sums[slot], axis=0, keepdims=True)[:, :span]
        raw[pl.ds(PAIR * step + slot, 1), :] = line
        total_ref[...] = total_ref[...] + line * line

    @pl.when(step == pl.num_programs(0) - 1)
    def _():
        squares_ref[...] = jnp.sum(total_ref[...], axis=1, keepdims=True)
        turn = reversal(rows)
        for a in range(n):
            tile = raw[:, (n - 1 - a) * rows : (n - a) * rows].astype(BF16)
            out_ref[a] = jnp.dot(tile, turn, preferred_element_type=F32).astype(BF16)


def filter_products(received, cpd, gpd, chunks):
    n, _, rows = received.shape
    span = n * rows
    raw_rows = round_up(gpd * chunks, 16)
    pairs = gpd * chunks // PAIR
    pair_rows = 2 * cpd * chunks // pairs
    return pl.pallas_call(
        functools.partial(gram_kernel, cpd // gpd),
        grid=(pairs,),
        in_specs=[pl.BlockSpec((n, pair_rows, rows), lambda i: (0, i, 0))],
        out_specs=[
            pl.BlockSpec((n, raw_rows, rows), lambda i: (0, 0, 0)),
            pl.BlockSpec((1, 1), lambda i: (0, 0)),
        ],
        out_shape=[
            jax.ShapeDtypeStruct((n, raw_rows, rows), BF16),
            jax.ShapeDtypeStruct((1, 1), F32),
        ],
        scratch_shapes=[
            pltpu.VMEM((PAIR, rows, span + rows), F32),
            pltpu.VMEM((raw_rows, span), F32),
            pltpu.VMEM((1, span), F32),
        ],
        compiler_params=params(LONG_VMEM),
        cost_estimate=pl.CostEstimate(
            flops=2 * cpd * chunks * span * span,
            bytes_accessed=2 * received.size,
            transcendentals=0,
        ),
        name="filter_products",
    )(received)


def taps_anti(ext_ref, signals, afters, filters):
    rows = signals[0].shape[0]
    for j, signal in enumerate(signals):
        ext_ref[j, 0:rows, :] = signal
        ext_ref[j, rows : rows + EDGE, :] = afters[j]
    totals = [taps[0:1] * signal for signal, taps in zip(signals, filters)]
    for s in range(1, filters[0].shape[0]):
        for j, taps in enumerate(filters):
            totals[j] = totals[j] + taps[s : s + 1] * ext_ref[j, s : s + rows, :]
    return totals


def short_edge(before, signal, filter_taps):
    both = jnp.concatenate([before, signal], 0)
    total = filter_taps[0:1] * signal
    for s in range(1, filter_taps.shape[0]):
        total = total + filter_taps[s : s + 1] * both[EDGE - s : 2 * EDGE - s]
    return total


def after_kernel(
    cpd, gpd, chunks, last, bound, in_ref, og_ref, k_ref, v_ref, tail_ref, next_ref, taps_ref, *refs
):
    *refs, ext_q, ext_k, ext_v, ext_in_k, ext_in_v = refs
    if last:
        *refs, raw_ref, raw_rows, total_ref = refs
    dq_ref, dk_ref, dv_ref = refs[-3:]
    step = pl.program_id(0)
    per_tile, in_rows, rows = in_ref.shape
    halo_rows = 2 * EDGE * max(1, cpd // LANES)
    halo_at = 2 * cpd
    turn = reversal(rows)
    places = columns_of(og_ref.shape[1])
    tails = [tail_ref[:, at].astype(F32) for at in places]
    nexts = [next_ref[:, at].astype(F32) for at in places]
    convs, backs, halos = [], [], []
    for j in range(len(places)):
        if cpd >= LANES:
            dest, low = j * LANES // cpd, j * LANES % cpd
            conv = get_pairs(in_ref, dest, low, LANES, cpd // gpd, 0)
            back = get_pairs(in_ref, dest, low, LANES, cpd // gpd, 1)
            edge = halo_at + 2 * EDGE * (low // LANES)
            halo = in_ref[dest, edge : edge + 2 * EDGE, :].astype(F32)
        else:
            dests = range(j * LANES // cpd, (j + 1) * LANES // cpd)
            conv = jnp.concatenate([get_pairs(in_ref, d, 0, cpd, cpd // gpd, 0) for d in dests], 0)
            back = jnp.concatenate([get_pairs(in_ref, d, 0, cpd, cpd // gpd, 1) for d in dests], 0)
            halo = jnp.concatenate(
                [in_ref[d, halo_at : halo_at + halo_rows, :].astype(F32)[:, :cpd] for d in dests], 1
            )
        convs.append(conv)
        backs.append(back)
        halos.append(halo)
    convs = [conv.astype(F32).T for conv in convs]
    backs = [jnp.dot(back, turn, preferred_element_type=F32) for back in backs]
    backs = [back.T for back in backs]
    taps = [[taps_ref[which, :, at] for at in places] for which in range(3)]
    keys = [k_ref[:, at].astype(F32) for at in places]
    values = [v_ref[:, at].astype(F32) for at in places]
    short_k = taps_causal(ext_in_k, [tail[EDGE : 2 * EDGE] for tail in tails], keys, taps[1])
    short_v = taps_causal(ext_in_v, [tail[2 * EDGE : 3 * EDGE] for tail in tails], values, taps[2])
    next_k = [
        short_edge(k[rows - EDGE :], f[EDGE : 2 * EDGE], t) for k, f, t in zip(keys, nexts, taps[1])
    ]
    next_v = [
        short_edge(v[rows - EDGE :], f[2 * EDGE : 3 * EDGE], t)
        for v, f, t in zip(values, nexts, taps[2])
    ]

    def store(ref, ext, signals, afters, filters):
        for at, total in zip(places, taps_anti(ext, signals, afters, filters)):
            ref[:, at] = total.astype(BF16)

    store(
        dq_ref,
        ext_q,
        [og_ref[:, at].astype(F32) * conv for at, conv in zip(places, convs)],
        [f[0:EDGE] * halo[0:EDGE] for f, halo in zip(nexts, halos)],
        taps[0],
    )
    store(
        dk_ref,
        ext_k,
        [back * v for back, v in zip(backs, short_v)],
        [halo[EDGE:] * v for halo, v in zip(halos, next_v)],
        taps[1],
    )
    store(
        dv_ref,
        ext_v,
        [back * k for back, k in zip(backs, short_k)],
        [halo[EDGE:] * k for halo, k in zip(halos, next_k)],
        taps[2],
    )
    if not last:
        return
    squares = jnp.zeros((1, LANES), F32)
    for dest in range(per_tile):
        parts = in_ref[dest, halo_at : halo_at + 2 * EDGE, :].astype(F32)
        squares = squares + parts[EDGE - 2 : EDGE - 1] + parts[EDGE - 1 : EDGE]

    @pl.when(step == 0)
    def _():
        total_ref[...] = jnp.zeros_like(total_ref)

    total_ref[...] = total_ref[...] + squares
    half = raw_rows.shape[0] // chunks
    for dest in range(per_tile):
        lines = in_ref[dest, halo_at + halo_rows :, :].astype(F32)
        for chunk in range(chunks):
            at = chunk * half + (step * per_tile + dest) * gpd
            raw_rows[pl.ds(at, gpd), :] = lines[chunk * gpd : (chunk + 1) * gpd]

    @pl.when(step == pl.num_programs(0) - 1)
    def _():
        factor = jnp.minimum(1.0, bound / jnp.sqrt(total_ref[...]))[:, 0:1]
        raw_ref[...] = raw_rows[...].T * factor


def after_exchange(
    returned, out_grad, key, value, tail, following, taps, groups, chunk, chunks, grads, bound
):
    n, in_rows, rows = returned.shape
    channels = out_grad.shape[1] // chunks
    cpd, gpd = channels // n, groups // (n * chunks)
    last = chunk + 1 == chunks
    tile = min(channels, max(256, cpd))
    per_tile = tile // cpd
    first = chunk * channels // tile
    block = pl.BlockSpec((rows, tile), lambda i: (0, first + i))
    ext = pltpu.VMEM((tile // LANES, rows + EDGE, LANES), F32)
    grad = jax.ShapeDtypeStruct(out_grad.shape, BF16)
    return pl.pallas_call(
        functools.partial(after_kernel, cpd, gpd, chunks, last, bound),
        grid=(channels // tile,),
        in_specs=[
            pl.BlockSpec((per_tile, in_rows, rows), lambda i: (i, 0, 0)),
            block,
            block,
            block,
            pl.BlockSpec((3 * EDGE, tile), lambda i: (0, first + i)),
            pl.BlockSpec((3 * EDGE, tile), lambda i: (0, first + i)),
            pl.BlockSpec((3, taps.shape[1], tile), lambda i: (0, 0, first + i)),
        ]
        + [pl.BlockSpec(memory_space=pl.ANY)] * len(grads),
        input_output_aliases={7 + i: i for i in range(len(grads))},
        out_specs=[block] * 3 + [pl.BlockSpec((rows, groups), lambda i: (0, 0))] * last,
        out_shape=[grad] * 3 + [jax.ShapeDtypeStruct((rows, groups), F32)] * last,
        scratch_shapes=[pltpu.VMEM((groups, rows), F32), pltpu.VMEM((1, LANES), F32)] * last
        + [ext] * 5,
        compiler_params=params(),
        cost_estimate=pl.CostEstimate(
            flops=90 * rows * channels, bytes_accessed=18 * rows * channels, transcendentals=0
        ),
        name="after_exchange",
    )(returned, out_grad, key, value, tail, following, taps, *grads)


def on_device(
    query_heads,
    key_heads,
    value_heads,
    hyena_query,
    hyena_key,
    hyena_value,
    short_filter,
    long_filter,
    output_grad,
):
    rows, channels = query_heads.shape
    groups = long_filter.shape[1]
    n = lax.axis_size("ctx")
    tp = lax.axis_size("tp")
    cpd, gpd = channels // n, groups // n
    position = lax.axis_index("ctx")
    tail = shifted(edge_rows((hyena_query, hyena_key, hyena_value), False), "ctx", 1)
    half = channels // 2
    chunks = 2 if gpd % 4 == 0 else 1
    cpd, gpd = cpd // chunks, gpd // chunks
    send = before_exchange(
        hyena_query, hyena_key, hyena_value, output_grad, tail, short_filter, long_filter, n, chunks
    )
    send, query, key, value, *sources = lax.optimization_barrier(
        (send, query_heads, key_heads, value_heads, output_grad, hyena_key, hyena_value)
    )
    received = lax.all_to_all(send, "ctx", split_axis=0, concat_axis=0, tiled=True)
    following = shifted(edge_rows(sources, True), "ctx", -1)
    query_next = shifted(query[:, :half], "ctx", -1)
    key_prev = shifted(key[:, half:], "ctx", 1)
    value_prev = value[:, half:]
    returned = []
    for chunk in range(chunks):
        raw = ()
        if chunk + 1 == chunks:
            raw, squares = filter_products(received, cpd, gpd, chunks)
            query_next, raw, squares = lax.optimization_barrier((query_next, raw, squares))
            raw = (raw, total_over(squares, "tp"))
        results = long_convs(received, raw, cpd, gpd, chunk, chunks)
        if chunks == 1:
            value_prev = shifted(value_prev, "ctx", 1)
        if chunk + 1 == chunks:
            part = attend_part(query_next, key_heads, value_heads, half, False)
            results, part, value_prev = lax.optimization_barrier((results, part, value_prev))
        if chunk == 0:
            results, received, query_next, key_prev, value_prev, following = lax.optimization_barrier(
                (results, received, query_next, key_prev, value_prev, following)
            )
            if chunks > 1:
                value_prev = shifted(value_prev, "ctx", 1)
        returned.append(lax.all_to_all(results, "ctx", split_axis=0, concat_axis=0, tiled=True))
    part = shifted(part, "ctx", 1)
    place = position.astype(jnp.int32).reshape(1)
    whole = attend_whole(query_heads, key_heads, value_heads, key_prev, value_prev, place)
    own = attend_part(query_heads, key_heads, value_heads, half, True)
    bound = math.sqrt(rows * n * groups * tp)
    grads = ()
    for chunk in range(chunks):
        if chunk > 0:
            returned[chunk], whole, own, *grads = lax.optimization_barrier(
                (returned[chunk], whole, own, *grads)
            )
        grads = after_exchange(
            returned[chunk], output_grad, hyena_key, hyena_value, tail, following, short_filter, groups,
            chunk, chunks, grads, bound,
        )
    part, *grads = lax.optimization_barrier((part, *grads))
    return (combine(own, part, whole, place), *grads)


def solution(mesh):
    whole = P("ctx", "tp")
    in_specs = (whole,) * 6 + (P(None, None, "tp"), whole, whole)
    return jax.shard_map(
        on_device, mesh=mesh, in_specs=in_specs, out_specs=(whole,) * 5, check_vma=False
    )
```

```python
import functools
import math

import jax
import jax.numpy as jnp
from jax import lax
from jax.experimental import pallas as pl
from jax.experimental.pallas import tpu as pltpu
from jax.sharding import PartitionSpec as P

HEAD_DIM = 128
LANES = 128
EDGE = 8
F32 = jnp.float32
BF16 = jnp.bfloat16
VMEM_BYTES = 60 * 1024 * 1024
LONG_VMEM = 24 * 1024 * 1024


def params(size=VMEM_BYTES):
    return pltpu.CompilerParams(vmem_limit_bytes=size)


def shifted(block, axis, distance):
    devices = range(lax.axis_size(axis))
    route = [(i - distance, i) for i in devices if i - distance in devices]
    return lax.ppermute(block, axis, route)


def total_over(value, axis):
    size = lax.axis_size(axis)
    distance = 1
    while distance < size:
        value = value + lax.ppermute(value, axis, [(i, i ^ distance) for i in range(size)])
        distance *= 2
    return value


def round_up(value, step):
    return -(-value // step) * step


def reversal(size):
    row = lax.broadcasted_iota(jnp.int32, (size, size), 0)
    col = lax.broadcasted_iota(jnp.int32, (size, size), 1)
    return jnp.where(row + col == size - 1, 1.0, 0.0).astype(BF16)


SCALE = 1.0 / math.sqrt(HEAD_DIM)
NT = (((1,), (1,)), ((), ()))


LOG_LANES = 32


def places_of(width):
    return [slice(head * HEAD_DIM, (head + 1) * HEAD_DIM) for head in range(width // HEAD_DIM)]


def attend_part_kernel(causal, q_ref, k_ref, v_ref, out_ref, logs_ref):
    rows, width = q_ref.shape
    heads = width // HEAD_DIM
    step = pl.program_id(0)
    row = lax.broadcasted_iota(jnp.int32, (rows, rows), 0)
    col = lax.broadcasted_iota(jnp.int32, (rows, rows), 1)
    lane = lax.broadcasted_iota(jnp.int32, (rows, LANES), 1)

    @pl.when(step == 0)
    def _():
        logs_ref[...] = jnp.zeros_like(logs_ref)

    places = places_of(width)
    scores = [
        lax.dot_general(q_ref[:, at], k_ref[:, at], NT, preferred_element_type=F32) * SCALE
        for at in places
    ]
    if causal:
        scores = [jnp.where(col <= row, score, -jnp.inf) for score in scores]
    largest = [jnp.max(score, axis=1, keepdims=True) for score in scores]
    raised = [jnp.exp(score - top) for score, top in zip(scores, largest)]
    totals = [jnp.sum(r, axis=1, keepdims=True) for r in raised]
    weights = [(r * (1.0 / total)).astype(BF16) for r, total in zip(raised, totals)]
    mixed = [
        jnp.dot(weight, v_ref[:, at], preferred_element_type=F32) for weight, at in zip(weights, places)
    ]
    logs = logs_ref[...]
    for head in range(heads):
        log = largest[head] + jnp.log(totals[head])
        logs = jnp.where(lane == step * heads + head, log, logs)
    logs_ref[...] = logs
    first = pl.multiple_of(step * width, LANES)
    out_ref[:, pl.ds(first, width)] = jnp.concatenate([m.astype(BF16) for m in mixed], 1)

    @pl.when(step == pl.num_programs(0) - 1)
    def _():
        upper = logs.astype(BF16).astype(F32)
        middle = (logs - upper).astype(BF16).astype(F32)
        lower = logs - upper - middle
        terms = upper + pltpu.roll(middle, LOG_LANES, 1) + pltpu.roll(lower, 2 * LOG_LANES, 1)
        out_ref[:, out_ref.shape[1] - LANES :] = terms.astype(BF16)


def combine_kernel(place_ref, own_ref, prev_ref, own_log_ref, prev_log_ref, _, out_ref, own_share, prev_share):
    rows, width = own_ref.shape
    heads = width // HEAD_DIM
    step = pl.program_id(0)
    @pl.when(step == 0)
    def _():
        def joined(ref):
            terms = ref[...].astype(F32)
            middle = pltpu.roll(terms, LANES - LOG_LANES, 1)
            return terms + (middle + pltpu.roll(terms, LANES - 2 * LOG_LANES, 1))

        own = joined(own_log_ref)
        has_prev = jnp.broadcast_to(place_ref[0], (rows, LANES)) > 0
        prev = jnp.where(has_prev, joined(prev_log_ref), -jnp.inf)
        largest = jnp.maximum(own, prev)
        own, prev = jnp.exp(own - largest), jnp.exp(prev - largest)
        inverse = 1.0 / (own + prev)
        own_share[...] = own * inverse
        prev_share[...] = prev * inverse

    row = lax.broadcasted_iota(jnp.int32, (LANES, width), 0)
    col = lax.broadcasted_iota(jnp.int32, (LANES, width), 1)
    spread = jnp.where(row == step * heads + col // HEAD_DIM, 1.0, 0.0).astype(BF16)

    def spread_out(ref):
        upper = ref[...].astype(BF16)
        lower = (ref[...] - upper.astype(F32)).astype(BF16)
        return jnp.dot(upper, spread, preferred_element_type=F32) + jnp.dot(
            lower, spread, preferred_element_type=F32
        )

    total = spread_out(own_share) * own_ref[...].astype(F32)
    total = total + spread_out(prev_share) * prev_ref[...].astype(F32)
    out_ref[...] = total.astype(BF16)


def attend_whole_kernel(place_ref, q_ref, k_ref, v_ref, kp_ref, vp_ref, out_ref):
    rows, width = q_ref.shape
    row = lax.broadcasted_iota(jnp.int32, (rows, rows), 0)
    col = lax.broadcasted_iota(jnp.int32, (rows, rows), 1)
    own_ok = col <= row
    prev_ok = jnp.broadcast_to(place_ref[0], (rows, rows)) > 0
    places = places_of(width)

    def scores(ref, allowed):
        products = [
            lax.dot_general(q_ref[:, at], ref[:, at], NT, preferred_element_type=F32) for at in places
        ]
        return [jnp.where(allowed, product * SCALE, -jnp.inf) for product in products]

    own, prev = scores(k_ref, own_ok), scores(kp_ref, prev_ok)
    largest = [jnp.max(jnp.maximum(o, p), axis=1, keepdims=True) for o, p in zip(own, prev)]
    own = [jnp.exp(o - top) for o, top in zip(own, largest)]
    prev = [jnp.exp(p - top) for p, top in zip(prev, largest)]
    totals = [jnp.sum(o + p, axis=1, keepdims=True) for o, p in zip(own, prev)]
    inverses = [1.0 / total for total in totals]
    own = [(o * inverse).astype(BF16) for o, inverse in zip(own, inverses)]
    prev = [(p * inverse).astype(BF16) for p, inverse in zip(prev, inverses)]
    mixed = [
        jnp.dot(o, v_ref[:, at], preferred_element_type=F32)
        + jnp.dot(p, vp_ref[:, at], preferred_element_type=F32)
        for o, p, at in zip(own, prev, places)
    ]
    for head, at in enumerate(places):
        out_ref[:, at] = mixed[head].astype(BF16)


def attend_cost(rows, channels):
    heads = channels // HEAD_DIM
    return pl.CostEstimate(
        flops=4 * heads * rows * rows * HEAD_DIM,
        bytes_accessed=10 * rows * channels,
        transcendentals=heads * rows * rows,
    )


def attend_part(query, key, value, channels, causal):
    rows = query.shape[0]
    tile = min(512, channels)
    block = pl.BlockSpec((rows, tile), lambda i: (0, i))
    return pl.pallas_call(
        functools.partial(attend_part_kernel, causal),
        grid=(channels // tile,),
        in_specs=[block] * 3,
        out_specs=pl.BlockSpec((rows, channels + LANES), lambda i: (0, 0)),
        out_shape=jax.ShapeDtypeStruct((rows, channels + LANES), BF16),
        scratch_shapes=[pltpu.VMEM((rows, LANES), F32)],
        compiler_params=params(LONG_VMEM),
        cost_estimate=attend_cost(rows, channels),
        name="attend_part",
    )(query, key, value)


def attend_whole(query, key, value, previous, place):
    rows, channels = query.shape
    half = channels // 2
    tile = min(512, half)
    steps = half // tile
    first = pl.BlockSpec((rows, tile), lambda i: (0, i))
    second = pl.BlockSpec((rows, tile), lambda i: (0, steps + i))
    return pl.pallas_call(
        attend_whole_kernel,
        grid=(steps,),
        in_specs=[
            pl.BlockSpec(memory_space=pltpu.SMEM),
            second,
            second,
            second,
            first,
            pl.BlockSpec((rows, tile), lambda i: (1, i)),
        ],
        out_specs=second,
        out_shape=jax.ShapeDtypeStruct((rows, channels), BF16),
        compiler_params=params(LONG_VMEM),
        cost_estimate=attend_cost(rows, channels),
        name="attend_whole",
    )(place, query, key, value, previous, previous)


def combine(own, prev, whole, place):
    rows, channels = whole.shape
    half = channels // 2
    tile = min(1024, half)
    block = pl.BlockSpec((rows, tile), lambda i: (0, i))
    log_at = half // LANES
    log = pl.BlockSpec((rows, LANES), lambda i: (0, log_at))
    share = pltpu.VMEM((rows, LANES), F32)
    return pl.pallas_call(
        combine_kernel,
        grid=(half // tile,),
        in_specs=[pl.BlockSpec(memory_space=pltpu.SMEM), block, block, log, log]
        + [pl.BlockSpec(memory_space=pl.ANY)],
        out_specs=block,
        out_shape=jax.ShapeDtypeStruct((rows, channels), BF16),
        input_output_aliases={5: 0},
        scratch_shapes=[share, share],
        compiler_params=params(),
        cost_estimate=attend_cost(rows, half // 4),
        name="combine",
    )(place, own, prev, own, prev, whole)


def edge_kernel(first, *refs):
    *sources, out_ref = refs
    parts = [r[...].astype(F32) for r in sources]
    parts = [p[:EDGE] if first else p[p.shape[0] - EDGE :] for p in parts]
    out_ref[...] = jnp.concatenate(parts, 0).astype(BF16)


def edge_rows(arrays, first):
    rows, channels = arrays[0].shape
    block = pl.BlockSpec((16, channels), lambda i: (0 if first else rows // 16 - 1, 0))
    return pl.pallas_call(
        functools.partial(edge_kernel, first),
        grid=(1,),
        in_specs=[block] * len(arrays),
        out_specs=pl.BlockSpec((len(arrays) * EDGE, channels), lambda i: (0, 0)),
        out_shape=jax.ShapeDtypeStruct((len(arrays) * EDGE, channels), BF16),
        compiler_params=params(LONG_VMEM if first else VMEM_BYTES),
        name="edge_rows",
    )(*arrays)


def taps_causal(ext_ref, befores, signals, filters):
    rows = signals[0].shape[0]
    for j, signal in enumerate(signals):
        ext_ref[j, 0:EDGE, :] = befores[j]
        ext_ref[j, EDGE : EDGE + rows, :] = signal
    totals = [taps[0:1] * signal for signal, taps in zip(signals, filters)]
    for s in range(1, filters[0].shape[0]):
        for j, taps in enumerate(filters):
            totals[j] = totals[j] + taps[s : s + 1] * ext_ref[j, EDGE - s : EDGE - s + rows, :]
    return totals


def columns_of(width):
    return [slice(j * LANES, (j + 1) * LANES) for j in range(width // LANES)]


PAIR = 2


def put_pairs(ref, dest, channel, gw, first, second):
    width = PAIR * gw
    for piece in range(first.shape[0] // width):
        at = slice(piece * width, (piece + 1) * width)
        low = 2 * (channel + piece * width)
        ref[dest, low : low + width, :] = first[at]
        ref[dest, low + width : low + 2 * width, :] = second[at]


def get_pairs(ref, dest, channel, count, gw, which):
    width = PAIR * gw
    lows = [2 * (channel + low) + which * width for low in range(0, count, width)]
    return jnp.concatenate([ref[dest, low : low + width, :] for low in lows], 0)


def before_kernel(cpd, gpd, chunks, *refs):
    *refs, long_ref, send_ref, long_rows, ext_q, ext_k, ext_v = refs
    step = pl.program_id(0)
    groups = long_ref.shape[1]
    per_tile, send_rows, rows = send_ref.shape
    gw = cpd // gpd
    filter_rows = send_rows - 2 * cpd * chunks
    half = groups // chunks

    @pl.when(step == 0)
    def _():
        long_rows[...] = jnp.zeros_like(long_rows)
        long_rows[0:groups, :] = long_ref[...].T

    turn = reversal(rows)
    for chunk in range(chunks):
        q_ref, k_ref, v_ref, og_ref, tail_ref, taps_ref = refs[6 * chunk : 6 * chunk + 6]
        places = columns_of(q_ref.shape[1])
        tails = [tail_ref[:, at].astype(F32) for at in places]

        def short(which, ref, ext, tails=tails, places=places, taps_ref=taps_ref, chunk=chunk):
            return taps_causal(
                ext.at[chunk],
                [tail[which * EDGE : (which + 1) * EDGE] for tail in tails],
                [ref[:, at].astype(F32) for at in places],
                [taps_ref[which, :, at] for at in places],
            )

        short_k, short_v = short(1, k_ref, ext_k), short(2, v_ref, ext_v)
        mixed = [(k * v).T.astype(BF16) for k, v in zip(short_k, short_v)]
        short_q = short(0, q_ref, ext_q)
        delta = [(og_ref[:, at].astype(F32) * q).T.astype(BF16) for q, at in zip(short_q, places)]
        delta = [jnp.dot(d, turn, preferred_element_type=F32).astype(BF16) for d in delta]
        width = min(cpd, LANES)
        for j in range(len(places)):
            for piece in range(LANES // width):
                channel = j * LANES + piece * width
                dest, low = channel // cpd, channel % cpd
                at = slice(piece * width, (piece + 1) * width)
                put_pairs(send_ref, dest, chunk * cpd + low, gw, mixed[j][at], delta[j][at])
    for dest in range(per_tile):
        lines = []
        for chunk in range(chunks):
            first = chunk * half + (step * per_tile + dest) * gpd
            lines.append(long_rows[pl.ds(first, filter_rows if chunks == 1 else gpd), :])
        send_ref[dest, 2 * cpd * chunks :, :] = jnp.concatenate(lines, 0).astype(BF16)


def before_exchange(query, key, value, out_grad, tail, taps, long_filter, n, chunks):
    rows, channels = query.shape
    groups = long_filter.shape[1]
    cpd, gpd = channels // (n * chunks), groups // (n * chunks)
    tile = min(channels // chunks, max(1024 // chunks, cpd))
    per_tile = tile // cpd
    filter_rows = round_up(gpd * chunks, 16)
    send_rows = 2 * cpd * chunks + filter_rows
    steps = n // per_tile
    specs = []
    for chunk in range(chunks):
        first = chunk * steps
        specs += [pl.BlockSpec((rows, tile), lambda i, f=first: (0, f + i))] * 4
        specs.append(pl.BlockSpec((3 * EDGE, tile), lambda i, f=first: (0, f + i)))
        specs.append(pl.BlockSpec((3, taps.shape[1], tile), lambda i, f=first: (0, 0, f + i)))
    ext = pltpu.VMEM((chunks, tile // LANES, rows + EDGE, LANES), F32)
    return pl.pallas_call(
        functools.partial(before_kernel, cpd, gpd, chunks),
        grid=(steps,),
        in_specs=specs + [pl.BlockSpec((rows, groups), lambda i: (0, 0))],
        out_specs=pl.BlockSpec((per_tile, send_rows, rows), lambda i: (i, 0, 0)),
        out_shape=jax.ShapeDtypeStruct((n, send_rows, rows), BF16),
        scratch_shapes=[pltpu.VMEM((round_up(groups, 8) + filter_rows, rows), F32), ext, ext, ext],
        compiler_params=params(),
        cost_estimate=pl.CostEstimate(
            flops=50 * rows * channels, bytes_accessed=12 * rows * channels, transcendentals=0
        ),
        name="before_exchange",
    )(*((query, key, value, out_grad, tail, taps) * chunks), long_filter)


def conv_kernel(cpd, gpd, chunk, in_ref, filter_ref, *refs):
    *raw_ref, out_ref, taps, wide = refs
    step = pl.program_id(0)
    n, _, rows = in_ref.shape
    gw = cpd // gpd
    span = n * rows
    slots = range(PAIR)

    @pl.when(step == 0)
    def _():
        taps[:, 0:rows] = jnp.zeros((taps.shape[0], rows), F32)
        for a in range(n):
            taps[:, (a + 1) * rows : (a + 2) * rows] = filter_ref[a].astype(F32)
        for slot in slots:
            wide[slot, :, 0:rows] = jnp.zeros((rows, rows), BF16)

    bases = []
    for slot in slots:
        line = taps[pl.ds(chunk * gpd + PAIR * step + slot, 1), :]
        line = jnp.broadcast_to(line, (16, span + rows))
        bases.append(pltpu.roll(line, 0, 1, stride=1, stride_axis=0).astype(BF16))
    for m in range(rows // 16):
        for slot in slots:
            moved = bases[slot] if m == 0 else pltpu.roll(bases[slot], 16 * m, 1)
            wide[slot, 16 * m : 16 * m + 16, rows:] = moved[:, rows:]
    stacks = []
    for slot in slots:
        x = in_ref[:, slot * gw : (slot + 1) * gw, :]
        d = in_ref[:, (PAIR + slot) * gw : (PAIR + slot + 1) * gw, :]
        both = [jnp.concatenate([x[a], d[n - 1 - a]], 0) for a in range(n)]
        stacks.append(
            jnp.concatenate([jnp.concatenate([both[a], both[a + 1]], 1) for a in range(0, n, 2)], 0)
        )
    totals = [None] * PAIR
    for k in range(n // 2):
        skip = 2 * gw * k
        low = 2 * rows * k
        for slot in slots:
            tile = jnp.concatenate(
                [wide[slot, :, low + rows : low + 3 * rows], wide[slot, :, low : low + 2 * rows]], 0
            )
            part = jnp.dot(stacks[slot][: n * gw - skip], tile, preferred_element_type=F32)
            total = totals[slot]
            totals[slot] = part if k == 0 else jnp.concatenate([total[:skip], total[skip:] + part], 0)
    for slot in slots:
        total = totals[slot]
        first = pl.multiple_of(2 * PAIR * gw * step + slot * gw, gw)
        second = pl.multiple_of(2 * PAIR * gw * step + (PAIR + slot) * gw, gw)
        for a in range(n):
            at = slice(a % 2 * rows, (a % 2 + 1) * rows)
            top = a // 2 * 2 * gw
            out_ref[a, pl.ds(first, gw), :] = total[top : top + gw, at].astype(BF16)
            out_ref[n - 1 - a, pl.ds(second, gw), :] = total[top + gw : top + 2 * gw, at].astype(BF16)

    @pl.when(step == pl.num_programs(0) - 1)
    def _():
        finish_conv(cpd, gw, out_ref, raw_ref)


def finish_conv(cpd, gw, out_ref, raw_ref):
    n, _, rows = out_ref.shape
    upper = lower = 0.0
    if raw_ref:
        *raw_ref, squares_ref = raw_ref
        upper = squares_ref[...].astype(BF16).astype(F32)
        lower = squares_ref[...] - upper
    halo_at = 2 * cpd
    row = lax.broadcasted_iota(jnp.int32, (2 * EDGE, 2 * rows), 0)
    lane = lax.broadcasted_iota(jnp.int32, (2 * EDGE, 2 * rows), 1)
    wanted = jnp.where(row < EDGE, row, 2 * rows - 1 + EDGE - row)
    pick = jnp.where(lane == wanted, 1.0, 0.0).astype(BF16)
    row_out = lax.broadcasted_iota(jnp.int32, (2 * EDGE, rows), 0)
    for a in range(n):
        if a + 1 < n:
            results = [get_pairs(out_ref, a + 1, 0, cpd, gw, which) for which in range(2)]
            results = jnp.concatenate(results, 1)
            halo = lax.dot_general(
                pick, results, (((1,), (1,)), ((), ())), preferred_element_type=F32
            )
            if cpd < LANES:
                halo = jnp.concatenate([halo, jnp.zeros((2 * EDGE, LANES - cpd), F32)], 1)
        else:
            halo = jnp.zeros((2 * EDGE, max(cpd, LANES)), F32)
        for j in range(halo.shape[1] // LANES):
            at = halo_at + 2 * EDGE * j
            tile = halo[:, j * LANES : (j + 1) * LANES]
            tile = jnp.where(row_out == EDGE - 2, upper, jnp.where(row_out == EDGE - 1, lower, tile))
            out_ref[a, at : at + 2 * EDGE, :] = tile.astype(BF16)
    for ref in raw_ref:
        out_ref[:, out_ref.shape[1] - ref.shape[1] :, :] = ref[...]


def long_convs(received, raw, cpd, gpd, chunk, chunks):
    n, send_rows, rows = received.shape
    filter_rows = send_rows - 2 * cpd * chunks
    out_rows = 2 * cpd + 2 * EDGE * max(1, cpd // LANES) + sum(r.shape[1] for r in raw[:1])
    span = n * rows
    pairs = gpd // PAIR
    pair_rows = 2 * cpd // pairs
    filter_at = 2 * cpd * chunks // filter_rows
    return pl.pallas_call(
        functools.partial(conv_kernel, cpd, gpd, chunk),
        grid=(pairs,),
        in_specs=[
            pl.BlockSpec((n, pair_rows, rows), lambda i: (0, chunk * pairs + i, 0)),
            pl.BlockSpec((n, filter_rows, rows), lambda i: (0, filter_at, 0)),
        ]
        + [pl.BlockSpec(r.shape, lambda i, r=r: (0,) * r.ndim) for r in raw],
        out_specs=pl.BlockSpec((n, out_rows, rows), lambda i: (0, 0, 0)),
        out_shape=jax.ShapeDtypeStruct((n, out_rows, rows), BF16),
        scratch_shapes=[
            pltpu.VMEM((filter_rows, span + rows), F32),
            pltpu.VMEM((PAIR, rows, span + rows), BF16),
        ],
        compiler_params=params(LONG_VMEM),
        cost_estimate=pl.CostEstimate(
            flops=4 * cpd * span * span, bytes_accessed=4 * n * out_rows * rows, transcendentals=0
        ),
        name="long_convs",
    )(received, received, *raw)


def gram_kernel(gw, in_ref, out_ref, squares_ref, gram, raw, total_ref):
    step = pl.program_id(0)
    n, _, rows = in_ref.shape
    span = n * rows
    slots = range(PAIR)

    @pl.when(step == 0)
    def _():
        for slot in slots:
            gram[slot, :, span:] = jnp.zeros((rows, rows), F32)
        raw[...] = jnp.zeros_like(raw)
        total_ref[...] = jnp.zeros_like(total_ref)

    no_rows = jnp.zeros((n * gw, rows), BF16)

    def offset(d, k):
        held = (k + 1) * gw
        if held == n * gw:
            return d
        return jnp.concatenate([d[n * gw - held :], no_rows[held:]], 0)

    turned, shifting = [], []
    for slot in slots:
        x = in_ref[:, slot * gw : (slot + 1) * gw, :].reshape(n * gw, rows)
        d = in_ref[:, (PAIR + slot) * gw : (PAIR + slot + 1) * gw, :]
        shifting.append(d.reshape(n * gw, rows))
        turned.append(x.astype(F32).T.astype(BF16))
    for k in range(0, n, 2):
        for slot in slots:
            d = shifting[slot]
            pairs = jnp.concatenate([offset(d, k), offset(d, k + 1)], 1)
            gram[slot, :, k * rows : (k + 2) * rows] = jnp.dot(
                turned[slot], pairs, preferred_element_type=F32
            )
    sums = [gram[slot, 0:8, :] for slot in slots]
    for m in range(1, rows // 8):
        for slot in slots:
            sums[slot] = sums[slot] + pltpu.roll(gram[slot, 8 * m : 8 * m + 8, :], 8 * m, 1)
    sums = [pltpu.roll(total, 0, 1, stride=1, stride_axis=0) for total in sums]
    for slot in slots:
        line = jnp.sum(sums[slot], axis=0, keepdims=True)[:, :span]
        raw[pl.ds(PAIR * step + slot, 1), :] = line
        total_ref[...] = total_ref[...] + line * line

    @pl.when(step == pl.num_programs(0) - 1)
    def _():
        squares_ref[...] = jnp.sum(total_ref[...], axis=1, keepdims=True)
        turn = reversal(rows)
        for a in range(n):
            tile = raw[:, (n - 1 - a) * rows : (n - a) * rows].astype(BF16)
            out_ref[a] = jnp.dot(tile, turn, preferred_element_type=F32).astype(BF16)


def filter_products(received, cpd, gpd, chunks):
    n, _, rows = received.shape
    span = n * rows
    raw_rows = round_up(gpd * chunks, 16)
    pairs = gpd * chunks // PAIR
    pair_rows = 2 * cpd * chunks // pairs
    return pl.pallas_call(
        functools.partial(gram_kernel, cpd // gpd),
        grid=(pairs,),
        in_specs=[pl.BlockSpec((n, pair_rows, rows), lambda i: (0, i, 0))],
        out_specs=[
            pl.BlockSpec((n, raw_rows, rows), lambda i: (0, 0, 0)),
            pl.BlockSpec((1, 1), lambda i: (0, 0)),
        ],
        out_shape=[
            jax.ShapeDtypeStruct((n, raw_rows, rows), BF16),
            jax.ShapeDtypeStruct((1, 1), F32),
        ],
        scratch_shapes=[
            pltpu.VMEM((PAIR, rows, span + rows), F32),
            pltpu.VMEM((raw_rows, span), F32),
            pltpu.VMEM((1, span), F32),
        ],
        compiler_params=params(LONG_VMEM),
        cost_estimate=pl.CostEstimate(
            flops=2 * cpd * chunks * span * span,
            bytes_accessed=2 * received.size,
            transcendentals=0,
        ),
        name="filter_products",
    )(received)


def taps_anti(ext_ref, signals, afters, filters):
    rows = signals[0].shape[0]
    for j, signal in enumerate(signals):
        ext_ref[j, 0:rows, :] = signal
        ext_ref[j, rows : rows + EDGE, :] = afters[j]
    totals = [taps[0:1] * signal for signal, taps in zip(signals, filters)]
    for s in range(1, filters[0].shape[0]):
        for j, taps in enumerate(filters):
            totals[j] = totals[j] + taps[s : s + 1] * ext_ref[j, s : s + rows, :]
    return totals


def short_edge(before, signal, filter_taps):
    both = jnp.concatenate([before, signal], 0)
    total = filter_taps[0:1] * signal
    for s in range(1, filter_taps.shape[0]):
        total = total + filter_taps[s : s + 1] * both[EDGE - s : 2 * EDGE - s]
    return total


def after_kernel(
    cpd, gpd, chunks, last, bound, in_ref, og_ref, k_ref, v_ref, tail_ref, next_ref, taps_ref, *refs
):
    *refs, ext_q, ext_k, ext_v, ext_in_k, ext_in_v = refs
    if last:
        *refs, raw_ref, raw_rows, total_ref = refs
    dq_ref, dk_ref, dv_ref = refs[-3:]
    step = pl.program_id(0)
    per_tile, in_rows, rows = in_ref.shape
    halo_rows = 2 * EDGE * max(1, cpd // LANES)
    halo_at = 2 * cpd
    turn = reversal(rows)
    places = columns_of(og_ref.shape[1])
    tails = [tail_ref[:, at].astype(F32) for at in places]
    nexts = [next_ref[:, at].astype(F32) for at in places]
    convs, backs, halos = [], [], []
    for j in range(len(places)):
        if cpd >= LANES:
            dest, low = j * LANES // cpd, j * LANES % cpd
            conv = get_pairs(in_ref, dest, low, LANES, cpd // gpd, 0)
            back = get_pairs(in_ref, dest, low, LANES, cpd // gpd, 1)
            edge = halo_at + 2 * EDGE * (low // LANES)
            halo = in_ref[dest, edge : edge + 2 * EDGE, :].astype(F32)
        else:
            dests = range(j * LANES // cpd, (j + 1) * LANES // cpd)
            conv = jnp.concatenate([get_pairs(in_ref, d, 0, cpd, cpd // gpd, 0) for d in dests], 0)
            back = jnp.concatenate([get_pairs(in_ref, d, 0, cpd, cpd // gpd, 1) for d in dests], 0)
            halo = jnp.concatenate(
                [in_ref[d, halo_at : halo_at + halo_rows, :].astype(F32)[:, :cpd] for d in dests], 1
            )
        convs.append(conv)
        backs.append(back)
        halos.append(halo)
    convs = [conv.astype(F32).T for conv in convs]
    backs = [jnp.dot(back, turn, preferred_element_type=F32) for back in backs]
    backs = [back.T for back in backs]
    taps = [[taps_ref[which, :, at] for at in places] for which in range(3)]
    keys = [k_ref[:, at].astype(F32) for at in places]
    values = [v_ref[:, at].astype(F32) for at in places]
    short_k = taps_causal(ext_in_k, [tail[EDGE : 2 * EDGE] for tail in tails], keys, taps[1])
    short_v = taps_causal(ext_in_v, [tail[2 * EDGE : 3 * EDGE] for tail in tails], values, taps[2])
    next_k = [
        short_edge(k[rows - EDGE :], f[EDGE : 2 * EDGE], t) for k, f, t in zip(keys, nexts, taps[1])
    ]
    next_v = [
        short_edge(v[rows - EDGE :], f[2 * EDGE : 3 * EDGE], t)
        for v, f, t in zip(values, nexts, taps[2])
    ]

    def store(ref, ext, signals, afters, filters):
        for at, total in zip(places, taps_anti(ext, signals, afters, filters)):
            ref[:, at] = total.astype(BF16)

    store(
        dq_ref,
        ext_q,
        [og_ref[:, at].astype(F32) * conv for at, conv in zip(places, convs)],
        [f[0:EDGE] * halo[0:EDGE] for f, halo in zip(nexts, halos)],
        taps[0],
    )
    store(
        dk_ref,
        ext_k,
        [back * v for back, v in zip(backs, short_v)],
        [halo[EDGE:] * v for halo, v in zip(halos, next_v)],
        taps[1],
    )
    store(
        dv_ref,
        ext_v,
        [back * k for back, k in zip(backs, short_k)],
        [halo[EDGE:] * k for halo, k in zip(halos, next_k)],
        taps[2],
    )
    if not last:
        return
    squares = jnp.zeros((1, LANES), F32)
    for dest in range(per_tile):
        parts = in_ref[dest, halo_at : halo_at + 2 * EDGE, :].astype(F32)
        squares = squares + parts[EDGE - 2 : EDGE - 1] + parts[EDGE - 1 : EDGE]

    @pl.when(step == 0)
    def _():
        total_ref[...] = jnp.zeros_like(total_ref)

    total_ref[...] = total_ref[...] + squares
    half = raw_rows.shape[0] // chunks
    for dest in range(per_tile):
        lines = in_ref[dest, halo_at + halo_rows :, :].astype(F32)
        for chunk in range(chunks):
            at = chunk * half + (step * per_tile + dest) * gpd
            raw_rows[pl.ds(at, gpd), :] = lines[chunk * gpd : (chunk + 1) * gpd]

    @pl.when(step == pl.num_programs(0) - 1)
    def _():
        factor = jnp.minimum(1.0, bound / jnp.sqrt(total_ref[...]))[:, 0:1]
        raw_ref[...] = raw_rows[...].T * factor


def after_exchange(
    returned, out_grad, key, value, tail, following, taps, groups, chunk, chunks, grads, bound
):
    n, in_rows, rows = returned.shape
    channels = out_grad.shape[1] // chunks
    cpd, gpd = channels // n, groups // (n * chunks)
    last = chunk + 1 == chunks
    tile = min(channels, max(512, cpd))
    per_tile = tile // cpd
    first = chunk * channels // tile
    block = pl.BlockSpec((rows, tile), lambda i: (0, first + i))
    ext = pltpu.VMEM((tile // LANES, rows + EDGE, LANES), F32)
    grad = jax.ShapeDtypeStruct(out_grad.shape, BF16)
    return pl.pallas_call(
        functools.partial(after_kernel, cpd, gpd, chunks, last, bound),
        grid=(channels // tile,),
        in_specs=[
            pl.BlockSpec((per_tile, in_rows, rows), lambda i: (i, 0, 0)),
            block,
            block,
            block,
            pl.BlockSpec((3 * EDGE, tile), lambda i: (0, first + i)),
            pl.BlockSpec((3 * EDGE, tile), lambda i: (0, first + i)),
            pl.BlockSpec((3, taps.shape[1], tile), lambda i: (0, 0, first + i)),
        ]
        + [pl.BlockSpec(memory_space=pl.ANY)] * len(grads),
        input_output_aliases={7 + i: i for i in range(len(grads))},
        out_specs=[block] * 3 + [pl.BlockSpec((rows, groups), lambda i: (0, 0))] * last,
        out_shape=[grad] * 3 + [jax.ShapeDtypeStruct((rows, groups), F32)] * last,
        scratch_shapes=[pltpu.VMEM((groups, rows), F32), pltpu.VMEM((1, LANES), F32)] * last
        + [ext] * 5,
        compiler_params=params(),
        cost_estimate=pl.CostEstimate(
            flops=90 * rows * channels, bytes_accessed=18 * rows * channels, transcendentals=0
        ),
        name="after_exchange",
    )(returned, out_grad, key, value, tail, following, taps, *grads)


def on_device(
    query_heads,
    key_heads,
    value_heads,
    hyena_query,
    hyena_key,
    hyena_value,
    short_filter,
    long_filter,
    output_grad,
):
    rows, channels = query_heads.shape
    groups = long_filter.shape[1]
    n = lax.axis_size("ctx")
    tp = lax.axis_size("tp")
    cpd, gpd = channels // n, groups // n
    position = lax.axis_index("ctx")
    tail = shifted(edge_rows((hyena_query, hyena_key, hyena_value), False), "ctx", 1)
    half = channels // 2
    chunks = 2 if gpd % 4 == 0 else 1
    cpd, gpd = cpd // chunks, gpd // chunks
    send = before_exchange(
        hyena_query, hyena_key, hyena_value, output_grad, tail, short_filter, long_filter, n, chunks
    )
    send, query, key, value, *sources = lax.optimization_barrier(
        (send, query_heads, key_heads, value_heads, output_grad, hyena_key, hyena_value)
    )
    received = lax.all_to_all(send, "ctx", split_axis=0, concat_axis=0, tiled=True)
    following = shifted(edge_rows(sources, True), "ctx", -1)
    query_next = shifted(query[:, :half], "ctx", -1)
    previous = shifted(jnp.concatenate([key[:, half:], value[:, half:]], 0), "ctx", 1)
    returned = []
    for chunk in range(chunks):
        raw = ()
        if chunk + 1 == chunks:
            raw, squares = filter_products(received, cpd, gpd, chunks)
            query_next, raw, squares = lax.optimization_barrier((query_next, raw, squares))
            raw = (raw, total_over(squares, "tp"))
        results = long_convs(received, raw, cpd, gpd, chunk, chunks)
        if chunk + 1 == chunks:
            part = attend_part(query_next, key_heads, value_heads, half, False)
            results, part = lax.optimization_barrier((results, part))
        if chunk == 0:
            results, received, query_next, previous, following = lax.optimization_barrier(
                (results, received, query_next, previous, following)
            )
        returned.append(lax.all_to_all(results, "ctx", split_axis=0, concat_axis=0, tiled=True))
    part = shifted(part, "ctx", 1)
    place = position.astype(jnp.int32).reshape(1)
    whole = attend_whole(query_heads, key_heads, value_heads, previous, place)
    own = attend_part(query_heads, key_heads, value_heads, half, True)
    bound = math.sqrt(rows * n * groups * tp)
    grads = ()
    for chunk in range(chunks):
        if chunk > 0:
            returned[chunk], whole, own, *grads = lax.optimization_barrier(
                (returned[chunk], whole, own, *grads)
            )
        grads = after_exchange(
            returned[chunk], output_grad, hyena_key, hyena_value, tail, following, short_filter, groups,
            chunk, chunks, grads, bound,
        )
    part, *grads = lax.optimization_barrier((part, *grads))
    return (combine(own, part, whole, place), *grads)


def solution(mesh):
    whole = P("ctx", "tp")
    in_specs = (whole,) * 6 + (P(None, None, "tp"), whole, whole)
    return jax.shard_map(
        on_device, mesh=mesh, in_specs=in_specs, out_specs=(whole,) * 5, check_vma=False
    )
```

```python
import functools
import math

import jax
import jax.numpy as jnp
from jax import lax
from jax.experimental import pallas as pl
from jax.experimental.pallas import tpu as pltpu
from jax.sharding import PartitionSpec as P

HEAD_DIM = 128
LANES = 128
EDGE = 8
F32 = jnp.float32
BF16 = jnp.bfloat16
VMEM_BYTES = 60 * 1024 * 1024
LONG_VMEM = 24 * 1024 * 1024


def params(size=VMEM_BYTES):
    return pltpu.CompilerParams(vmem_limit_bytes=size)


def shifted(block, axis, distance):
    devices = range(lax.axis_size(axis))
    route = [(i - distance, i) for i in devices if i - distance in devices]
    return lax.ppermute(block, axis, route)


def total_over(value, axis):
    size = lax.axis_size(axis)
    distance = 1
    while distance < size:
        value = value + lax.ppermute(value, axis, [(i, i ^ distance) for i in range(size)])
        distance *= 2
    return value


def round_up(value, step):
    return -(-value // step) * step


def reversal(size):
    row = lax.broadcasted_iota(jnp.int32, (size, size), 0)
    col = lax.broadcasted_iota(jnp.int32, (size, size), 1)
    return jnp.where(row + col == size - 1, 1.0, 0.0).astype(BF16)


SCALE = 1.0 / math.sqrt(HEAD_DIM)
NT = (((1,), (1,)), ((), ()))


LOG_LANES = 32


def places_of(width):
    return [slice(head * HEAD_DIM, (head + 1) * HEAD_DIM) for head in range(width // HEAD_DIM)]


def attend_part_kernel(causal, q_ref, k_ref, v_ref, out_ref, logs_ref):
    rows, width = q_ref.shape
    heads = width // HEAD_DIM
    step = pl.program_id(0)
    row = lax.broadcasted_iota(jnp.int32, (rows, rows), 0)
    col = lax.broadcasted_iota(jnp.int32, (rows, rows), 1)
    lane = lax.broadcasted_iota(jnp.int32, (rows, LANES), 1)

    @pl.when(step == 0)
    def _():
        logs_ref[...] = jnp.zeros_like(logs_ref)

    places = places_of(width)
    scores = [
        lax.dot_general(q_ref[:, at], k_ref[:, at], NT, preferred_element_type=F32) * SCALE
        for at in places
    ]
    if causal:
        scores = [jnp.where(col <= row, score, -jnp.inf) for score in scores]
    largest = [jnp.max(score, axis=1, keepdims=True) for score in scores]
    raised = [jnp.exp(score - top) for score, top in zip(scores, largest)]
    totals = [jnp.sum(r, axis=1, keepdims=True) for r in raised]
    weights = [(r * (1.0 / total)).astype(BF16) for r, total in zip(raised, totals)]
    mixed = [
        jnp.dot(weight, v_ref[:, at], preferred_element_type=F32) for weight, at in zip(weights, places)
    ]
    logs = logs_ref[...]
    for head in range(heads):
        log = largest[head] + jnp.log(totals[head])
        logs = jnp.where(lane == step * heads + head, log, logs)
    logs_ref[...] = logs
    first = pl.multiple_of(step * width, LANES)
    out_ref[:, pl.ds(first, width)] = jnp.concatenate([m.astype(BF16) for m in mixed], 1)

    @pl.when(step == pl.num_programs(0) - 1)
    def _():
        upper = logs.astype(BF16).astype(F32)
        middle = (logs - upper).astype(BF16).astype(F32)
        lower = logs - upper - middle
        terms = upper + pltpu.roll(middle, LOG_LANES, 1) + pltpu.roll(lower, 2 * LOG_LANES, 1)
        out_ref[:, out_ref.shape[1] - LANES :] = terms.astype(BF16)


def combine_kernel(place_ref, own_ref, prev_ref, own_log_ref, prev_log_ref, _, out_ref, own_share, prev_share):
    rows, width = own_ref.shape
    heads = width // HEAD_DIM
    step = pl.program_id(0)
    @pl.when(step == 0)
    def _():
        def joined(ref):
            terms = ref[...].astype(F32)
            middle = pltpu.roll(terms, LANES - LOG_LANES, 1)
            return terms + (middle + pltpu.roll(terms, LANES - 2 * LOG_LANES, 1))

        own = joined(own_log_ref)
        has_prev = jnp.broadcast_to(place_ref[0], (rows, LANES)) > 0
        prev = jnp.where(has_prev, joined(prev_log_ref), -jnp.inf)
        largest = jnp.maximum(own, prev)
        own, prev = jnp.exp(own - largest), jnp.exp(prev - largest)
        inverse = 1.0 / (own + prev)
        own_share[...] = own * inverse
        prev_share[...] = prev * inverse

    row = lax.broadcasted_iota(jnp.int32, (LANES, width), 0)
    col = lax.broadcasted_iota(jnp.int32, (LANES, width), 1)
    spread = jnp.where(row == step * heads + col // HEAD_DIM, 1.0, 0.0).astype(BF16)

    def spread_out(ref):
        upper = ref[...].astype(BF16)
        lower = (ref[...] - upper.astype(F32)).astype(BF16)
        return jnp.dot(upper, spread, preferred_element_type=F32) + jnp.dot(
            lower, spread, preferred_element_type=F32
        )

    total = spread_out(own_share) * own_ref[...].astype(F32)
    total = total + spread_out(prev_share) * prev_ref[...].astype(F32)
    out_ref[...] = total.astype(BF16)


def attend_whole_kernel(place_ref, q_ref, k_ref, v_ref, kp_ref, vp_ref, out_ref):
    rows, width = q_ref.shape
    row = lax.broadcasted_iota(jnp.int32, (rows, rows), 0)
    col = lax.broadcasted_iota(jnp.int32, (rows, rows), 1)
    own_ok = col <= row
    prev_ok = jnp.broadcast_to(place_ref[0], (rows, rows)) > 0
    places = places_of(width)

    def scores(ref, allowed):
        products = [
            lax.dot_general(q_ref[:, at], ref[:, at], NT, preferred_element_type=F32) for at in places
        ]
        return [jnp.where(allowed, product * SCALE, -jnp.inf) for product in products]

    own, prev = scores(k_ref, own_ok), scores(kp_ref, prev_ok)
    largest = [jnp.max(jnp.maximum(o, p), axis=1, keepdims=True) for o, p in zip(own, prev)]
    own = [jnp.exp(o - top) for o, top in zip(own, largest)]
    prev = [jnp.exp(p - top) for p, top in zip(prev, largest)]
    totals = [jnp.sum(o + p, axis=1, keepdims=True) for o, p in zip(own, prev)]
    inverses = [1.0 / total for total in totals]
    own = [(o * inverse).astype(BF16) for o, inverse in zip(own, inverses)]
    prev = [(p * inverse).astype(BF16) for p, inverse in zip(prev, inverses)]
    mixed = [
        jnp.dot(o, v_ref[:, at], preferred_element_type=F32)
        + jnp.dot(p, vp_ref[:, at], preferred_element_type=F32)
        for o, p, at in zip(own, prev, places)
    ]
    for head, at in enumerate(places):
        out_ref[:, at] = mixed[head].astype(BF16)


def attend_cost(rows, channels):
    heads = channels // HEAD_DIM
    return pl.CostEstimate(
        flops=4 * heads * rows * rows * HEAD_DIM,
        bytes_accessed=10 * rows * channels,
        transcendentals=heads * rows * rows,
    )


def attend_part(query, key, value, channels, causal):
    rows = query.shape[0]
    tile = min(512, channels)
    block = pl.BlockSpec((rows, tile), lambda i: (0, i))
    return pl.pallas_call(
        functools.partial(attend_part_kernel, causal),
        grid=(channels // tile,),
        in_specs=[block] * 3,
        out_specs=pl.BlockSpec((rows, channels + LANES), lambda i: (0, 0)),
        out_shape=jax.ShapeDtypeStruct((rows, channels + LANES), BF16),
        scratch_shapes=[pltpu.VMEM((rows, LANES), F32)],
        compiler_params=params(LONG_VMEM),
        cost_estimate=attend_cost(rows, channels),
        name="attend_part",
    )(query, key, value)


def attend_whole(query, key, value, previous, place):
    rows, channels = query.shape
    half = channels // 2
    tile = min(512, half)
    steps = half // tile
    first = pl.BlockSpec((rows, tile), lambda i: (0, i))
    second = pl.BlockSpec((rows, tile), lambda i: (0, steps + i))
    return pl.pallas_call(
        attend_whole_kernel,
        grid=(steps,),
        in_specs=[
            pl.BlockSpec(memory_space=pltpu.SMEM),
            second,
            second,
            second,
            first,
            pl.BlockSpec((rows, tile), lambda i: (1, i)),
        ],
        out_specs=second,
        out_shape=jax.ShapeDtypeStruct((rows, channels), BF16),
        compiler_params=params(LONG_VMEM),
        cost_estimate=attend_cost(rows, channels),
        name="attend_whole",
    )(place, query, key, value, previous, previous)


def combine(own, prev, whole, place):
    rows, channels = whole.shape
    half = channels // 2
    tile = min(1024, half)
    block = pl.BlockSpec((rows, tile), lambda i: (0, i))
    log_at = half // LANES
    log = pl.BlockSpec((rows, LANES), lambda i: (0, log_at))
    share = pltpu.VMEM((rows, LANES), F32)
    return pl.pallas_call(
        combine_kernel,
        grid=(half // tile,),
        in_specs=[pl.BlockSpec(memory_space=pltpu.SMEM), block, block, log, log]
        + [pl.BlockSpec(memory_space=pl.ANY)],
        out_specs=block,
        out_shape=jax.ShapeDtypeStruct((rows, channels), BF16),
        input_output_aliases={5: 0},
        scratch_shapes=[share, share],
        compiler_params=params(),
        cost_estimate=attend_cost(rows, half // 4),
        name="combine",
    )(place, own, prev, own, prev, whole)


def edge_kernel(first, *refs):
    *sources, out_ref = refs
    parts = [r[...].astype(F32) for r in sources]
    parts = [p[:EDGE] if first else p[p.shape[0] - EDGE :] for p in parts]
    out_ref[...] = jnp.concatenate(parts, 0).astype(BF16)


def edge_rows(arrays, first):
    rows, channels = arrays[0].shape
    block = pl.BlockSpec((16, channels), lambda i: (0 if first else rows // 16 - 1, 0))
    return pl.pallas_call(
        functools.partial(edge_kernel, first),
        grid=(1,),
        in_specs=[block] * len(arrays),
        out_specs=pl.BlockSpec((len(arrays) * EDGE, channels), lambda i: (0, 0)),
        out_shape=jax.ShapeDtypeStruct((len(arrays) * EDGE, channels), BF16),
        compiler_params=params(LONG_VMEM if first else VMEM_BYTES),
        name="edge_rows",
    )(*arrays)


def taps_causal(ext_ref, befores, signals, filters):
    rows = signals[0].shape[0]
    for j, signal in enumerate(signals):
        ext_ref[j, 0:EDGE, :] = befores[j]
        ext_ref[j, EDGE : EDGE + rows, :] = signal
    totals = [taps[0:1] * signal for signal, taps in zip(signals, filters)]
    for s in range(1, filters[0].shape[0]):
        for j, taps in enumerate(filters):
            totals[j] = totals[j] + taps[s : s + 1] * ext_ref[j, EDGE - s : EDGE - s + rows, :]
    return totals


def columns_of(width):
    return [slice(j * LANES, (j + 1) * LANES) for j in range(width // LANES)]


PAIR = 2


def put_pairs(ref, dest, channel, gw, first, second):
    width = PAIR * gw
    for piece in range(first.shape[0] // width):
        at = slice(piece * width, (piece + 1) * width)
        low = 2 * (channel + piece * width)
        ref[dest, low : low + width, :] = first[at]
        ref[dest, low + width : low + 2 * width, :] = second[at]


def get_pairs(ref, dest, channel, count, gw, which):
    width = PAIR * gw
    lows = [2 * (channel + low) + which * width for low in range(0, count, width)]
    return jnp.concatenate([ref[dest, low : low + width, :] for low in lows], 0)


def before_kernel(cpd, gpd, chunks, *refs):
    *refs, long_ref, send_ref, long_rows, ext_q, ext_k, ext_v = refs
    step = pl.program_id(0)
    groups = long_ref.shape[1]
    per_tile, send_rows, rows = send_ref.shape
    gw = cpd // gpd
    filter_rows = send_rows - 2 * cpd * chunks
    half = groups // chunks

    @pl.when(step == 0)
    def _():
        long_rows[...] = jnp.zeros_like(long_rows)
        long_rows[0:groups, :] = long_ref[...].T

    turn = reversal(rows)
    for chunk in range(chunks):
        q_ref, k_ref, v_ref, og_ref, tail_ref, taps_ref = refs[6 * chunk : 6 * chunk + 6]
        places = columns_of(q_ref.shape[1])
        tails = [tail_ref[:, at].astype(F32) for at in places]

        def short(which, ref, ext, tails=tails, places=places, taps_ref=taps_ref, chunk=chunk):
            return taps_causal(
                ext.at[chunk],
                [tail[which * EDGE : (which + 1) * EDGE] for tail in tails],
                [ref[:, at].astype(F32) for at in places],
                [taps_ref[which, :, at] for at in places],
            )

        short_k, short_v = short(1, k_ref, ext_k), short(2, v_ref, ext_v)
        mixed = [(k * v).T.astype(BF16) for k, v in zip(short_k, short_v)]
        short_q = short(0, q_ref, ext_q)
        delta = [(og_ref[:, at].astype(F32) * q).T.astype(BF16) for q, at in zip(short_q, places)]
        delta = [jnp.dot(d, turn, preferred_element_type=F32).astype(BF16) for d in delta]
        width = min(cpd, LANES)
        for j in range(len(places)):
            for piece in range(LANES // width):
                channel = j * LANES + piece * width
                dest, low = channel // cpd, channel % cpd
                at = slice(piece * width, (piece + 1) * width)
                put_pairs(send_ref, dest, chunk * cpd + low, gw, mixed[j][at], delta[j][at])
    for dest in range(per_tile):
        lines = []
        for chunk in range(chunks):
            first = chunk * half + (step * per_tile + dest) * gpd
            lines.append(long_rows[pl.ds(first, filter_rows if chunks == 1 else gpd), :])
        send_ref[dest, 2 * cpd * chunks :, :] = jnp.concatenate(lines, 0).astype(BF16)


def before_exchange(query, key, value, out_grad, tail, taps, long_filter, n, chunks):
    rows, channels = query.shape
    groups = long_filter.shape[1]
    cpd, gpd = channels // (n * chunks), groups // (n * chunks)
    tile = min(channels // chunks, max(1024 // chunks, cpd))
    per_tile = tile // cpd
    filter_rows = round_up(gpd * chunks, 16)
    send_rows = 2 * cpd * chunks + filter_rows
    steps = n // per_tile
    specs = []
    for chunk in range(chunks):
        first = chunk * steps
        specs += [pl.BlockSpec((rows, tile), lambda i, f=first: (0, f + i))] * 4
        specs.append(pl.BlockSpec((3 * EDGE, tile), lambda i, f=first: (0, f + i)))
        specs.append(pl.BlockSpec((3, taps.shape[1], tile), lambda i, f=first: (0, 0, f + i)))
    ext = pltpu.VMEM((chunks, tile // LANES, rows + EDGE, LANES), F32)
    return pl.pallas_call(
        functools.partial(before_kernel, cpd, gpd, chunks),
        grid=(steps,),
        in_specs=specs + [pl.BlockSpec((rows, groups), lambda i: (0, 0))],
        out_specs=pl.BlockSpec((per_tile, send_rows, rows), lambda i: (i, 0, 0)),
        out_shape=jax.ShapeDtypeStruct((n, send_rows, rows), BF16),
        scratch_shapes=[pltpu.VMEM((round_up(groups, 8) + filter_rows, rows), F32), ext, ext, ext],
        compiler_params=params(),
        cost_estimate=pl.CostEstimate(
            flops=50 * rows * channels, bytes_accessed=12 * rows * channels, transcendentals=0
        ),
        name="before_exchange",
    )(*((query, key, value, out_grad, tail, taps) * chunks), long_filter)


def conv_kernel(cpd, gpd, chunk, in_ref, filter_ref, *refs):
    *raw_ref, out_ref, taps, wide = refs
    step = pl.program_id(0)
    n, _, rows = in_ref.shape
    gw = cpd // gpd
    span = n * rows
    slots = range(PAIR)

    @pl.when(step == 0)
    def _():
        taps[:, 0:rows] = jnp.zeros((taps.shape[0], rows), F32)
        for a in range(n):
            taps[:, (a + 1) * rows : (a + 2) * rows] = filter_ref[a].astype(F32)
        for slot in slots:
            wide[slot, :, 0:rows] = jnp.zeros((rows, rows), BF16)

    bases = []
    for slot in slots:
        line = taps[pl.ds(chunk * gpd + PAIR * step + slot, 1), :]
        line = jnp.broadcast_to(line, (16, span + rows))
        bases.append(pltpu.roll(line, 0, 1, stride=1, stride_axis=0).astype(BF16))
    for m in range(rows // 16):
        for slot in slots:
            moved = bases[slot] if m == 0 else pltpu.roll(bases[slot], 16 * m, 1)
            wide[slot, 16 * m : 16 * m + 16, rows:] = moved[:, rows:]
    stacks = []
    for slot in slots:
        x = in_ref[:, slot * gw : (slot + 1) * gw, :]
        d = in_ref[:, (PAIR + slot) * gw : (PAIR + slot + 1) * gw, :]
        both = [jnp.concatenate([x[a], d[n - 1 - a]], 0) for a in range(n)]
        stacks.append(
            jnp.concatenate([jnp.concatenate([both[a], both[a + 1]], 1) for a in range(0, n, 2)], 0)
        )
    totals = [None] * PAIR
    for k in range(n // 2):
        skip = 2 * gw * k
        low = 2 * rows * k
        for slot in slots:
            tile = jnp.concatenate(
                [wide[slot, :, low + rows : low + 3 * rows], wide[slot, :, low : low + 2 * rows]], 0
            )
            part = jnp.dot(stacks[slot][: n * gw - skip], tile, preferred_element_type=F32)
            total = totals[slot]
            totals[slot] = part if k == 0 else jnp.concatenate([total[:skip], total[skip:] + part], 0)
    for slot in slots:
        total = totals[slot]
        first = pl.multiple_of(2 * PAIR * gw * step + slot * gw, gw)
        second = pl.multiple_of(2 * PAIR * gw * step + (PAIR + slot) * gw, gw)
        for a in range(n):
            at = slice(a % 2 * rows, (a % 2 + 1) * rows)
            top = a // 2 * 2 * gw
            out_ref[a, pl.ds(first, gw), :] = total[top : top + gw, at].astype(BF16)
            out_ref[n - 1 - a, pl.ds(second, gw), :] = total[top + gw : top + 2 * gw, at].astype(BF16)

    @pl.when(step == pl.num_programs(0) - 1)
    def _():
        finish_conv(cpd, gw, out_ref, raw_ref)


def finish_conv(cpd, gw, out_ref, raw_ref):
    n, _, rows = out_ref.shape
    upper = lower = 0.0
    if raw_ref:
        *raw_ref, squares_ref = raw_ref
        upper = squares_ref[...].astype(BF16).astype(F32)
        lower = squares_ref[...] - upper
    halo_at = 2 * cpd
    row = lax.broadcasted_iota(jnp.int32, (2 * EDGE, 2 * rows), 0)
    lane = lax.broadcasted_iota(jnp.int32, (2 * EDGE, 2 * rows), 1)
    wanted = jnp.where(row < EDGE, row, 2 * rows - 1 + EDGE - row)
    pick = jnp.where(lane == wanted, 1.0, 0.0).astype(BF16)
    row_out = lax.broadcasted_iota(jnp.int32, (2 * EDGE, rows), 0)
    for a in range(n):
        if a + 1 < n:
            results = [get_pairs(out_ref, a + 1, 0, cpd, gw, which) for which in range(2)]
            results = jnp.concatenate(results, 1)
            halo = lax.dot_general(
                pick, results, (((1,), (1,)), ((), ())), preferred_element_type=F32
            )
            if cpd < LANES:
                halo = jnp.concatenate([halo, jnp.zeros((2 * EDGE, LANES - cpd), F32)], 1)
        else:
            halo = jnp.zeros((2 * EDGE, max(cpd, LANES)), F32)
        for j in range(halo.shape[1] // LANES):
            at = halo_at + 2 * EDGE * j
            tile = halo[:, j * LANES : (j + 1) * LANES]
            tile = jnp.where(row_out == EDGE - 2, upper, jnp.where(row_out == EDGE - 1, lower, tile))
            out_ref[a, at : at + 2 * EDGE, :] = tile.astype(BF16)
    for ref in raw_ref:
        out_ref[:, out_ref.shape[1] - ref.shape[1] :, :] = ref[...]


def long_convs(received, raw, cpd, gpd, chunk, chunks):
    n, send_rows, rows = received.shape
    filter_rows = send_rows - 2 * cpd * chunks
    out_rows = 2 * cpd + 2 * EDGE * max(1, cpd // LANES) + sum(r.shape[1] for r in raw[:1])
    span = n * rows
    pairs = gpd // PAIR
    pair_rows = 2 * cpd // pairs
    filter_at = 2 * cpd * chunks // filter_rows
    return pl.pallas_call(
        functools.partial(conv_kernel, cpd, gpd, chunk),
        grid=(pairs,),
        in_specs=[
            pl.BlockSpec((n, pair_rows, rows), lambda i: (0, chunk * pairs + i, 0)),
            pl.BlockSpec((n, filter_rows, rows), lambda i: (0, filter_at, 0)),
        ]
        + [pl.BlockSpec(r.shape, lambda i, r=r: (0,) * r.ndim) for r in raw],
        out_specs=pl.BlockSpec((n, out_rows, rows), lambda i: (0, 0, 0)),
        out_shape=jax.ShapeDtypeStruct((n, out_rows, rows), BF16),
        scratch_shapes=[
            pltpu.VMEM((filter_rows, span + rows), F32),
            pltpu.VMEM((PAIR, rows, span + rows), BF16),
        ],
        compiler_params=params(LONG_VMEM),
        cost_estimate=pl.CostEstimate(
            flops=4 * cpd * span * span, bytes_accessed=4 * n * out_rows * rows, transcendentals=0
        ),
        name="long_convs",
    )(received, received, *raw)


def gram_kernel(gw, in_ref, out_ref, squares_ref, gram, raw, total_ref):
    step = pl.program_id(0)
    n, _, rows = in_ref.shape
    span = n * rows
    slots = range(PAIR)

    @pl.when(step == 0)
    def _():
        for slot in slots:
            gram[slot, :, span:] = jnp.zeros((rows, rows), F32)
        raw[...] = jnp.zeros_like(raw)
        total_ref[...] = jnp.zeros_like(total_ref)

    no_rows = jnp.zeros((n * gw, rows), BF16)

    def offset(d, k):
        held = (k + 1) * gw
        if held == n * gw:
            return d
        return jnp.concatenate([d[n * gw - held :], no_rows[held:]], 0)

    turned, shifting = [], []
    for slot in slots:
        x = in_ref[:, slot * gw : (slot + 1) * gw, :].reshape(n * gw, rows)
        d = in_ref[:, (PAIR + slot) * gw : (PAIR + slot + 1) * gw, :]
        shifting.append(d.reshape(n * gw, rows))
        turned.append(x.astype(F32).T.astype(BF16))
    for k in range(0, n, 2):
        for slot in slots:
            d = shifting[slot]
            pairs = jnp.concatenate([offset(d, k), offset(d, k + 1)], 1)
            gram[slot, :, k * rows : (k + 2) * rows] = jnp.dot(
                turned[slot], pairs, preferred_element_type=F32
            )
    sums = [gram[slot, 0:8, :] for slot in slots]
    for m in range(1, rows // 8):
        for slot in slots:
            sums[slot] = sums[slot] + pltpu.roll(gram[slot, 8 * m : 8 * m + 8, :], 8 * m, 1)
    sums = [pltpu.roll(total, 0, 1, stride=1, stride_axis=0) for total in sums]
    for slot in slots:
        line = jnp.sum(sums[slot], axis=0, keepdims=True)[:, :span]
        raw[pl.ds(PAIR * step + slot, 1), :] = line
        total_ref[...] = total_ref[...] + line * line

    @pl.when(step == pl.num_programs(0) - 1)
    def _():
        squares_ref[...] = jnp.sum(total_ref[...], axis=1, keepdims=True)
        turn = reversal(rows)
        for a in range(n):
            tile = raw[:, (n - 1 - a) * rows : (n - a) * rows].astype(BF16)
            out_ref[a] = jnp.dot(tile, turn, preferred_element_type=F32).astype(BF16)


def filter_products(received, cpd, gpd, chunks):
    n, _, rows = received.shape
    span = n * rows
    raw_rows = round_up(gpd * chunks, 16)
    pairs = gpd * chunks // PAIR
    pair_rows = 2 * cpd * chunks // pairs
    return pl.pallas_call(
        functools.partial(gram_kernel, cpd // gpd),
        grid=(pairs,),
        in_specs=[pl.BlockSpec((n, pair_rows, rows), lambda i: (0, i, 0))],
        out_specs=[
            pl.BlockSpec((n, raw_rows, rows), lambda i: (0, 0, 0)),
            pl.BlockSpec((1, 1), lambda i: (0, 0)),
        ],
        out_shape=[
            jax.ShapeDtypeStruct((n, raw_rows, rows), BF16),
            jax.ShapeDtypeStruct((1, 1), F32),
        ],
        scratch_shapes=[
            pltpu.VMEM((PAIR, rows, span + rows), F32),
            pltpu.VMEM((raw_rows, span), F32),
            pltpu.VMEM((1, span), F32),
        ],
        compiler_params=params(LONG_VMEM),
        cost_estimate=pl.CostEstimate(
            flops=2 * cpd * chunks * span * span,
            bytes_accessed=2 * received.size,
            transcendentals=0,
        ),
        name="filter_products",
    )(received)


def taps_anti(ext_ref, signals, afters, filters):
    rows = signals[0].shape[0]
    for j, signal in enumerate(signals):
        ext_ref[j, 0:rows, :] = signal
        ext_ref[j, rows : rows + EDGE, :] = afters[j]
    totals = [taps[0:1] * signal for signal, taps in zip(signals, filters)]
    for s in range(1, filters[0].shape[0]):
        for j, taps in enumerate(filters):
            totals[j] = totals[j] + taps[s : s + 1] * ext_ref[j, s : s + rows, :]
    return totals


def short_edge(before, signal, filter_taps):
    both = jnp.concatenate([before, signal], 0)
    total = filter_taps[0:1] * signal
    for s in range(1, filter_taps.shape[0]):
        total = total + filter_taps[s : s + 1] * both[EDGE - s : 2 * EDGE - s]
    return total


def after_kernel(
    cpd, gpd, chunks, last, bound, in_ref, og_ref, k_ref, v_ref, tail_ref, next_ref, taps_ref, *refs
):
    *refs, ext_q, ext_k, ext_v, ext_in_k, ext_in_v = refs
    if last:
        *refs, raw_ref, raw_rows, total_ref = refs
    dq_ref, dk_ref, dv_ref = refs[-3:]
    step = pl.program_id(0)
    per_tile, in_rows, rows = in_ref.shape
    halo_rows = 2 * EDGE * max(1, cpd // LANES)
    halo_at = 2 * cpd
    turn = reversal(rows)
    places = columns_of(og_ref.shape[1])
    tails = [tail_ref[:, at].astype(F32) for at in places]
    nexts = [next_ref[:, at].astype(F32) for at in places]
    convs, backs, halos = [], [], []
    for j in range(len(places)):
        if cpd >= LANES:
            dest, low = j * LANES // cpd, j * LANES % cpd
            conv = get_pairs(in_ref, dest, low, LANES, cpd // gpd, 0)
            back = get_pairs(in_ref, dest, low, LANES, cpd // gpd, 1)
            edge = halo_at + 2 * EDGE * (low // LANES)
            halo = in_ref[dest, edge : edge + 2 * EDGE, :].astype(F32)
        else:
            dests = range(j * LANES // cpd, (j + 1) * LANES // cpd)
            conv = jnp.concatenate([get_pairs(in_ref, d, 0, cpd, cpd // gpd, 0) for d in dests], 0)
            back = jnp.concatenate([get_pairs(in_ref, d, 0, cpd, cpd // gpd, 1) for d in dests], 0)
            halo = jnp.concatenate(
                [in_ref[d, halo_at : halo_at + halo_rows, :].astype(F32)[:, :cpd] for d in dests], 1
            )
        convs.append(conv)
        backs.append(back)
        halos.append(halo)
    convs = [conv.astype(F32).T for conv in convs]
    backs = [jnp.dot(back, turn, preferred_element_type=F32) for back in backs]
    backs = [back.T for back in backs]
    taps = [[taps_ref[which, :, at] for at in places] for which in range(3)]
    keys = [k_ref[:, at].astype(F32) for at in places]
    values = [v_ref[:, at].astype(F32) for at in places]
    short_k = taps_causal(ext_in_k, [tail[EDGE : 2 * EDGE] for tail in tails], keys, taps[1])
    short_v = taps_causal(ext_in_v, [tail[2 * EDGE : 3 * EDGE] for tail in tails], values, taps[2])
    next_k = [
        short_edge(k[rows - EDGE :], f[EDGE : 2 * EDGE], t) for k, f, t in zip(keys, nexts, taps[1])
    ]
    next_v = [
        short_edge(v[rows - EDGE :], f[2 * EDGE : 3 * EDGE], t)
        for v, f, t in zip(values, nexts, taps[2])
    ]

    def store(ref, ext, signals, afters, filters):
        for at, total in zip(places, taps_anti(ext, signals, afters, filters)):
            ref[:, at] = total.astype(BF16)

    store(
        dq_ref,
        ext_q,
        [og_ref[:, at].astype(F32) * conv for at, conv in zip(places, convs)],
        [f[0:EDGE] * halo[0:EDGE] for f, halo in zip(nexts, halos)],
        taps[0],
    )
    store(
        dk_ref,
        ext_k,
        [back * v for back, v in zip(backs, short_v)],
        [halo[EDGE:] * v for halo, v in zip(halos, next_v)],
        taps[1],
    )
    store(
        dv_ref,
        ext_v,
        [back * k for back, k in zip(backs, short_k)],
        [halo[EDGE:] * k for halo, k in zip(halos, next_k)],
        taps[2],
    )
    if not last:
        return
    squares = jnp.zeros((1, LANES), F32)
    for dest in range(per_tile):
        parts = in_ref[dest, halo_at : halo_at + 2 * EDGE, :].astype(F32)
        squares = squares + parts[EDGE - 2 : EDGE - 1] + parts[EDGE - 1 : EDGE]

    @pl.when(step == 0)
    def _():
        total_ref[...] = jnp.zeros_like(total_ref)

    total_ref[...] = total_ref[...] + squares
    half = raw_rows.shape[0] // chunks
    for dest in range(per_tile):
        lines = in_ref[dest, halo_at + halo_rows :, :].astype(F32)
        for chunk in range(chunks):
            at = chunk * half + (step * per_tile + dest) * gpd
            raw_rows[pl.ds(at, gpd), :] = lines[chunk * gpd : (chunk + 1) * gpd]

    @pl.when(step == pl.num_programs(0) - 1)
    def _():
        factor = jnp.minimum(1.0, bound / jnp.sqrt(total_ref[...]))[:, 0:1]
        raw_ref[...] = raw_rows[...].T * factor


def after_exchange(
    returned, out_grad, key, value, tail, following, taps, groups, chunk, chunks, grads, bound
):
    n, in_rows, rows = returned.shape
    channels = out_grad.shape[1] // chunks
    cpd, gpd = channels // n, groups // (n * chunks)
    last = chunk + 1 == chunks
    tile = min(channels, max(1024, cpd))
    per_tile = tile // cpd
    first = chunk * channels // tile
    block = pl.BlockSpec((rows, tile), lambda i: (0, first + i))
    ext = pltpu.VMEM((tile // LANES, rows + EDGE, LANES), F32)
    grad = jax.ShapeDtypeStruct(out_grad.shape, BF16)
    return pl.pallas_call(
        functools.partial(after_kernel, cpd, gpd, chunks, last, bound),
        grid=(channels // tile,),
        in_specs=[
            pl.BlockSpec((per_tile, in_rows, rows), lambda i: (i, 0, 0)),
            block,
            block,
            block,
            pl.BlockSpec((3 * EDGE, tile), lambda i: (0, first + i)),
            pl.BlockSpec((3 * EDGE, tile), lambda i: (0, first + i)),
            pl.BlockSpec((3, taps.shape[1], tile), lambda i: (0, 0, first + i)),
        ]
        + [pl.BlockSpec(memory_space=pl.ANY)] * len(grads),
        input_output_aliases={7 + i: i for i in range(len(grads))},
        out_specs=[block] * 3 + [pl.BlockSpec((rows, groups), lambda i: (0, 0))] * last,
        out_shape=[grad] * 3 + [jax.ShapeDtypeStruct((rows, groups), F32)] * last,
        scratch_shapes=[pltpu.VMEM((groups, rows), F32), pltpu.VMEM((1, LANES), F32)] * last
        + [ext] * 5,
        compiler_params=params(),
        cost_estimate=pl.CostEstimate(
            flops=90 * rows * channels, bytes_accessed=18 * rows * channels, transcendentals=0
        ),
        name="after_exchange",
    )(returned, out_grad, key, value, tail, following, taps, *grads)


def on_device(
    query_heads,
    key_heads,
    value_heads,
    hyena_query,
    hyena_key,
    hyena_value,
    short_filter,
    long_filter,
    output_grad,
):
    rows, channels = query_heads.shape
    groups = long_filter.shape[1]
    n = lax.axis_size("ctx")
    tp = lax.axis_size("tp")
    cpd, gpd = channels // n, groups // n
    position = lax.axis_index("ctx")
    tail = shifted(edge_rows((hyena_query, hyena_key, hyena_value), False), "ctx", 1)
    half = channels // 2
    chunks = 2 if gpd % 4 == 0 else 1
    cpd, gpd = cpd // chunks, gpd // chunks
    send = before_exchange(
        hyena_query, hyena_key, hyena_value, output_grad, tail, short_filter, long_filter, n, chunks
    )
    send, query, key, value, *sources = lax.optimization_barrier(
        (send, query_heads, key_heads, value_heads, output_grad, hyena_key, hyena_value)
    )
    received = lax.all_to_all(send, "ctx", split_axis=0, concat_axis=0, tiled=True)
    following = shifted(edge_rows(sources, True), "ctx", -1)
    query_next = shifted(query[:, :half], "ctx", -1)
    previous = shifted(jnp.concatenate([key[:, half:], value[:, half:]], 0), "ctx", 1)
    returned = []
    for chunk in range(chunks):
        raw = ()
        if chunk + 1 == chunks:
            raw, squares = filter_products(received, cpd, gpd, chunks)
            query_next, raw, squares = lax.optimization_barrier((query_next, raw, squares))
            raw = (raw, total_over(squares, "tp"))
        results = long_convs(received, raw, cpd, gpd, chunk, chunks)
        if chunk + 1 == chunks:
            part = attend_part(query_next, key_heads, value_heads, half, False)
            results, part = lax.optimization_barrier((results, part))
        if chunk == 0:
            results, received, query_next, previous, following = lax.optimization_barrier(
                (results, received, query_next, previous, following)
            )
        returned.append(lax.all_to_all(results, "ctx", split_axis=0, concat_axis=0, tiled=True))
    part = shifted(part, "ctx", 1)
    place = position.astype(jnp.int32).reshape(1)
    whole = attend_whole(query_heads, key_heads, value_heads, previous, place)
    own = attend_part(query_heads, key_heads, value_heads, half, True)
    bound = math.sqrt(rows * n * groups * tp)
    grads = ()
    for chunk in range(chunks):
        if chunk > 0:
            returned[chunk], whole, own, *grads = lax.optimization_barrier(
                (returned[chunk], whole, own, *grads)
            )
        grads = after_exchange(
            returned[chunk], output_grad, hyena_key, hyena_value, tail, following, short_filter, groups,
            chunk, chunks, grads, bound,
        )
    part, *grads = lax.optimization_barrier((part, *grads))
    return (combine(own, part, whole, place), *grads)


def solution(mesh):
    whole = P("ctx", "tp")
    in_specs = (whole,) * 6 + (P(None, None, "tp"), whole, whole)
    return jax.shard_map(
        on_device, mesh=mesh, in_specs=in_specs, out_specs=(whole,) * 5, check_vma=False
    )
```
